32 devices in a mesh: dp: 2 (over core), seq: 16 (over z, y, x).
Axes of the slice: x: 2, y: 2, z: 4, core: 2. Of those that a mesh axis runs over, the one named last changes fastest.
Arguments:
- byte_ids: int32 [2, 2304], P('dp', 'seq'), may hold values from 0 to 255
- targets: int32 [2, 2304], P('dp', 'seq'), may hold values from 0 to 255
- item_lengths: int32 [2, 8], P('dp'), may hold values from 1 to 576, 2304 in all within a row
- w_qkv: float32 [2, 512, 1536], P(None, ('dp', 'seq')), may hold values from -0.25 to 0.25
- w_out: float32 [2, 512, 512], P(None, ('dp', 'seq')), may hold values from -2 to 2
- w_up: float32 [2, 512, 2048], P(None, ('dp', 'seq')), may hold values from -0.25 to 0.25
- w_down: float32 [2, 2048, 512], P(None, ('dp', 'seq')), may hold values from -0.125 to 0.125
- embed: float32 [256, 512], P(('dp', 'seq')), may hold values from -6 to 6
- head: float32 [512, 256], P(('dp', 'seq')), may hold values from -0.25 to 0.25
- gains: float32 [5, 512], P(None, ('dp', 'seq')), may hold values from 0.35 to 3.25
- mom_qkv: float32 [2, 512, 1536], P(None, ('dp', 'seq')), may hold values from -4.7683716e-06 to 4.7683716e-06
- mom_out: float32 [2, 512, 512], P(None, ('dp', 'seq')), may hold values from -4.7683716e-06 to 4.7683716e-06
- mom_up: float32 [2, 512, 2048], P(None, ('dp', 'seq')), may hold values from -4.7683716e-06 to 4.7683716e-06
- mom_down: float32 [2, 2048, 512], P(None, ('dp', 'seq')), may hold values from -4.7683716e-06 to 4.7683716e-06
- mom_embed: float32 [256, 512], P(('dp', 'seq')), may hold values from -4.7683716e-06 to 4.7683716e-06
- mom_head: float32 [512, 256], P(('dp', 'seq')), may hold values from -4.7683716e-06 to 4.7683716e-06
- mom_gains: float32 [5, 512], P(None, ('dp', 'seq')), may hold values from -7.6293945e-05 to 7.6293945e-05
- sec_qkv: float32 [2, 512, 1536], P(None, ('dp', 'seq')), may hold values from 3.2030945e-12 to 1.2812378e-11
- sec_out: float32 [2, 512, 512], P(None, ('dp', 'seq')), may hold values from 3.2030945e-12 to 1.2812378e-11
- sec_up: float32 [2, 512, 2048], P(None, ('dp', 'seq')), may hold values from 3.2030945e-12 to 1.2812378e-11
- sec_down: float32 [2, 2048, 512], P(None, ('dp', 'seq')), may hold values from 3.2030945e-12 to 1.2812378e-11
- sec_embed: float32 [256, 512], P(('dp', 'seq')), may hold values from 3.2030945e-12 to 1.2812378e-11
- sec_head: float32 [512, 256], P(('dp', 'seq')), may hold values from 3.2030945e-12 to 1.2812378e-11
- sec_gains: float32 [5, 512], P(None, ('dp', 'seq')), may hold values from 3.8132077e-11 to 1.5252831e-10
Outputs:
- loss_sum: float32 [], replicated
- grad_norm: float32 [], replicated
- w_qkv_new: float32 [2, 512, 1536], P(None, ('dp', 'seq'))
- w_out_new: float32 [2, 512, 512], P(None, ('dp', 'seq'))
- w_up_new: float32 [2, 512, 2048], P(None, ('dp', 'seq'))
- w_down_new: float32 [2, 2048, 512], P(None, ('dp', 'seq'))
- embed_new: float32 [256, 512], P(('dp', 'seq'))
- head_new: float32 [512, 256], P(('dp', 'seq'))
- gains_new: float32 [5, 512], P(None, ('dp', 'seq'))
- mom_qkv_new: float32 [2, 512, 1536], P(None, ('dp', 'seq'))
- mom_out_new: float32 [2, 512, 512], P(None, ('dp', 'seq'))
- mom_up_new: float32 [2, 512, 2048], P(None, ('dp', 'seq'))
- mom_down_new: float32 [2, 2048, 512], P(None, ('dp', 'seq'))
- mom_embed_new: float32 [256, 512], P(('dp', 'seq'))
- mom_head_new: float32 [512, 256], P(('dp', 'seq'))
- mom_gains_new: float32 [5, 512], P(None, ('dp', 'seq'))
- sec_qkv_new: float32 [2, 512, 1536], P(None, ('dp', 'seq'))
- sec_out_new: float32 [2, 512, 512], P(None, ('dp', 'seq'))
- sec_up_new: float32 [2, 512, 2048], P(None, ('dp', 'seq'))
- sec_down_new: float32 [2, 2048, 512], P(None, ('dp', 'seq'))
- sec_embed_new: float32 [256, 512], P(('dp', 'seq'))
- sec_head_new: float32 [512, 256], P(('dp', 'seq'))
- sec_gains_new: float32 [5, 512], P(None, ('dp', 'seq'))
The draws below stay inside these ranges and needn't reach their ends.
Inputs may be any that keep to these rules, and one draw needn't show every extreme that they name: `item_lengths`: the item lengths of each group add up to 2304; the longest is exactly 576.
All inputs are finite; a program needn't handle non-finite values.
Results may differ from the reference program's by a relative error of at most 0.02.
Values may be sent and summed in bfloat16 or wider, within the bound.
A program may use at most 576 MiB of HBM per device.

```python
import math
import jax
import jax.numpy as jnp
import numpy as np
from jax import lax

D = 512
HEADS = 8
FF = 2048
VOCAB = 256
LAYERS = 2
RATE = 3
ITEMS = 8
STEP = 10
GROUPS = 2
TOKENS = 2304
ITEM_MAX = 576
GAINS = 5
PARAMS = 6556160


def draw_gains(key, part):
    key = jax.random.fold_in(key, 11)
    ramp = jnp.arange(D, dtype=jnp.float32) / D
    rising = 0.6 + 1.2 * ramp
    jitter = jax.random.uniform(key, (GAINS, D), jnp.float32, 0.85, 1.15)
    return rising[None, :] * jitter


def plant(result, stream_key, smallest, largest):
    shape = result.shape
    place = [jax.random.randint(jax.random.fold_in(stream_key, axis), (), 0, shape[axis]) for axis in range(len(shape))]
    result = result.at[tuple(place)].set(smallest)
    longest = shape.index(max(shape))
    place[longest] = (place[longest] + 1) % shape[longest]
    return result.at[tuple(place)].set(largest)


def block_scale(own_key, dims, shards, low, largest):
    level, own = 1.0, jax.random.fold_in(own_key, 6)
    for axis_at, shards_of in shards:
        heights = jnp.exp(jax.random.uniform(jax.random.fold_in(own, axis_at), (shards_of,), jnp.float32, low / len(shards), largest / len(shards)))
        level = level * jnp.repeat(heights, dims[axis_at] // shards_of).reshape([-1 if axis == axis_at else 1 for axis in range(len(dims))])
    return level


def rank_table(count, lean):
    portions = [(1 << 20) // math.isqrt(standing ** lean) + 1 for standing in range(1, count + 1)]
    scale = 1 + sum(portions) // (1 << 30)
    return np.cumsum(np.array([max(1, weight // scale) for weight in portions]))


def skewed_ids(stream_key, dims, count, lean):
    listing = rank_table(count, lean)
    pick = jax.random.randint(jax.random.fold_in(stream_key, 1), dims, 0, int(listing[count - 1]))
    grade = jnp.searchsorted(jnp.asarray(listing, jnp.int32), pick, side="right")
    return jax.random.permutation(jax.random.fold_in(stream_key, 2), count)[grade].astype(jnp.int32)


def profile(count, total, most, slope):
    weights = [(1 << 20) // math.isqrt(standing ** slope) + 1 for standing in range(2, count + 1)]
    spare, counts = total - most - (count - 1), [1] * (count - 1)
    while spare > 0:
        movable = [i for i in range(count - 1) if counts[i] < most]
        mass, left = sum([weights[i] for i in movable]), spare
        for i in movable:
            more = min(most - counts[i], max(1, left * weights[i] // mass), spare)
            counts[i] = counts[i] + more
            spare = spare - more
    return np.array([most] + counts)


def ragged_sizes(key, count, total, reach, skew):
    if count == 2:
        one = jax.random.randint(key, (), max(1, total - reach), min(reach, total - 1) + 1)
        return jnp.stack([one, total - one])
    tallies = jnp.asarray(profile(count, total, reach, skew), jnp.int32)
    twos = (count - 1) // 2
    source_of, sink = tallies[1:1 + 2 * twos:2], tallies[2:2 + 2 * twos:2]
    room = jnp.minimum(source_of - 1, reach - sink)
    moved = jax.random.randint(jax.random.fold_in(key, 1), (twos,), 0, 1 << 20) % (room + 1)
    tallies = tallies.at[1:1 + 2 * twos:2].set(source_of - moved).at[2:2 + 2 * twos:2].set(sink + moved)
    return tallies[jax.random.permutation(jax.random.fold_in(key, 2), count)]


def normal_values(key, dims, deviation, most, split=(), kind=jnp.bfloat16):
    result = jax.random.normal(key, dims, jnp.float32) * deviation
    if len(split) > 0:
        result = block_scale(key, dims, split, -0.22, 0.18) * result
    return jnp.clip(result, min=-most, max=most).astype(kind)


def setup_inputs(seed: int = 0) -> dict:
    streams_of = jax.random.split(jax.random.key(seed), 25)
    return {
        "byte_ids": plant(skewed_ids(streams_of[0], (GROUPS, TOKENS), VOCAB, 2), jax.random.fold_in(streams_of[0], 3), 0, VOCAB - 1).astype(jnp.int32),
        "targets": plant(skewed_ids(streams_of[1], (GROUPS, TOKENS), VOCAB, 2), jax.random.fold_in(streams_of[1], 3), 0, VOCAB - 1).astype(jnp.int32),
        "item_lengths": jax.vmap(lambda own: ragged_sizes(own, ITEMS, TOKENS, ITEM_MAX, 2))(jax.random.split(streams_of[2], GROUPS)).reshape((GROUPS, ITEMS)).astype(jnp.int32),
        "w_qkv": normal_values(streams_of[3], (LAYERS, D, 3 * D), D ** -0.5, 0.25, ((1, 32),), jnp.float32),
        "w_out": normal_values(streams_of[4], (LAYERS, D, D), (D // 64) ** -0.5, 2.0, ((1, 32),), jnp.float32),
        "w_up": normal_values(streams_of[5], (LAYERS, D, FF), D ** -0.5, 0.25, ((1, 32),), jnp.float32),
        "w_down": normal_values(streams_of[6], (LAYERS, FF, D), FF ** -0.5, 0.125, ((1, 32),), jnp.float32),
        "embed": normal_values(streams_of[7], (VOCAB, D), 1.0, 6.0, ((0, 32),), jnp.float32),
        "head": normal_values(streams_of[8], (D, VOCAB), D ** -0.5, 0.25, ((0, 32),), jnp.float32),
        "gains": draw_gains(jax.random.fold_in(streams_of[24], 71), 0),
        "mom_qkv": normal_values(streams_of[10], (LAYERS, D, 3 * D), (0.0022 / PARAMS ** 0.5), 4.76837158203125e-06, ((1, 32),), jnp.float32),
        "mom_out": normal_values(streams_of[11], (LAYERS, D, D), (0.0022 / PARAMS ** 0.5), 4.76837158203125e-06, ((1, 32),), jnp.float32),
        "mom_up": normal_values(streams_of[12], (LAYERS, D, FF), (0.0022 / PARAMS ** 0.5), 4.76837158203125e-06, ((1, 32),), jnp.float32),
        "mom_down": normal_values(streams_of[13], (LAYERS, FF, D), (0.0022 / PARAMS ** 0.5), 4.76837158203125e-06, ((1, 32),), jnp.float32),
        "mom_embed": normal_values(streams_of[14], (VOCAB, D), (0.0022 / PARAMS ** 0.5), 4.76837158203125e-06, ((0, 32),), jnp.float32),
        "mom_head": normal_values(streams_of[15], (D, VOCAB), (0.0022 / PARAMS ** 0.5), 4.76837158203125e-06, ((0, 32),), jnp.float32),
        "mom_gains": normal_values(streams_of[16], (GAINS, D), (0.035 / PARAMS ** 0.5), 7.62939453125e-05, ((1, 32),), jnp.float32),
        "sec_qkv": jnp.clip(jnp.exp(math.log(1.2812377894744209e-11) - 1.3862944 * jax.random.uniform(streams_of[17], (LAYERS, D, 3 * D), jnp.float32) ** block_scale(streams_of[17], (LAYERS, D, 3 * D), ((1, 32),), -0.2, 0.2)), 3.2030944736860523e-12, 1.2812377894744209e-11),
        "sec_out": jnp.clip(jnp.exp(math.log(1.2812377894744209e-11) - 1.3862944 * jax.random.uniform(streams_of[18], (LAYERS, D, D), jnp.float32) ** block_scale(streams_of[18], (LAYERS, D, D), ((1, 32),), -0.2, 0.2)), 3.2030944736860523e-12, 1.2812377894744209e-11),
        "sec_up": jnp.clip(jnp.exp(math.log(1.2812377894744209e-11) - 1.3862944 * jax.random.uniform(streams_of[19], (LAYERS, D, FF), jnp.float32) ** block_scale(streams_of[19], (LAYERS, D, FF), ((1, 32),), -0.2, 0.2)), 3.2030944736860523e-12, 1.2812377894744209e-11),
        "sec_down": jnp.clip(jnp.exp(math.log(1.2812377894744209e-11) - 1.3862944 * jax.random.uniform(streams_of[20], (LAYERS, FF, D), jnp.float32) ** block_scale(streams_of[20], (LAYERS, FF, D), ((1, 32),), -0.2, 0.2)), 3.2030944736860523e-12, 1.2812377894744209e-11),
        "sec_embed": jnp.clip(jnp.exp(math.log(1.2812377894744209e-11) - 1.3862944 * jax.random.uniform(streams_of[21], (VOCAB, D), jnp.float32) ** block_scale(streams_of[21], (VOCAB, D), ((0, 32),), -0.2, 0.2)), 3.2030944736860523e-12, 1.2812377894744209e-11),
        "sec_head": jnp.clip(jnp.exp(math.log(1.2812377894744209e-11) - 1.3862944 * jax.random.uniform(streams_of[22], (D, VOCAB), jnp.float32) ** block_scale(streams_of[22], (D, VOCAB), ((0, 32),), -0.2, 0.2)), 3.2030944736860523e-12, 1.2812377894744209e-11),
        "sec_gains": jnp.clip(jnp.exp(math.log(1.525283094272467e-10) - 1.3862944 * jax.random.uniform(streams_of[23], (GAINS, D), jnp.float32) ** block_scale(streams_of[23], (GAINS, D), ((1, 32),), -0.2, 0.2)), 3.813207735681168e-11, 1.525283094272467e-10),
    }


CLIP_NORM = 0.02
BETA_ONE = 0.9
BETA_TWO = 0.95
STEP_RATES = (0.03, 0.2, 0.03, 0.03, 0.6, 0.03, 0.2)
WEIGHT_DECAYS = (0.1, 0.1, 0.1, 0.1, 0.1, 0.1, 0.0)
EPSILON = 1e-08
NORM_EPS = 1e-05
MASK_FILL = -1e+30
HIGHEST = lax.Precision.HIGHEST

@jax.custom_vjp
def low(v):
    return lax.optimization_barrier(v.astype(jnp.bfloat16)).astype(jnp.float32)

@jax.custom_vjp
def low_back(v):
    return v

def low_keep(v):
    return (low(v), None)

def low_pass(kept, grad):
    return (grad,)

def back_keep(v):
    return (v, None)

def back_low(kept, grad):
    return (low(grad),)
low.defvjp(low_keep, low_pass)
low_back.defvjp(back_keep, back_low)

def layer_norm(values, gain):
    center = values - lax.optimization_barrier(jnp.mean(values, axis=-1, keepdims=True))
    spread = lax.optimization_barrier(jnp.mean(center * center, axis=-1, keepdims=True))
    return center * lax.rsqrt(spread + NORM_EPS) * gain

def rotate(joined, positions, num_heads):
    parts = joined.reshape(joined.shape[0], 3, num_heads, -1)
    half_size = parts.shape[-1] // 2
    freqs = 10000.0 ** (-jnp.arange(half_size, dtype=jnp.float32) / half_size)
    angles = positions.astype(jnp.float32)[:, None] * freqs[None, :]
    cosine = jnp.cos(angles)[:, None, :]
    sine = jnp.sin(angles)[:, None, :]

    def rotate_half(values):
        first_half = values[..., :half_size]
        second_half = values[..., half_size:]
        return jnp.concatenate([first_half * cosine - second_half * sine, first_half * sine + second_half * cosine], axis=-1)
    return (rotate_half(parts[:, 0]), rotate_half(parts[:, 1]), parts[:, 2])

def attention(queries, keys, values, positions):
    length, num_heads, head_size = queries.shape
    blocks = 16
    score_scale = head_size ** (-0.5)

    def one_block(block_args):
        query_block, query_pos = block_args
        scores = low_back(jnp.einsum('rhe,phe->hrp', query_block, keys, precision=HIGHEST) * score_scale)
        causal = query_pos[:, None] >= positions[None, :]
        attn_prob = jax.nn.softmax(jnp.where(causal[None], scores, MASK_FILL), axis=-1)
        return jnp.einsum('hrp,phe->rhe', low(attn_prob), values, precision=HIGHEST)
    outputs = lax.map(jax.checkpoint(one_block), (queries.reshape(blocks, length // blocks, num_heads, head_size), positions.reshape(blocks, length // blocks)))
    return outputs.reshape(length, num_heads, head_size)

def layer(hidden, positions, w_joined, w_proj, w_rise, w_fall, gain_attn, gain_ffn):
    normed = low(layer_norm(hidden, gain_attn))
    joined = low_back(jnp.dot(normed, w_joined, precision=HIGHEST))
    queries, keys, values = rotate(joined, positions, HEADS)
    attended = attention(low(queries), low(keys), low(values), positions)
    attended = low_back(low(attended)).reshape(hidden.shape[0], -1)
    middle = hidden + low_back(jnp.dot(attended, w_proj, precision=HIGHEST))
    second = low(layer_norm(middle, gain_ffn))
    pre_act = low_back(jnp.dot(second, w_rise, precision=HIGHEST))
    activated = low(jax.nn.gelu(pre_act))
    return middle + low_back(jnp.dot(activated, w_fall, precision=HIGHEST))

def group_loss(weights, byte_row, target_row, lengths):
    w_qkv, w_out, w_up, w_down, embed, head, gains = weights
    positions = jnp.arange(TOKENS, dtype=jnp.int32)
    first_out = layer(embed[byte_row], positions, w_qkv[0], w_out[0], w_up[0], w_down[0], gains[0], gains[1])
    shifted = jnp.concatenate([jnp.zeros((RATE - 1, D), jnp.float32), first_out[:TOKENS - RATE + 1]], axis=0)
    pooled = lax.optimization_barrier(jnp.mean(shifted.reshape(TOKENS // RATE, RATE, D), axis=1))
    short_pos = jnp.arange(TOKENS // RATE, dtype=jnp.int32)
    short_out = layer(pooled, short_pos, w_qkv[1], w_out[1], w_up[1], w_down[1], gains[2], gains[3])
    upsampled = first_out + jnp.repeat(short_out, RATE, axis=0)
    final = low(layer_norm(upsampled, gains[GAINS - 1]))
    logits = low_back(jnp.dot(final, head, precision=HIGHEST))
    log_total = jax.nn.logsumexp(logits, axis=-1)
    picked = jnp.take_along_axis(logits, target_row[:, None], axis=1)[:, 0]
    ends = jnp.cumsum(lengths)
    doc_index = lax.optimization_barrier(jnp.sum((positions[:, None] >= ends[None, :]).astype(jnp.int32), axis=1))
    doc_length = lengths[doc_index].astype(jnp.float32)
    return jnp.sum((log_total - picked) / doc_length)

def adam_update(weight, gradient, moment_one, moment_two, step_rate, decay_rate):
    moment_one = BETA_ONE * moment_one + (1.0 - BETA_ONE) * gradient
    moment_two = BETA_TWO * moment_two + (1.0 - BETA_TWO) * gradient * gradient
    first_hat = moment_one / (1.0 - BETA_ONE ** STEP)
    second_hat = moment_two / (1.0 - BETA_TWO ** STEP)
    weight = weight - step_rate * (first_hat / (jnp.sqrt(second_hat) + EPSILON) + decay_rate * weight)
    return (weight, moment_one, moment_two)

def reference(byte_ids, targets, item_lengths, w_qkv, w_out, w_up, w_down, embed, head, gains, mom_qkv, mom_out, mom_up, mom_down, mom_embed, mom_head, mom_gains, sec_qkv, sec_out, sec_up, sec_down, sec_embed, sec_head, sec_gains):
    masters = (w_qkv, w_out, w_up, w_down, embed, head, gains)

    def total_loss(params):
        lowered = tuple((low(master) for master in params))
        loss_total = jnp.zeros((), jnp.float32)
        for group_index in range(GROUPS):
            loss_total = loss_total + group_loss(lowered, byte_ids[group_index], targets[group_index], item_lengths[group_index])
        return loss_total
    loss_sum, pull_back = jax.vjp(total_loss, masters)
    gradients = pull_back(jnp.ones((), jnp.float32))[0]
    grad_norm = jnp.sqrt(sum((jnp.sum(gradient * gradient) for gradient in gradients)))
    clip_factor = jnp.minimum(1.0, CLIP_NORM / grad_norm)
    firsts = (mom_qkv, mom_out, mom_up, mom_down, mom_embed, mom_head, mom_gains)
    seconds = (sec_qkv, sec_out, sec_up, sec_down, sec_embed, sec_head, sec_gains)
    results = []
    for slot_index in range(7):
        results.append(adam_update(masters[slot_index], gradients[slot_index] * clip_factor, firsts[slot_index], seconds[slot_index], STEP_RATES[slot_index], WEIGHT_DECAYS[slot_index]))
    return (loss_sum, grad_norm, results[0][0], results[1][0], results[2][0], results[3][0], results[4][0], results[5][0], results[6][0], results[0][1], results[1][1], results[2][1], results[3][1], results[4][1], results[5][1], results[6][1], results[0][2], results[1][2], results[2][2], results[3][2], results[4][2], results[5][2], results[6][2])
```

```python
import functools

import jax
import jax.numpy as jnp
from jax import lax
from jax.experimental import pallas as pl
from jax.experimental.pallas import tpu as pltpu
from jax.sharding import PartitionSpec as P

HEADS = 8
VOCAB = 256
RATE = 3
STEP = 10

CLIP_NORM = 0.02
BETA_ONE = 0.9
BETA_TWO = 0.95
STEP_RATES = (0.03, 0.2, 0.03, 0.03, 0.6, 0.03, 0.2)
WEIGHT_DECAYS = (0.1, 0.1, 0.1, 0.1, 0.1, 0.1, 0.0)
EPSILON = 1e-08
NORM_EPS = 1e-05
MASK_FILL = -1e30


def shifted_2(value, axis, steps):
    count = lax.axis_size(axis)
    leading, last = (max(0, -steps), min(count, count - steps))
    return lax.ppermute(value, axis, [(source, source + steps) for source in range(leading, last)])


def to_low(values):
    return values.astype(jnp.bfloat16)


def layer_norm(values, gain):
    center = values - jnp.mean(values, axis=-1, keepdims=True)
    spread = jnp.mean(center * center, axis=-1, keepdims=True)
    return center * lax.rsqrt(spread + NORM_EPS) * gain


def rotate(joined, positions, num_heads):
    parts = joined.reshape(joined.shape[0], 3, num_heads, -1)
    half_size = parts.shape[-1] // 2
    freqs = 10000.0 ** (-jnp.arange(half_size, dtype=jnp.float32) / half_size)
    angles = positions.astype(jnp.float32)[:, None] * freqs[None, :]
    cosine = jnp.cos(angles)[:, None, :]
    sine = jnp.sin(angles)[:, None, :]

    def rotate_half(values):
        first_half = values[..., :half_size]
        second_half = values[..., half_size:]
        return jnp.concatenate(
            [first_half * cosine - second_half * sine, first_half * sine + second_half * cosine],
            axis=-1,
        )

    return (rotate_half(parts[:, 0]), rotate_half(parts[:, 1]), parts[:, 2])


def scores_for(q_low, k_low, query_pos, key_pos):
    scores = jnp.einsum(
        "rhe,phe->hrp", q_low, k_low, preferred_element_type=jnp.float32
    ) * q_low.shape[-1] ** (-0.5)
    causal = query_pos[:, None] >= key_pos[None, :]
    return (scores, causal)


def attend(q_low, k_low, v_low, query_pos):
    num_rows, num_heads, head_size = q_low.shape
    key_piece = (
        lax.all_gather(k_low, "seq", axis=0, tiled=True),
        lax.all_gather(v_low, "seq", axis=0, tiled=True),
    )
    running_max = jnp.full((num_heads, num_rows), MASK_FILL, jnp.float32)
    accum = jnp.zeros((num_rows, num_heads, head_size), jnp.float32)
    key_pos = jnp.arange(key_piece[0].shape[0], dtype=jnp.int32)
    scores, causal = scores_for(q_low, key_piece[0], query_pos, key_pos)
    scores = jnp.where(causal[None], scores, MASK_FILL)
    new_max = jnp.maximum(running_max, jnp.max(scores, axis=-1))
    factor = jnp.exp(running_max - new_max)
    attn_prob = jnp.where(causal[None], jnp.exp(scores - new_max[..., None]), 0.0)
    denom = jnp.sum(attn_prob, axis=-1)
    accum = accum * factor.T[:, :, None] + jnp.einsum(
        "hrp,phe->rhe", to_low(attn_prob), key_piece[1], preferred_element_type=jnp.float32
    )
    running_max, denom, accum = (new_max, denom, accum)
    return (accum / denom.T[:, :, None], (running_max + jnp.log(denom)).T)


def block_grads(q_low, grad_low, log_total, row_delta, query_pos, k_low, v_low, key_pos):
    scores, causal = scores_for(q_low, k_low, query_pos, key_pos)
    attn_prob = jnp.where(causal[None], jnp.exp(scores - log_total.T[:, :, None]), 0.0)
    grad_prob = jnp.einsum("rhe,phe->hrp", grad_low, v_low, preferred_element_type=jnp.float32)
    grad_score = to_low(attn_prob * (grad_prob - row_delta.T[:, :, None]))
    score_scale = q_low.shape[-1] ** (-0.5)
    grad_q = (
        jnp.einsum("hrp,phe->rhe", grad_score, k_low, preferred_element_type=jnp.float32)
        * score_scale
    )
    grad_k = (
        jnp.einsum("hrp,rhe->phe", grad_score, q_low, preferred_element_type=jnp.float32)
        * score_scale
    )
    grad_v = jnp.einsum(
        "hrp,rhe->phe", to_low(attn_prob), grad_low, preferred_element_type=jnp.float32
    )
    return (grad_q, grad_k, grad_v)


def attend_back(q_low, k_low, v_low, grad_low, log_total, row_delta, query_pos):
    key_piece = (
        lax.all_gather(k_low, "seq", axis=0, tiled=True),
        lax.all_gather(v_low, "seq", axis=0, tiled=True),
    )
    key_pos = jnp.arange(key_piece[0].shape[0], dtype=jnp.int32)
    grad_q = block_grads(
        q_low, grad_low, log_total, row_delta, query_pos, key_piece[0], key_piece[1], key_pos
    )[0]
    all_totals, all_deltas = (
        lax.all_gather(log_total, "seq", axis=0, tiled=True),
        lax.all_gather(row_delta, "seq", axis=0, tiled=True),
    )
    query_piece = (
        lax.all_gather(q_low, "seq", axis=0, tiled=True),
        lax.all_gather(grad_low, "seq", axis=0, tiled=True),
    )
    piece_rows = query_piece[0].shape[0]
    piece_pos = jnp.arange(piece_rows, dtype=jnp.int32)
    unused_q, grad_k_blk, grad_v_blk = block_grads(
        query_piece[0], query_piece[1], all_totals, all_deltas, piece_pos, k_low, v_low, query_pos
    )
    return (grad_q, grad_k_blk, grad_v_blk)


def layer_forward(hidden, weights, gain_pair, positions):
    w_joined, w_proj, w_rise, w_fall = weights
    num_rows = hidden.shape[0]
    normed = to_low(layer_norm(hidden, gain_pair[0]))
    joined = jnp.dot(normed, w_joined, preferred_element_type=jnp.float32)
    queries, keys, values = rotate(joined, positions, HEADS)
    q_low, k_low, v_low = (to_low(queries), to_low(keys), to_low(values))
    attended, log_total = attend(q_low, k_low, v_low, positions)
    flat_low = to_low(attended.reshape(num_rows, -1))
    middle = hidden + jnp.dot(flat_low, w_proj, preferred_element_type=jnp.float32)
    second = to_low(layer_norm(middle, gain_pair[1]))
    pre_act = jnp.dot(second, w_rise, preferred_element_type=jnp.float32)
    activated = to_low(jax.nn.gelu(pre_act))
    output = middle + jnp.dot(activated, w_fall, preferred_element_type=jnp.float32)
    saved = (
        normed,
        joined,
        q_low,
        k_low,
        v_low,
        attended,
        log_total,
        flat_low,
        middle,
        second,
        pre_act,
        activated,
    )
    return (output, saved)


def layer_backward(hidden, weights, gain_pair, positions, grad_out):
    w_joined, w_proj, w_rise, w_fall = weights
    unused_out, saved = layer_forward(hidden, weights, gain_pair, positions)
    (
        normed,
        joined,
        q_low,
        k_low,
        v_low,
        attended,
        log_total,
        flat_low,
        middle,
        second,
        pre_act,
        activated,
    ) = saved
    fall_low = to_low(grad_out)
    grad_fall = jnp.dot(activated.T, fall_low, preferred_element_type=jnp.float32)
    grad_act = jnp.dot(fall_low, w_fall.T, preferred_element_type=jnp.float32)
    grad_pre = to_low(jax.vjp(jax.nn.gelu, pre_act)[1](grad_act)[0])
    grad_rise = jnp.dot(second.T, grad_pre, preferred_element_type=jnp.float32)
    grad_second = jnp.dot(grad_pre, w_rise.T, preferred_element_type=jnp.float32)
    grad_middle_n, grad_gain_ffn = jax.vjp(layer_norm, middle, gain_pair[1])[1](grad_second)
    grad_middle = grad_out + grad_middle_n
    proj_low = to_low(grad_middle)
    grad_proj = jnp.dot(flat_low.T, proj_low, preferred_element_type=jnp.float32)
    grad_att = to_low(
        jnp.dot(proj_low, w_proj.T, preferred_element_type=jnp.float32).reshape(attended.shape)
    )
    row_delta = jnp.sum(grad_att.astype(jnp.float32) * attended, axis=-1)
    grad_q, grad_k, grad_v = attend_back(
        q_low, k_low, v_low, grad_att, log_total, row_delta, positions
    )

    def rotate_joined(joined_in):
        return rotate(joined_in, positions, HEADS)

    grad_joined = to_low(jax.vjp(rotate_joined, joined)[1]((grad_q, grad_k, grad_v))[0])
    grad_w_joined = jnp.dot(normed.T, grad_joined, preferred_element_type=jnp.float32)
    grad_normed = jnp.dot(grad_joined, w_joined.T, preferred_element_type=jnp.float32)
    grad_in_n, grad_gain_attn = jax.vjp(layer_norm, hidden, gain_pair[0])[1](grad_normed)
    return (
        grad_middle + grad_in_n,
        (grad_w_joined, grad_proj, grad_rise, grad_fall),
        jnp.stack([grad_gain_attn, grad_gain_ffn]),
    )


def adam_update(weight, gradient, moment_one, moment_two, step_rate, decay_rate):
    moment_one = BETA_ONE * moment_one + (1.0 - BETA_ONE) * gradient
    moment_two = BETA_TWO * moment_two + (1.0 - BETA_TWO) * gradient * gradient
    first_hat = moment_one / (1.0 - BETA_ONE**STEP)
    second_hat = moment_two / (1.0 - BETA_TWO**STEP)
    weight = weight - step_rate * (
        first_hat / (jnp.sqrt(second_hat) + EPSILON) + decay_rate * weight
    )
    return (weight, moment_one, moment_two)


def on_device_general(
    byte_ids,
    targets,
    item_lengths,
    w_qkv,
    w_out,
    w_up,
    w_down,
    embed,
    head,
    gains,
    mom_qkv,
    mom_out,
    mom_up,
    mom_down,
    mom_embed,
    mom_head,
    mom_gains,
    sec_qkv,
    sec_out,
    sec_up,
    sec_down,
    sec_embed,
    sec_head,
    sec_gains,
):
    low_qkv, low_out, low_up, low_down, low_embed, low_head, low_gains = (
        lax.all_gather(to_low(w_qkv), ("dp", "seq"), axis=1, tiled=True),
        lax.all_gather(to_low(w_out), ("dp", "seq"), axis=1, tiled=True),
        lax.all_gather(to_low(w_up), ("dp", "seq"), axis=1, tiled=True),
        lax.all_gather(to_low(w_down), ("dp", "seq"), axis=1, tiled=True),
        lax.all_gather(to_low(embed), ("dp", "seq"), axis=0, tiled=True),
        lax.all_gather(to_low(head), ("dp", "seq"), axis=0, tiled=True),
        lax.all_gather(to_low(gains), ("dp", "seq"), axis=1, tiled=True),
    )
    gain_rows = low_gains.astype(jnp.float32)
    byte_row = byte_ids[0]
    num_rows = byte_row.shape[0]
    short_rows = num_rows // RATE
    seq_place = lax.axis_index("seq")
    positions = seq_place * num_rows + jnp.arange(num_rows, dtype=jnp.int32)
    short_pos = seq_place * short_rows + jnp.arange(short_rows, dtype=jnp.int32)
    vocab_ids = jnp.arange(VOCAB, dtype=jnp.int32)
    one_hot_in = (byte_row[:, None] == vocab_ids[None, :]).astype(jnp.float32)
    embedded = jnp.dot(
        one_hot_in.astype(jnp.bfloat16), low_embed, preferred_element_type=jnp.float32
    )
    lower_weights = (low_qkv[0], low_out[0], low_up[0], low_down[0])
    upper_weights = (low_qkv[1], low_out[1], low_up[1], low_down[1])
    first_out, unused_first = layer_forward(embedded, lower_weights, gain_rows[0:2], positions)
    left_rim = shifted_2(first_out[num_rows - RATE + 1 :], "seq", 1)
    shifted = jnp.concatenate([left_rim, first_out[: num_rows - RATE + 1]], axis=0)
    pooled = jnp.mean(shifted.reshape(short_rows, RATE, -1), axis=1)
    short_out, unused_short = layer_forward(pooled, upper_weights, gain_rows[2:4], short_pos)
    upsampled = first_out + jnp.repeat(short_out, RATE, axis=0)
    top_gain = gain_rows[gain_rows.shape[0] - 1]
    final_low = to_low(layer_norm(upsampled, top_gain))
    logits = jnp.dot(final_low, low_head, preferred_element_type=jnp.float32)
    row_max = jnp.max(logits, axis=-1, keepdims=True)
    log_total = row_max[:, 0] + jnp.log(jnp.sum(jnp.exp(logits - row_max), axis=-1))
    one_hot_out = (targets[0][:, None] == vocab_ids[None, :]).astype(jnp.float32)
    picked = jnp.sum(one_hot_out * logits, axis=-1)
    lengths = item_lengths[0]
    ends = jnp.cumsum(lengths)
    doc_index = jnp.sum((positions[:, None] >= ends[None, :]).astype(jnp.int32), axis=1)
    item_ids = jnp.arange(lengths.shape[0], dtype=jnp.int32)
    doc_length = jnp.sum(
        jnp.where(item_ids[None, :] == doc_index[:, None], lengths[None, :], 0), axis=1
    ).astype(jnp.float32)
    loss_local = jnp.sum((log_total - picked) / doc_length)
    loss_sum = lax.psum(loss_local, ("dp", "seq"))
    grad_logits = to_low((jnp.exp(logits - log_total[:, None]) - one_hot_out) / doc_length[:, None])
    grad_head = jnp.dot(final_low.T, grad_logits, preferred_element_type=jnp.float32)
    grad_final = jnp.dot(grad_logits, low_head.T, preferred_element_type=jnp.float32)
    grad_upsampled, grad_gain_top = jax.vjp(layer_norm, upsampled, top_gain)[1](grad_final)
    grad_short = jnp.sum(grad_upsampled.reshape(short_rows, RATE, -1), axis=1)
    grad_pooled, upper_grads, upper_gain_grads = layer_backward(
        pooled, upper_weights, gain_rows[2:4], short_pos, grad_short
    )
    grad_shifted = jnp.repeat(grad_pooled / RATE, RATE, axis=0)
    rim_grad = shifted_2(grad_shifted[: RATE - 1], "seq", -1)
    grad_first = grad_upsampled + jnp.concatenate([grad_shifted[RATE - 1 :], rim_grad], axis=0)
    grad_embedded, lower_grads, lower_gain_grads = layer_backward(
        embedded, lower_weights, gain_rows[0:2], positions, grad_first
    )
    grad_embed = jnp.dot(one_hot_in.T, grad_embedded, precision=lax.Precision.HIGHEST)
    grad_gains = jnp.concatenate(
        [lower_gain_grads, upper_gain_grads, grad_gain_top[None, :]], axis=0
    )
    shard_grads = (
        lax.psum_scatter(
            jnp.stack([lower_grads[0], upper_grads[0]]),
            ("dp", "seq"),
            scatter_dimension=1,
            tiled=True,
        ),
        lax.psum_scatter(
            jnp.stack([lower_grads[1], upper_grads[1]]),
            ("dp", "seq"),
            scatter_dimension=1,
            tiled=True,
        ),
        lax.psum_scatter(
            jnp.stack([lower_grads[2], upper_grads[2]]),
            ("dp", "seq"),
            scatter_dimension=1,
            tiled=True,
        ),
        lax.psum_scatter(
            jnp.stack([lower_grads[3], upper_grads[3]]),
            ("dp", "seq"),
            scatter_dimension=1,
            tiled=True,
        ),
        lax.psum_scatter(grad_embed, ("dp", "seq"), scatter_dimension=0, tiled=True),
        lax.psum_scatter(grad_head, ("dp", "seq"), scatter_dimension=0, tiled=True),
        lax.psum_scatter(grad_gains, ("dp", "seq"), scatter_dimension=1, tiled=True),
    )
    squares = sum((jnp.sum(piece_grad * piece_grad) for piece_grad in shard_grads))
    total_squares = lax.psum(squares, ("dp", "seq"))
    grad_norm = jnp.sqrt(total_squares)
    clip_factor = jnp.minimum(1.0, CLIP_NORM / grad_norm)
    masters = (w_qkv, w_out, w_up, w_down, embed, head, gains)
    firsts = (mom_qkv, mom_out, mom_up, mom_down, mom_embed, mom_head, mom_gains)
    seconds = (sec_qkv, sec_out, sec_up, sec_down, sec_embed, sec_head, sec_gains)
    results = []
    for slot_index in range(7):
        results.append(
            adam_update(
                masters[slot_index],
                shard_grads[slot_index] * clip_factor,
                firsts[slot_index],
                seconds[slot_index],
                STEP_RATES[slot_index],
                WEIGHT_DECAYS[slot_index],
            )
        )
    return (
        loss_sum,
        grad_norm,
        results[0][0],
        results[1][0],
        results[2][0],
        results[3][0],
        results[4][0],
        results[5][0],
        results[6][0],
        results[0][1],
        results[1][1],
        results[2][1],
        results[3][1],
        results[4][1],
        results[5][1],
        results[6][1],
        results[0][2],
        results[1][2],
        results[2][2],
        results[3][2],
        results[4][2],
        results[5][2],
        results[6][2],
    )


LOW = jnp.bfloat16
F32 = jnp.float32
MESH = pl.DeviceIdType.MESH
D = 512

EH, GN, LAYER0, LAYER_ROWS = 0, 16, 32, 192
QKV, OUT, UP, DOWN = 0, 48, 64, 128
ROWS = LAYER0 + 2 * LAYER_ROWS


def dot(a, b):
    return jnp.dot(a, b, preferred_element_type=F32)


def dot_nt(a, b):
    return lax.dot_general(a, b, (((1,), (1,)), ((), ())), preferred_element_type=F32)


def dot_tn(a, b):
    return lax.dot_general(a, b, (((0,), (0,)), ((), ())), preferred_element_type=F32)


def low(v):
    return v.astype(LOW)


def lanes(shape):
    return lax.broadcasted_iota(jnp.int32, shape, len(shape) - 1)


def roll64(v):
    return pltpu.roll(v, 64, 1)


def swap32(v):
    return jnp.where(lanes(v.shape) % 64 < 32, pltpu.roll(v, 96, 1), pltpu.roll(v, 32, 1))


def norm_parts(v):
    center = v - jnp.mean(v, axis=-1, keepdims=True)
    scale = lax.rsqrt(jnp.mean(center * center, axis=-1, keepdims=True) + NORM_EPS)
    return center * scale, scale


def norm_back(v, gain, grad):
    unit, scale = norm_parts(v)
    g = grad * gain
    out = scale * (g - jnp.mean(g, axis=-1, keepdims=True) - unit * jnp.mean(g * unit, axis=-1, keepdims=True))
    return out, jnp.sum(grad * unit, axis=0, keepdims=True)


GELU_A, GELU_B = 0.7978845608028654, 0.044715


def gelu(v):
    return 0.5 * v * (1.0 + jnp.tanh(GELU_A * (v + GELU_B * v * v * v)))


def gelu_grad(v):
    t = jnp.tanh(GELU_A * (v + GELU_B * v * v * v))
    return 0.5 * (1.0 + t) + 0.5 * v * (1.0 - t * t) * (GELU_A * (1.0 + 3.0 * GELU_B * v * v))


class Bag:
    pass


def remote(src, dst, send, recv, device):
    return pltpu.make_async_remote_copy(
        src_ref=src, dst_ref=dst, send_sem=send, recv_sem=recv, device_id=device, device_id_type=MESH
    )


def pack_pair(block, odd):
    half = block.shape[0] // 2
    top, bottom = block[:half], block[half:]
    if odd:
        top = roll64(top)
    else:
        bottom = roll64(bottom)
    return jnp.where(lanes(top.shape) < 64, top, bottom)


def unpack_pair(even, odd):
    left = lanes(even.shape) < 64
    top = jnp.where(left, even, roll64(odd))
    bottom = jnp.where(left, roll64(even), odd)
    return jnp.concatenate([top, bottom], axis=0)


def unpack_left(x):
    left = lanes(x.shape) < 64
    return jnp.concatenate([jnp.where(left, x, 0.0), jnp.where(left, roll64(x), 0.0)], axis=0)


def unpack_right(x):
    left = lanes(x.shape) < 64
    return jnp.concatenate([jnp.where(left, 0.0, roll64(x)), jnp.where(left, 0.0, x)], axis=0)


def pack_left(x):
    half = x.shape[0] // 2
    return jnp.where(lanes((half, 128)) < 64, x[:half], roll64(x[half:]))


def pack_right(x):
    half = x.shape[0] // 2
    return jnp.where(lanes((half, 128)) < 64, roll64(x[:half]), x[half:])


def kernel(*refs):
    k = Bag()
    names = IN_NAMES + OUT_NAMES + tuple(SCRATCH)
    for name, ref in zip(names, refs[:-2]):
        setattr(k, name, ref)
    k.ss, k.rs = refs[-2:]
    for name in PER_LAYER:
        setattr(k, name, [getattr(k, name + "0"), getattr(k, name + "1")])
    k.hold = []
    for layer in range(2):
        hold = Bag()
        for name in HELD:
            setattr(hold, name, getattr(k, "h_" + name + str(layer)))
        k.hold.append(hold)
    g = lax.axis_index("dp")
    s = lax.axis_index("seq")
    z, y, x = s // 4, lax.rem(s // 2, 2), lax.rem(s, 2)
    k.g, k.s, k.z, k.y, k.x = g, s, z, y, x
    k.side = lax.rem(x + y, 2)
    k.cursor = 0

    def dev(g, z, y, x):
        return (g, z * 4 + y * 2 + x)

    k.dev = dev

    barrier = pltpu.get_barrier_semaphore()
    me = g * 16 + s

    @pl.loop(1, 32)
    def _(i):
        t = lax.rem(me + i, 32)
        pl.semaphore_signal(barrier, inc=1, device_id=(t // 16, lax.rem(t, 16)), device_id_type=MESH)

    own = k.pk.at[g, z, y, x]
    own[EH : EH + 16, 0:256] = low(k.head[...])
    own[EH : EH + 16, 256:512] = low(jnp.concatenate([k.embed[:, 0:256], k.embed[:, 256:512]], axis=0))
    own[GN : GN + 16, :] = low(k.gains[...])
    for layer in range(2):
        base = LAYER0 + layer * LAYER_ROWS
        own[base + QKV : base + QKV + 16, :] = low(k.w_qkv[layer, :, 0:512])
        for pair in range(4):
            keys = k.w_qkv[layer, :, 512 + 128 * pair : 640 + 128 * pair]
            vals = k.w_qkv[layer, :, 1024 + 128 * pair : 1152 + 128 * pair]
            left = lanes(keys.shape) < 64
            row = base + QKV + 16 + 16 * (pair // 2)
            col = 256 * (pair % 2)
            own[row : row + 16, col : col + 128] = low(jnp.where(left, keys, roll64(vals)))
            own[row : row + 16, col + 128 : col + 256] = low(jnp.where(left, roll64(keys), vals))
        own[base + OUT : base + OUT + 16, :] = low(k.w_out[layer])
        for j in range(4):
            own[base + UP + 16 * j : base + UP + 16 * j + 16, :] = low(k.w_up[layer, :, 512 * j : 512 * j + 512])
        own[base + DOWN : base + DOWN + 64, :] = low(k.w_down[layer])

    pl.semaphore_wait(barrier, 31)
    gather_weights(k)
    forward_backward(k)
    reduce_grads(k)


def sem(k, count=1):
    at = k.cursor
    k.cursor += count
    assert k.cursor <= SEMS
    return at


def start_all(copies):
    for copy in copies:
        copy.start()


def wait_all(copies):
    for copy in copies:
        copy.wait()


def gather_piece(k, r0, rm, r1):
    g, z, y, x, dev, pk = k.g, k.z, k.y, k.x, k.dev, k.pk

    def send(ref, device):
        i = sem(k)
        return remote(ref, ref, k.ss.at[i], k.rs.at[i], device)

    stage = [
        send(pk.at[g, z, y, x, pl.ds(r0, r1 - r0)], dev(g, lax.rem(z + hop, 4), y, x)) for hop in (1, 2, 3)
    ]
    start_all(stage)
    wait_all(stage)
    stage = [
        send(pk.at[g, :, y, x, pl.ds(r0, rm - r0)], dev(g, z, 1 - y, x)),
        send(pk.at[g, :, y, x, pl.ds(rm, r1 - rm)], dev(g, z, y, 1 - x)),
    ]
    start_all(stage)
    wait_all(stage)
    stage = [
        send(pk.at[g, :, :, x, pl.ds(r0, rm - r0)], dev(g, z, y, 1 - x)),
        send(pk.at[g, :, y, :, pl.ds(rm, r1 - rm)], dev(g, z, 1 - y, x)),
    ]
    start_all(stage)
    wait_all(stage)
    stage = [send(pk.at[g, :, :, :, pl.ds(r0, r1 - r0)], dev(1 - g, z, y, x))]
    start_all(stage)
    wait_all(stage)


def gather_weights(k):
    gather_piece(k, 0, ROWS // 2, ROWS)


def block(ref, row):
    return ref[:, :, :, :, row : row + 16, :].reshape(512, 512)


def put_block(ref, row, value):
    ref[:, :, :, :, row : row + 16, :] = low(value).reshape(2, 4, 2, 2, 16, 512)


def down_block(ref, row, c):
    return ref[c // 2, (c % 2) * 2 : (c % 2) * 2 + 2, :, :, row : row + 64, :].reshape(512, 512)


def put_down(ref, row, c, value):
    ref[c // 2, (c % 2) * 2 : (c % 2) * 2 + 2, :, :, row : row + 64, :] = low(value).reshape(2, 2, 2, 64, 512)


def my_blocks(k):
    return [4 * j + (k.side_own if half == 0 else 3 - k.side_own) for j in range(4) for half in range(2)]


def to_heads(k, source, target, after=None):
    base = sem(k, 16)
    out = sem(k, 8)
    selves = []
    for h in range(8):
        chip = k.g * 8 + h
        is_self = jnp.logical_and(chip == k.s, k.side == k.g)
        copy = remote(source.at[h], target.at[k.s], k.ss.at[out + h], k.rs.at[base + k.s], (k.side, chip))
        selves.append((is_self, copy))

        @pl.when(is_self)
        def _():
            pltpu.make_async_copy(source.at[h], target.at[k.s], k.rs.at[base + k.s]).start()

        @pl.when(jnp.logical_not(is_self))
        def _():
            copy.start()

    for b in my_blocks(k):
        pltpu.make_async_copy(target.at[b], target.at[b], k.rs.at[base + b]).wait()
        if after is not None:
            after(b)
    return selves


def from_heads(k, source, target):
    base = sem(k, 8)
    out = sem(k, 8)
    selves = []
    group, head = k.s // 8, lax.rem(k.s, 8)
    for i, b in enumerate(my_blocks(k)):
        is_self = jnp.logical_and(group == k.g, b == k.s)
        copy = remote(source.at[i], target.at[head], k.ss.at[out + i], k.rs.at[base + head], (group, b))
        selves.append((is_self, copy))

        @pl.when(is_self)
        def _():
            pltpu.make_async_copy(source.at[i], target.at[head], k.rs.at[base + head]).start()

        @pl.when(jnp.logical_not(is_self))
        def _():
            copy.start()

    for h in range(8):
        pltpu.make_async_copy(target.at[h], target.at[h], k.rs.at[base + h]).wait()
    return selves


def finish(selves):
    for is_self, copy in selves:
        @pl.when(jnp.logical_not(is_self))
        def _():
            copy.wait_send()


def rotate_block(v, cosine, sine):
    return v * cosine + swap32(v) * sine


def layer_sizes(layer):
    rows = 144 if layer == 0 else 48
    return rows, (rows // 2 + 15) // 16 * 16


def attend_loop(k, layer, body):
    for part in range(2):
        @pl.loop(0, 4)
        def _(n):
            i = part * 4 + n
            j, half = i // 2, lax.rem(i, 2)
            b = 4 * j + jnp.where(half == 0, k.side_own, 3 - k.side_own)
            body(i, b, 8 * (part + 1))


def masked_scores(k, layer, b, q, kv):
    rows, _ = layer_sizes(layer)
    scores = dot_nt(q, kv)
    shape = scores.shape
    visible = lanes(shape) <= b * rows + lax.broadcasted_iota(jnp.int32, shape, 0)
    return jnp.where(visible, scores, MASK_FILL)


def queries(inbox, b, rows):
    return low(unpack_left(inbox[b, 0 : (rows // 2 + 15) // 16 * 16, :].astype(F32)[: rows // 2]) * 0.125)


def attention_forward(k, layer):
    rows, pad = layer_sizes(layer)
    inbox, outbox, lse, keep = k.inbox[layer], k.abox[layer], k.lse[layer], k.att[layer]

    def body(i, b, blocks):
        q = queries(inbox, b, rows)
        kv = inbox[0:blocks, pad : pad + rows, :].reshape(blocks * rows, 128)
        scores = masked_scores(k, layer, b, q, kv)
        top = jnp.max(scores, axis=-1, keepdims=True)
        prob = jnp.exp(scores - top)
        total = jnp.sum(prob, axis=-1, keepdims=True)
        out = dot(low(prob), kv) / total
        lse[i] = jnp.broadcast_to(top + jnp.log(total), (rows, 128))
        keep[i] = out
        outbox[i, 0 : rows // 2, :] = low(pack_right(out))

    attend_loop(k, layer, body)


def attention_backward(k, layer):
    rows, pad = layer_sizes(layer)
    inbox, gradbox, lse, keep = k.inbox[layer], k.gbox[layer], k.lse[layer], k.att[layer]
    dkvt, outbox = k.dkvt[layer], k.dbox[layer]
    dkvt[...] = jnp.zeros_like(dkvt)

    def body(i, b, blocks):
        q = queries(inbox, b, rows)
        kv = inbox[0:blocks, pad : pad + rows, :].reshape(blocks * rows, 128)
        grad = unpack_right(gradbox[b].astype(F32)[: rows // 2])
        delta = jnp.sum(grad * keep[i], axis=-1, keepdims=True)
        grad = low(grad)
        prob = jnp.exp(masked_scores(k, layer, b, q, kv) - lse[i][:, 0:1])
        grad_prob = dot_nt(grad, kv)
        ds = low(prob * (grad_prob - delta))
        dq = dot(ds, kv) * 0.125
        outbox[i, 0 : rows // 2, :] = low(pack_left(dq))
        both = dot_tn(q, ds) + dot_tn(grad, low(prob))
        dkvt[:, 0 : blocks * rows] += both

    attend_loop(k, layer, body)
    dkv, theirs, got = k.dkv[layer], k.dkv_out[layer], k.dkv_in[layer]
    dkv[...] = dkvt[...].T.reshape(16, rows, 128)
    mine = my_blocks(k)
    for i in range(8):
        j, half = i // 2, i % 2
        other = 4 * j + ((1 - k.side_own) if half == 0 else 2 + k.side_own)
        theirs[i] = dkv[other]
    at = sem(k)
    copy = remote(theirs, got, k.ss.at[at], k.rs.at[at], k.dev(1 - k.g, k.z, k.y, k.x))
    copy.start()
    copy.wait()
    for i, b in enumerate(mine):
        outbox[i, pad : pad + rows, :] = low(dkv[b] + got[i])


def layer_ahead(k, layer, hidden):
    rows, pad = layer_sizes(layer)
    base = LAYER0 + layer * LAYER_ROWS
    hold = k.hold[layer]
    hold.hidden[...] = hidden
    unit, _ = norm_parts(hidden)
    normed = low(unit * k.gain[2 * layer : 2 * layer + 1, :])
    hold.normed[...] = normed
    cosine, sine = k.cos[layer][...], k.sin[layer][...]
    left = lanes(cosine.shape) < 64
    cos_kv, sin_kv = jnp.where(left, cosine, 1.0), jnp.where(left, sine, 0.0)
    sendbox = k.sendbox[layer]
    for part in range(3):
        joined = dot(normed, block(k.pk, base + QKV + 16 * part))
        for n in range(4):
            piece = joined[:, 128 * n : 128 * n + 128]
            if part == 0:
                piece = rotate_block(piece, cosine, sine)
                sendbox[2 * n, 0 : rows // 2, :] = low(pack_pair(piece, 0))
                sendbox[2 * n + 1, 0 : rows // 2, :] = low(pack_pair(piece, 1))
            else:
                sendbox[4 * part - 4 + n, pad : pad + rows, :] = low(rotate_block(piece, cos_kv, sin_kv))
    inbox = k.inbox[layer]
    at = sem(k, 16)
    share = sem(k, 16)
    passed = []

    def pass_on(b):
        copy = remote(
            inbox.at[b, pl.ds(pad, rows)],
            inbox.at[b, pl.ds(pad, rows)],
            k.ss.at[share + b],
            k.rs.at[at + b],
            k.dev(1 - k.g, k.z, k.y, k.x),
        )
        copy.start()
        passed.append(copy)

    selves = to_heads(k, sendbox, inbox, pass_on)
    for i in range(8):
        j, half = i // 2, i % 2
        other = 4 * j + ((1 - k.side_own) if half == 0 else 2 + k.side_own)
        ref = inbox.at[other, pl.ds(pad, rows)]
        pltpu.make_async_copy(ref, ref, k.rs.at[at + other]).wait()
    attention_forward(k, layer)
    home = k.home[layer]
    selves = selves + from_heads(k, k.abox[layer], home)
    for n in range(4):
        pair = unpack_pair(
            home[2 * n].astype(F32)[: rows // 2], home[2 * n + 1].astype(F32)[: rows // 2]
        )
        hold.flat[:, 128 * n : 128 * n + 128] = low(pair)
    middle = hidden + dot(hold.flat[...], block(k.pk, base + OUT))
    hold.middle[...] = middle
    unit, _ = norm_parts(middle)
    second = low(unit * k.gain[2 * layer + 1 : 2 * layer + 2, :])
    hold.second[...] = second
    for j in range(4):
        pre = dot(second, block(k.pk, base + UP + 16 * j))
        hold.pre[:, 512 * j : 512 * j + 512] = pre
        hold.act[:, 512 * j : 512 * j + 512] = low(gelu(pre))
    output = middle
    for c in range(4):
        output = output + dot(hold.act[:, 512 * c : 512 * c + 512], down_block(k.pk, base + DOWN, c))
    finish(selves)
    for copy in passed:
        copy.wait_send()
    return output


def layer_back(k, layer, grad_out):
    rows, pad = layer_sizes(layer)
    base = LAYER0 + layer * LAYER_ROWS
    hold = k.hold[layer]
    fall = low(grad_out)
    grad_second = jnp.zeros((rows, D), F32)
    second = hold.second[...]
    for c in range(4):
        cols = slice(512 * c, 512 * c + 512)
        put_down(k.gr, base + DOWN, c, dot_tn(hold.act[:, cols], fall))
        grad_act = dot_nt(fall, down_block(k.pk, base + DOWN, c))
        grad_pre = low(grad_act * gelu_grad(hold.pre[:, cols]))
        put_block(k.gr, base + UP + 16 * c, dot_tn(second, grad_pre))
        grad_second = grad_second + dot_nt(grad_pre, block(k.pk, base + UP + 16 * c))
    gain = k.gain[2 * layer + 1 : 2 * layer + 2, :]
    grad_mid, k.gain_grads[2 * layer + 1] = norm_back(hold.middle[...], gain, grad_second)
    grad_middle = grad_out + grad_mid
    hold.middle[...] = grad_middle
    proj = low(grad_middle)
    put_block(k.gr, base + OUT, dot_tn(hold.flat[...], proj))
    grad_att = dot_nt(proj, block(k.pk, base + OUT))
    gsend = k.gsend[layer]
    for n in range(4):
        piece = grad_att[:, 128 * n : 128 * n + 128]
        gsend[2 * n, 0 : rows // 2, :] = low(pack_pair(piece, 0))
        gsend[2 * n + 1, 0 : rows // 2, :] = low(pack_pair(piece, 1))
    selves = to_heads(k, gsend, k.gbox[layer])
    attention_backward(k, layer)
    back = k.back[layer]
    selves = selves + from_heads(k, k.dbox[layer], back)
    cosine, sine = k.cos[layer][...], k.sin[layer][...]
    left = lanes(cosine.shape) < 64
    cos_kv, sin_kv = jnp.where(left, cosine, 1.0), jnp.where(left, sine, 0.0)
    normed = hold.normed[...]
    grad_normed = jnp.zeros((rows, D), F32)
    for part in range(3):
        for n in range(4):
            if part == 0:
                piece = unpack_pair(
                    back[2 * n, 0:pad, :].astype(F32)[: rows // 2],
                    back[2 * n + 1, 0:pad, :].astype(F32)[: rows // 2],
                )
                piece = rotate_block(piece, cosine, -sine)
            else:
                piece = back[4 * part - 4 + n, pad : pad + rows, :].astype(F32)
                piece = rotate_block(piece, cos_kv, -sin_kv)
            hold.gj[:, 128 * n : 128 * n + 128] = low(piece)
        gj = hold.gj[...]
        put_block(k.gr, base + QKV + 16 * part, dot_tn(normed, gj))
        grad_normed = grad_normed + dot_nt(gj, block(k.pk, base + QKV + 16 * part))
    gain = k.gain[2 * layer : 2 * layer + 1, :]
    grad_in, k.gain_grads[2 * layer] = norm_back(hold.hidden[...], gain, grad_normed)
    finish(selves)
    return hold.middle[...] + grad_in


def byte_matrix(ids, half):
    n = lanes((ids.shape[0], 512))
    return low(jnp.where((n // 16 * 8 + n % 8 == ids) & (n // 8 % 2 == half), 1.0, 0.0))


def forward_backward(k):
    k.side_own = k.g
    rows, short = 144, 48
    k.gain[...] = jnp.sum(k.pk[:, :, :, :, GN : GN + 16, :].astype(F32).reshape(32, 16, 512), axis=0)
    k.gain_grads = [None] * 5
    table = k.pk[:, :, :, :, EH : EH + 16, 256:512].reshape(512, 256)
    ids = k.ids[...]
    first_in = jnp.concatenate([dot(byte_matrix(ids, 0), table), dot(byte_matrix(ids, 1), table)], axis=1)
    first = layer_ahead(k, 0, first_in)
    k.shift[8 : 8 + rows, :] = first
    at = sem(k)
    rim = remote(
        k.shift.at[pl.ds(rows, 8)], k.shift.at[pl.ds(0, 8)], k.ss.at[at], k.rs.at[at], (k.g, lax.rem(k.s + 1, 16))
    )

    @pl.when(k.s < 15)
    def _():
        rim.start()

    @pl.when(k.s > 0)
    def _():
        rim.wait_recv()

    @pl.when(k.s == 0)
    def _():
        k.shift[0:8, :] = jnp.zeros((8, D), F32)

    @pl.when(k.s < 15)
    def _():
        rim.wait_send()

    def pool_matrix(shape, offset, axis):
        j = lax.broadcasted_iota(jnp.int32, shape, axis)
        t = lax.broadcasted_iota(jnp.int32, shape, 1 - axis) - offset
        return jnp.where((t >= 3 * j) & (t < 3 * j + 3), 1.0, 0.0)

    exact = functools.partial(jnp.dot, preferred_element_type=F32, precision=lax.Precision.HIGHEST)
    pooled = exact(pool_matrix((short, rows + 8), 6, 0), k.shift[...]) / 3.0
    short_out = layer_ahead(k, 1, pooled)
    upsampled = k.shift[8 : 8 + rows, :] + exact(pool_matrix((rows, short), 0, 1), short_out)
    gain = k.gain[4:5, :]
    unit, _ = norm_parts(upsampled)
    final = low(unit * gain)
    head = k.pk[:, :, :, :, EH : EH + 16, 0:256].reshape(512, 256)
    logits = dot(final, head)
    top = jnp.max(logits, axis=-1, keepdims=True)
    log_total = top + jnp.log(jnp.sum(jnp.exp(logits - top), axis=-1, keepdims=True))
    hot = jnp.where(lanes((rows, 256)) == k.targets[...], 1.0, 0.0)
    picked = jnp.sum(hot * logits, axis=-1, keepdims=True)
    position = k.s * rows + lax.broadcasted_iota(jnp.int32, (rows, 1), 0)
    length = jnp.zeros((rows, 1), F32)
    begin = jnp.int32(0)
    for i in range(8):
        size = k.lengths[0, i]
        inside = (position >= begin) & (position < begin + size)
        length = jnp.where(inside, size.astype(F32), length)
        begin = begin + size
    k.loss = jnp.sum((log_total - picked) / length, axis=0, keepdims=True)
    grad_logits = low((jnp.exp(logits - log_total) - hot) / length)
    k.gr[:, :, :, :, EH : EH + 16, 0:256] = low(dot_tn(final, grad_logits)).reshape(2, 4, 2, 2, 16, 256)
    grad_final = dot_nt(grad_logits, head)
    grad_up, k.gain_grads[4] = norm_back(upsampled, gain, grad_final)
    k.up[...] = grad_up
    grad_short = exact(pool_matrix((short, rows), 0, 0), grad_up)
    grad_pooled = layer_back(k, 1, grad_short)
    k.pool[0:short, :] = grad_pooled
    at = sem(k)
    rim2 = remote(
        k.pool.at[pl.ds(0, 8)], k.pool.at[pl.ds(short, 8)], k.ss.at[at], k.rs.at[at], (k.g, lax.rem(k.s + 15, 16))
    )

    @pl.when(k.s > 0)
    def _():
        rim2.start()

    @pl.when(k.s < 15)
    def _():
        rim2.wait_recv()

    @pl.when(k.s == 15)
    def _():
        k.pool[short : short + 8, :] = jnp.zeros((8, D), F32)

    @pl.when(k.s > 0)
    def _():
        rim2.wait_send()

    t = lax.broadcasted_iota(jnp.int32, (rows, short + 8), 0)
    j = lax.broadcasted_iota(jnp.int32, (rows, short + 8), 1)
    spread = jnp.where((t + 2 >= 3 * j) & (t + 2 < 3 * j + 3), 1.0, 0.0)
    grad_first = k.up[...] + exact(spread, k.pool[...] / 3.0)
    grad_in = layer_back(k, 0, grad_first)
    table_grad = dot_tn(byte_matrix(ids, 0), low(grad_in[:, 0:256])) + dot_tn(
        byte_matrix(ids, 1), low(grad_in[:, 256:512])
    )
    k.gr[:, :, :, :, EH : EH + 16, 256:512] = low(table_grad).reshape(2, 4, 2, 2, 16, 256)
    gains = jnp.concatenate(k.gain_grads + [jnp.zeros((11, D), F32)], axis=0)
    k.gr[:, :, :, :, GN : GN + 16, :] = low(jnp.broadcast_to(gains[None], (32, 16, 512))).reshape(2, 4, 2, 2, 16, 512)


def add_into(ref, other):
    ref[...] = low(ref[...].astype(F32) + other[...].astype(F32))


def reduce_grads(k):
    g, z, y, x, dev, gr = k.g, k.z, k.y, k.x, k.dev, k.gr
    half = ROWS // 2
    a, b = pl.ds(0, half), pl.ds(half, half)

    def send(src, dst, device):
        i = sem(k)
        return remote(src, dst, k.ss.at[i], k.rs.at[i], device)

    copy = send(gr.at[1 - g], k.rc, dev(1 - g, z, y, x))
    copy.start()
    copy.wait()

    @pl.loop(0, 16)
    def _(n):
        add_into(gr.at[g, n // 4, lax.rem(n // 2, 2), lax.rem(n, 2)], k.rc.at[n // 4, lax.rem(n // 2, 2), lax.rem(n, 2)])

    stage = [
        send(gr.at[g, :, :, 1 - x, a], k.r2.at[:, :, a], dev(g, z, y, 1 - x)),
        send(gr.at[g, :, 1 - y, :, b], k.r2.at[:, :, b], dev(g, z, 1 - y, x)),
    ]
    start_all(stage)
    wait_all(stage)

    @pl.loop(0, 8)
    def _(n):
        add_into(gr.at[g, n // 2, lax.rem(n, 2), x, a], k.r2.at[n // 2, lax.rem(n, 2), a])
        add_into(gr.at[g, n // 2, y, lax.rem(n, 2), b], k.r2.at[n // 2, lax.rem(n, 2), b])

    stage = [
        send(gr.at[g, :, 1 - y, x, a], k.r1.at[:, a], dev(g, z, 1 - y, x)),
        send(gr.at[g, :, y, 1 - x, b], k.r1.at[:, b], dev(g, z, y, 1 - x)),
    ]
    start_all(stage)
    wait_all(stage)

    @pl.loop(0, 4)
    def _(n):
        add_into(gr.at[g, n, y, x], k.r1.at[n])

    stage = []
    for hop in (1, 2, 3):
        to = lax.rem(z + hop, 4)
        stage.append(send(gr.at[g, to, y, x], k.rz.at[hop - 1], dev(g, to, y, x)))
    start_all(stage)
    wait_all(stage)
    k.sq = jnp.zeros((1, 1), F32)

    def total(row, count):
        rows = pl.ds(row, count)
        v = gr[g, z, y, x, rows].astype(F32)
        for i in range(3):
            v = v + k.rz[i, rows].astype(F32)
        return v

    def square(v):
        k.sq = k.sq + jnp.sum(jnp.sum(v * v, axis=1, keepdims=True), axis=0, keepdims=True)

    v = total(EH, 16)
    square(v)
    k.g_head[...] = v[:, 0:256]
    k.g_embed[:, 0:256] = v[0:8, 256:512]
    k.g_embed[:, 256:512] = v[8:16, 256:512]
    v = total(GN, 16)
    pick = (
        lax.broadcasted_iota(jnp.int32, (D, 16), 0) - 16 * (g * 16 + k.s)
        == lax.broadcasted_iota(jnp.int32, (D, 16), 1)
    )
    v = jnp.dot(v, jnp.where(pick, 1.0, 0.0), preferred_element_type=F32, precision=lax.Precision.HIGHEST)
    square(v)
    k.g_gains[...] = v[0:5]
    for layer in range(2):
        base = LAYER0 + layer * LAYER_ROWS
        v = total(base + QKV, 48)
        square(v)
        k.g_qkv[layer, :, 0:512] = v[0:16]
        for pair in range(4):
            row, col = 16 + 16 * (pair // 2), 256 * (pair % 2)
            even = v[row : row + 16, col : col + 128]
            odd = v[row : row + 16, col + 128 : col + 256]
            left = lanes(even.shape) < 64
            k.g_qkv[layer, :, 512 + 128 * pair : 640 + 128 * pair] = jnp.where(left, even, roll64(odd))
            k.g_qkv[layer, :, 1024 + 128 * pair : 1152 + 128 * pair] = jnp.where(left, roll64(even), odd)
        v = total(base + OUT, 16)
        square(v)
        k.g_out[layer] = v
        v = total(base + UP, 64)
        square(v)
        for j in range(4):
            k.g_up[layer, :, 512 * j : 512 * j + 512] = v[16 * j : 16 * j + 16]
        v = total(base + DOWN, 64)
        square(v)
        k.g_down[layer] = v

    lane = lanes((8, 128))
    k.stat[0] = jnp.where(lane == 0, k.sq, jnp.where(lane == 1, k.loss, 0.0))
    me = g * 16 + k.s
    base, out = sem(k, 32), sem(k, 32)

    def stat_copy(i):
        t = lax.rem(me + i, 32)
        return remote(
            k.stat.at[0], k.stat.at[i], k.ss.at[out + i], k.rs.at[base + i], (t // 16, lax.rem(t, 16))
        )

    @pl.loop(1, 32)
    def _(i):
        stat_copy(i).start()

    @pl.loop(1, 32)
    def _(i):
        stat_copy(i).wait()

    k.stats[...] = jnp.sum(k.stat[...], axis=0)


IN_NAMES = (
    "ids", "targets", "lengths", "w_qkv", "w_out", "w_up", "w_down", "embed", "head", "gains",
    "cos0", "sin0", "cos1", "sin1",
)
OUT_NAMES = ("g_qkv", "g_out", "g_up", "g_down", "g_embed", "g_head", "g_gains", "stats")
SEMS = 384


def scratch_shapes():
    shapes = {
        "pk": ((2, 4, 2, 2, ROWS, D), LOW),
        "gr": ((2, 4, 2, 2, ROWS, D), LOW),
        "rc": ((4, 2, 2, ROWS, D), LOW),
        "r2": ((4, 2, ROWS, D), LOW),
        "r1": ((4, ROWS, D), LOW),
        "rz": ((3, ROWS, D), LOW),
        "gain": ((16, D), F32),
        "shift": ((152, D), F32),
        "pool": ((56, D), F32),
        "up": ((144, D), F32),
        "stat": ((32, 8, 128), F32),
    }
    for layer in range(2):
        rows, pad = layer_sizes(layer)
        for name, shape, kind in (
            ("sendbox", (8, pad + rows, 128), LOW),
            ("inbox", (16, pad + rows, 128), LOW),
            ("abox", (8, pad, 128), LOW),
            ("home", (8, pad, 128), LOW),
            ("gsend", (8, pad, 128), LOW),
            ("gbox", (16, pad, 128), LOW),
            ("dbox", (8, pad + rows, 128), LOW),
            ("back", (8, pad + rows, 128), LOW),
            ("lse", (8, rows, 128), F32),
            ("att", (8, rows, 128), F32),
            ("dkvt", (128, 16 * rows), F32),
            ("dkv", (16, rows, 128), F32),
            ("dkv_out", (8, rows, 128), F32),
            ("dkv_in", (8, rows, 128), F32),
            ("h_hidden", (rows, D), F32),
            ("h_normed", (rows, D), LOW),
            ("h_flat", (rows, D), LOW),
            ("h_middle", (rows, D), F32),
            ("h_second", (rows, D), LOW),
            ("h_pre", (rows, 4 * D), F32),
            ("h_act", (rows, 4 * D), LOW),
            ("h_gj", (rows, D), LOW),
        ):
            shapes[name + str(layer)] = (shape, kind)
    return shapes


SCRATCH = scratch_shapes()
PER_LAYER = (
    "cos", "sin", "sendbox", "inbox", "abox", "home", "gsend", "gbox", "dbox", "back", "lse", "att", "dkvt", "dkv",
    "dkv_out", "dkv_in",
)
HELD = ("hidden", "normed", "flat", "middle", "second", "pre", "act", "gj")


def update_kernel(*refs):
    stats, grads, masters, firsts, seconds = refs[0], refs[1:8], refs[8:15], refs[15:22], refs[22:29]
    outs = refs[29:]
    norm = jnp.sqrt(stats[0:1, 0:1])
    clip = jnp.minimum(1.0, CLIP_NORM / norm)
    for i in range(7):
        results = adam_update(
            masters[i][...], grads[i][...] * clip, firsts[i][...], seconds[i][...], STEP_RATES[i], WEIGHT_DECAYS[i]
        )
        for j in range(3):
            outs[7 * j + i][...] = results[j]


def on_device_fast(byte_ids, targets, item_lengths, *arrays):
    masters, firsts, seconds = arrays[0:7], arrays[7:14], arrays[14:21]
    gains = masters[6]
    rows = byte_ids.shape[1]
    place = lax.axis_index("seq")
    own = lax.axis_index("dp") * lax.axis_size("seq") + place
    lane = jnp.arange(D, dtype=jnp.int32)
    spread = jnp.where(lane[None, :] // gains.shape[1] == own, jnp.tile(gains, (1, D // gains.shape[1])), 0.0)
    spread = jnp.pad(spread, ((0, 16 - gains.shape[0]), (0, 0)))
    freqs = 10000.0 ** (-jnp.arange(32, dtype=jnp.float32) / 32)
    freqs = jnp.tile(freqs, 4)
    sign = jnp.where(jnp.arange(128) % 64 < 32, -1.0, 1.0)
    tables = []
    for count in (rows, rows // RATE):
        positions = place * count + jnp.arange(count, dtype=jnp.int32)
        angles = positions.astype(jnp.float32)[:, None] * freqs[None, :]
        tables += [jnp.cos(angles), jnp.sin(angles) * sign[None, :]]
    vmem = pl.BlockSpec(memory_space=pltpu.VMEM)
    shard_shapes = [jax.ShapeDtypeStruct(master.shape, F32) for master in masters]
    outs = pl.pallas_call(
        kernel,
        name="step",
        out_shape=shard_shapes + [jax.ShapeDtypeStruct((8, 128), F32)],
        in_specs=[vmem, vmem, pl.BlockSpec(memory_space=pltpu.SMEM)] + [vmem] * 11,
        out_specs=[vmem] * 8,
        scratch_shapes=[pltpu.VMEM(shape, kind) for shape, kind in SCRATCH.values()]
        + [pltpu.SemaphoreType.DMA((SEMS,)), pltpu.SemaphoreType.DMA((SEMS,))],
        compiler_params=pltpu.CompilerParams(collective_id=0, has_side_effects=True, vmem_limit_bytes=63 << 20),
    )(byte_ids.reshape(rows, 1), targets.reshape(rows, 1), item_lengths, *masters[:6], spread, *tables)
    grads, stats = outs[:7], outs[7]
    results = pl.pallas_call(
        update_kernel,
        name="update",
        out_shape=shard_shapes * 3,
        in_specs=[vmem] * 29,
        out_specs=[vmem] * 21,
        compiler_params=pltpu.CompilerParams(vmem_limit_bytes=32 << 20),
    )(stats, *grads, *masters, *firsts, *seconds)
    return (stats[0, 1], jnp.sqrt(stats[0, 0]), *results)


def solution(mesh):
    tuned = mesh.shape["dp"] == 2 and mesh.shape["seq"] == 16
    row = P(None, ("dp", "seq"), None)
    flat = P(("dp", "seq"), None)
    shards = (row, row, row, row, flat, flat, P(None, ("dp", "seq")))
    return jax.shard_map(
        on_device_fast if tuned else on_device_general,
        mesh=mesh,
        in_specs=(P("dp", "seq"), P("dp", "seq"), P("dp", None)) + shards * 3,
        out_specs=(P(), P()) + shards * 3,
        check_vma=False,
    )
```

```python
import functools

import jax
import jax.numpy as jnp
from jax import lax
from jax.experimental import pallas as pl
from jax.experimental.pallas import tpu as pltpu
from jax.sharding import PartitionSpec as P

HEADS = 8
VOCAB = 256
RATE = 3
STEP = 10

CLIP_NORM = 0.02
BETA_ONE = 0.9
BETA_TWO = 0.95
STEP_RATES = (0.03, 0.2, 0.03, 0.03, 0.6, 0.03, 0.2)
WEIGHT_DECAYS = (0.1, 0.1, 0.1, 0.1, 0.1, 0.1, 0.0)
EPSILON = 1e-08
NORM_EPS = 1e-05
MASK_FILL = -1e30


def shifted_2(value, axis, steps):
    count = lax.axis_size(axis)
    leading, last = (max(0, -steps), min(count, count - steps))
    return lax.ppermute(value, axis, [(source, source + steps) for source in range(leading, last)])


def to_low(values):
    return values.astype(jnp.bfloat16)


def layer_norm(values, gain):
    center = values - jnp.mean(values, axis=-1, keepdims=True)
    spread = jnp.mean(center * center, axis=-1, keepdims=True)
    return center * lax.rsqrt(spread + NORM_EPS) * gain


def rotate(joined, positions, num_heads):
    parts = joined.reshape(joined.shape[0], 3, num_heads, -1)
    half_size = parts.shape[-1] // 2
    freqs = 10000.0 ** (-jnp.arange(half_size, dtype=jnp.float32) / half_size)
    angles = positions.astype(jnp.float32)[:, None] * freqs[None, :]
    cosine = jnp.cos(angles)[:, None, :]
    sine = jnp.sin(angles)[:, None, :]

    def rotate_half(values):
        first_half = values[..., :half_size]
        second_half = values[..., half_size:]
        return jnp.concatenate(
            [first_half * cosine - second_half * sine, first_half * sine + second_half * cosine],
            axis=-1,
        )

    return (rotate_half(parts[:, 0]), rotate_half(parts[:, 1]), parts[:, 2])


def scores_for(q_low, k_low, query_pos, key_pos):
    scores = jnp.einsum(
        "rhe,phe->hrp", q_low, k_low, preferred_element_type=jnp.float32
    ) * q_low.shape[-1] ** (-0.5)
    causal = query_pos[:, None] >= key_pos[None, :]
    return (scores, causal)


def attend(q_low, k_low, v_low, query_pos):
    num_rows, num_heads, head_size = q_low.shape
    key_piece = (
        lax.all_gather(k_low, "seq", axis=0, tiled=True),
        lax.all_gather(v_low, "seq", axis=0, tiled=True),
    )
    running_max = jnp.full((num_heads, num_rows), MASK_FILL, jnp.float32)
    accum = jnp.zeros((num_rows, num_heads, head_size), jnp.float32)
    key_pos = jnp.arange(key_piece[0].shape[0], dtype=jnp.int32)
    scores, causal = scores_for(q_low, key_piece[0], query_pos, key_pos)
    scores = jnp.where(causal[None], scores, MASK_FILL)
    new_max = jnp.maximum(running_max, jnp.max(scores, axis=-1))
    factor = jnp.exp(running_max - new_max)
    attn_prob = jnp.where(causal[None], jnp.exp(scores - new_max[..., None]), 0.0)
    denom = jnp.sum(attn_prob, axis=-1)
    accum = accum * factor.T[:, :, None] + jnp.einsum(
        "hrp,phe->rhe", to_low(attn_prob), key_piece[1], preferred_element_type=jnp.float32
    )
    running_max, denom, accum = (new_max, denom, accum)
    return (accum / denom.T[:, :, None], (running_max + jnp.log(denom)).T)


def block_grads(q_low, grad_low, log_total, row_delta, query_pos, k_low, v_low, key_pos):
    scores, causal = scores_for(q_low, k_low, query_pos, key_pos)
    attn_prob = jnp.where(causal[None], jnp.exp(scores - log_total.T[:, :, None]), 0.0)
    grad_prob = jnp.einsum("rhe,phe->hrp", grad_low, v_low, preferred_element_type=jnp.float32)
    grad_score = to_low(attn_prob * (grad_prob - row_delta.T[:, :, None]))
    score_scale = q_low.shape[-1] ** (-0.5)
    grad_q = (
        jnp.einsum("hrp,phe->rhe", grad_score, k_low, preferred_element_type=jnp.float32)
        * score_scale
    )
    grad_k = (
        jnp.einsum("hrp,rhe->phe", grad_score, q_low, preferred_element_type=jnp.float32)
        * score_scale
    )
    grad_v = jnp.einsum(
        "hrp,rhe->phe", to_low(attn_prob), grad_low, preferred_element_type=jnp.float32
    )
    return (grad_q, grad_k, grad_v)


def attend_back(q_low, k_low, v_low, grad_low, log_total, row_delta, query_pos):
    key_piece = (
        lax.all_gather(k_low, "seq", axis=0, tiled=True),
        lax.all_gather(v_low, "seq", axis=0, tiled=True),
    )
    key_pos = jnp.arange(key_piece[0].shape[0], dtype=jnp.int32)
    grad_q = block_grads(
        q_low, grad_low, log_total, row_delta, query_pos, key_piece[0], key_piece[1], key_pos
    )[0]
    all_totals, all_deltas = (
        lax.all_gather(log_total, "seq", axis=0, tiled=True),
        lax.all_gather(row_delta, "seq", axis=0, tiled=True),
    )
    query_piece = (
        lax.all_gather(q_low, "seq", axis=0, tiled=True),
        lax.all_gather(grad_low, "seq", axis=0, tiled=True),
    )
    piece_rows = query_piece[0].shape[0]
    piece_pos = jnp.arange(piece_rows, dtype=jnp.int32)
    unused_q, grad_k_blk, grad_v_blk = block_grads(
        query_piece[0], query_piece[1], all_totals, all_deltas, piece_pos, k_low, v_low, query_pos
    )
    return (grad_q, grad_k_blk, grad_v_blk)


def layer_forward(hidden, weights, gain_pair, positions):
    w_joined, w_proj, w_rise, w_fall = weights
    num_rows = hidden.shape[0]
    normed = to_low(layer_norm(hidden, gain_pair[0]))
    joined = jnp.dot(normed, w_joined, preferred_element_type=jnp.float32)
    queries, keys, values = rotate(joined, positions, HEADS)
    q_low, k_low, v_low = (to_low(queries), to_low(keys), to_low(values))
    attended, log_total = attend(q_low, k_low, v_low, positions)
    flat_low = to_low(attended.reshape(num_rows, -1))
    middle = hidden + jnp.dot(flat_low, w_proj, preferred_element_type=jnp.float32)
    second = to_low(layer_norm(middle, gain_pair[1]))
    pre_act = jnp.dot(second, w_rise, preferred_element_type=jnp.float32)
    activated = to_low(jax.nn.gelu(pre_act))
    output = middle + jnp.dot(activated, w_fall, preferred_element_type=jnp.float32)
    saved = (
        normed,
        joined,
        q_low,
        k_low,
        v_low,
        attended,
        log_total,
        flat_low,
        middle,
        second,
        pre_act,
        activated,
    )
    return (output, saved)


def layer_backward(hidden, weights, gain_pair, positions, grad_out):
    w_joined, w_proj, w_rise, w_fall = weights
    unused_out, saved = layer_forward(hidden, weights, gain_pair, positions)
    (
        normed,
        joined,
        q_low,
        k_low,
        v_low,
        attended,
        log_total,
        flat_low,
        middle,
        second,
        pre_act,
        activated,
    ) = saved
    fall_low = to_low(grad_out)
    grad_fall = jnp.dot(activated.T, fall_low, preferred_element_type=jnp.float32)
    grad_act = jnp.dot(fall_low, w_fall.T, preferred_element_type=jnp.float32)
    grad_pre = to_low(jax.vjp(jax.nn.gelu, pre_act)[1](grad_act)[0])
    grad_rise = jnp.dot(second.T, grad_pre, preferred_element_type=jnp.float32)
    grad_second = jnp.dot(grad_pre, w_rise.T, preferred_element_type=jnp.float32)
    grad_middle_n, grad_gain_ffn = jax.vjp(layer_norm, middle, gain_pair[1])[1](grad_second)
    grad_middle = grad_out + grad_middle_n
    proj_low = to_low(grad_middle)
    grad_proj = jnp.dot(flat_low.T, proj_low, preferred_element_type=jnp.float32)
    grad_att = to_low(
        jnp.dot(proj_low, w_proj.T, preferred_element_type=jnp.float32).reshape(attended.shape)
    )
    row_delta = jnp.sum(grad_att.astype(jnp.float32) * attended, axis=-1)
    grad_q, grad_k, grad_v = attend_back(
        q_low, k_low, v_low, grad_att, log_total, row_delta, positions
    )

    def rotate_joined(joined_in):
        return rotate(joined_in, positions, HEADS)

    grad_joined = to_low(jax.vjp(rotate_joined, joined)[1]((grad_q, grad_k, grad_v))[0])
    grad_w_joined = jnp.dot(normed.T, grad_joined, preferred_element_type=jnp.float32)
    grad_normed = jnp.dot(grad_joined, w_joined.T, preferred_element_type=jnp.float32)
    grad_in_n, grad_gain_attn = jax.vjp(layer_norm, hidden, gain_pair[0])[1](grad_normed)
    return (
        grad_middle + grad_in_n,
        (grad_w_joined, grad_proj, grad_rise, grad_fall),
        jnp.stack([grad_gain_attn, grad_gain_ffn]),
    )


def adam_update(weight, gradient, moment_one, moment_two, step_rate, decay_rate):
    moment_one = BETA_ONE * moment_one + (1.0 - BETA_ONE) * gradient
    moment_two = BETA_TWO * moment_two + (1.0 - BETA_TWO) * gradient * gradient
    first_hat = moment_one / (1.0 - BETA_ONE**STEP)
    second_hat = moment_two / (1.0 - BETA_TWO**STEP)
    weight = weight - step_rate * (
        first_hat / (jnp.sqrt(second_hat) + EPSILON) + decay_rate * weight
    )
    return (weight, moment_one, moment_two)


def on_device_general(
    byte_ids,
    targets,
    item_lengths,
    w_qkv,
    w_out,
    w_up,
    w_down,
    embed,
    head,
    gains,
    mom_qkv,
    mom_out,
    mom_up,
    mom_down,
    mom_embed,
    mom_head,
    mom_gains,
    sec_qkv,
    sec_out,
    sec_up,
    sec_down,
    sec_embed,
    sec_head,
    sec_gains,
):
    low_qkv, low_out, low_up, low_down, low_embed, low_head, low_gains = (
        lax.all_gather(to_low(w_qkv), ("dp", "seq"), axis=1, tiled=True),
        lax.all_gather(to_low(w_out), ("dp", "seq"), axis=1, tiled=True),
        lax.all_gather(to_low(w_up), ("dp", "seq"), axis=1, tiled=True),
        lax.all_gather(to_low(w_down), ("dp", "seq"), axis=1, tiled=True),
        lax.all_gather(to_low(embed), ("dp", "seq"), axis=0, tiled=True),
        lax.all_gather(to_low(head), ("dp", "seq"), axis=0, tiled=True),
        lax.all_gather(to_low(gains), ("dp", "seq"), axis=1, tiled=True),
    )
    gain_rows = low_gains.astype(jnp.float32)
    byte_row = byte_ids[0]
    num_rows = byte_row.shape[0]
    short_rows = num_rows // RATE
    seq_place = lax.axis_index("seq")
    positions = seq_place * num_rows + jnp.arange(num_rows, dtype=jnp.int32)
    short_pos = seq_place * short_rows + jnp.arange(short_rows, dtype=jnp.int32)
    vocab_ids = jnp.arange(VOCAB, dtype=jnp.int32)
    one_hot_in = (byte_row[:, None] == vocab_ids[None, :]).astype(jnp.float32)
    embedded = jnp.dot(
        one_hot_in.astype(jnp.bfloat16), low_embed, preferred_element_type=jnp.float32
    )
    lower_weights = (low_qkv[0], low_out[0], low_up[0], low_down[0])
    upper_weights = (low_qkv[1], low_out[1], low_up[1], low_down[1])
    first_out, unused_first = layer_forward(embedded, lower_weights, gain_rows[0:2], positions)
    left_rim = shifted_2(first_out[num_rows - RATE + 1 :], "seq", 1)
    shifted = jnp.concatenate([left_rim, first_out[: num_rows - RATE + 1]], axis=0)
    pooled = jnp.mean(shifted.reshape(short_rows, RATE, -1), axis=1)
    short_out, unused_short = layer_forward(pooled, upper_weights, gain_rows[2:4], short_pos)
    upsampled = first_out + jnp.repeat(short_out, RATE, axis=0)
    top_gain = gain_rows[gain_rows.shape[0] - 1]
    final_low = to_low(layer_norm(upsampled, top_gain))
    logits = jnp.dot(final_low, low_head, preferred_element_type=jnp.float32)
    row_max = jnp.max(logits, axis=-1, keepdims=True)
    log_total = row_max[:, 0] + jnp.log(jnp.sum(jnp.exp(logits - row_max), axis=-1))
    one_hot_out = (targets[0][:, None] == vocab_ids[None, :]).astype(jnp.float32)
    picked = jnp.sum(one_hot_out * logits, axis=-1)
    lengths = item_lengths[0]
    ends = jnp.cumsum(lengths)
    doc_index = jnp.sum((positions[:, None] >= ends[None, :]).astype(jnp.int32), axis=1)
    item_ids = jnp.arange(lengths.shape[0], dtype=jnp.int32)
    doc_length = jnp.sum(
        jnp.where(item_ids[None, :] == doc_index[:, None], lengths[None, :], 0), axis=1
    ).astype(jnp.float32)
    loss_local = jnp.sum((log_total - picked) / doc_length)
    loss_sum = lax.psum(loss_local, ("dp", "seq"))
    grad_logits = to_low((jnp.exp(logits - log_total[:, None]) - one_hot_out) / doc_length[:, None])
    grad_head = jnp.dot(final_low.T, grad_logits, preferred_element_type=jnp.float32)
    grad_final = jnp.dot(grad_logits, low_head.T, preferred_element_type=jnp.float32)
    grad_upsampled, grad_gain_top = jax.vjp(layer_norm, upsampled, top_gain)[1](grad_final)
    grad_short = jnp.sum(grad_upsampled.reshape(short_rows, RATE, -1), axis=1)
    grad_pooled, upper_grads, upper_gain_grads = layer_backward(
        pooled, upper_weights, gain_rows[2:4], short_pos, grad_short
    )
    grad_shifted = jnp.repeat(grad_pooled / RATE, RATE, axis=0)
    rim_grad = shifted_2(grad_shifted[: RATE - 1], "seq", -1)
    grad_first = grad_upsampled + jnp.concatenate([grad_shifted[RATE - 1 :], rim_grad], axis=0)
    grad_embedded, lower_grads, lower_gain_grads = layer_backward(
        embedded, lower_weights, gain_rows[0:2], positions, grad_first
    )
    grad_embed = jnp.dot(one_hot_in.T, grad_embedded, precision=lax.Precision.HIGHEST)
    grad_gains = jnp.concatenate(
        [lower_gain_grads, upper_gain_grads, grad_gain_top[None, :]], axis=0
    )
    shard_grads = (
        lax.psum_scatter(
            jnp.stack([lower_grads[0], upper_grads[0]]),
            ("dp", "seq"),
            scatter_dimension=1,
            tiled=True,
        ),
        lax.psum_scatter(
            jnp.stack([lower_grads[1], upper_grads[1]]),
            ("dp", "seq"),
            scatter_dimension=1,
            tiled=True,
        ),
        lax.psum_scatter(
            jnp.stack([lower_grads[2], upper_grads[2]]),
            ("dp", "seq"),
            scatter_dimension=1,
            tiled=True,
        ),
        lax.psum_scatter(
            jnp.stack([lower_grads[3], upper_grads[3]]),
            ("dp", "seq"),
            scatter_dimension=1,
            tiled=True,
        ),
        lax.psum_scatter(grad_embed, ("dp", "seq"), scatter_dimension=0, tiled=True),
        lax.psum_scatter(grad_head, ("dp", "seq"), scatter_dimension=0, tiled=True),
        lax.psum_scatter(grad_gains, ("dp", "seq"), scatter_dimension=1, tiled=True),
    )
    squares = sum((jnp.sum(piece_grad * piece_grad) for piece_grad in shard_grads))
    total_squares = lax.psum(squares, ("dp", "seq"))
    grad_norm = jnp.sqrt(total_squares)
    clip_factor = jnp.minimum(1.0, CLIP_NORM / grad_norm)
    masters = (w_qkv, w_out, w_up, w_down, embed, head, gains)
    firsts = (mom_qkv, mom_out, mom_up, mom_down, mom_embed, mom_head, mom_gains)
    seconds = (sec_qkv, sec_out, sec_up, sec_down, sec_embed, sec_head, sec_gains)
    results = []
    for slot_index in range(7):
        results.append(
            adam_update(
                masters[slot_index],
                shard_grads[slot_index] * clip_factor,
                firsts[slot_index],
                seconds[slot_index],
                STEP_RATES[slot_index],
                WEIGHT_DECAYS[slot_index],
            )
        )
    return (
        loss_sum,
        grad_norm,
        results[0][0],
        results[1][0],
        results[2][0],
        results[3][0],
        results[4][0],
        results[5][0],
        results[6][0],
        results[0][1],
        results[1][1],
        results[2][1],
        results[3][1],
        results[4][1],
        results[5][1],
        results[6][1],
        results[0][2],
        results[1][2],
        results[2][2],
        results[3][2],
        results[4][2],
        results[5][2],
        results[6][2],
    )


LOW = jnp.bfloat16
F32 = jnp.float32
MESH = pl.DeviceIdType.MESH
D = 512

EG, LAYER0, LAYER_ROWS = 0, 16, 192
QKV, OUT, UP, DOWN = 0, 48, 64, 128
HEAD = LAYER0 + 2 * LAYER_ROWS
ROWS = HEAD + 16
PIECES = {"A": (0, 32, 64), "B": (64, 144, 208), "C": (208, 240, 272), "D": (272, 336, ROWS)}
SCHEDULE = {
    "start": "A",
    "packed": "ABAABCDA",
    "f0_sent": "B",
    "f0_got": "",
    "f0_part0": "BC",
    "f0_part1": "C",
    "f0_home": "B",
    "f0_up": "CD",
    "f0_end": "C",
    "f1_sent": "D",
    "f1_got": "",
    "f1_part0": "",
    "f1_home": "D",
    "f1_up": "D",
    "f1_end": "",
    "b1_ff": "D",
    "b1_sent": "D",
    "b1_part0": "D",
    "b1_sums": "",
    "b1_home": "D",
    "b1_end": "C",
    "b0_ff": "BC",
    "b0_sent": "BD",
    "b0_part1": "C",
    "b0_part0": "B",
    "b0_sums": "C",
    "b0_home": "B",
    "b0_end": "",
}


def dot(a, b):
    return jnp.dot(a, b, preferred_element_type=F32)


def dot_nt(a, b):
    return lax.dot_general(a, b, (((1,), (1,)), ((), ())), preferred_element_type=F32)


def dot_tn(a, b):
    return lax.dot_general(a, b, (((0,), (0,)), ((), ())), preferred_element_type=F32)


def low(v):
    return v.astype(LOW)


exact = functools.partial(jnp.dot, preferred_element_type=F32, precision=lax.Precision.HIGHEST)


def lanes(shape):
    return lax.broadcasted_iota(jnp.int32, shape, len(shape) - 1)


def roll64(v):
    return pltpu.roll(v, 64, 1)


def swap32(v):
    return jnp.where(lanes(v.shape) % 64 < 32, pltpu.roll(v, 96, 1), pltpu.roll(v, 32, 1))


def norm_parts(v):
    center = v - jnp.mean(v, axis=-1, keepdims=True)
    scale = lax.rsqrt(jnp.mean(center * center, axis=-1, keepdims=True) + NORM_EPS)
    return center * scale, scale


def norm_back(v, gain, grad):
    unit, scale = norm_parts(v)
    g = grad * gain
    out = scale * (g - jnp.mean(g, axis=-1, keepdims=True) - unit * jnp.mean(g * unit, axis=-1, keepdims=True))
    return out, jnp.sum(grad * unit, axis=0, keepdims=True)


GELU_A, GELU_B = 0.7978845608028654, 0.044715


def gelu(v):
    return 0.5 * v * (1.0 + jnp.tanh(GELU_A * (v + GELU_B * v * v * v)))


def gelu_grad(v):
    t = jnp.tanh(GELU_A * (v + GELU_B * v * v * v))
    return 0.5 * (1.0 + t) + 0.5 * v * (1.0 - t * t) * (GELU_A * (1.0 + 3.0 * GELU_B * v * v))


class Bag:
    pass


def remote(src, dst, send, recv, device):
    return pltpu.make_async_remote_copy(
        src_ref=src, dst_ref=dst, send_sem=send, recv_sem=recv, device_id=device, device_id_type=MESH
    )


def pack_pair(block, odd):
    half = block.shape[0] // 2
    top, bottom = block[:half], block[half:]
    if odd:
        top = roll64(top)
    else:
        bottom = roll64(bottom)
    return jnp.where(lanes(top.shape) < 64, top, bottom)


def unpack_pair(even, odd):
    left = lanes(even.shape) < 64
    top = jnp.where(left, even, roll64(odd))
    bottom = jnp.where(left, roll64(even), odd)
    return jnp.concatenate([top, bottom], axis=0)


def unpack_left(x):
    left = lanes(x.shape) < 64
    return jnp.concatenate([jnp.where(left, x, 0.0), jnp.where(left, roll64(x), 0.0)], axis=0)


def unpack_right(x):
    left = lanes(x.shape) < 64
    return jnp.concatenate([jnp.where(left, 0.0, roll64(x)), jnp.where(left, 0.0, x)], axis=0)


def pack_left(x):
    half = x.shape[0] // 2
    return jnp.where(lanes((half, 128)) < 64, x[:half], roll64(x[half:]))


def pack_right(x):
    half = x.shape[0] // 2
    return jnp.where(lanes((half, 128)) < 64, roll64(x[:half]), x[half:])


def kernel(*refs):
    k = Bag()
    names = IN_NAMES + OUT_NAMES + tuple(SCRATCH)
    for name, ref in zip(names, refs[:-2]):
        setattr(k, name, ref)
    k.ss, k.rs = refs[-2:]
    for name in PER_LAYER:
        setattr(k, name, [getattr(k, name + "0"), getattr(k, name + "1")])
    k.hold = []
    for layer in range(2):
        hold = Bag()
        for name in HELD:
            setattr(hold, name, getattr(k, "h_" + name + str(layer)))
        k.hold.append(hold)
    g = lax.axis_index("dp")
    s = lax.axis_index("seq")
    z, y, x = s // 4, lax.rem(s // 2, 2), lax.rem(s, 2)
    k.g, k.s, k.z, k.y, k.x = g, s, z, y, x
    k.side = lax.rem(x + y, 2)
    k.cursor = 0

    def dev(g, z, y, x):
        return (g, z * 4 + y * 2 + x)

    k.dev = dev

    barrier = pltpu.get_barrier_semaphore()
    me = g * 16 + s

    @pl.loop(1, 32)
    def _(i):
        t = lax.rem(me + i, 32)
        pl.semaphore_signal(barrier, inc=1, device_id=(t // 16, lax.rem(t, 16)), device_id_type=MESH)

    own = k.pk.at[g, z, y, x]
    own[EG : EG + 16, 0:256] = low(jnp.concatenate([k.embed[:, 0:256], k.embed[:, 256:512]], axis=0))
    place = lanes((16, 256)) - 16 * s == lax.broadcasted_iota(jnp.int32, (16, 256), 0)
    gains = exact(k.gains[...], jnp.where(place, 1.0, 0.0))
    gains = jnp.concatenate([gains, jnp.zeros((3, 256), F32)], axis=0)
    gains = jnp.concatenate([jnp.where(g == 0, gains, 0.0), jnp.where(g == 1, gains, 0.0)], axis=0)
    own[EG : EG + 16, 256:512] = low(gains)
    pack_layer(k, own, 0)
    pl.semaphore_wait(barrier, 31)
    k.gathers = {name: gather_piece(k, *rows) for name, rows in PIECES.items()}
    k.reduces = {name: reduce_piece(k, *rows) for name, rows in PIECES.items()}
    k.ready, k.summed = set(), set()
    point(k, "start")
    own[HEAD : HEAD + 16, 0:256] = low(k.head[...])
    own[HEAD : HEAD + 16, 256:512] = jnp.zeros((16, 256), LOW)
    pack_layer(k, own, 1)
    point(k, "packed")
    forward_backward(k)
    finish_grads(k)


def point(k, name):
    moving = k.gathers if name[0] in "spf" else k.reduces
    for piece in SCHEDULE[name]:
        next(moving[piece])


def pack_layer(k, own, layer):
    base = LAYER0 + layer * LAYER_ROWS
    own[base + QKV : base + QKV + 16, :] = low(k.w_qkv[layer, :, 0:512])
    for pair in range(4):
        keys = k.w_qkv[layer, :, 512 + 128 * pair : 640 + 128 * pair]
        vals = k.w_qkv[layer, :, 1024 + 128 * pair : 1152 + 128 * pair]
        left = lanes(keys.shape) < 64
        row = base + QKV + 16 + 16 * (pair // 2)
        col = 256 * (pair % 2)
        own[row : row + 16, col : col + 128] = low(jnp.where(left, keys, roll64(vals)))
        own[row : row + 16, col + 128 : col + 256] = low(jnp.where(left, roll64(keys), vals))
    own[base + OUT : base + OUT + 16, :] = low(k.w_out[layer])
    for j in range(4):
        own[base + UP + 16 * j : base + UP + 16 * j + 16, :] = low(k.w_up[layer, :, 512 * j : 512 * j + 512])
    own[base + DOWN : base + DOWN + 64, :] = low(k.w_down[layer])


def sem(k, count=1):
    at = k.cursor
    k.cursor += count
    assert k.cursor <= SEMS
    return at


def start_all(copies):
    for copy in copies:
        copy.start()


def wait_all(copies):
    for copy in copies:
        copy.wait()


def hop(k, src, dst, device):
    at = sem(k)
    return remote(src, dst, k.ss.at[at], k.rs.at[at], device)


def gather_piece(k, r0, rm, r1):
    g, z, y, x, dev, pk = k.g, k.z, k.y, k.x, k.dev, k.pk
    a, b, every = pl.ds(r0, rm - r0), pl.ds(rm, r1 - rm), pl.ds(r0, r1 - r0)

    def send(ref, device):
        return hop(k, ref, ref, device)

    stages = (
        lambda: [send(pk.at[g, z, y, x, every], dev(g, lax.rem(z + n, 4), y, x)) for n in (2, 1, 3)],
        lambda: [
            send(pk.at[g, :, y, x, a], dev(g, z, 1 - y, x)),
            send(pk.at[g, :, y, x, b], dev(g, z, y, 1 - x)),
        ],
        lambda: [
            send(pk.at[g, :, :, x, a], dev(g, z, y, 1 - x)),
            send(pk.at[g, :, y, :, b], dev(g, z, 1 - y, x)),
        ],
        lambda: [send(pk.at[g, :, :, :, every], dev(1 - g, z, y, x))],
    )
    waiting = []
    for stage in stages:
        wait_all(waiting)
        waiting = stage()
        start_all(waiting)
        yield
    wait_all(waiting)
    k.ready.update(range(r0, r1, 16))
    yield


def need(k, row, count=16):
    assert k.ready.issuperset(range(row, row + count, 16)), row


def block(k, row):
    need(k, row)
    return k.pk[:, :, :, :, row : row + 16, :].reshape(512, 512)


def put_block(ref, row, value):
    ref[:, :, :, :, row : row + 16, :] = low(value).reshape(2, 4, 2, 2, 16, 512)


def down_block(k, row, c):
    need(k, row, 64)
    return k.pk[c // 2, (c % 2) * 2 : (c % 2) * 2 + 2, :, :, row : row + 64, :].reshape(512, 512)


def put_down(ref, row, c, value):
    ref[c // 2, (c % 2) * 2 : (c % 2) * 2 + 2, :, :, row : row + 64, :] = low(value).reshape(2, 2, 2, 64, 512)


def my_blocks(k):
    return [4 * j + (k.g if half == 0 else 3 - k.g) for j in range(4) for half in range(2)]


def other_blocks(k):
    return [4 * j + (1 - k.g if half == 0 else 2 + k.g) for j in range(4) for half in range(2)]


def my_block(k, i):
    return 4 * (i // 2) + jnp.where(lax.rem(i, 2) == 0, k.g, 3 - k.g)


class Post:
    def __init__(self, k, sends, receives):
        self.k, self.out, self.base = k, sem(k, sends), sem(k, receives)
        self.sent = []

    def copy(self, src, dst, i, slot, device):
        k = self.k
        is_self = jnp.logical_and(device[0] == k.g, device[1] == k.s)
        return is_self, remote(src, dst, k.ss.at[self.out + i], k.rs.at[self.base + slot], device)

    def start(self, src, dst, i, slot, device):
        k = self.k
        is_self, copy = self.copy(src, dst, i, slot, device)

        @pl.when(is_self)
        def _():
            pltpu.make_async_copy(src, dst, k.rs.at[self.base + slot]).start()

        @pl.when(jnp.logical_not(is_self))
        def _():
            copy.start()

    def wait(self, dst, slot):
        pltpu.make_async_copy(dst, dst, self.k.rs.at[self.base + slot]).wait()

    def finish(self, src, dst, i, slot, device):
        is_self, copy = self.copy(src, dst, i, slot, device)

        @pl.when(jnp.logical_not(is_self))
        def _():
            copy.wait_send()


class ToHeads(Post):
    def __init__(self, k, source, target):
        super().__init__(k, 8, 16)
        self.source, self.target = source, target

    def each(self, act):
        k = self.k
        for h in range(8):
            act(self.source.at[h], self.target.at[k.s], h, k.s, (k.side, k.g * 8 + h))

    def send(self):
        self.each(self.start)

    def take(self, b):
        self.wait(self.target.at[b], b)

    def done(self):
        self.each(self.finish)


class FromHeads(Post):
    def __init__(self, k, source, target, rows):
        super().__init__(k, 8, 8)
        self.source, self.target, self.rows = source, target, rows

    def args(self, i, b):
        k = self.k
        head = lax.rem(k.s, 8)
        return self.source.at[i, self.rows], self.target.at[head, self.rows], i, head, (k.s // 8, b)

    def send(self, i, b):
        self.start(*self.args(i, b))

    def take(self, h):
        self.wait(self.target.at[h, self.rows], h)

    def done(self):
        for i, b in enumerate(my_blocks(self.k)):
            self.finish(*self.args(i, b))


def rotate_block(v, cosine, sine):
    return v * cosine + swap32(v) * sine


def rotary_tables(k, layer):
    rows, _ = layer_sizes(layer)
    lane = lanes((1, 128))
    freqs = jnp.zeros((1, 128), F32)
    for i in range(32):
        freqs = jnp.where(lane % 32 == i, 10000.0 ** (-i / 32), freqs)
    position = k.s * rows + lax.broadcasted_iota(jnp.int32, (rows, 1), 0)
    angles = position.astype(F32) * freqs
    k.cos[layer][...] = jnp.cos(angles)
    k.sin[layer][...] = jnp.sin(angles) * jnp.where(lane % 64 < 32, -1.0, 1.0)


def layer_sizes(layer):
    rows = 144 if layer == 0 else 48
    return rows, (rows // 2 + 15) // 16 * 16


def attend_loop(layer, part, body, between=None):
    if layer == 1:
        body(list(range(8)), 16)
        return
    for first in (0, 2):
        @pl.loop(first, first + 2)
        def _(n):
            body([part * 4 + n], 8 * (part + 1))

        if between is not None and first == 0:
            between()


def stack(pieces):
    return pieces[0] if len(pieces) == 1 else jnp.concatenate(pieces, axis=0)


def masked_scores(q, kv, places):
    scores = dot_nt(q, kv)
    return jnp.where(lanes(scores.shape) <= places, scores, MASK_FILL)


def stacked_queries(k, layer, items):
    rows, pad = layer_sizes(layer)
    blocks = [my_block(k, i) for i in items]
    q = stack([unpack_left(k.inbox[layer][b, 0:pad, :].astype(F32)[: rows // 2]) for b in blocks])
    places = stack([b * rows + lax.broadcasted_iota(jnp.int32, (rows, 1), 0) for b in blocks])
    return low(q * 0.125), blocks, places


def attention_forward(k, layer, part, post):
    rows, pad = layer_sizes(layer)
    inbox, outbox, lse, keep = k.inbox[layer], k.abox[layer], k.lse[layer], k.att[layer]

    def body(items, count):
        q, blocks, places = stacked_queries(k, layer, items)
        kv = inbox[0:count, pad : pad + rows, :].reshape(count * rows, 128)
        scores = masked_scores(q, kv, places)
        top = jnp.max(scores, axis=-1, keepdims=True)
        prob = jnp.exp(scores - top)
        total = jnp.sum(prob, axis=-1, keepdims=True)
        out = dot(low(prob), kv) / total
        stat = jnp.broadcast_to(top + jnp.log(total), out.shape)
        for n, (i, b) in enumerate(zip(items, blocks)):
            span = slice(n * rows, (n + 1) * rows)
            lse[i] = stat[span]
            keep[i] = out[span]
            outbox[i, 0 : rows // 2, :] = low(pack_right(out[span]))
            post.send(i, b)

    attend_loop(layer, part, body)


def attention_backward(k, layer, part, post, between=None):
    rows, pad = layer_sizes(layer)
    inbox, gradbox, lse, keep = k.inbox[layer], k.gbox[layer], k.lse[layer], k.att[layer]
    dkvt, outbox = k.dkvt[layer], k.dbox[layer]

    def body(items, count):
        q, blocks, places = stacked_queries(k, layer, items)
        kv = inbox[0:count, pad : pad + rows, :].reshape(count * rows, 128)
        grad = stack([unpack_right(gradbox[b].astype(F32)[: rows // 2]) for b in blocks])
        delta = jnp.sum(grad * stack([keep[i] for i in items]), axis=-1, keepdims=True)
        grad = low(grad)
        prob = jnp.exp(masked_scores(q, kv, places) - stack([lse[i] for i in items])[:, 0:1])
        grad_prob = dot_nt(grad, kv)
        ds = low(prob * (grad_prob - delta))
        dq = dot(ds, kv) * 0.125
        for n, (i, b) in enumerate(zip(items, blocks)):
            outbox[i, 0 : rows // 2, :] = low(pack_left(dq[n * rows : (n + 1) * rows]))
            post.send(i, b)
        dkvt[:, 0 : count * rows] += dot_tn(q, ds) + dot_tn(grad, low(prob))

    attend_loop(layer, part, body, between)


class KeySums:
    def __init__(self, k, layer, part, post):
        rows, _ = layer_sizes(layer)
        self.k, self.layer, self.post = k, layer, post
        self.items = range(8) if layer == 1 else range(4 * part, 4 * part + 4)
        first, count = (0, 16) if layer == 1 else (8 * part, 8)
        k.dkv[layer][first : first + count] = (
            k.dkvt[layer][:, first * rows : (first + count) * rows].T.reshape(count, rows, 128)
        )
        others = other_blocks(k)
        for i in self.items:
            k.dkv_out[layer][i] = k.dkv[layer][others[i]]
        span = pl.ds(self.items[0], len(self.items))
        self.copy = hop(k, k.dkv_out[layer].at[span], k.dkv_in[layer].at[span], k.dev(1 - k.g, k.z, k.y, k.x))
        self.copy.start()

    def send(self):
        k, layer = self.k, self.layer
        rows, pad = layer_sizes(layer)
        self.copy.wait()
        mine = my_blocks(k)
        for i in self.items:
            k.dbox[layer][i, pad : pad + rows, :] = low(k.dkv[layer][mine[i]] + k.dkv_in[layer][i])
            self.post.send(i, mine[i])


def layer_ahead(k, layer, hidden):
    rows, pad = layer_sizes(layer)
    base = LAYER0 + layer * LAYER_ROWS
    hold = k.hold[layer]
    hold.hidden[...] = hidden
    unit, _ = norm_parts(hidden)
    normed = low(unit * k.gain[2 * layer : 2 * layer + 1, :])
    hold.normed[...] = normed
    cosine, sine = k.cos[layer][...], k.sin[layer][...]
    left = lanes(cosine.shape) < 64
    cos_kv, sin_kv = jnp.where(left, cosine, 1.0), jnp.where(left, sine, 0.0)
    sendbox = k.sendbox[layer]
    for part in range(3):
        joined = dot(normed, block(k, base + QKV + 16 * part))
        for n in range(4):
            piece = joined[:, 128 * n : 128 * n + 128]
            if part == 0:
                piece = rotate_block(piece, cosine, sine)
                sendbox[2 * n, 0 : rows // 2, :] = low(pack_pair(piece, 0))
                sendbox[2 * n + 1, 0 : rows // 2, :] = low(pack_pair(piece, 1))
            else:
                sendbox[4 * part - 4 + n, pad : pad + rows, :] = low(rotate_block(piece, cos_kv, sin_kv))
    inbox = k.inbox[layer]
    out = ToHeads(k, sendbox, inbox)
    out.send()
    point(k, f"f{layer}_sent")
    share, shared = sem(k, 16), sem(k, 16)
    passed = []
    for b in my_blocks(k):
        out.take(b)
        ref = inbox.at[b, pl.ds(pad, rows)]
        passed.append(remote(ref, ref, k.ss.at[share + b], k.rs.at[shared + b], k.dev(1 - k.g, k.z, k.y, k.x)))
        passed[-1].start()
    point(k, f"f{layer}_got")
    home = k.home[layer]
    back = FromHeads(k, k.abox[layer], home, pl.ds(0, pad))
    others = other_blocks(k)
    for part in range(2 - layer):
        for b in others if layer == 1 else others[4 * part : 4 * part + 4]:
            ref = inbox.at[b, pl.ds(pad, rows)]
            pltpu.make_async_copy(ref, ref, k.rs.at[shared + b]).wait()
        attention_forward(k, layer, part, back)
        point(k, f"f{layer}_part{part}")
    for h in range(8):
        back.take(h)
    point(k, f"f{layer}_home")
    for n in range(4):
        pair = unpack_pair(
            home[2 * n].astype(F32)[: rows // 2], home[2 * n + 1].astype(F32)[: rows // 2]
        )
        hold.flat[:, 128 * n : 128 * n + 128] = low(pair)
    middle = hidden + dot(hold.flat[...], block(k, base + OUT))
    point(k, f"f{layer}_up")
    hold.middle[...] = middle
    unit, _ = norm_parts(middle)
    second = low(unit * k.gain[2 * layer + 1 : 2 * layer + 2, :])
    hold.second[...] = second
    for j in range(4):
        pre = dot(second, block(k, base + UP + 16 * j))
        hold.pre[:, 512 * j : 512 * j + 512] = pre
        hold.act[:, 512 * j : 512 * j + 512] = low(gelu(pre))
    output = middle
    for c in range(4):
        output = output + dot(hold.act[:, 512 * c : 512 * c + 512], down_block(k, base + DOWN, c))
    out.done()
    back.done()
    for copy in passed:
        copy.wait_send()
    point(k, f"f{layer}_end")
    return output


def layer_back(k, layer, grad_out):
    rows, pad = layer_sizes(layer)
    base = LAYER0 + layer * LAYER_ROWS
    hold = k.hold[layer]
    fall = low(grad_out)
    grad_second = jnp.zeros((rows, D), F32)
    second = hold.second[...]
    for c in range(4):
        cols = slice(512 * c, 512 * c + 512)
        put_down(k.gr, base + DOWN, c, dot_tn(hold.act[:, cols], fall))
        grad_act = dot_nt(fall, down_block(k, base + DOWN, c))
        grad_pre = low(grad_act * gelu_grad(hold.pre[:, cols]))
        put_block(k.gr, base + UP + 16 * c, dot_tn(second, grad_pre))
        grad_second = grad_second + dot_nt(grad_pre, block(k, base + UP + 16 * c))
    if layer == 1:
        point(k, "b1_ff")
    gain = k.gain[2 * layer + 1 : 2 * layer + 2, :]
    grad_mid, k.gain_grads[2 * layer + 1] = norm_back(hold.middle[...], gain, grad_second)
    grad_middle = grad_out + grad_mid
    hold.middle[...] = grad_middle
    proj = low(grad_middle)
    put_block(k.gr, base + OUT, dot_tn(hold.flat[...], proj))
    grad_att = dot_nt(proj, block(k, base + OUT))
    gsend = k.gsend[layer]
    for n in range(4):
        piece = grad_att[:, 128 * n : 128 * n + 128]
        gsend[2 * n, 0 : rows // 2, :] = low(pack_pair(piece, 0))
        gsend[2 * n + 1, 0 : rows // 2, :] = low(pack_pair(piece, 1))
    out = ToHeads(k, gsend, k.gbox[layer])
    out.send()
    if layer == 0:
        point(k, "b0_ff")
    back = k.back[layer]
    home_q = FromHeads(k, k.dbox[layer], back, pl.ds(0, pad))
    home_kv = FromHeads(k, k.dbox[layer], back, pl.ds(pad, rows))
    k.dkvt[layer][...] = jnp.zeros_like(k.dkvt[layer])
    point(k, f"b{layer}_sent")
    mine = my_blocks(k)
    sums = None
    for part in reversed(range(2 - layer)):
        for b in mine if layer == 1 else mine[4 * part : 4 * part + 4]:
            out.take(b)
        attention_backward(k, layer, part, home_q, None if sums is None else sums.send)
        sums = KeySums(k, layer, part, home_kv)
        point(k, f"b{layer}_part{part}")
    sums.send()
    point(k, f"b{layer}_sums")
    for h in range(8):
        home_q.take(h)
    cosine, sine = k.cos[layer][...], k.sin[layer][...]
    left = lanes(cosine.shape) < 64
    cos_kv, sin_kv = jnp.where(left, cosine, 1.0), jnp.where(left, sine, 0.0)
    normed = hold.normed[...]
    grad_normed = jnp.zeros((rows, D), F32)
    for part in range(3):
        if part == 1:
            for h in range(8):
                home_kv.take(h)
            point(k, f"b{layer}_home")
        for n in range(4):
            if part == 0:
                piece = unpack_pair(
                    back[2 * n, 0:pad, :].astype(F32)[: rows // 2],
                    back[2 * n + 1, 0:pad, :].astype(F32)[: rows // 2],
                )
                piece = rotate_block(piece, cosine, -sine)
            else:
                piece = back[4 * part - 4 + n, pad : pad + rows, :].astype(F32)
                piece = rotate_block(piece, cos_kv, -sin_kv)
            hold.gj[:, 128 * n : 128 * n + 128] = low(piece)
        gj = hold.gj[...]
        put_block(k.gr, base + QKV + 16 * part, dot_tn(normed, gj))
        grad_normed = grad_normed + dot_nt(gj, block(k, base + QKV + 16 * part))
    gain = k.gain[2 * layer : 2 * layer + 1, :]
    grad_in, k.gain_grads[2 * layer] = norm_back(hold.hidden[...], gain, grad_normed)
    out.done()
    home_q.done()
    home_kv.done()
    if layer == 1:
        point(k, "b1_end")
    return hold.middle[...] + grad_in


def byte_matrix(ids, half):
    n = lanes((ids.shape[0], 512))
    return low(jnp.where((n // 16 * 8 + n % 8 == ids) & (n // 8 % 2 == half), 1.0, 0.0))


def forward_backward(k):
    rows, short = 144, 48
    need(k, EG)
    gains = jnp.sum(k.pk[:, :, :, :, EG : EG + 16, 256:512].astype(F32).reshape(32, 16, 256), axis=0)
    k.gain[:, 0:256] = gains[0:8]
    k.gain[:, 256:512] = gains[8:16]
    k.gain_grads = [None] * 5
    table = k.pk[:, :, :, :, EG : EG + 16, 0:256].reshape(512, 256)
    k.columns[0:1, 0:rows] = k.ids[...].astype(F32)
    k.columns[1:2, 0:rows] = k.targets[...].astype(F32)
    columns = k.columns[...].T
    ids, targets = columns[0:rows, 0:1].astype(jnp.int32), columns[0:rows, 1:2].astype(jnp.int32)
    for layer in range(2):
        rotary_tables(k, layer)
    first_in = jnp.concatenate([dot(byte_matrix(ids, 0), table), dot(byte_matrix(ids, 1), table)], axis=1)
    first = layer_ahead(k, 0, first_in)
    k.shift[8 : 8 + rows, :] = first
    at = sem(k)
    rim = remote(
        k.shift.at[pl.ds(rows, 8)], k.shift.at[pl.ds(0, 8)], k.ss.at[at], k.rs.at[at], (k.g, lax.rem(k.s + 1, 16))
    )

    @pl.when(k.s < 15)
    def _():
        rim.start()

    @pl.when(k.s > 0)
    def _():
        rim.wait_recv()

    @pl.when(k.s == 0)
    def _():
        k.shift[0:8, :] = jnp.zeros((8, D), F32)

    @pl.when(k.s < 15)
    def _():
        rim.wait_send()

    def pool_matrix(shape, offset, axis):
        j = lax.broadcasted_iota(jnp.int32, shape, axis)
        t = lax.broadcasted_iota(jnp.int32, shape, 1 - axis) - offset
        return jnp.where((t >= 3 * j) & (t < 3 * j + 3), 1.0, 0.0)

    pooled = exact(pool_matrix((short, rows + 8), 6, 0), k.shift[...]) / 3.0
    short_out = layer_ahead(k, 1, pooled)
    upsampled = k.shift[8 : 8 + rows, :] + exact(pool_matrix((rows, short), 0, 1), short_out)
    gain = k.gain[4:5, :]
    unit, _ = norm_parts(upsampled)
    final = low(unit * gain)
    need(k, HEAD)
    head = k.pk[:, :, :, :, HEAD : HEAD + 16, 0:256].reshape(512, 256)
    logits = dot(final, head)
    top = jnp.max(logits, axis=-1, keepdims=True)
    log_total = top + jnp.log(jnp.sum(jnp.exp(logits - top), axis=-1, keepdims=True))
    hot = jnp.where(lanes((rows, 256)) == targets, 1.0, 0.0)
    picked = jnp.sum(hot * logits, axis=-1, keepdims=True)
    position = k.s * rows + lax.broadcasted_iota(jnp.int32, (rows, 1), 0)
    length = jnp.zeros((rows, 1), F32)
    begin = jnp.int32(0)
    for i in range(8):
        size = k.lengths[0, i]
        inside = (position >= begin) & (position < begin + size)
        length = jnp.where(inside, size.astype(F32), length)
        begin = begin + size
    k.loss = jnp.sum((log_total - picked) / length, axis=0, keepdims=True)
    grad_logits = low((jnp.exp(logits - log_total) - hot) / length)
    k.gr[:, :, :, :, HEAD : HEAD + 16, 0:256] = low(dot_tn(final, grad_logits)).reshape(2, 4, 2, 2, 16, 256)
    k.gr[:, :, :, :, HEAD : HEAD + 16, 256:512] = jnp.zeros((2, 4, 2, 2, 16, 256), LOW)
    grad_final = dot_nt(grad_logits, head)
    grad_up, k.gain_grads[4] = norm_back(upsampled, gain, grad_final)
    k.up[...] = grad_up
    grad_short = exact(pool_matrix((short, rows), 0, 0), grad_up)
    grad_pooled = layer_back(k, 1, grad_short)
    k.pool[0:short, :] = grad_pooled
    at = sem(k)
    rim2 = remote(
        k.pool.at[pl.ds(0, 8)], k.pool.at[pl.ds(short, 8)], k.ss.at[at], k.rs.at[at], (k.g, lax.rem(k.s + 15, 16))
    )

    @pl.when(k.s > 0)
    def _():
        rim2.start()

    @pl.when(k.s < 15)
    def _():
        rim2.wait_recv()

    @pl.when(k.s == 15)
    def _():
        k.pool[short : short + 8, :] = jnp.zeros((8, D), F32)

    @pl.when(k.s > 0)
    def _():
        rim2.wait_send()

    t = lax.broadcasted_iota(jnp.int32, (rows, short + 8), 0)
    j = lax.broadcasted_iota(jnp.int32, (rows, short + 8), 1)
    spread = jnp.where((t + 2 >= 3 * j) & (t + 2 < 3 * j + 3), 1.0, 0.0)
    grad_first = k.up[...] + exact(spread, k.pool[...] / 3.0)
    grad_in = layer_back(k, 0, grad_first)
    table_grad = dot_tn(byte_matrix(ids, 0), low(grad_in[:, 0:256])) + dot_tn(
        byte_matrix(ids, 1), low(grad_in[:, 256:512])
    )
    k.gr[:, :, :, :, EG : EG + 16, 0:256] = low(table_grad).reshape(2, 4, 2, 2, 16, 256)
    fill = [jnp.zeros((3, 256), F32)]
    gains = jnp.concatenate(
        [v[:, 0:256] for v in k.gain_grads] + fill + [v[:, 256:512] for v in k.gain_grads] + fill, axis=0
    )
    gains = jnp.broadcast_to(low(gains)[None], (32, 16, 256))
    k.gr[:, :, :, :, EG : EG + 16, 256:512] = gains.reshape(2, 4, 2, 2, 16, 256)
    point(k, "b0_end")


def add_into(ref, other):
    ref[...] = low(ref[...].astype(F32) + other[...].astype(F32))


def reduce_piece(k, r0, rm, r1):
    g, z, y, x, dev, gr = k.g, k.z, k.y, k.x, k.dev, k.gr
    a, b, every = pl.ds(r0, rm - r0), pl.ds(rm, r1 - rm), pl.ds(r0, r1 - r0)
    waiting = [hop(k, gr.at[1 - g, :, :, :, every], k.rc.at[:, :, :, every], dev(1 - g, z, y, x))]
    start_all(waiting)
    yield
    wait_all(waiting)

    @pl.loop(0, 16)
    def _(n):
        place = (n // 4, lax.rem(n // 2, 2), lax.rem(n, 2), every)
        add_into(gr.at[(g,) + place], k.rc.at[place])

    waiting = [
        hop(k, gr.at[g, :, :, 1 - x, a], k.r2.at[:, :, a], dev(g, z, y, 1 - x)),
        hop(k, gr.at[g, :, 1 - y, :, b], k.r2.at[:, :, b], dev(g, z, 1 - y, x)),
    ]
    start_all(waiting)
    yield
    wait_all(waiting)

    @pl.loop(0, 8)
    def _(n):
        add_into(gr.at[g, n // 2, lax.rem(n, 2), x, a], k.r2.at[n // 2, lax.rem(n, 2), a])
        add_into(gr.at[g, n // 2, y, lax.rem(n, 2), b], k.r2.at[n // 2, lax.rem(n, 2), b])

    waiting = [
        hop(k, gr.at[g, :, 1 - y, x, a], k.r1.at[:, a], dev(g, z, 1 - y, x)),
        hop(k, gr.at[g, :, y, 1 - x, b], k.r1.at[:, b], dev(g, z, y, 1 - x)),
    ]
    start_all(waiting)
    yield
    wait_all(waiting)

    @pl.loop(0, 4)
    def _(n):
        add_into(gr.at[g, n, y, x, every], k.r1.at[n, every])

    waiting = []
    for n in (2, 1, 3):
        to = lax.rem(z + n, 4)
        waiting.append(hop(k, gr.at[g, to, y, x, every], k.rz.at[n - 1, every], dev(g, to, y, x)))
    start_all(waiting)
    yield
    wait_all(waiting)
    k.summed.update(range(r0, r1, 16))
    yield


def own_sum(k, row, count):
    assert k.summed.issuperset(range(row, row + count, 16))
    rows = pl.ds(row, count)
    v = k.gr[k.g, k.z, k.y, k.x, rows].astype(F32)
    for i in range(3):
        v = v + k.rz[i, rows].astype(F32)
    return v


def square(k, v):
    k.sq = k.sq + jnp.sum(jnp.sum(v * v, axis=1, keepdims=True), axis=0, keepdims=True)


def store_qkv(k, layer):
    v = own_sum(k, LAYER0 + layer * LAYER_ROWS + QKV, 48)
    square(k, v)
    k.g_qkv[layer, :, 0:512] = v[0:16]
    for pair in range(4):
        row, col = 16 + 16 * (pair // 2), 256 * (pair % 2)
        even = v[row : row + 16, col : col + 128]
        odd = v[row : row + 16, col + 128 : col + 256]
        left = lanes(even.shape) < 64
        k.g_qkv[layer, :, 512 + 128 * pair : 640 + 128 * pair] = jnp.where(left, even, roll64(odd))
        k.g_qkv[layer, :, 1024 + 128 * pair : 1152 + 128 * pair] = jnp.where(left, roll64(even), odd)


def store_out(k, layer):
    v = own_sum(k, LAYER0 + layer * LAYER_ROWS + OUT, 16)
    square(k, v)
    k.g_out[layer] = v


def store_ff(k, layer):
    v = own_sum(k, LAYER0 + layer * LAYER_ROWS + UP, 64)
    square(k, v)
    for j in range(4):
        k.g_up[layer, :, 512 * j : 512 * j + 512] = v[16 * j : 16 * j + 16]
    v = own_sum(k, LAYER0 + layer * LAYER_ROWS + DOWN, 64)
    square(k, v)
    k.g_down[layer] = v


def store_head(k):
    v = own_sum(k, HEAD, 16)[:, 0:256]
    square(k, v)
    k.g_head[...] = v


def store_rest(k):
    v = own_sum(k, EG, 16)
    square(k, v[:, 0:256])
    k.g_embed[:, 0:256] = v[0:8, 0:256]
    k.g_embed[:, 256:512] = v[8:16, 0:256]
    gains = jnp.where(k.g == 0, v[0:8, 256:512], v[8:16, 256:512])
    row, column = lax.broadcasted_iota(jnp.int32, (256, 16), 0), lax.broadcasted_iota(jnp.int32, (256, 16), 1)
    gains = exact(gains, jnp.where(row - 16 * k.s == column, 1.0, 0.0))[0:5]
    square(k, gains)
    k.g_gains[...] = gains


def finish_grads(k):
    g = k.g
    k.sq = jnp.zeros((1, 1), F32)

    def complete(name):
        for _ in k.reduces[name]:
            pass

    next(k.reduces["A"])
    complete("D")
    store_ff(k, 1)
    store_head(k)
    next(k.reduces["A"])
    complete("C")
    store_qkv(k, 1)
    store_out(k, 1)
    next(k.reduces["A"])
    complete("B")
    store_out(k, 0)
    store_ff(k, 0)
    complete("A")
    store_qkv(k, 0)
    store_rest(k)
    lane = lanes((8, 128))
    k.stat[0] = jnp.where(lane == 0, k.sq, jnp.where(lane == 1, k.loss, 0.0))
    me = g * 16 + k.s
    base, out = sem(k, 32), sem(k, 32)

    def stat_copy(i):
        t = lax.rem(me + i, 32)
        return remote(
            k.stat.at[0], k.stat.at[i], k.ss.at[out + i], k.rs.at[base + i], (t // 16, lax.rem(t, 16))
        )

    @pl.loop(1, 32)
    def _(i):
        stat_copy(i).start()

    @pl.loop(1, 32)
    def _(i):
        stat_copy(i).wait()

    k.stats[...] = jnp.sum(k.stat[...], axis=0)


IN_NAMES = (
    "ids", "targets", "lengths", "w_qkv", "w_out", "w_up", "w_down", "embed", "head", "gains",
)
OUT_NAMES = ("g_qkv", "g_out", "g_up", "g_down", "g_embed", "g_head", "g_gains", "stats")
SEMS = 512


def scratch_shapes():
    shapes = {
        "pk": ((2, 4, 2, 2, ROWS, D), LOW),
        "gr": ((2, 4, 2, 2, ROWS, D), LOW),
        "rc": ((4, 2, 2, ROWS, D), LOW),
        "r2": ((4, 2, ROWS, D), LOW),
        "r1": ((4, ROWS, D), LOW),
        "rz": ((3, ROWS, D), LOW),
        "gain": ((8, D), F32),
        "shift": ((152, D), F32),
        "pool": ((56, D), F32),
        "up": ((144, D), F32),
        "stat": ((32, 8, 128), F32),
        "columns": ((128, 256), F32),
    }
    for layer in range(2):
        rows, pad = layer_sizes(layer)
        for name, shape, kind in (
            ("cos", (rows, 128), F32),
            ("sin", (rows, 128), F32),
            ("sendbox", (8, pad + rows, 128), LOW),
            ("inbox", (16, pad + rows, 128), LOW),
            ("abox", (8, pad, 128), LOW),
            ("home", (8, pad, 128), LOW),
            ("gsend", (8, pad, 128), LOW),
            ("gbox", (16, pad, 128), LOW),
            ("dbox", (8, pad + rows, 128), LOW),
            ("back", (8, pad + rows, 128), LOW),
            ("lse", (8, rows, 128), F32),
            ("att", (8, rows, 128), F32),
            ("dkvt", (128, 16 * rows), F32),
            ("dkv", (16, rows, 128), F32),
            ("dkv_out", (8, rows, 128), F32),
            ("dkv_in", (8, rows, 128), F32),
            ("h_hidden", (rows, D), F32),
            ("h_normed", (rows, D), LOW),
            ("h_flat", (rows, D), LOW),
            ("h_middle", (rows, D), F32),
            ("h_second", (rows, D), LOW),
            ("h_pre", (rows, 4 * D), F32),
            ("h_act", (rows, 4 * D), LOW),
            ("h_gj", (rows, D), LOW),
        ):
            shapes[name + str(layer)] = (shape, kind)
    return shapes


SCRATCH = scratch_shapes()
PER_LAYER = (
    "cos", "sin", "sendbox", "inbox", "abox", "home", "gsend", "gbox", "dbox", "back", "lse", "att", "dkvt", "dkv",
    "dkv_out", "dkv_in",
)
HELD = ("hidden", "normed", "flat", "middle", "second", "pre", "act", "gj")


def update_kernel(*refs):
    stats, grads, state, outs = refs[0], refs[1:8], refs[8:29], refs[29:50]
    held, got, sems = refs[50:57], refs[57:78], refs[78]
    copies = [pltpu.make_async_copy(src, dst, sems.at[i]) for i, (src, dst) in enumerate(zip(grads + state, held + got))]
    start_all(copies)
    norm = jnp.sqrt(stats[0:1, 0:1])
    clip = jnp.minimum(1.0, CLIP_NORM / norm)
    for i in range(7):
        for j in range(4):
            copies[7 * j + i].wait()
        results = adam_update(
            got[i][...], held[i][...] * clip, got[7 + i][...], got[14 + i][...], STEP_RATES[i], WEIGHT_DECAYS[i]
        )
        for j in range(3):
            outs[7 * j + i][...] = results[j]


def on_device_fast(byte_ids, targets, item_lengths, *arrays):
    masters, firsts, seconds = arrays[0:7], arrays[7:14], arrays[14:21]
    vmem = pl.BlockSpec(memory_space=pltpu.VMEM)
    shard_shapes = [jax.ShapeDtypeStruct(master.shape, F32) for master in masters]
    outs = pl.pallas_call(
        kernel,
        name="step",
        out_shape=shard_shapes + [jax.ShapeDtypeStruct((8, 128), F32)],
        in_specs=[vmem, vmem, pl.BlockSpec(memory_space=pltpu.SMEM)] + [vmem] * 7,
        out_specs=[vmem] * 8,
        scratch_shapes=[pltpu.VMEM(shape, kind) for shape, kind in SCRATCH.values()]
        + [pltpu.SemaphoreType.DMA((SEMS,)), pltpu.SemaphoreType.DMA((SEMS,))],
        compiler_params=pltpu.CompilerParams(collective_id=0, has_side_effects=True, vmem_limit_bytes=63 << 20),
    )(byte_ids, targets, item_lengths, *masters)
    grads, stats = outs[:7], outs[7]
    results = pl.pallas_call(
        update_kernel,
        name="update",
        out_shape=shard_shapes * 3,
        in_specs=[vmem] + [pl.BlockSpec(memory_space=pl.ANY)] * 28,
        out_specs=[vmem] * 21,
        scratch_shapes=[pltpu.VMEM(shard.shape, F32) for shard in shard_shapes * 4] + [pltpu.SemaphoreType.DMA((28,))],
        compiler_params=pltpu.CompilerParams(vmem_limit_bytes=63 << 20),
    )(stats, *grads, *masters, *firsts, *seconds)
    return (stats[0, 1], jnp.sqrt(stats[0, 0]), *results)


def solution(mesh):
    tuned = mesh.shape["dp"] == 2 and mesh.shape["seq"] == 16
    row = P(None, ("dp", "seq"), None)
    flat = P(("dp", "seq"), None)
    shards = (row, row, row, row, flat, flat, P(None, ("dp", "seq")))
    return jax.shard_map(
        on_device_fast if tuned else on_device_general,
        mesh=mesh,
        in_specs=(P("dp", "seq"), P("dp", "seq"), P("dp", None)) + shards * 3,
        out_specs=(P(), P()) + shards * 3,
        check_vma=False,
    )
```

```python
import contextlib
import functools

import jax
import jax.numpy as jnp
from jax import lax
from jax.experimental import pallas as pl
from jax.experimental.pallas import tpu as pltpu
from jax.sharding import PartitionSpec as P

HEADS = 8
VOCAB = 256
RATE = 3
STEP = 10

CLIP_NORM = 0.02
BETA_ONE = 0.9
BETA_TWO = 0.95
STEP_RATES = (0.03, 0.2, 0.03, 0.03, 0.6, 0.03, 0.2)
WEIGHT_DECAYS = (0.1, 0.1, 0.1, 0.1, 0.1, 0.1, 0.0)
EPSILON = 1e-08
NORM_EPS = 1e-05
MASK_FILL = -1e30


def shifted_2(value, axis, steps):
    count = lax.axis_size(axis)
    leading, last = (max(0, -steps), min(count, count - steps))
    return lax.ppermute(value, axis, [(source, source + steps) for source in range(leading, last)])


def to_low(values):
    return values.astype(jnp.bfloat16)


def layer_norm(values, gain):
    center = values - jnp.mean(values, axis=-1, keepdims=True)
    spread = jnp.mean(center * center, axis=-1, keepdims=True)
    return center * lax.rsqrt(spread + NORM_EPS) * gain


def rotate(joined, positions, num_heads):
    parts = joined.reshape(joined.shape[0], 3, num_heads, -1)
    half_size = parts.shape[-1] // 2
    freqs = 10000.0 ** (-jnp.arange(half_size, dtype=jnp.float32) / half_size)
    angles = positions.astype(jnp.float32)[:, None] * freqs[None, :]
    cosine = jnp.cos(angles)[:, None, :]
    sine = jnp.sin(angles)[:, None, :]

    def rotate_half(values):
        first_half = values[..., :half_size]
        second_half = values[..., half_size:]
        return jnp.concatenate(
            [first_half * cosine - second_half * sine, first_half * sine + second_half * cosine],
            axis=-1,
        )

    return (rotate_half(parts[:, 0]), rotate_half(parts[:, 1]), parts[:, 2])


def scores_for(q_low, k_low, query_pos, key_pos):
    scores = jnp.einsum(
        "rhe,phe->hrp", q_low, k_low, preferred_element_type=jnp.float32
    ) * q_low.shape[-1] ** (-0.5)
    causal = query_pos[:, None] >= key_pos[None, :]
    return (scores, causal)


def attend(q_low, k_low, v_low, query_pos):
    num_rows, num_heads, head_size = q_low.shape
    key_piece = (
        lax.all_gather(k_low, "seq", axis=0, tiled=True),
        lax.all_gather(v_low, "seq", axis=0, tiled=True),
    )
    running_max = jnp.full((num_heads, num_rows), MASK_FILL, jnp.float32)
    accum = jnp.zeros((num_rows, num_heads, head_size), jnp.float32)
    key_pos = jnp.arange(key_piece[0].shape[0], dtype=jnp.int32)
    scores, causal = scores_for(q_low, key_piece[0], query_pos, key_pos)
    scores = jnp.where(causal[None], scores, MASK_FILL)
    new_max = jnp.maximum(running_max, jnp.max(scores, axis=-1))
    factor = jnp.exp(running_max - new_max)
    attn_prob = jnp.where(causal[None], jnp.exp(scores - new_max[..., None]), 0.0)
    denom = jnp.sum(attn_prob, axis=-1)
    accum = accum * factor.T[:, :, None] + jnp.einsum(
        "hrp,phe->rhe", to_low(attn_prob), key_piece[1], preferred_element_type=jnp.float32
    )
    running_max, denom, accum = (new_max, denom, accum)
    return (accum / denom.T[:, :, None], (running_max + jnp.log(denom)).T)


def block_grads(q_low, grad_low, log_total, row_delta, query_pos, k_low, v_low, key_pos):
    scores, causal = scores_for(q_low, k_low, query_pos, key_pos)
    attn_prob = jnp.where(causal[None], jnp.exp(scores - log_total.T[:, :, None]), 0.0)
    grad_prob = jnp.einsum("rhe,phe->hrp", grad_low, v_low, preferred_element_type=jnp.float32)
    grad_score = to_low(attn_prob * (grad_prob - row_delta.T[:, :, None]))
    score_scale = q_low.shape[-1] ** (-0.5)
    grad_q = (
        jnp.einsum("hrp,phe->rhe", grad_score, k_low, preferred_element_type=jnp.float32)
        * score_scale
    )
    grad_k = (
        jnp.einsum("hrp,rhe->phe", grad_score, q_low, preferred_element_type=jnp.float32)
        * score_scale
    )
    grad_v = jnp.einsum(
        "hrp,rhe->phe", to_low(attn_prob), grad_low, preferred_element_type=jnp.float32
    )
    return (grad_q, grad_k, grad_v)


def attend_back(q_low, k_low, v_low, grad_low, log_total, row_delta, query_pos):
    key_piece = (
        lax.all_gather(k_low, "seq", axis=0, tiled=True),
        lax.all_gather(v_low, "seq", axis=0, tiled=True),
    )
    key_pos = jnp.arange(key_piece[0].shape[0], dtype=jnp.int32)
    grad_q = block_grads(
        q_low, grad_low, log_total, row_delta, query_pos, key_piece[0], key_piece[1], key_pos
    )[0]
    all_totals, all_deltas = (
        lax.all_gather(log_total, "seq", axis=0, tiled=True),
        lax.all_gather(row_delta, "seq", axis=0, tiled=True),
    )
    query_piece = (
        lax.all_gather(q_low, "seq", axis=0, tiled=True),
        lax.all_gather(grad_low, "seq", axis=0, tiled=True),
    )
    piece_rows = query_piece[0].shape[0]
    piece_pos = jnp.arange(piece_rows, dtype=jnp.int32)
    unused_q, grad_k_blk, grad_v_blk = block_grads(
        query_piece[0], query_piece[1], all_totals, all_deltas, piece_pos, k_low, v_low, query_pos
    )
    return (grad_q, grad_k_blk, grad_v_blk)


def layer_forward(hidden, weights, gain_pair, positions):
    w_joined, w_proj, w_rise, w_fall = weights
    num_rows = hidden.shape[0]
    normed = to_low(layer_norm(hidden, gain_pair[0]))
    joined = jnp.dot(normed, w_joined, preferred_element_type=jnp.float32)
    queries, keys, values = rotate(joined, positions, HEADS)
    q_low, k_low, v_low = (to_low(queries), to_low(keys), to_low(values))
    attended, log_total = attend(q_low, k_low, v_low, positions)
    flat_low = to_low(attended.reshape(num_rows, -1))
    middle = hidden + jnp.dot(flat_low, w_proj, preferred_element_type=jnp.float32)
    second = to_low(layer_norm(middle, gain_pair[1]))
    pre_act = jnp.dot(second, w_rise, preferred_element_type=jnp.float32)
    activated = to_low(jax.nn.gelu(pre_act))
    output = middle + jnp.dot(activated, w_fall, preferred_element_type=jnp.float32)
    saved = (
        normed,
        joined,
        q_low,
        k_low,
        v_low,
        attended,
        log_total,
        flat_low,
        middle,
        second,
        pre_act,
        activated,
    )
    return (output, saved)


def layer_backward(hidden, weights, gain_pair, positions, grad_out):
    w_joined, w_proj, w_rise, w_fall = weights
    unused_out, saved = layer_forward(hidden, weights, gain_pair, positions)
    (
        normed,
        joined,
        q_low,
        k_low,
        v_low,
        attended,
        log_total,
        flat_low,
        middle,
        second,
        pre_act,
        activated,
    ) = saved
    fall_low = to_low(grad_out)
    grad_fall = jnp.dot(activated.T, fall_low, preferred_element_type=jnp.float32)
    grad_act = jnp.dot(fall_low, w_fall.T, preferred_element_type=jnp.float32)
    grad_pre = to_low(jax.vjp(jax.nn.gelu, pre_act)[1](grad_act)[0])
    grad_rise = jnp.dot(second.T, grad_pre, preferred_element_type=jnp.float32)
    grad_second = jnp.dot(grad_pre, w_rise.T, preferred_element_type=jnp.float32)
    grad_middle_n, grad_gain_ffn = jax.vjp(layer_norm, middle, gain_pair[1])[1](grad_second)
    grad_middle = grad_out + grad_middle_n
    proj_low = to_low(grad_middle)
    grad_proj = jnp.dot(flat_low.T, proj_low, preferred_element_type=jnp.float32)
    grad_att = to_low(
        jnp.dot(proj_low, w_proj.T, preferred_element_type=jnp.float32).reshape(attended.shape)
    )
    row_delta = jnp.sum(grad_att.astype(jnp.float32) * attended, axis=-1)
    grad_q, grad_k, grad_v = attend_back(
        q_low, k_low, v_low, grad_att, log_total, row_delta, positions
    )

    def rotate_joined(joined_in):
        return rotate(joined_in, positions, HEADS)

    grad_joined = to_low(jax.vjp(rotate_joined, joined)[1]((grad_q, grad_k, grad_v))[0])
    grad_w_joined = jnp.dot(normed.T, grad_joined, preferred_element_type=jnp.float32)
    grad_normed = jnp.dot(grad_joined, w_joined.T, preferred_element_type=jnp.float32)
    grad_in_n, grad_gain_attn = jax.vjp(layer_norm, hidden, gain_pair[0])[1](grad_normed)
    return (
        grad_middle + grad_in_n,
        (grad_w_joined, grad_proj, grad_rise, grad_fall),
        jnp.stack([grad_gain_attn, grad_gain_ffn]),
    )


def adam_update(weight, gradient, moment_one, moment_two, step_rate, decay_rate):
    moment_one = BETA_ONE * moment_one + (1.0 - BETA_ONE) * gradient
    moment_two = BETA_TWO * moment_two + (1.0 - BETA_TWO) * gradient * gradient
    first_hat = moment_one / (1.0 - BETA_ONE**STEP)
    second_hat = moment_two / (1.0 - BETA_TWO**STEP)
    weight = weight - step_rate * (
        first_hat / (jnp.sqrt(second_hat) + EPSILON) + decay_rate * weight
    )
    return (weight, moment_one, moment_two)


def on_device_general(
    byte_ids,
    targets,
    item_lengths,
    w_qkv,
    w_out,
    w_up,
    w_down,
    embed,
    head,
    gains,
    mom_qkv,
    mom_out,
    mom_up,
    mom_down,
    mom_embed,
    mom_head,
    mom_gains,
    sec_qkv,
    sec_out,
    sec_up,
    sec_down,
    sec_embed,
    sec_head,
    sec_gains,
):
    low_qkv, low_out, low_up, low_down, low_embed, low_head, low_gains = (
        lax.all_gather(to_low(w_qkv), ("dp", "seq"), axis=1, tiled=True),
        lax.all_gather(to_low(w_out), ("dp", "seq"), axis=1, tiled=True),
        lax.all_gather(to_low(w_up), ("dp", "seq"), axis=1, tiled=True),
        lax.all_gather(to_low(w_down), ("dp", "seq"), axis=1, tiled=True),
        lax.all_gather(to_low(embed), ("dp", "seq"), axis=0, tiled=True),
        lax.all_gather(to_low(head), ("dp", "seq"), axis=0, tiled=True),
        lax.all_gather(to_low(gains), ("dp", "seq"), axis=1, tiled=True),
    )
    gain_rows = low_gains.astype(jnp.float32)
    byte_row = byte_ids[0]
    num_rows = byte_row.shape[0]
    short_rows = num_rows // RATE
    seq_place = lax.axis_index("seq")
    positions = seq_place * num_rows + jnp.arange(num_rows, dtype=jnp.int32)
    short_pos = seq_place * short_rows + jnp.arange(short_rows, dtype=jnp.int32)
    vocab_ids = jnp.arange(VOCAB, dtype=jnp.int32)
    one_hot_in = (byte_row[:, None] == vocab_ids[None, :]).astype(jnp.float32)
    embedded = jnp.dot(
        one_hot_in.astype(jnp.bfloat16), low_embed, preferred_element_type=jnp.float32
    )
    lower_weights = (low_qkv[0], low_out[0], low_up[0], low_down[0])
    upper_weights = (low_qkv[1], low_out[1], low_up[1], low_down[1])
    first_out, unused_first = layer_forward(embedded, lower_weights, gain_rows[0:2], positions)
    left_rim = shifted_2(first_out[num_rows - RATE + 1 :], "seq", 1)
    shifted = jnp.concatenate([left_rim, first_out[: num_rows - RATE + 1]], axis=0)
    pooled = jnp.mean(shifted.reshape(short_rows, RATE, -1), axis=1)
    short_out, unused_short = layer_forward(pooled, upper_weights, gain_rows[2:4], short_pos)
    upsampled = first_out + jnp.repeat(short_out, RATE, axis=0)
    top_gain = gain_rows[gain_rows.shape[0] - 1]
    final_low = to_low(layer_norm(upsampled, top_gain))
    logits = jnp.dot(final_low, low_head, preferred_element_type=jnp.float32)
    row_max = jnp.max(logits, axis=-1, keepdims=True)
    log_total = row_max[:, 0] + jnp.log(jnp.sum(jnp.exp(logits - row_max), axis=-1))
    one_hot_out = (targets[0][:, None] == vocab_ids[None, :]).astype(jnp.float32)
    picked = jnp.sum(one_hot_out * logits, axis=-1)
    lengths = item_lengths[0]
    ends = jnp.cumsum(lengths)
    doc_index = jnp.sum((positions[:, None] >= ends[None, :]).astype(jnp.int32), axis=1)
    item_ids = jnp.arange(lengths.shape[0], dtype=jnp.int32)
    doc_length = jnp.sum(
        jnp.where(item_ids[None, :] == doc_index[:, None], lengths[None, :], 0), axis=1
    ).astype(jnp.float32)
    loss_local = jnp.sum((log_total - picked) / doc_length)
    loss_sum = lax.psum(loss_local, ("dp", "seq"))
    grad_logits = to_low((jnp.exp(logits - log_total[:, None]) - one_hot_out) / doc_length[:, None])
    grad_head = jnp.dot(final_low.T, grad_logits, preferred_element_type=jnp.float32)
    grad_final = jnp.dot(grad_logits, low_head.T, preferred_element_type=jnp.float32)
    grad_upsampled, grad_gain_top = jax.vjp(layer_norm, upsampled, top_gain)[1](grad_final)
    grad_short = jnp.sum(grad_upsampled.reshape(short_rows, RATE, -1), axis=1)
    grad_pooled, upper_grads, upper_gain_grads = layer_backward(
        pooled, upper_weights, gain_rows[2:4], short_pos, grad_short
    )
    grad_shifted = jnp.repeat(grad_pooled / RATE, RATE, axis=0)
    rim_grad = shifted_2(grad_shifted[: RATE - 1], "seq", -1)
    grad_first = grad_upsampled + jnp.concatenate([grad_shifted[RATE - 1 :], rim_grad], axis=0)
    grad_embedded, lower_grads, lower_gain_grads = layer_backward(
        embedded, lower_weights, gain_rows[0:2], positions, grad_first
    )
    grad_embed = jnp.dot(one_hot_in.T, grad_embedded, precision=lax.Precision.HIGHEST)
    grad_gains = jnp.concatenate(
        [lower_gain_grads, upper_gain_grads, grad_gain_top[None, :]], axis=0
    )
    shard_grads = (
        lax.psum_scatter(
            jnp.stack([lower_grads[0], upper_grads[0]]),
            ("dp", "seq"),
            scatter_dimension=1,
            tiled=True,
        ),
        lax.psum_scatter(
            jnp.stack([lower_grads[1], upper_grads[1]]),
            ("dp", "seq"),
            scatter_dimension=1,
            tiled=True,
        ),
        lax.psum_scatter(
            jnp.stack([lower_grads[2], upper_grads[2]]),
            ("dp", "seq"),
            scatter_dimension=1,
            tiled=True,
        ),
        lax.psum_scatter(
            jnp.stack([lower_grads[3], upper_grads[3]]),
            ("dp", "seq"),
            scatter_dimension=1,
            tiled=True,
        ),
        lax.psum_scatter(grad_embed, ("dp", "seq"), scatter_dimension=0, tiled=True),
        lax.psum_scatter(grad_head, ("dp", "seq"), scatter_dimension=0, tiled=True),
        lax.psum_scatter(grad_gains, ("dp", "seq"), scatter_dimension=1, tiled=True),
    )
    squares = sum((jnp.sum(piece_grad * piece_grad) for piece_grad in shard_grads))
    total_squares = lax.psum(squares, ("dp", "seq"))
    grad_norm = jnp.sqrt(total_squares)
    clip_factor = jnp.minimum(1.0, CLIP_NORM / grad_norm)
    masters = (w_qkv, w_out, w_up, w_down, embed, head, gains)
    firsts = (mom_qkv, mom_out, mom_up, mom_down, mom_embed, mom_head, mom_gains)
    seconds = (sec_qkv, sec_out, sec_up, sec_down, sec_embed, sec_head, sec_gains)
    results = []
    for slot_index in range(7):
        results.append(
            adam_update(
                masters[slot_index],
                shard_grads[slot_index] * clip_factor,
                firsts[slot_index],
                seconds[slot_index],
                STEP_RATES[slot_index],
                WEIGHT_DECAYS[slot_index],
            )
        )
    return (
        loss_sum,
        grad_norm,
        results[0][0],
        results[1][0],
        results[2][0],
        results[3][0],
        results[4][0],
        results[5][0],
        results[6][0],
        results[0][1],
        results[1][1],
        results[2][1],
        results[3][1],
        results[4][1],
        results[5][1],
        results[6][1],
        results[0][2],
        results[1][2],
        results[2][2],
        results[3][2],
        results[4][2],
        results[5][2],
        results[6][2],
    )


LOW = jnp.bfloat16
F32 = jnp.float32
MESH = pl.DeviceIdType.MESH
D = 512

EG, LAYER0, LAYER_ROWS = 0, 16, 192
QKV, OUT, UP, DOWN = 0, 48, 64, 128
HEAD = LAYER0 + 2 * LAYER_ROWS
ROWS = HEAD + 16
PIECES = {
    "A": (0, 16, 32),
    "a": (32, 48, 64),
    "B": (64, 96, 144),
    "b": (144, 176, 208),
    "C": (208, 240, 272),
    "D": (272, 304, 336),
    "d": (336, 384, ROWS),
}
SCHEDULE = {
    "start": "Aa",
    "packed": "AaBAabCAaBAa",
    "f0_sent": "Bb",
    "f0_got": "CDd",
    "f0_part0": "bB",
    "f0_part1": "C",
    "f0_home": "B",
    "f0_up": "Dbb",
    "f0_rim": "Cd",
    "f0_end": "C",
    "f1_sent": "D",
    "f1_got": "",
    "f1_part0": "dD",
    "f1_home": "",
    "f1_out": "D",
    "f1_up": "dd",
    "b1_ff": "dD",
    "b1_sent": "D",
    "b1_part0": "",
    "b1_sums": "d",
    "b1_home": "",
    "b1_end": "C",
    "b1_rim": "D",
    "b0_ff": "BbCd",
    "b0_sent": "D",
    "b0_part1": "Bd",
    "b0_part0": "",
    "b0_sums": "bC",
    "b0_home": "B",
    "b0_kv": "a",
    "b0_end": "A",
    "tail0": "aA",
    "tail1": "b",
    "tail2": "aA",
    "tail3": "b",
    "tail4": "aA",
}


def dot(a, b):
    return jnp.dot(a, b, preferred_element_type=F32)


def dot_nt(a, b):
    return lax.dot_general(a, b, (((1,), (1,)), ((), ())), preferred_element_type=F32)


def dot_tn(a, b):
    return lax.dot_general(a, b, (((0,), (0,)), ((), ())), preferred_element_type=F32)


def low(v):
    return v.astype(LOW)


exact = functools.partial(jnp.dot, preferred_element_type=F32, precision=lax.Precision.HIGHEST)


def lanes(shape):
    return lax.broadcasted_iota(jnp.int32, shape, len(shape) - 1)


def roll64(v):
    return pltpu.roll(v, 64, 1)


def swap32(v):
    return jnp.where(lanes(v.shape) % 64 < 32, pltpu.roll(v, 96, 1), pltpu.roll(v, 32, 1))


def norm_parts(v):
    center = v - jnp.mean(v, axis=-1, keepdims=True)
    scale = lax.rsqrt(jnp.mean(center * center, axis=-1, keepdims=True) + NORM_EPS)
    return center * scale, scale


def norm_back(v, gain, grad):
    unit, scale = norm_parts(v)
    g = grad * gain
    out = scale * (g - jnp.mean(g, axis=-1, keepdims=True) - unit * jnp.mean(g * unit, axis=-1, keepdims=True))
    return out, jnp.sum(grad * unit, axis=0, keepdims=True)


GELU_A, GELU_B = 0.7978845608028654, 0.044715


def gelu(v):
    return 0.5 * v * (1.0 + jnp.tanh(GELU_A * (v + GELU_B * v * v * v)))


def gelu_grad(v):
    t = jnp.tanh(GELU_A * (v + GELU_B * v * v * v))
    return 0.5 * (1.0 + t) + 0.5 * v * (1.0 - t * t) * (GELU_A * (1.0 + 3.0 * GELU_B * v * v))


class Bag:
    pass


def scope(name):
    return contextlib.nullcontext()


def remote(src, dst, send, recv, device):
    return pltpu.make_async_remote_copy(
        src_ref=src, dst_ref=dst, send_sem=send, recv_sem=recv, device_id=device, device_id_type=MESH
    )


def pack_pair(block, odd):
    half = block.shape[0] // 2
    top, bottom = block[:half], block[half:]
    if odd:
        top = roll64(top)
    else:
        bottom = roll64(bottom)
    return jnp.where(lanes(top.shape) < 64, top, bottom)


def unpack_pair(even, odd):
    left = lanes(even.shape) < 64
    top = jnp.where(left, even, roll64(odd))
    bottom = jnp.where(left, roll64(even), odd)
    return jnp.concatenate([top, bottom], axis=0)


def unpack_left(x):
    left = lanes(x.shape) < 64
    return jnp.concatenate([jnp.where(left, x, 0.0), jnp.where(left, roll64(x), 0.0)], axis=0)


def unpack_right(x):
    left = lanes(x.shape) < 64
    return jnp.concatenate([jnp.where(left, 0.0, roll64(x)), jnp.where(left, 0.0, x)], axis=0)


def pack_left(x):
    half = x.shape[0] // 2
    return jnp.where(lanes((half, 128)) < 64, x[:half], roll64(x[half:]))


def pack_right(x):
    half = x.shape[0] // 2
    return jnp.where(lanes((half, 128)) < 64, roll64(x[:half]), x[half:])


def kernel(*refs):
    k = Bag()
    names = IN_NAMES + OUT_NAMES + tuple(SCRATCH)
    for name, ref in zip(names, refs[:-1]):
        setattr(k, name, ref)
    k.sems = refs[-1]
    for name in PER_LAYER:
        setattr(k, name, [getattr(k, name + "0"), getattr(k, name + "1")])
    k.hold = []
    for layer in range(2):
        hold = Bag()
        for name in HELD:
            setattr(hold, name, getattr(k, "h_" + name + str(layer)))
        k.hold.append(hold)
    g = lax.axis_index("dp")
    s = lax.axis_index("seq")
    z, y, x = s // 4, lax.rem(s // 2, 2), lax.rem(s, 2)
    k.g, k.s, k.z, k.y, k.x = g, s, z, y, x
    k.side = lax.rem(x + y, 2)
    k.cursor = 0

    def dev(g, z, y, x):
        return (g, z * 4 + y * 2 + x)

    k.dev = dev

    barrier = pltpu.get_barrier_semaphore()
    me = g * 16 + s

    @pl.loop(1, 32)
    def _(i):
        t = lax.rem(me + i, 32)
        pl.semaphore_signal(barrier, inc=1, device_id=(t // 16, lax.rem(t, 16)), device_id_type=MESH)

    own = k.pk.at[g, z, y, x]
    own[EG : EG + 16, 0:256] = low(jnp.concatenate([k.embed[:, 0:256], k.embed[:, 256:512]], axis=0))
    place = lanes((16, 256)) - 16 * s == lax.broadcasted_iota(jnp.int32, (16, 256), 0)
    gains = exact(k.gains[...], jnp.where(place, 1.0, 0.0))
    gains = jnp.concatenate([gains, jnp.zeros((3, 256), F32)], axis=0)
    gains = jnp.concatenate([jnp.where(g == 0, gains, 0.0), jnp.where(g == 1, gains, 0.0)], axis=0)
    own[EG : EG + 16, 256:512] = low(gains)
    pack_layer(k, own, 0)
    with scope("barrier"):
        pl.semaphore_wait(barrier, 31)
    k.gathers = {name: gather_piece(k, name, *rows) for name, rows in PIECES.items()}
    k.reduces = {name: reduce_piece(k, name, *rows) for name, rows in PIECES.items()}
    k.ready, k.summed = set(), set()
    point(k, "start")
    own[HEAD : HEAD + 16, 0:256] = low(k.head[...])
    own[HEAD : HEAD + 16, 256:512] = jnp.zeros((16, 256), LOW)
    pack_layer(k, own, 1)
    point(k, "packed")
    forward_backward(k)
    finish_grads(k)


def point(k, name):
    moving = k.gathers if name[0] in "spf" else k.reduces
    for piece in SCHEDULE[name]:
        next(moving[piece])


def pack_layer(k, own, layer):
    base = LAYER0 + layer * LAYER_ROWS
    own[base + QKV : base + QKV + 16, :] = low(k.w_qkv[layer, :, 0:512])
    for pair in range(4):
        keys = k.w_qkv[layer, :, 512 + 128 * pair : 640 + 128 * pair]
        vals = k.w_qkv[layer, :, 1024 + 128 * pair : 1152 + 128 * pair]
        left = lanes(keys.shape) < 64
        row = base + QKV + 16 + 16 * (pair // 2)
        col = 256 * (pair % 2)
        own[row : row + 16, col : col + 128] = low(jnp.where(left, keys, roll64(vals)))
        own[row : row + 16, col + 128 : col + 256] = low(jnp.where(left, roll64(keys), vals))
    own[base + OUT : base + OUT + 16, :] = low(k.w_out[layer])
    for j in range(4):
        own[base + UP + 16 * j : base + UP + 16 * j + 16, :] = low(k.w_up[layer, :, 512 * j : 512 * j + 512])
    own[base + DOWN : base + DOWN + 64, :] = low(k.w_down[layer])


def sem(k):
    k.cursor += 1
    assert k.cursor <= SEMS
    return k.sems.at[k.cursor - 1]


def start_all(copies):
    for copy in copies:
        copy.start()


def wait_all(copies):
    for copy in copies:
        copy.wait()


def drain(semaphore, ref):
    pltpu.make_async_copy(ref, ref, semaphore).wait()


class Stage:
    def __init__(self, k, total, moves):
        self.total, self.sent, self.got = total, sem(k), sem(k)
        start_all([remote(src, dst, self.sent, self.got, device) for src, dst, device in moves])

    def wait(self):
        drain(self.got, self.total)
        drain(self.sent, self.total)


def gather_piece(k, name, r0, rm, r1):
    g, z, y, x, dev, pk = k.g, k.z, k.y, k.x, k.dev, k.pk
    a, b, every = pl.ds(r0, rm - r0), pl.ds(rm, r1 - rm), pl.ds(r0, r1 - r0)

    def stage(total, *moves):
        return Stage(k, total, [(ref, ref, device) for ref, device in moves])

    stages = (
        lambda: stage(
            pk.at[g, pl.ds(0, 3), y, x, every],
            *[(pk.at[g, z, y, x, every], dev(g, lax.rem(z + n, 4), y, x)) for n in (2, 1, 3)],
        ),
        lambda: stage(
            pk.at[g, :, y, x, every],
            (pk.at[g, :, y, x, a], dev(g, z, 1 - y, x)),
            (pk.at[g, :, y, x, b], dev(g, z, y, 1 - x)),
        ),
        lambda: stage(
            pk.at[g, :, :, x, every],
            (pk.at[g, :, :, x, a], dev(g, z, y, 1 - x)),
            (pk.at[g, :, y, :, b], dev(g, z, 1 - y, x)),
        ),
        lambda: stage(pk.at[1 - g, :, :, :, every], (pk.at[g, :, :, :, every], dev(1 - g, z, y, x))),
    )
    waiting = None
    for begin in stages:
        if waiting is not None:
            with scope(f"gw_{name}"):
                waiting.wait()
        waiting = begin()
        yield
    with scope(f"gw_{name}"):
        waiting.wait()
    k.ready.update(range(r0, r1, 16))
    yield


def need(k, row, count=16):
    assert k.ready.issuperset(range(row, row + count, 16)), row


def block(k, row):
    need(k, row)
    return k.pk[:, :, :, :, row : row + 16, :].reshape(512, 512)


def put_block(ref, row, value):
    ref[:, :, :, :, row : row + 16, :] = low(value).reshape(2, 4, 2, 2, 16, 512)


def down_block(k, row, c):
    need(k, row, 64)
    return k.pk[c // 2, (c % 2) * 2 : (c % 2) * 2 + 2, :, :, row : row + 64, :].reshape(512, 512)


def put_down(ref, row, c, value):
    ref[c // 2, (c % 2) * 2 : (c % 2) * 2 + 2, :, :, row : row + 64, :] = low(value).reshape(2, 2, 2, 64, 512)


def my_blocks(k):
    return [4 * j + (k.g if half == 0 else 3 - k.g) for j in range(4) for half in range(2)]


def other_blocks(k):
    return [4 * j + (1 - k.g if half == 0 else 2 + k.g) for j in range(4) for half in range(2)]


def my_block(k, i):
    return 4 * (i // 2) + jnp.where(lax.rem(i, 2) == 0, k.g, 3 - k.g)


class Post:
    def __init__(self, k, source, groups):
        self.k, self.source = k, source
        self.sent, self.got = sem(k), [sem(k) for _ in range(groups)]

    def start(self, src, dst, got, device):
        k = self.k
        is_self = jnp.logical_and(device[0] == k.g, device[1] == k.s)

        @pl.when(is_self)
        def _():
            pltpu.make_async_copy(src, dst, got).start()

        @pl.when(jnp.logical_not(is_self))
        def _():
            remote(src, dst, self.sent, got, device).start()

    def finish(self, one_is_self):
        @pl.when(one_is_self)
        def _():
            drain(self.sent, self.source.at[pl.ds(0, 7)])

        @pl.when(jnp.logical_not(one_is_self))
        def _():
            drain(self.sent, self.source)


class ToHeads(Post):
    def __init__(self, k, source, target):
        super().__init__(k, source, 2)
        self.target = target

    def send(self):
        k = self.k
        for part in range(2):

            @pl.when(k.s // 8 == part)
            def _():
                for h in range(8):
                    self.start(self.source.at[h], self.target.at[k.s], self.got[part], (k.side, k.g * 8 + h))

    def take(self, part):
        drain(self.got[part], self.target.at[pl.ds(0, 4)])

    def done(self):
        k = self.k
        self.finish(jnp.logical_and(k.s // 8 == k.g, k.side == k.g))


class FromHeads(Post):
    def __init__(self, k, source, target):
        super().__init__(k, source, 1)
        self.target = target

    def send(self, i, b):
        k = self.k
        head = lax.rem(k.s, 8)
        self.start(self.source.at[i], self.target.at[head], self.got[0], (k.s // 8, b))

    def take(self):
        drain(self.got[0], self.target)

    def done(self):
        k = self.k
        self.finish(jnp.logical_and(k.s // 8 == k.g, k.side == k.g))


def rotate_block(v, cosine, sine):
    return v * cosine + swap32(v) * sine


def rotary_tables(k, layer):
    rows, _ = layer_sizes(layer)
    lane = lanes((1, 128))
    freqs = jnp.zeros((1, 128), F32)
    for i in range(32):
        freqs = jnp.where(lane % 32 == i, 10000.0 ** (-i / 32), freqs)
    position = k.s * rows + lax.broadcasted_iota(jnp.int32, (rows, 1), 0)
    angles = position.astype(F32) * freqs
    k.cos[layer][...] = jnp.cos(angles)
    k.sin[layer][...] = jnp.sin(angles) * jnp.where(lane % 64 < 32, -1.0, 1.0)


def layer_sizes(layer):
    rows = 144 if layer == 0 else 48
    return rows, (rows // 2 + 15) // 16 * 16


def attend_loop(layer, part, body, between=None):
    if layer == 1:
        body(list(range(8)), 16)
        return
    for first in (0, 2):
        @pl.loop(first, first + 2)
        def _(n):
            body([part * 4 + n], 8 * (part + 1))

        if between is not None and first == 0:
            between()


def stack(pieces):
    return pieces[0] if len(pieces) == 1 else jnp.concatenate(pieces, axis=0)


def masked_scores(q, kv, places):
    scores = dot_nt(q, kv)
    return jnp.where(lanes(scores.shape) <= places, scores, MASK_FILL)


def stacked_queries(k, layer, items):
    rows, pad = layer_sizes(layer)
    blocks = [my_block(k, i) for i in items]
    q = stack([unpack_left(k.inbox[layer][b, 0:pad, :].astype(F32)[: rows // 2]) for b in blocks])
    places = stack([b * rows + lax.broadcasted_iota(jnp.int32, (rows, 1), 0) for b in blocks])
    return low(q * 0.125), blocks, places


def attention_forward(k, layer, part, post):
    rows, pad = layer_sizes(layer)
    inbox, outbox, lse, keep = k.inbox[layer], k.abox[layer], k.lse[layer], k.att[layer]

    def body(items, count):
        q, blocks, places = stacked_queries(k, layer, items)
        kv = inbox[0:count, pad : pad + rows, :].reshape(count * rows, 128)
        scores = masked_scores(q, kv, places)
        top = jnp.max(scores, axis=-1, keepdims=True)
        prob = jnp.exp(scores - top)
        total = jnp.sum(prob, axis=-1, keepdims=True)
        out = dot(low(prob), kv) / total
        stat = jnp.broadcast_to(top + jnp.log(total), out.shape)
        for n, (i, b) in enumerate(zip(items, blocks)):
            span = slice(n * rows, (n + 1) * rows)
            lse[i] = stat[span]
            keep[i] = out[span]
            outbox[i, 0 : rows // 2, :] = low(pack_right(out[span]))
            post.send(i, b)

    attend_loop(layer, part, body)


def attention_backward(k, layer, part, post, between=None):
    rows, pad = layer_sizes(layer)
    inbox, gradbox, lse, keep = k.inbox[layer], k.gbox[layer], k.lse[layer], k.att[layer]
    dkvt, outbox = k.dkvt[layer], k.dbox[layer]

    def body(items, count):
        q, blocks, places = stacked_queries(k, layer, items)
        kv = inbox[0:count, pad : pad + rows, :].reshape(count * rows, 128)
        grad = stack([unpack_right(gradbox[b].astype(F32)[: rows // 2]) for b in blocks])
        delta = jnp.sum(grad * stack([keep[i] for i in items]), axis=-1, keepdims=True)
        grad = low(grad)
        prob = jnp.exp(masked_scores(q, kv, places) - stack([lse[i] for i in items])[:, 0:1])
        grad_prob = dot_nt(grad, kv)
        ds = low(prob * (grad_prob - delta))
        dq = dot(ds, kv) * 0.125
        for n, (i, b) in enumerate(zip(items, blocks)):
            outbox[i, 0 : rows // 2, :] = low(pack_left(dq[n * rows : (n + 1) * rows]))
            post.send(i, b)
        dkvt[:, 0 : count * rows] += dot_tn(q, ds) + dot_tn(grad, low(prob))

    attend_loop(layer, part, body, between)


class KeySums:
    def __init__(self, k, layer, part, post):
        rows, _ = layer_sizes(layer)
        self.k, self.layer, self.post = k, layer, post
        self.items = range(8) if layer == 1 else range(4 * part, 4 * part + 4)
        first, count = (0, 16) if layer == 1 else (8 * part, 8)
        k.dkv[layer][first : first + count] = (
            k.dkvt[layer][:, first * rows : (first + count) * rows].T.reshape(count, rows, 128)
        )
        others = other_blocks(k)
        for i in self.items:
            k.dkv_out[layer][i] = k.dkv[layer][others[i]]
        span = pl.ds(self.items[0], len(self.items))
        self.copy = Stage(
            k,
            k.dkv_in[layer].at[span],
            [(k.dkv_out[layer].at[span], k.dkv_in[layer].at[span], k.dev(1 - k.g, k.z, k.y, k.x))],
        )

    def send(self):
        k, layer = self.k, self.layer
        self.copy.wait()
        mine = my_blocks(k)
        for i in self.items:
            k.kvbox[layer][i] = low(k.dkv[layer][mine[i]] + k.dkv_in[layer][i])
            self.post.send(i, mine[i])


def layer_ahead(k, layer, hidden):
    rows, pad = layer_sizes(layer)
    base = LAYER0 + layer * LAYER_ROWS
    hold = k.hold[layer]
    hold.hidden[...] = hidden
    unit, _ = norm_parts(hidden)
    normed = low(unit * k.gain[2 * layer : 2 * layer + 1, :])
    hold.normed[...] = normed
    cosine, sine = k.cos[layer][...], k.sin[layer][...]
    left = lanes(cosine.shape) < 64
    cos_kv, sin_kv = jnp.where(left, cosine, 1.0), jnp.where(left, sine, 0.0)
    sendbox = k.sendbox[layer]
    for part in range(3):
        joined = dot(normed, block(k, base + QKV + 16 * part))
        for n in range(4):
            piece = joined[:, 128 * n : 128 * n + 128]
            if part == 0:
                piece = rotate_block(piece, cosine, sine)
                sendbox[2 * n, 0 : rows // 2, :] = low(pack_pair(piece, 0))
                sendbox[2 * n + 1, 0 : rows // 2, :] = low(pack_pair(piece, 1))
            else:
                sendbox[4 * part - 4 + n, pad : pad + rows, :] = low(rotate_block(piece, cos_kv, sin_kv))
    inbox = k.inbox[layer]
    out = ToHeads(k, sendbox, inbox)
    out.send()
    point(k, f"f{layer}_sent")
    sent, shared = sem(k), [sem(k), sem(k)]
    mine, others = my_blocks(k), other_blocks(k)
    for part in range(2):
        with scope("take"):
            out.take(part)
        for b in mine[4 * part : 4 * part + 4]:
            ref = inbox.at[b, pl.ds(pad, rows)]
            remote(ref, ref, sent, shared[part], k.dev(1 - k.g, k.z, k.y, k.x)).start()
    point(k, f"f{layer}_got")
    home = k.home[layer]
    back = FromHeads(k, k.abox[layer], home)
    for part in range(2 - layer):
        for half in range(2) if layer == 1 else [part]:
            with scope("share"):
                drain(shared[half], inbox.at[pl.ds(0, 4), pl.ds(pad, rows)])
        with scope("attend"):
            attention_forward(k, layer, part, back)
        point(k, f"f{layer}_part{part}")
    with scope("home"):
        back.take()
    point(k, f"f{layer}_home")
    if layer == 1:
        point(k, "f1_out")
    for n in range(4):
        pair = unpack_pair(
            home[2 * n].astype(F32)[: rows // 2], home[2 * n + 1].astype(F32)[: rows // 2]
        )
        hold.flat[:, 128 * n : 128 * n + 128] = low(pair)
    middle = hidden + dot(hold.flat[...], block(k, base + OUT))
    hold.middle[...] = middle
    unit, _ = norm_parts(middle)
    second = low(unit * k.gain[2 * layer + 1 : 2 * layer + 2, :])
    hold.second[...] = second
    for j in range(4):
        pre = dot(second, block(k, base + UP + 16 * j))
        hold.pre[:, 512 * j : 512 * j + 512] = pre
        hold.act[:, 512 * j : 512 * j + 512] = low(gelu(pre))
    output = middle
    point(k, f"f{layer}_up")
    for c in range(4):
        output = output + dot(hold.act[:, 512 * c : 512 * c + 512], down_block(k, base + DOWN, c))
    out.done()
    back.done()
    drain(sent, inbox.at[pl.ds(0, 8), pl.ds(pad, rows)])
    return output


def layer_back(k, layer, grad_out):
    rows, pad = layer_sizes(layer)
    base = LAYER0 + layer * LAYER_ROWS
    hold = k.hold[layer]
    fall = low(grad_out)
    grad_second = jnp.zeros((rows, D), F32)
    second = hold.second[...]
    for c in range(4):
        cols = slice(512 * c, 512 * c + 512)
        put_down(k.gr, base + DOWN, c, dot_tn(hold.act[:, cols], fall))
        grad_act = dot_nt(fall, down_block(k, base + DOWN, c))
        grad_pre = low(grad_act * gelu_grad(hold.pre[:, cols]))
        put_block(k.gr, base + UP + 16 * c, dot_tn(second, grad_pre))
        grad_second = grad_second + dot_nt(grad_pre, block(k, base + UP + 16 * c))
    if layer == 1:
        point(k, "b1_ff")
    gain = k.gain[2 * layer + 1 : 2 * layer + 2, :]
    grad_mid, k.gain_grads[2 * layer + 1] = norm_back(hold.middle[...], gain, grad_second)
    grad_middle = grad_out + grad_mid
    hold.middle[...] = grad_middle
    proj = low(grad_middle)
    put_block(k.gr, base + OUT, dot_tn(hold.flat[...], proj))
    grad_att = dot_nt(proj, block(k, base + OUT))
    gsend = k.gsend[layer]
    for n in range(4):
        piece = grad_att[:, 128 * n : 128 * n + 128]
        gsend[2 * n, 0 : rows // 2, :] = low(pack_pair(piece, 0))
        gsend[2 * n + 1, 0 : rows // 2, :] = low(pack_pair(piece, 1))
    out = ToHeads(k, gsend, k.gbox[layer])
    out.send()
    if layer == 0:
        point(k, "b0_ff")
    back = k.back[layer]
    home_q = FromHeads(k, k.dbox[layer], back)
    home_kv = FromHeads(k, k.kvbox[layer], k.kvback[layer])
    k.dkvt[layer][...] = jnp.zeros_like(k.dkvt[layer])
    point(k, f"b{layer}_sent")
    sums = None
    for part in reversed(range(2 - layer)):
        with scope("take"):
            for half in range(2) if layer == 1 else [part]:
                out.take(half)
        with scope("unattend"):
            attention_backward(k, layer, part, home_q, None if sums is None else sums.send)
        sums = KeySums(k, layer, part, home_kv)
        point(k, f"b{layer}_part{part}")
    with scope("sums"):
        sums.send()
    point(k, f"b{layer}_sums")
    with scope("home_q"):
        home_q.take()
    cosine, sine = k.cos[layer][...], k.sin[layer][...]
    left = lanes(cosine.shape) < 64
    cos_kv, sin_kv = jnp.where(left, cosine, 1.0), jnp.where(left, sine, 0.0)
    normed = hold.normed[...]
    grad_normed = jnp.zeros((rows, D), F32)
    for part in range(3):
        if part == 1:
            with scope("home_kv"):
                home_kv.take()
            point(k, f"b{layer}_home")
        for n in range(4):
            if part == 0:
                piece = unpack_pair(
                    back[2 * n].astype(F32)[: rows // 2],
                    back[2 * n + 1].astype(F32)[: rows // 2],
                )
                piece = rotate_block(piece, cosine, -sine)
            else:
                piece = k.kvback[layer][4 * part - 4 + n].astype(F32)
                piece = rotate_block(piece, cos_kv, -sin_kv)
            hold.gj[:, 128 * n : 128 * n + 128] = low(piece)
        gj = hold.gj[...]
        put_block(k.gr, base + QKV + 16 * part, dot_tn(normed, gj))
        grad_normed = grad_normed + dot_nt(gj, block(k, base + QKV + 16 * part))
    if layer == 0:
        point(k, "b0_kv")
    gain = k.gain[2 * layer : 2 * layer + 1, :]
    grad_in, k.gain_grads[2 * layer] = norm_back(hold.hidden[...], gain, grad_normed)
    out.done()
    home_q.done()
    home_kv.done()
    if layer == 1:
        point(k, "b1_end")
    return hold.middle[...] + grad_in


def byte_matrix(ids, half):
    n = lanes((ids.shape[0], 512))
    return low(jnp.where((n // 16 * 8 + n % 8 == ids) & (n // 8 % 2 == half), 1.0, 0.0))


def forward_backward(k):
    rows, short = 144, 48
    need(k, EG)
    gains = jnp.sum(k.pk[:, :, :, :, EG : EG + 16, 256:512].astype(F32).reshape(32, 16, 256), axis=0)
    k.gain[:, 0:256] = gains[0:8]
    k.gain[:, 256:512] = gains[8:16]
    k.gain_grads = [None] * 5
    table = k.pk[:, :, :, :, EG : EG + 16, 0:256].reshape(512, 256)
    k.columns[0:1, 0:rows] = k.ids[...].astype(F32)
    k.columns[1:2, 0:rows] = k.targets[...].astype(F32)
    columns = k.columns[...].T
    ids, targets = columns[0:rows, 0:1].astype(jnp.int32), columns[0:rows, 1:2].astype(jnp.int32)
    for layer in range(2):
        rotary_tables(k, layer)
    first_in = jnp.concatenate([dot(byte_matrix(ids, 0), table), dot(byte_matrix(ids, 1), table)], axis=1)
    first = layer_ahead(k, 0, first_in)
    k.shift[8 : 8 + rows, :] = first
    rim = remote(
        k.shift.at[pl.ds(rows, 8)], k.shift.at[pl.ds(0, 8)], sem(k), sem(k), (k.g, lax.rem(k.s + 1, 16))
    )

    @pl.when(k.s < 15)
    def _():
        rim.start()

    point(k, "f0_rim")

    @pl.when(k.s > 0)
    def _():
        rim.wait_recv()

    @pl.when(k.s == 0)
    def _():
        k.shift[0:8, :] = jnp.zeros((8, D), F32)

    @pl.when(k.s < 15)
    def _():
        rim.wait_send()

    def pool_matrix(shape, offset, axis):
        j = lax.broadcasted_iota(jnp.int32, shape, axis)
        t = lax.broadcasted_iota(jnp.int32, shape, 1 - axis) - offset
        return jnp.where((t >= 3 * j) & (t < 3 * j + 3), 1.0, 0.0)

    pooled = exact(pool_matrix((short, rows + 8), 6, 0), k.shift[...]) / 3.0
    point(k, "f0_end")
    short_out = layer_ahead(k, 1, pooled)
    upsampled = k.shift[8 : 8 + rows, :] + exact(pool_matrix((rows, short), 0, 1), short_out)
    gain = k.gain[4:5, :]
    unit, _ = norm_parts(upsampled)
    final = low(unit * gain)
    need(k, HEAD)
    head = k.pk[:, :, :, :, HEAD : HEAD + 16, 0:256].reshape(512, 256)
    logits = dot(final, head)
    top = jnp.max(logits, axis=-1, keepdims=True)
    log_total = top + jnp.log(jnp.sum(jnp.exp(logits - top), axis=-1, keepdims=True))
    hot = jnp.where(lanes((rows, 256)) == targets, 1.0, 0.0)
    picked = jnp.sum(hot * logits, axis=-1, keepdims=True)
    position = k.s * rows + lax.broadcasted_iota(jnp.int32, (rows, 1), 0)
    length = jnp.zeros((rows, 1), F32)
    begin = jnp.int32(0)
    for i in range(8):
        size = k.lengths[0, i]
        inside = (position >= begin) & (position < begin + size)
        length = jnp.where(inside, size.astype(F32), length)
        begin = begin + size
    k.loss = jnp.sum((log_total - picked) / length, axis=0, keepdims=True)
    grad_logits = low((jnp.exp(logits - log_total) - hot) / length)
    k.gr[:, :, :, :, HEAD : HEAD + 16, 0:256] = low(dot_tn(final, grad_logits)).reshape(2, 4, 2, 2, 16, 256)
    k.gr[:, :, :, :, HEAD : HEAD + 16, 256:512] = jnp.zeros((2, 4, 2, 2, 16, 256), LOW)
    grad_final = dot_nt(grad_logits, head)
    grad_up, k.gain_grads[4] = norm_back(upsampled, gain, grad_final)
    k.up[...] = grad_up
    grad_short = exact(pool_matrix((short, rows), 0, 0), grad_up)
    grad_pooled = layer_back(k, 1, grad_short)
    k.pool[0:short, :] = grad_pooled
    rim2 = remote(
        k.pool.at[pl.ds(0, 8)], k.pool.at[pl.ds(short, 8)], sem(k), sem(k), (k.g, lax.rem(k.s + 15, 16))
    )

    @pl.when(k.s > 0)
    def _():
        rim2.start()

    point(k, "b1_rim")

    @pl.when(k.s < 15)
    def _():
        rim2.wait_recv()

    @pl.when(k.s == 15)
    def _():
        k.pool[short : short + 8, :] = jnp.zeros((8, D), F32)

    @pl.when(k.s > 0)
    def _():
        rim2.wait_send()

    t = lax.broadcasted_iota(jnp.int32, (rows, short + 8), 0)
    j = lax.broadcasted_iota(jnp.int32, (rows, short + 8), 1)
    spread = jnp.where((t + 2 >= 3 * j) & (t + 2 < 3 * j + 3), 1.0, 0.0)
    grad_first = k.up[...] + exact(spread, k.pool[...] / 3.0)
    grad_in = layer_back(k, 0, grad_first)
    table_grad = dot_tn(byte_matrix(ids, 0), low(grad_in[:, 0:256])) + dot_tn(
        byte_matrix(ids, 1), low(grad_in[:, 256:512])
    )
    k.gr[:, :, :, :, EG : EG + 16, 0:256] = low(table_grad).reshape(2, 4, 2, 2, 16, 256)
    fill = [jnp.zeros((3, 256), F32)]
    gains = jnp.concatenate(
        [v[:, 0:256] for v in k.gain_grads] + fill + [v[:, 256:512] for v in k.gain_grads] + fill, axis=0
    )
    gains = jnp.broadcast_to(low(gains)[None], (32, 16, 256))
    k.gr[:, :, :, :, EG : EG + 16, 256:512] = gains.reshape(2, 4, 2, 2, 16, 256)
    point(k, "b0_end")


def add_into(ref, other):
    ref[...] = low(ref[...].astype(F32) + other[...].astype(F32))


def reduce_piece(k, name, r0, rm, r1):
    g, z, y, x, dev, gr = k.g, k.z, k.y, k.x, k.dev, k.gr
    a, b, every = pl.ds(r0, rm - r0), pl.ds(rm, r1 - rm), pl.ds(r0, r1 - r0)
    waiting = Stage(
        k, k.rc.at[:, :, :, every], [(gr.at[1 - g, :, :, :, every], k.rc.at[:, :, :, every], dev(1 - g, z, y, x))]
    )
    yield
    with scope(f"rw_{name}"):
        waiting.wait()

    with scope("radd"):

        @pl.loop(0, 16)
        def _(n):
            place = (n // 4, lax.rem(n // 2, 2), lax.rem(n, 2), every)
            add_into(gr.at[(g,) + place], k.rc.at[place])

    waiting = Stage(
        k,
        k.r2.at[:, :, every],
        [
            (gr.at[g, :, :, 1 - x, a], k.r2.at[:, :, a], dev(g, z, y, 1 - x)),
            (gr.at[g, :, 1 - y, :, b], k.r2.at[:, :, b], dev(g, z, 1 - y, x)),
        ],
    )
    yield
    with scope(f"rw_{name}"):
        waiting.wait()

    @pl.loop(0, 8)
    def _(n):
        add_into(gr.at[g, n // 2, lax.rem(n, 2), x, a], k.r2.at[n // 2, lax.rem(n, 2), a])
        add_into(gr.at[g, n // 2, y, lax.rem(n, 2), b], k.r2.at[n // 2, lax.rem(n, 2), b])

    waiting = Stage(
        k,
        k.r1.at[:, every],
        [
            (gr.at[g, :, 1 - y, x, a], k.r1.at[:, a], dev(g, z, 1 - y, x)),
            (gr.at[g, :, y, 1 - x, b], k.r1.at[:, b], dev(g, z, y, 1 - x)),
        ],
    )
    yield
    with scope(f"rw_{name}"):
        waiting.wait()

    @pl.loop(0, 4)
    def _(n):
        add_into(gr.at[g, n, y, x, every], k.r1.at[n, every])

    moves = []
    for n in (2, 1, 3):
        to = lax.rem(z + n, 4)
        moves.append((gr.at[g, to, y, x, every], k.rz.at[n - 1, every], dev(g, to, y, x)))
    waiting = Stage(k, k.rz.at[:, every], moves)
    yield
    with scope(f"rw_{name}"):
        waiting.wait()
    k.summed.update(range(r0, r1, 16))
    yield


def own_sum(k, row, count):
    assert k.summed.issuperset(range(row, row + count, 16))
    rows = pl.ds(row, count)
    v = k.gr[k.g, k.z, k.y, k.x, rows].astype(F32)
    for i in range(3):
        v = v + k.rz[i, rows].astype(F32)
    return v


def square(k, v):
    k.sq = k.sq + jnp.sum(jnp.sum(v * v, axis=1, keepdims=True), axis=0, keepdims=True)


def flush(k, name, layer=None):
    src, dst = getattr(k, "s_" + name), getattr(k, "g_" + name)
    if layer is not None:
        src, dst = src.at[layer], dst.at[layer]
    copy = pltpu.make_async_copy(src, dst, sem(k))
    copy.start()
    k.flushed.append(copy)


def store_qkv(k, layer):
    v = own_sum(k, LAYER0 + layer * LAYER_ROWS + QKV, 48)
    square(k, v)
    k.s_qkv[layer, :, 0:512] = v[0:16]
    for pair in range(4):
        row, col = 16 + 16 * (pair // 2), 256 * (pair % 2)
        even = v[row : row + 16, col : col + 128]
        odd = v[row : row + 16, col + 128 : col + 256]
        left = lanes(even.shape) < 64
        k.s_qkv[layer, :, 512 + 128 * pair : 640 + 128 * pair] = jnp.where(left, even, roll64(odd))
        k.s_qkv[layer, :, 1024 + 128 * pair : 1152 + 128 * pair] = jnp.where(left, roll64(even), odd)
    flush(k, "qkv", layer)


def store_out(k, layer):
    v = own_sum(k, LAYER0 + layer * LAYER_ROWS + OUT, 16)
    square(k, v)
    k.s_out[layer] = v
    flush(k, "out", layer)


def store_ff(k, layer):
    v = own_sum(k, LAYER0 + layer * LAYER_ROWS + UP, 64)
    square(k, v)
    for j in range(4):
        k.s_up[layer, :, 512 * j : 512 * j + 512] = v[16 * j : 16 * j + 16]
    v = own_sum(k, LAYER0 + layer * LAYER_ROWS + DOWN, 64)
    square(k, v)
    k.s_down[layer] = v
    flush(k, "up", layer)
    flush(k, "down", layer)


def store_head(k):
    v = own_sum(k, HEAD, 16)[:, 0:256]
    square(k, v)
    k.s_head[...] = v
    flush(k, "head")


def store_rest(k):
    v = own_sum(k, EG, 16)
    square(k, v[:, 0:256])
    k.s_embed[:, 0:256] = v[0:8, 0:256]
    k.s_embed[:, 256:512] = v[8:16, 0:256]
    gains = jnp.where(k.g == 0, v[0:8, 256:512], v[8:16, 256:512])
    row, column = lax.broadcasted_iota(jnp.int32, (256, 16), 0), lax.broadcasted_iota(jnp.int32, (256, 16), 1)
    gains = exact(gains, jnp.where(row - 16 * k.s == column, 1.0, 0.0))[0:5]
    square(k, gains)
    k.s_gains[...] = gains
    flush(k, "embed")
    flush(k, "gains")


def finish_grads(k):
    g = k.g
    k.sq = jnp.zeros((1, 1), F32)
    k.flushed = []

    def complete(name):
        for _ in k.reduces[name]:
            pass

    point(k, "tail0")
    complete("D")
    complete("d")
    store_ff(k, 1)
    store_head(k)
    point(k, "tail1")
    complete("C")
    store_qkv(k, 1)
    store_out(k, 1)
    point(k, "tail2")
    complete("B")
    store_out(k, 0)
    point(k, "tail3")
    complete("b")
    store_ff(k, 0)
    point(k, "tail4")
    complete("A")
    store_rest(k)
    complete("a")
    store_qkv(k, 0)
    lane = lanes((8, 128))
    k.stat[0] = jnp.where(lane == 0, k.sq, jnp.where(lane == 1, k.loss, 0.0))
    me = g * 16 + k.s
    sent, got = sem(k), sem(k)

    @pl.loop(1, 32)
    def _(i):
        t = lax.rem(me + i, 32)
        remote(k.stat.at[0], k.stat.at[i], sent, got, (t // 16, lax.rem(t, 16))).start()

    with scope("stats"):
        drain(got, k.stat.at[pl.ds(1, 31)])
        drain(sent, k.stat.at[pl.ds(1, 31)])
    k.stats[...] = jnp.sum(k.stat[...], axis=0)
    wait_all(k.flushed)


IN_NAMES = (
    "ids", "targets", "lengths", "w_qkv", "w_out", "w_up", "w_down", "embed", "head", "gains",
)
OUT_NAMES = ("g_qkv", "g_out", "g_up", "g_down", "g_embed", "g_head", "g_gains", "stats")
SEMS = 200


def scratch_shapes():
    shapes = {
        "pk": ((2, 4, 2, 2, ROWS, D), LOW),
        "gr": ((2, 4, 2, 2, ROWS, D), LOW),
        "rc": ((4, 2, 2, ROWS, D), LOW),
        "r2": ((4, 2, ROWS, D), LOW),
        "r1": ((4, ROWS, D), LOW),
        "rz": ((3, ROWS, D), LOW),
        "gain": ((8, D), F32),
        "shift": ((152, D), F32),
        "pool": ((56, D), F32),
        "up": ((144, D), F32),
        "stat": ((32, 8, 128), F32),
        "columns": ((128, 256), F32),
        "s_qkv": ((2, 16, 3 * D), F32),
        "s_out": ((2, 16, D), F32),
        "s_up": ((2, 16, 4 * D), F32),
        "s_down": ((2, 64, D), F32),
        "s_embed": ((8, D), F32),
        "s_head": ((16, 256), F32),
        "s_gains": ((5, 16), F32),
    }
    for layer in range(2):
        rows, pad = layer_sizes(layer)
        for name, shape, kind in (
            ("cos", (rows, 128), F32),
            ("sin", (rows, 128), F32),
            ("sendbox", (8, pad + rows, 128), LOW),
            ("inbox", (16, pad + rows, 128), LOW),
            ("abox", (8, pad, 128), LOW),
            ("home", (8, pad, 128), LOW),
            ("gsend", (8, pad, 128), LOW),
            ("gbox", (16, pad, 128), LOW),
            ("dbox", (8, pad, 128), LOW),
            ("kvbox", (8, rows, 128), LOW),
            ("back", (8, pad, 128), LOW),
            ("kvback", (8, rows, 128), LOW),
            ("lse", (8, rows, 128), F32),
            ("att", (8, rows, 128), F32),
            ("dkvt", (128, 16 * rows), F32),
            ("dkv", (16, rows, 128), F32),
            ("dkv_out", (8, rows, 128), F32),
            ("dkv_in", (8, rows, 128), F32),
            ("h_hidden", (rows, D), F32),
            ("h_normed", (rows, D), LOW),
            ("h_flat", (rows, D), LOW),
            ("h_middle", (rows, D), F32),
            ("h_second", (rows, D), LOW),
            ("h_pre", (rows, 4 * D), F32),
            ("h_act", (rows, 4 * D), LOW),
            ("h_gj", (rows, D), LOW),
        ):
            shapes[name + str(layer)] = (shape, kind)
    return shapes


SCRATCH = scratch_shapes()
PER_LAYER = (
    "cos", "sin", "sendbox", "inbox", "abox", "home", "gsend", "gbox", "dbox", "back", "lse", "att", "dkvt", "dkv",
    "dkv_out", "dkv_in", "kvbox", "kvback",
)
HELD = ("hidden", "normed", "flat", "middle", "second", "pre", "act", "gj")


def update_kernel(*refs):
    stats, sources, outs, loss_ref, norm_ref = refs[0], refs[1:29], refs[29:50], refs[50], refs[51]
    held, made, sems, out_sems = refs[52:59], refs[59:66], refs[66], refs[67]
    order = (4, 5, 6, 1, 0, 2, 3)
    for i in order:
        start_all([pltpu.make_async_copy(sources[7 * j + i], held[i].at[j], sems.at[i]) for j in range(4)])
    norm = jnp.sqrt(stats[0:1, 0:1])
    loss_ref[...] = stats[0:1, 1:2]
    norm_ref[...] = norm
    clip = jnp.minimum(1.0, CLIP_NORM / norm)
    for i in order:
        drain(sems.at[i], held[i])
        gradient, master, first, second = (held[i][j] for j in range(4))
        results = adam_update(master, gradient * clip, first, second, STEP_RATES[i], WEIGHT_DECAYS[i])
        for j in range(3):
            made[i][j] = results[j]
        start_all([pltpu.make_async_copy(made[i].at[j], outs[7 * j + i], out_sems.at[i]) for j in range(3)])
    for i in order:
        drain(out_sems.at[i], made[i])


def on_device_fast(byte_ids, targets, item_lengths, *arrays):
    masters, firsts, seconds = arrays[0:7], arrays[7:14], arrays[14:21]
    vmem, anywhere = pl.BlockSpec(memory_space=pltpu.VMEM), pl.BlockSpec(memory_space=pl.ANY)
    shard_shapes = [jax.ShapeDtypeStruct(master.shape, F32) for master in masters]
    outs = pl.pallas_call(
        kernel,
        name="step",
        out_shape=shard_shapes + [jax.ShapeDtypeStruct((8, 128), F32)],
        in_specs=[vmem, vmem, pl.BlockSpec(memory_space=pltpu.SMEM)] + [vmem] * 7,
        out_specs=[anywhere] * 7 + [vmem],
        scratch_shapes=[pltpu.VMEM(shape, kind) for shape, kind in SCRATCH.values()]
        + [pltpu.SemaphoreType.DMA((SEMS,))],
        compiler_params=pltpu.CompilerParams(collective_id=0, has_side_effects=True, vmem_limit_bytes=63 << 20),
    )(byte_ids, targets, item_lengths, *masters)
    grads, stats = outs[:7], outs[7]
    results = pl.pallas_call(
        update_kernel,
        name="update",
        out_shape=shard_shapes * 3 + [jax.ShapeDtypeStruct((1, 1), F32)] * 2,
        in_specs=[vmem] + [anywhere] * 28,
        out_specs=[anywhere] * 21 + [vmem] * 2,
        scratch_shapes=[pltpu.VMEM((count, *shard.shape), F32) for count in (4, 3) for shard in shard_shapes]
        + [pltpu.SemaphoreType.DMA((7,)), pltpu.SemaphoreType.DMA((7,))],
        compiler_params=pltpu.CompilerParams(vmem_limit_bytes=63 << 20),
    )(stats, *grads, *masters, *firsts, *seconds)
    return (results[21].reshape(()), results[22].reshape(()), *results[:21])


def solution(mesh):
    tuned = mesh.shape["dp"] == 2 and mesh.shape["seq"] == 16
    row = P(None, ("dp", "seq"), None)
    flat = P(("dp", "seq"), None)
    shards = (row, row, row, row, flat, flat, P(None, ("dp", "seq")))
    return jax.shard_map(
        on_device_fast if tuned else on_device_general,
        mesh=mesh,
        in_specs=(P("dp", "seq"), P("dp", "seq"), P("dp", None)) + shards * 3,
        out_specs=(P(), P()) + shards * 3,
        check_vma=False,
    )
```

```python
import contextlib
import functools

import jax
import jax.numpy as jnp
from jax import lax
from jax.experimental import pallas as pl
from jax.experimental.pallas import tpu as pltpu
from jax.sharding import PartitionSpec as P

HEADS = 8
VOCAB = 256
RATE = 3
STEP = 10

CLIP_NORM = 0.02
BETA_ONE = 0.9
BETA_TWO = 0.95
STEP_RATES = (0.03, 0.2, 0.03, 0.03, 0.6, 0.03, 0.2)
WEIGHT_DECAYS = (0.1, 0.1, 0.1, 0.1, 0.1, 0.1, 0.0)
EPSILON = 1e-08
NORM_EPS = 1e-05
MASK_FILL = -1e30


def shifted_2(value, axis, steps):
    count = lax.axis_size(axis)
    leading, last = (max(0, -steps), min(count, count - steps))
    return lax.ppermute(value, axis, [(source, source + steps) for source in range(leading, last)])


def to_low(values):
    return values.astype(jnp.bfloat16)


def layer_norm(values, gain):
    center = values - jnp.mean(values, axis=-1, keepdims=True)
    spread = jnp.mean(center * center, axis=-1, keepdims=True)
    return center * lax.rsqrt(spread + NORM_EPS) * gain


def rotate(joined, positions, num_heads):
    parts = joined.reshape(joined.shape[0], 3, num_heads, -1)
    half_size = parts.shape[-1] // 2
    freqs = 10000.0 ** (-jnp.arange(half_size, dtype=jnp.float32) / half_size)
    angles = positions.astype(jnp.float32)[:, None] * freqs[None, :]
    cosine = jnp.cos(angles)[:, None, :]
    sine = jnp.sin(angles)[:, None, :]

    def rotate_half(values):
        first_half = values[..., :half_size]
        second_half = values[..., half_size:]
        return jnp.concatenate(
            [first_half * cosine - second_half * sine, first_half * sine + second_half * cosine],
            axis=-1,
        )

    return (rotate_half(parts[:, 0]), rotate_half(parts[:, 1]), parts[:, 2])


def scores_for(q_low, k_low, query_pos, key_pos):
    scores = jnp.einsum(
        "rhe,phe->hrp", q_low, k_low, preferred_element_type=jnp.float32
    ) * q_low.shape[-1] ** (-0.5)
    causal = query_pos[:, None] >= key_pos[None, :]
    return (scores, causal)


def attend(q_low, k_low, v_low, query_pos):
    num_rows, num_heads, head_size = q_low.shape
    key_piece = (
        lax.all_gather(k_low, "seq", axis=0, tiled=True),
        lax.all_gather(v_low, "seq", axis=0, tiled=True),
    )
    running_max = jnp.full((num_heads, num_rows), MASK_FILL, jnp.float32)
    accum = jnp.zeros((num_rows, num_heads, head_size), jnp.float32)
    key_pos = jnp.arange(key_piece[0].shape[0], dtype=jnp.int32)
    scores, causal = scores_for(q_low, key_piece[0], query_pos, key_pos)
    scores = jnp.where(causal[None], scores, MASK_FILL)
    new_max = jnp.maximum(running_max, jnp.max(scores, axis=-1))
    factor = jnp.exp(running_max - new_max)
    attn_prob = jnp.where(causal[None], jnp.exp(scores - new_max[..., None]), 0.0)
    denom = jnp.sum(attn_prob, axis=-1)
    accum = accum * factor.T[:, :, None] + jnp.einsum(
        "hrp,phe->rhe", to_low(attn_prob), key_piece[1], preferred_element_type=jnp.float32
    )
    running_max, denom, accum = (new_max, denom, accum)
    return (accum / denom.T[:, :, None], (running_max + jnp.log(denom)).T)


def block_grads(q_low, grad_low, log_total, row_delta, query_pos, k_low, v_low, key_pos):
    scores, causal = scores_for(q_low, k_low, query_pos, key_pos)
    attn_prob = jnp.where(causal[None], jnp.exp(scores - log_total.T[:, :, None]), 0.0)
    grad_prob = jnp.einsum("rhe,phe->hrp", grad_low, v_low, preferred_element_type=jnp.float32)
    grad_score = to_low(attn_prob * (grad_prob - row_delta.T[:, :, None]))
    score_scale = q_low.shape[-1] ** (-0.5)
    grad_q = (
        jnp.einsum("hrp,phe->rhe", grad_score, k_low, preferred_element_type=jnp.float32)
        * score_scale
    )
    grad_k = (
        jnp.einsum("hrp,rhe->phe", grad_score, q_low, preferred_element_type=jnp.float32)
        * score_scale
    )
    grad_v = jnp.einsum(
        "hrp,rhe->phe", to_low(attn_prob), grad_low, preferred_element_type=jnp.float32
    )
    return (grad_q, grad_k, grad_v)


def attend_back(q_low, k_low, v_low, grad_low, log_total, row_delta, query_pos):
    key_piece = (
        lax.all_gather(k_low, "seq", axis=0, tiled=True),
        lax.all_gather(v_low, "seq", axis=0, tiled=True),
    )
    key_pos = jnp.arange(key_piece[0].shape[0], dtype=jnp.int32)
    grad_q = block_grads(
        q_low, grad_low, log_total, row_delta, query_pos, key_piece[0], key_piece[1], key_pos
    )[0]
    all_totals, all_deltas = (
        lax.all_gather(log_total, "seq", axis=0, tiled=True),
        lax.all_gather(row_delta, "seq", axis=0, tiled=True),
    )
    query_piece = (
        lax.all_gather(q_low, "seq", axis=0, tiled=True),
        lax.all_gather(grad_low, "seq", axis=0, tiled=True),
    )
    piece_rows = query_piece[0].shape[0]
    piece_pos = jnp.arange(piece_rows, dtype=jnp.int32)
    unused_q, grad_k_blk, grad_v_blk = block_grads(
        query_piece[0], query_piece[1], all_totals, all_deltas, piece_pos, k_low, v_low, query_pos
    )
    return (grad_q, grad_k_blk, grad_v_blk)


def layer_forward(hidden, weights, gain_pair, positions):
    w_joined, w_proj, w_rise, w_fall = weights
    num_rows = hidden.shape[0]
    normed = to_low(layer_norm(hidden, gain_pair[0]))
    joined = jnp.dot(normed, w_joined, preferred_element_type=jnp.float32)
    queries, keys, values = rotate(joined, positions, HEADS)
    q_low, k_low, v_low = (to_low(queries), to_low(keys), to_low(values))
    attended, log_total = attend(q_low, k_low, v_low, positions)
    flat_low = to_low(attended.reshape(num_rows, -1))
    middle = hidden + jnp.dot(flat_low, w_proj, preferred_element_type=jnp.float32)
    second = to_low(layer_norm(middle, gain_pair[1]))
    pre_act = jnp.dot(second, w_rise, preferred_element_type=jnp.float32)
    activated = to_low(jax.nn.gelu(pre_act))
    output = middle + jnp.dot(activated, w_fall, preferred_element_type=jnp.float32)
    saved = (
        normed,
        joined,
        q_low,
        k_low,
        v_low,
        attended,
        log_total,
        flat_low,
        middle,
        second,
        pre_act,
        activated,
    )
    return (output, saved)


def layer_backward(hidden, weights, gain_pair, positions, grad_out):
    w_joined, w_proj, w_rise, w_fall = weights
    unused_out, saved = layer_forward(hidden, weights, gain_pair, positions)
    (
        normed,
        joined,
        q_low,
        k_low,
        v_low,
        attended,
        log_total,
        flat_low,
        middle,
        second,
        pre_act,
        activated,
    ) = saved
    fall_low = to_low(grad_out)
    grad_fall = jnp.dot(activated.T, fall_low, preferred_element_type=jnp.float32)
    grad_act = jnp.dot(fall_low, w_fall.T, preferred_element_type=jnp.float32)
    grad_pre = to_low(jax.vjp(jax.nn.gelu, pre_act)[1](grad_act)[0])
    grad_rise = jnp.dot(second.T, grad_pre, preferred_element_type=jnp.float32)
    grad_second = jnp.dot(grad_pre, w_rise.T, preferred_element_type=jnp.float32)
    grad_middle_n, grad_gain_ffn = jax.vjp(layer_norm, middle, gain_pair[1])[1](grad_second)
    grad_middle = grad_out + grad_middle_n
    proj_low = to_low(grad_middle)
    grad_proj = jnp.dot(flat_low.T, proj_low, preferred_element_type=jnp.float32)
    grad_att = to_low(
        jnp.dot(proj_low, w_proj.T, preferred_element_type=jnp.float32).reshape(attended.shape)
    )
    row_delta = jnp.sum(grad_att.astype(jnp.float32) * attended, axis=-1)
    grad_q, grad_k, grad_v = attend_back(
        q_low, k_low, v_low, grad_att, log_total, row_delta, positions
    )

    def rotate_joined(joined_in):
        return rotate(joined_in, positions, HEADS)

    grad_joined = to_low(jax.vjp(rotate_joined, joined)[1]((grad_q, grad_k, grad_v))[0])
    grad_w_joined = jnp.dot(normed.T, grad_joined, preferred_element_type=jnp.float32)
    grad_normed = jnp.dot(grad_joined, w_joined.T, preferred_element_type=jnp.float32)
    grad_in_n, grad_gain_attn = jax.vjp(layer_norm, hidden, gain_pair[0])[1](grad_normed)
    return (
        grad_middle + grad_in_n,
        (grad_w_joined, grad_proj, grad_rise, grad_fall),
        jnp.stack([grad_gain_attn, grad_gain_ffn]),
    )


def adam_update(weight, gradient, moment_one, moment_two, step_rate, decay_rate):
    moment_one = BETA_ONE * moment_one + (1.0 - BETA_ONE) * gradient
    moment_two = BETA_TWO * moment_two + (1.0 - BETA_TWO) * gradient * gradient
    first_hat = moment_one / (1.0 - BETA_ONE**STEP)
    second_hat = moment_two / (1.0 - BETA_TWO**STEP)
    weight = weight - step_rate * (
        first_hat / (jnp.sqrt(second_hat) + EPSILON) + decay_rate * weight
    )
    return (weight, moment_one, moment_two)


def on_device_general(
    byte_ids,
    targets,
    item_lengths,
    w_qkv,
    w_out,
    w_up,
    w_down,
    embed,
    head,
    gains,
    mom_qkv,
    mom_out,
    mom_up,
    mom_down,
    mom_embed,
    mom_head,
    mom_gains,
    sec_qkv,
    sec_out,
    sec_up,
    sec_down,
    sec_embed,
    sec_head,
    sec_gains,
):
    low_qkv, low_out, low_up, low_down, low_embed, low_head, low_gains = (
        lax.all_gather(to_low(w_qkv), ("dp", "seq"), axis=1, tiled=True),
        lax.all_gather(to_low(w_out), ("dp", "seq"), axis=1, tiled=True),
        lax.all_gather(to_low(w_up), ("dp", "seq"), axis=1, tiled=True),
        lax.all_gather(to_low(w_down), ("dp", "seq"), axis=1, tiled=True),
        lax.all_gather(to_low(embed), ("dp", "seq"), axis=0, tiled=True),
        lax.all_gather(to_low(head), ("dp", "seq"), axis=0, tiled=True),
        lax.all_gather(to_low(gains), ("dp", "seq"), axis=1, tiled=True),
    )
    gain_rows = low_gains.astype(jnp.float32)
    byte_row = byte_ids[0]
    num_rows = byte_row.shape[0]
    short_rows = num_rows // RATE
    seq_place = lax.axis_index("seq")
    positions = seq_place * num_rows + jnp.arange(num_rows, dtype=jnp.int32)
    short_pos = seq_place * short_rows + jnp.arange(short_rows, dtype=jnp.int32)
    vocab_ids = jnp.arange(VOCAB, dtype=jnp.int32)
    one_hot_in = (byte_row[:, None] == vocab_ids[None, :]).astype(jnp.float32)
    embedded = jnp.dot(
        one_hot_in.astype(jnp.bfloat16), low_embed, preferred_element_type=jnp.float32
    )
    lower_weights = (low_qkv[0], low_out[0], low_up[0], low_down[0])
    upper_weights = (low_qkv[1], low_out[1], low_up[1], low_down[1])
    first_out, unused_first = layer_forward(embedded, lower_weights, gain_rows[0:2], positions)
    left_rim = shifted_2(first_out[num_rows - RATE + 1 :], "seq", 1)
    shifted = jnp.concatenate([left_rim, first_out[: num_rows - RATE + 1]], axis=0)
    pooled = jnp.mean(shifted.reshape(short_rows, RATE, -1), axis=1)
    short_out, unused_short = layer_forward(pooled, upper_weights, gain_rows[2:4], short_pos)
    upsampled = first_out + jnp.repeat(short_out, RATE, axis=0)
    top_gain = gain_rows[gain_rows.shape[0] - 1]
    final_low = to_low(layer_norm(upsampled, top_gain))
    logits = jnp.dot(final_low, low_head, preferred_element_type=jnp.float32)
    row_max = jnp.max(logits, axis=-1, keepdims=True)
    log_total = row_max[:, 0] + jnp.log(jnp.sum(jnp.exp(logits - row_max), axis=-1))
    one_hot_out = (targets[0][:, None] == vocab_ids[None, :]).astype(jnp.float32)
    picked = jnp.sum(one_hot_out * logits, axis=-1)
    lengths = item_lengths[0]
    ends = jnp.cumsum(lengths)
    doc_index = jnp.sum((positions[:, None] >= ends[None, :]).astype(jnp.int32), axis=1)
    item_ids = jnp.arange(lengths.shape[0], dtype=jnp.int32)
    doc_length = jnp.sum(
        jnp.where(item_ids[None, :] == doc_index[:, None], lengths[None, :], 0), axis=1
    ).astype(jnp.float32)
    loss_local = jnp.sum((log_total - picked) / doc_length)
    loss_sum = lax.psum(loss_local, ("dp", "seq"))
    grad_logits = to_low((jnp.exp(logits - log_total[:, None]) - one_hot_out) / doc_length[:, None])
    grad_head = jnp.dot(final_low.T, grad_logits, preferred_element_type=jnp.float32)
    grad_final = jnp.dot(grad_logits, low_head.T, preferred_element_type=jnp.float32)
    grad_upsampled, grad_gain_top = jax.vjp(layer_norm, upsampled, top_gain)[1](grad_final)
    grad_short = jnp.sum(grad_upsampled.reshape(short_rows, RATE, -1), axis=1)
    grad_pooled, upper_grads, upper_gain_grads = layer_backward(
        pooled, upper_weights, gain_rows[2:4], short_pos, grad_short
    )
    grad_shifted = jnp.repeat(grad_pooled / RATE, RATE, axis=0)
    rim_grad = shifted_2(grad_shifted[: RATE - 1], "seq", -1)
    grad_first = grad_upsampled + jnp.concatenate([grad_shifted[RATE - 1 :], rim_grad], axis=0)
    grad_embedded, lower_grads, lower_gain_grads = layer_backward(
        embedded, lower_weights, gain_rows[0:2], positions, grad_first
    )
    grad_embed = jnp.dot(one_hot_in.T, grad_embedded, precision=lax.Precision.HIGHEST)
    grad_gains = jnp.concatenate(
        [lower_gain_grads, upper_gain_grads, grad_gain_top[None, :]], axis=0
    )
    shard_grads = (
        lax.psum_scatter(
            jnp.stack([lower_grads[0], upper_grads[0]]),
            ("dp", "seq"),
            scatter_dimension=1,
            tiled=True,
        ),
        lax.psum_scatter(
            jnp.stack([lower_grads[1], upper_grads[1]]),
            ("dp", "seq"),
            scatter_dimension=1,
            tiled=True,
        ),
        lax.psum_scatter(
            jnp.stack([lower_grads[2], upper_grads[2]]),
            ("dp", "seq"),
            scatter_dimension=1,
            tiled=True,
        ),
        lax.psum_scatter(
            jnp.stack([lower_grads[3], upper_grads[3]]),
            ("dp", "seq"),
            scatter_dimension=1,
            tiled=True,
        ),
        lax.psum_scatter(grad_embed, ("dp", "seq"), scatter_dimension=0, tiled=True),
        lax.psum_scatter(grad_head, ("dp", "seq"), scatter_dimension=0, tiled=True),
        lax.psum_scatter(grad_gains, ("dp", "seq"), scatter_dimension=1, tiled=True),
    )
    squares = sum((jnp.sum(piece_grad * piece_grad) for piece_grad in shard_grads))
    total_squares = lax.psum(squares, ("dp", "seq"))
    grad_norm = jnp.sqrt(total_squares)
    clip_factor = jnp.minimum(1.0, CLIP_NORM / grad_norm)
    masters = (w_qkv, w_out, w_up, w_down, embed, head, gains)
    firsts = (mom_qkv, mom_out, mom_up, mom_down, mom_embed, mom_head, mom_gains)
    seconds = (sec_qkv, sec_out, sec_up, sec_down, sec_embed, sec_head, sec_gains)
    results = []
    for slot_index in range(7):
        results.append(
            adam_update(
                masters[slot_index],
                shard_grads[slot_index] * clip_factor,
                firsts[slot_index],
                seconds[slot_index],
                STEP_RATES[slot_index],
                WEIGHT_DECAYS[slot_index],
            )
        )
    return (
        loss_sum,
        grad_norm,
        results[0][0],
        results[1][0],
        results[2][0],
        results[3][0],
        results[4][0],
        results[5][0],
        results[6][0],
        results[0][1],
        results[1][1],
        results[2][1],
        results[3][1],
        results[4][1],
        results[5][1],
        results[6][1],
        results[0][2],
        results[1][2],
        results[2][2],
        results[3][2],
        results[4][2],
        results[5][2],
        results[6][2],
    )


LOW = jnp.bfloat16
F32 = jnp.float32
MESH = pl.DeviceIdType.MESH
D = 512

EG, LAYER0, LAYER_ROWS = 0, 16, 192
QKV, OUT, UP, DOWN = 0, 48, 64, 128
HEAD = LAYER0 + 2 * LAYER_ROWS
ROWS = HEAD + 16
PIECES = {
    "A": (0, 16, 32),
    "a": (32, 48, 64),
    "B": (64, 96, 144),
    "b": (144, 176, 208),
    "C": (208, 240, 272),
    "D": (272, 304, 336),
    "d": (336, 384, 416),
}
SCHEDULE = {
    "start": "AaBAaA",
    "packed": "CabABaC",
    "f0_sent": "bB",
    "f0_take": "d",
    "f0_got": "DbC",
    "f0_part0": "B",
    "f0_part1": "DbdC",
    "f0_rim": "D",
    "f1_sent": "d",
    "f1_part0": "Dd",
    "b1_ff": "D",
    "b1_sent": "dD",
    "b1_sums": "D",
    "b1_rim": "dC",
    "b0_ff": "CBb",
    "b0_sent": "BD",
    "b0_part1": "C",
    "b0_sums": "CBd",
    "b0_home": "b",
    "b0_kv": "B",
    "b0_end": "AAdbaab",
    "tail": "AaAa",
}


def dot(a, b):
    return jnp.dot(a, b, preferred_element_type=F32)


def dot_nt(a, b):
    return lax.dot_general(a, b, (((1,), (1,)), ((), ())), preferred_element_type=F32)


def dot_tn(a, b):
    return lax.dot_general(a, b, (((0,), (0,)), ((), ())), preferred_element_type=F32)


def low(v):
    return v.astype(LOW)


exact = functools.partial(jnp.dot, preferred_element_type=F32, precision=lax.Precision.HIGHEST)


def lanes(shape):
    return lax.broadcasted_iota(jnp.int32, shape, len(shape) - 1)


def roll64(v):
    return pltpu.roll(v, 64, 1)


def swap32(v):
    return jnp.where(lanes(v.shape) % 64 < 32, pltpu.roll(v, 96, 1), pltpu.roll(v, 32, 1))


def norm_parts(v):
    center = v - jnp.mean(v, axis=-1, keepdims=True)
    scale = lax.rsqrt(jnp.mean(center * center, axis=-1, keepdims=True) + NORM_EPS)
    return center * scale, scale


def norm_back(v, gain, grad):
    unit, scale = norm_parts(v)
    g = grad * gain
    out = scale * (g - jnp.mean(g, axis=-1, keepdims=True) - unit * jnp.mean(g * unit, axis=-1, keepdims=True))
    return out, jnp.sum(grad * unit, axis=0, keepdims=True)


GELU_A, GELU_B = 0.7978845608028654, 0.044715


def gelu(v):
    return 0.5 * v * (1.0 + jnp.tanh(GELU_A * (v + GELU_B * v * v * v)))


def gelu_grad(v):
    t = jnp.tanh(GELU_A * (v + GELU_B * v * v * v))
    return 0.5 * (1.0 + t) + 0.5 * v * (1.0 - t * t) * (GELU_A * (1.0 + 3.0 * GELU_B * v * v))


class Bag:
    pass


def scope(name):
    return contextlib.nullcontext()


def remote(src, dst, send, recv, device):
    return pltpu.make_async_remote_copy(
        src_ref=src, dst_ref=dst, send_sem=send, recv_sem=recv, device_id=device, device_id_type=MESH
    )


def pack_pair(block, odd):
    half = block.shape[0] // 2
    top, bottom = block[:half], block[half:]
    if odd:
        top = roll64(top)
    else:
        bottom = roll64(bottom)
    return jnp.where(lanes(top.shape) < 64, top, bottom)


def unpack_pair(even, odd):
    left = lanes(even.shape) < 64
    top = jnp.where(left, even, roll64(odd))
    bottom = jnp.where(left, roll64(even), odd)
    return jnp.concatenate([top, bottom], axis=0)


def unpack_left(x):
    left = lanes(x.shape) < 64
    return jnp.concatenate([jnp.where(left, x, 0.0), jnp.where(left, roll64(x), 0.0)], axis=0)


def unpack_right(x):
    left = lanes(x.shape) < 64
    return jnp.concatenate([jnp.where(left, 0.0, roll64(x)), jnp.where(left, 0.0, x)], axis=0)


def pack_left(x):
    half = x.shape[0] // 2
    return jnp.where(lanes((half, 128)) < 64, x[:half], roll64(x[half:]))


def pack_right(x):
    half = x.shape[0] // 2
    return jnp.where(lanes((half, 128)) < 64, roll64(x[:half]), x[half:])


def kernel(*refs):
    k = Bag()
    names = IN_NAMES + OUT_NAMES + tuple(SCRATCH)
    for name, ref in zip(names, refs[:-1]):
        setattr(k, name, ref)
    k.sems = refs[-1]
    for name in PER_LAYER:
        setattr(k, name, [getattr(k, name + "0"), getattr(k, name + "1")])
    k.hold = []
    for layer in range(2):
        hold = Bag()
        for name in HELD:
            setattr(hold, name, getattr(k, "h_" + name + str(layer)))
        k.hold.append(hold)
    g = lax.axis_index("dp")
    s = lax.axis_index("seq")
    z, y, x = s // 4, lax.rem(s // 2, 2), lax.rem(s, 2)
    k.g, k.s, k.z, k.y, k.x = g, s, z, y, x
    k.side = lax.rem(x + y, 2)
    k.cursor = 0

    def dev(g, z, y, x):
        return (g, z * 4 + y * 2 + x)

    k.dev = dev

    barrier = pltpu.get_barrier_semaphore()
    me = g * 16 + s

    @pl.loop(1, 32)
    def _(i):
        t = lax.rem(me + i, 32)
        pl.semaphore_signal(barrier, inc=1, device_id=(t // 16, lax.rem(t, 16)), device_id_type=MESH)

    own = k.pk.at[g, z, y, x]
    own[EG : EG + 16, 0:256] = low(jnp.concatenate([k.embed[:, 0:256], k.embed[:, 256:512]], axis=0))
    place = lanes((16, 256)) - 16 * s == lax.broadcasted_iota(jnp.int32, (16, 256), 0)
    gains = exact(k.gains[...], jnp.where(place, 1.0, 0.0))
    gains = jnp.concatenate([gains, jnp.zeros((3, 256), F32)], axis=0)
    gains = jnp.concatenate([jnp.where(g == 0, gains, 0.0), jnp.where(g == 1, gains, 0.0)], axis=0)
    own[EG : EG + 16, 256:512] = low(gains)
    pack_layer(k, own, 0)
    with scope("barrier"):
        pl.semaphore_wait(barrier, 31)
    k.gathers = {name: gather_piece(k, name, *rows) for name, rows in PIECES.items()}
    k.reduces = {name: reduce_piece(k, name, *rows) for name, rows in PIECES.items()}
    k.made, k.summed, k.stored = set(), set(), set()
    k.flushed, k.sq = [], jnp.zeros((1, 1), F32)
    point(k, "start")
    own[HEAD : HEAD + 16, 0:256] = low(k.head[...])
    own[HEAD : HEAD + 16, 256:512] = jnp.zeros((16, 256), LOW)
    pack_layer(k, own, 1)
    point(k, "packed")
    forward_backward(k)
    finish_grads(k)


def point(k, name):
    coming = name[0] in "spf"
    for piece in SCHEDULE.get(name, ""):
        next((k.gathers if coming else k.reduces)[piece], None)
        if not coming:
            store_ready(k)


def touching(rows):
    return [name for name, (r0, _, r1) in PIECES.items() if r0 < rows.stop and r1 > rows.start]


def pack_layer(k, own, layer):
    base = LAYER0 + layer * LAYER_ROWS
    own[base + QKV : base + QKV + 16, :] = low(k.w_qkv[layer, :, 0:512])
    for pair in range(4):
        keys = k.w_qkv[layer, :, 512 + 128 * pair : 640 + 128 * pair]
        vals = k.w_qkv[layer, :, 1024 + 128 * pair : 1152 + 128 * pair]
        left = lanes(keys.shape) < 64
        row = base + QKV + 16 + 16 * (pair // 2)
        col = 256 * (pair % 2)
        own[row : row + 16, col : col + 128] = low(jnp.where(left, keys, roll64(vals)))
        own[row : row + 16, col + 128 : col + 256] = low(jnp.where(left, roll64(keys), vals))
    own[base + OUT : base + OUT + 16, :] = low(k.w_out[layer])
    for j in range(4):
        own[base + UP + 16 * j : base + UP + 16 * j + 16, :] = low(k.w_up[layer, :, 512 * j : 512 * j + 512])
    own[base + DOWN : base + DOWN + 64, :] = low(k.w_down[layer])


def sem(k):
    k.cursor += 1
    assert k.cursor <= SEMS
    return k.sems.at[k.cursor - 1]


def start_all(copies):
    for copy in copies:
        copy.start()


def wait_all(copies):
    for copy in copies:
        copy.wait()


def drain(semaphore, ref):
    pltpu.make_async_copy(ref, ref, semaphore).wait()


class Stage:
    def __init__(self, k, total, moves):
        self.total, self.sent, self.got = total, sem(k), sem(k)
        start_all([remote(src, dst, self.sent, self.got, device) for src, dst, device in moves])

    def wait(self):
        drain(self.got, self.total)
        drain(self.sent, self.total)


def gather_piece(k, name, r0, rm, r1):
    g, z, y, x, dev, pk = k.g, k.z, k.y, k.x, k.dev, k.pk
    a, b, every = pl.ds(r0, rm - r0), pl.ds(rm, r1 - rm), pl.ds(r0, r1 - r0)

    def stage(total, *moves):
        return Stage(k, total, [(ref, ref, device) for ref, device in moves])

    stages = (
        lambda: stage(
            pk.at[g, pl.ds(0, 3), y, x, every],
            *[(pk.at[g, z, y, x, every], dev(g, lax.rem(z + n, 4), y, x)) for n in (2, 1, 3)],
        ),
        lambda: stage(
            pk.at[g, :, y, x, every],
            (pk.at[g, :, y, x, a], dev(g, z, 1 - y, x)),
            (pk.at[g, :, y, x, b], dev(g, z, y, 1 - x)),
        ),
        lambda: stage(
            pk.at[g, :, :, x, every],
            (pk.at[g, :, :, x, a], dev(g, z, y, 1 - x)),
            (pk.at[g, :, y, :, b], dev(g, z, 1 - y, x)),
        ),
        lambda: stage(pk.at[1 - g, :, :, :, every], (pk.at[g, :, :, :, every], dev(1 - g, z, y, x))),
    )
    waiting = None
    for begin in stages:
        if waiting is not None:
            with scope(f"gw_{name}"):
                waiting.wait()
        waiting = begin()
        yield
    with scope(f"gw_{name}"):
        waiting.wait()
    yield


def need(k, row, count=16):
    for name in touching(range(row, row + count)):
        for _ in k.gathers[name]:
            pass


def block(k, row):
    need(k, row)
    return k.pk[:, :, :, :, row : row + 16, :].reshape(512, 512)


def put_block(k, row, value):
    k.made.add(row)
    k.gr[:, :, :, :, row : row + 16, :] = low(value).reshape(2, 4, 2, 2, 16, 512)


def down_block(k, row, c):
    need(k, row, 64)
    return k.pk[c // 2, (c % 2) * 2 : (c % 2) * 2 + 2, :, :, row : row + 64, :].reshape(512, 512)


def put_down(k, row, c, value):
    if c == 3:
        k.made.update(range(row, row + 64, 16))
    k.gr[c // 2, (c % 2) * 2 : (c % 2) * 2 + 2, :, :, row : row + 64, :] = low(value).reshape(2, 2, 2, 64, 512)


def my_blocks(k):
    return [4 * j + (k.g if half == 0 else 3 - k.g) for j in range(4) for half in range(2)]


def other_blocks(k):
    return [4 * j + (1 - k.g if half == 0 else 2 + k.g) for j in range(4) for half in range(2)]


def my_block(k, i):
    return 4 * (i // 2) + jnp.where(lax.rem(i, 2) == 0, k.g, 3 - k.g)


class Post:
    def __init__(self, k, source, groups):
        self.k, self.source = k, source
        self.sent, self.got = sem(k), [sem(k) for _ in range(groups)]

    def start(self, src, dst, got, device):
        k = self.k
        is_self = jnp.logical_and(device[0] == k.g, device[1] == k.s)

        @pl.when(is_self)
        def _():
            pltpu.make_async_copy(src, dst, got).start()

        @pl.when(jnp.logical_not(is_self))
        def _():
            remote(src, dst, self.sent, got, device).start()

    def finish(self, one_is_self):
        @pl.when(one_is_self)
        def _():
            drain(self.sent, self.source.at[pl.ds(0, 7)])

        @pl.when(jnp.logical_not(one_is_self))
        def _():
            drain(self.sent, self.source)


class ToHeads(Post):
    def __init__(self, k, source, target):
        super().__init__(k, source, 2)
        self.target = target

    def send(self):
        k = self.k
        for part in range(2):

            @pl.when(k.s // 8 == part)
            def _():
                for i in range(8):
                    h = lax.rem(k.s + i, 8)
                    self.start(self.source.at[h], self.target.at[k.s], self.got[part], (k.side, k.g * 8 + h))

    def take(self, part):
        drain(self.got[part], self.target.at[pl.ds(0, 4)])

    def done(self):
        k = self.k
        self.finish(jnp.logical_and(k.s // 8 == k.g, k.side == k.g))


class FromHeads(Post):
    def __init__(self, k, source, target):
        super().__init__(k, source, 1)
        self.target = target

    def send(self, i, b):
        k = self.k
        head = lax.rem(k.s, 8)
        self.start(self.source.at[i], self.target.at[head], self.got[0], (k.s // 8, b))

    def take(self):
        drain(self.got[0], self.target)

    def done(self):
        k = self.k
        self.finish(jnp.logical_and(k.s // 8 == k.g, k.side == k.g))


def rotate_block(v, cosine, sine):
    return v * cosine + swap32(v) * sine


def rotary_tables(k, layer):
    rows, _ = layer_sizes(layer)
    lane = lanes((1, 128))
    freqs = jnp.zeros((1, 128), F32)
    for i in range(32):
        freqs = jnp.where(lane % 32 == i, 10000.0 ** (-i / 32), freqs)
    position = k.s * rows + lax.broadcasted_iota(jnp.int32, (rows, 1), 0)
    angles = position.astype(F32) * freqs
    k.cos[layer][...] = jnp.cos(angles)
    k.sin[layer][...] = jnp.sin(angles) * jnp.where(lane % 64 < 32, -1.0, 1.0)


def layer_sizes(layer):
    rows = 144 if layer == 0 else 48
    return rows, (rows // 2 + 15) // 16 * 16


def attend_loop(layer, part, body, between=None):
    if layer == 1:
        body(list(range(8)), 16)
        return
    for first in (0, 2):
        @pl.loop(first, first + 2)
        def _(n):
            body([part * 4 + n], 8 * (part + 1))

        if between is not None and first == 0:
            between()


def stack(pieces):
    return pieces[0] if len(pieces) == 1 else jnp.concatenate(pieces, axis=0)


def masked_scores(q, kv, places):
    scores = dot_nt(q, kv)
    return jnp.where(lanes(scores.shape) <= places, scores, MASK_FILL)


def stacked_queries(k, layer, items):
    rows, pad = layer_sizes(layer)
    blocks = [my_block(k, i) for i in items]
    q = stack([unpack_left(k.inbox[layer][b, 0:pad, :].astype(F32)[: rows // 2]) for b in blocks])
    places = stack([b * rows + lax.broadcasted_iota(jnp.int32, (rows, 1), 0) for b in blocks])
    return low(q * 0.125), blocks, places


def attention_forward(k, layer, part, post, between):
    rows, pad = layer_sizes(layer)
    inbox, outbox, lse, keep = k.inbox[layer], k.abox[layer], k.lse[layer], k.att[layer]

    def body(items, count):
        q, blocks, places = stacked_queries(k, layer, items)
        kv = inbox[0:count, pad : pad + rows, :].reshape(count * rows, 128)
        scores = masked_scores(q, kv, places)
        top = jnp.max(scores, axis=-1, keepdims=True)
        prob = jnp.exp(scores - top)
        total = jnp.sum(prob, axis=-1, keepdims=True)
        out = dot(low(prob), kv) / total
        stat = jnp.broadcast_to(top + jnp.log(total), out.shape)
        for n, (i, b) in enumerate(zip(items, blocks)):
            span = slice(n * rows, (n + 1) * rows)
            lse[i] = stat[span]
            keep[i] = out[span]
            outbox[i, 0 : rows // 2, :] = low(pack_right(out[span]))
            post.send(i, b)

    attend_loop(layer, part, body, between)


def attention_backward(k, layer, part, post, between=None):
    rows, pad = layer_sizes(layer)
    inbox, gradbox, lse, keep = k.inbox[layer], k.gbox[layer], k.lse[layer], k.att[layer]
    dkvt, outbox = k.dkvt[layer], k.dbox[layer]

    def body(items, count):
        q, blocks, places = stacked_queries(k, layer, items)
        kv = inbox[0:count, pad : pad + rows, :].reshape(count * rows, 128)
        grad = stack([unpack_right(gradbox[b].astype(F32)[: rows // 2]) for b in blocks])
        delta = jnp.sum(grad * stack([keep[i] for i in items]), axis=-1, keepdims=True)
        grad = low(grad)
        prob = jnp.exp(masked_scores(q, kv, places) - stack([lse[i] for i in items])[:, 0:1])
        grad_prob = dot_nt(grad, kv)
        ds = low(prob * (grad_prob - delta))
        dq = dot(ds, kv) * 0.125
        for n, (i, b) in enumerate(zip(items, blocks)):
            outbox[i, 0 : rows // 2, :] = low(pack_left(dq[n * rows : (n + 1) * rows]))
            post.send(i, b)
        dkvt[:, 0 : count * rows] += dot_tn(q, ds) + dot_tn(grad, low(prob))

    attend_loop(layer, part, body, between)


class KeySums:
    def __init__(self, k, layer, part, post):
        rows, _ = layer_sizes(layer)
        self.k, self.layer, self.post = k, layer, post
        self.items = range(8) if layer == 1 else range(4 * part, 4 * part + 4)
        first, count = (0, 16) if layer == 1 else (8 * part, 8)
        k.dkv[layer][first : first + count] = (
            k.dkvt[layer][:, first * rows : (first + count) * rows].T.reshape(count, rows, 128)
        )
        others = other_blocks(k)
        for i in self.items:
            k.dkv_out[layer][i] = k.dkv[layer][others[i]]
        span = pl.ds(self.items[0], len(self.items))
        self.copy = Stage(
            k,
            k.dkv_in[layer].at[span],
            [(k.dkv_out[layer].at[span], k.dkv_in[layer].at[span], k.dev(1 - k.g, k.z, k.y, k.x))],
        )

    def send(self):
        k, layer = self.k, self.layer
        self.copy.wait()
        mine = my_blocks(k)
        for i in self.items:
            k.kvbox[layer][i] = low(k.dkv[layer][mine[i]] + k.dkv_in[layer][i])
            self.post.send(i, mine[i])


def layer_ahead(k, layer, hidden):
    rows, pad = layer_sizes(layer)
    base = LAYER0 + layer * LAYER_ROWS
    hold = k.hold[layer]
    hold.hidden[...] = hidden
    unit, _ = norm_parts(hidden)
    normed = low(unit * k.gain[2 * layer : 2 * layer + 1, :])
    hold.normed[...] = normed
    cosine, sine = k.cos[layer][...], k.sin[layer][...]
    left = lanes(cosine.shape) < 64
    cos_kv, sin_kv = jnp.where(left, cosine, 1.0), jnp.where(left, sine, 0.0)
    sendbox = k.sendbox[layer]
    for part in range(3):
        joined = dot(normed, block(k, base + QKV + 16 * part))
        for n in range(4):
            piece = joined[:, 128 * n : 128 * n + 128]
            if part == 0:
                piece = rotate_block(piece, cosine, sine)
                sendbox[2 * n, 0 : rows // 2, :] = low(pack_pair(piece, 0))
                sendbox[2 * n + 1, 0 : rows // 2, :] = low(pack_pair(piece, 1))
            else:
                sendbox[4 * part - 4 + n, pad : pad + rows, :] = low(rotate_block(piece, cos_kv, sin_kv))
    inbox = k.inbox[layer]
    out = ToHeads(k, sendbox, inbox)
    out.send()
    point(k, f"f{layer}_sent")
    sent, shared = sem(k), [sem(k), sem(k)]
    mine, others = my_blocks(k), other_blocks(k)
    for part in range(2):
        if part == 1:
            point(k, f"f{layer}_take")
        with scope("take"):
            out.take(part)
        for b in mine[4 * part : 4 * part + 4]:
            ref = inbox.at[b, pl.ds(pad, rows)]
            remote(ref, ref, sent, shared[part], k.dev(1 - k.g, k.z, k.y, k.x)).start()
    point(k, f"f{layer}_got")
    home = k.home[layer]
    back = FromHeads(k, k.abox[layer], home)
    for part in range(2 - layer):
        for half in range(2) if layer == 1 else [part]:
            with scope("share"):
                drain(shared[half], inbox.at[pl.ds(0, 4), pl.ds(pad, rows)])
        with scope("attend"):
            attention_forward(k, layer, part, back, lambda: point(k, f"f0_mid{part}"))
        point(k, f"f{layer}_part{part}")
    with scope("home"):
        back.take()
    point(k, f"f{layer}_home")
    if layer == 1:
        point(k, "f1_out")
    for n in range(4):
        pair = unpack_pair(
            home[2 * n].astype(F32)[: rows // 2], home[2 * n + 1].astype(F32)[: rows // 2]
        )
        hold.flat[:, 128 * n : 128 * n + 128] = low(pair)
    middle = hidden + dot(hold.flat[...], block(k, base + OUT))
    hold.middle[...] = middle
    unit, _ = norm_parts(middle)
    second = low(unit * k.gain[2 * layer + 1 : 2 * layer + 2, :])
    hold.second[...] = second
    for j in range(4):
        pre = dot(second, block(k, base + UP + 16 * j))
        hold.pre[:, 512 * j : 512 * j + 512] = pre
        hold.act[:, 512 * j : 512 * j + 512] = low(gelu(pre))
    output = middle
    point(k, f"f{layer}_up")
    for c in range(4):
        output = output + dot(hold.act[:, 512 * c : 512 * c + 512], down_block(k, base + DOWN, c))
    out.done()
    back.done()
    drain(sent, inbox.at[pl.ds(0, 8), pl.ds(pad, rows)])
    return output


def layer_back(k, layer, grad_out):
    rows, pad = layer_sizes(layer)
    base = LAYER0 + layer * LAYER_ROWS
    hold = k.hold[layer]
    fall = low(grad_out)
    grad_second = jnp.zeros((rows, D), F32)
    second = hold.second[...]
    for c in range(4):
        cols = slice(512 * c, 512 * c + 512)
        put_down(k, base + DOWN, c, dot_tn(hold.act[:, cols], fall))
        grad_act = dot_nt(fall, down_block(k, base + DOWN, c))
        grad_pre = low(grad_act * gelu_grad(hold.pre[:, cols]))
        put_block(k, base + UP + 16 * c, dot_tn(second, grad_pre))
        grad_second = grad_second + dot_nt(grad_pre, block(k, base + UP + 16 * c))
    if layer == 1:
        point(k, "b1_ff")
    gain = k.gain[2 * layer + 1 : 2 * layer + 2, :]
    grad_mid, k.gain_grads[2 * layer + 1] = norm_back(hold.middle[...], gain, grad_second)
    grad_middle = grad_out + grad_mid
    hold.middle[...] = grad_middle
    proj = low(grad_middle)
    put_block(k, base + OUT, dot_tn(hold.flat[...], proj))
    grad_att = dot_nt(proj, block(k, base + OUT))
    gsend = k.gsend[layer]
    for n in range(4):
        piece = grad_att[:, 128 * n : 128 * n + 128]
        gsend[2 * n, 0 : rows // 2, :] = low(pack_pair(piece, 0))
        gsend[2 * n + 1, 0 : rows // 2, :] = low(pack_pair(piece, 1))
    out = ToHeads(k, gsend, k.gbox[layer])
    out.send()
    if layer == 0:
        point(k, "b0_ff")
    back = k.back[layer]
    home_q = FromHeads(k, k.dbox[layer], back)
    home_kv = FromHeads(k, k.kvbox[layer], k.kvback[layer])
    k.dkvt[layer][...] = jnp.zeros_like(k.dkvt[layer])
    point(k, f"b{layer}_sent")
    sums = None
    for part in reversed(range(2 - layer)):
        with scope("take"):
            for half in range(2) if layer == 1 else [part]:
                out.take(half)
        with scope("unattend"):
            def between(part=part, sums=sums):
                if sums is not None:
                    sums.send()
                point(k, f"b0_mid{part}")

            attention_backward(k, layer, part, home_q, between)
        sums = KeySums(k, layer, part, home_kv)
        point(k, f"b{layer}_part{part}")
    with scope("sums"):
        sums.send()
    point(k, f"b{layer}_sums")
    with scope("home_q"):
        home_q.take()
    cosine, sine = k.cos[layer][...], k.sin[layer][...]
    left = lanes(cosine.shape) < 64
    cos_kv, sin_kv = jnp.where(left, cosine, 1.0), jnp.where(left, sine, 0.0)
    normed = hold.normed[...]
    grad_normed = jnp.zeros((rows, D), F32)
    for part in range(3):
        if part == 1:
            if layer == 0:
                point(k, "b0_q")
            with scope("home_kv"):
                home_kv.take()
            point(k, f"b{layer}_home")
        for n in range(4):
            if part == 0:
                piece = unpack_pair(
                    back[2 * n].astype(F32)[: rows // 2],
                    back[2 * n + 1].astype(F32)[: rows // 2],
                )
                piece = rotate_block(piece, cosine, -sine)
            else:
                piece = k.kvback[layer][4 * part - 4 + n].astype(F32)
                piece = rotate_block(piece, cos_kv, -sin_kv)
            hold.gj[:, 128 * n : 128 * n + 128] = low(piece)
        gj = hold.gj[...]
        put_block(k, base + QKV + 16 * part, dot_tn(normed, gj))
        grad_normed = grad_normed + dot_nt(gj, block(k, base + QKV + 16 * part))
    if layer == 0:
        point(k, "b0_kv")
    gain = k.gain[2 * layer : 2 * layer + 1, :]
    grad_in, k.gain_grads[2 * layer] = norm_back(hold.hidden[...], gain, grad_normed)
    out.done()
    home_q.done()
    home_kv.done()
    if layer == 1:
        point(k, "b1_end")
    return hold.middle[...] + grad_in


def byte_matrix(ids, half):
    n = lanes((ids.shape[0], 512))
    return low(jnp.where((n // 16 * 8 + n % 8 == ids) & (n // 8 % 2 == half), 1.0, 0.0))


def forward_backward(k):
    rows, short = 144, 48
    need(k, EG)
    gains = jnp.sum(k.pk[:, :, :, :, EG : EG + 16, 256:512].astype(F32).reshape(32, 16, 256), axis=0)
    k.gain[:, 0:256] = gains[0:8]
    k.gain[:, 256:512] = gains[8:16]
    k.gain_grads = [None] * 5
    table = k.pk[:, :, :, :, EG : EG + 16, 0:256].reshape(512, 256)
    k.columns[0:1, 0:rows] = k.ids[...].astype(F32)
    k.columns[1:2, 0:rows] = k.targets[...].astype(F32)
    columns = k.columns[...].T
    ids, targets = columns[0:rows, 0:1].astype(jnp.int32), columns[0:rows, 1:2].astype(jnp.int32)
    for layer in range(2):
        rotary_tables(k, layer)
    first_in = jnp.concatenate([dot(byte_matrix(ids, 0), table), dot(byte_matrix(ids, 1), table)], axis=1)
    first = layer_ahead(k, 0, first_in)
    k.shift[8 : 8 + rows, :] = first
    rim = remote(
        k.shift.at[pl.ds(rows, 8)], k.shift.at[pl.ds(0, 8)], sem(k), sem(k), (k.g, lax.rem(k.s + 1, 16))
    )

    @pl.when(k.s < 15)
    def _():
        rim.start()

    point(k, "f0_rim")

    @pl.when(k.s > 0)
    def _():
        rim.wait_recv()

    @pl.when(k.s == 0)
    def _():
        k.shift[0:8, :] = jnp.zeros((8, D), F32)

    @pl.when(k.s < 15)
    def _():
        rim.wait_send()

    def pool_matrix(shape, offset, axis):
        j = lax.broadcasted_iota(jnp.int32, shape, axis)
        t = lax.broadcasted_iota(jnp.int32, shape, 1 - axis) - offset
        return jnp.where((t >= 3 * j) & (t < 3 * j + 3), 1.0, 0.0)

    pooled = exact(pool_matrix((short, rows + 8), 6, 0), k.shift[...]) / 3.0
    point(k, "f0_end")
    short_out = layer_ahead(k, 1, pooled)
    upsampled = k.shift[8 : 8 + rows, :] + exact(pool_matrix((rows, short), 0, 1), short_out)
    gain = k.gain[4:5, :]
    unit, _ = norm_parts(upsampled)
    final = low(unit * gain)
    need(k, HEAD)
    head = k.pk[:, :, :, :, HEAD : HEAD + 16, 0:256].reshape(512, 256)
    logits = dot(final, head)
    top = jnp.max(logits, axis=-1, keepdims=True)
    log_total = top + jnp.log(jnp.sum(jnp.exp(logits - top), axis=-1, keepdims=True))
    hot = jnp.where(lanes((rows, 256)) == targets, 1.0, 0.0)
    picked = jnp.sum(hot * logits, axis=-1, keepdims=True)
    position = k.s * rows + lax.broadcasted_iota(jnp.int32, (rows, 1), 0)
    length = jnp.zeros((rows, 1), F32)
    begin = jnp.int32(0)
    for i in range(8):
        size = k.lengths[0, i]
        inside = (position >= begin) & (position < begin + size)
        length = jnp.where(inside, size.astype(F32), length)
        begin = begin + size
    k.loss = jnp.sum((log_total - picked) / length, axis=0, keepdims=True)
    grad_logits = low((jnp.exp(logits - log_total) - hot) / length)
    k.gr[:, :, :, :, HEAD : HEAD + 16, 0:256] = low(dot_tn(final, grad_logits)).reshape(2, 4, 2, 2, 16, 256)
    k.made.add(HEAD)
    k.gr[:, :, :, :, HEAD : HEAD + 16, 256:512] = jnp.zeros((2, 4, 2, 2, 16, 256), LOW)
    grad_final = dot_nt(grad_logits, head)
    grad_up, k.gain_grads[4] = norm_back(upsampled, gain, grad_final)
    k.up[...] = grad_up
    grad_short = exact(pool_matrix((short, rows), 0, 0), grad_up)
    grad_pooled = layer_back(k, 1, grad_short)
    k.pool[0:short, :] = grad_pooled
    rim2 = remote(
        k.pool.at[pl.ds(0, 8)], k.pool.at[pl.ds(short, 8)], sem(k), sem(k), (k.g, lax.rem(k.s + 15, 16))
    )

    @pl.when(k.s > 0)
    def _():
        rim2.start()

    point(k, "b1_rim")

    @pl.when(k.s < 15)
    def _():
        rim2.wait_recv()

    @pl.when(k.s == 15)
    def _():
        k.pool[short : short + 8, :] = jnp.zeros((8, D), F32)

    @pl.when(k.s > 0)
    def _():
        rim2.wait_send()

    t = lax.broadcasted_iota(jnp.int32, (rows, short + 8), 0)
    j = lax.broadcasted_iota(jnp.int32, (rows, short + 8), 1)
    spread = jnp.where((t + 2 >= 3 * j) & (t + 2 < 3 * j + 3), 1.0, 0.0)
    grad_first = k.up[...] + exact(spread, k.pool[...] / 3.0)
    grad_in = layer_back(k, 0, grad_first)
    table_grad = dot_tn(byte_matrix(ids, 0), low(grad_in[:, 0:256])) + dot_tn(
        byte_matrix(ids, 1), low(grad_in[:, 256:512])
    )
    k.gr[:, :, :, :, EG : EG + 16, 0:256] = low(table_grad).reshape(2, 4, 2, 2, 16, 256)
    fill = [jnp.zeros((3, 256), F32)]
    gains = jnp.concatenate(
        [v[:, 0:256] for v in k.gain_grads] + fill + [v[:, 256:512] for v in k.gain_grads] + fill, axis=0
    )
    gains = jnp.broadcast_to(low(gains)[None], (32, 16, 256))
    k.gr[:, :, :, :, EG : EG + 16, 256:512] = gains.reshape(2, 4, 2, 2, 16, 256)
    k.made.add(EG)
    point(k, "b0_end")


def add_into(ref, other):
    ref[...] = low(ref[...].astype(F32) + other[...].astype(F32))


def reduce_piece(k, name, r0, rm, r1):
    g, z, y, x, dev, gr = k.g, k.z, k.y, k.x, k.dev, k.gr
    a, b, every = pl.ds(r0, rm - r0), pl.ds(rm, r1 - rm), pl.ds(r0, r1 - r0)
    assert k.made.issuperset(range(r0, r1, 16)), name
    waiting = Stage(
        k, k.rc.at[:, :, :, every], [(gr.at[1 - g, :, :, :, every], k.rc.at[:, :, :, every], dev(1 - g, z, y, x))]
    )
    yield
    with scope(f"rw_{name}"):
        waiting.wait()

    with scope("radd"):

        @pl.loop(0, 16)
        def _(n):
            place = (n // 4, lax.rem(n // 2, 2), lax.rem(n, 2), every)
            add_into(gr.at[(g,) + place], k.rc.at[place])

    waiting = Stage(
        k,
        k.r2.at[:, :, every],
        [
            (gr.at[g, :, :, 1 - x, a], k.r2.at[:, :, a], dev(g, z, y, 1 - x)),
            (gr.at[g, :, 1 - y, :, b], k.r2.at[:, :, b], dev(g, z, 1 - y, x)),
        ],
    )
    yield
    with scope(f"rw_{name}"):
        waiting.wait()

    @pl.loop(0, 8)
    def _(n):
        add_into(gr.at[g, n // 2, lax.rem(n, 2), x, a], k.r2.at[n // 2, lax.rem(n, 2), a])
        add_into(gr.at[g, n // 2, y, lax.rem(n, 2), b], k.r2.at[n // 2, lax.rem(n, 2), b])

    waiting = Stage(
        k,
        k.r1.at[:, every],
        [
            (gr.at[g, :, 1 - y, x, a], k.r1.at[:, a], dev(g, z, 1 - y, x)),
            (gr.at[g, :, y, 1 - x, b], k.r1.at[:, b], dev(g, z, y, 1 - x)),
        ],
    )
    yield
    with scope(f"rw_{name}"):
        waiting.wait()

    @pl.loop(0, 4)
    def _(n):
        add_into(gr.at[g, n, y, x, every], k.r1.at[n, every])

    moves = []
    for n in (2, 1, 3):
        to = lax.rem(z + n, 4)
        moves.append((gr.at[g, to, y, x, every], k.rz.at[n - 1, every], dev(g, to, y, x)))
    waiting = Stage(k, k.rz.at[:, every], moves)
    yield
    with scope(f"rw_{name}"):
        waiting.wait()
    k.summed.update(range(r0, r1, 16))
    yield


def own_sum(k, row, count):
    rows = pl.ds(row, count)
    v = k.gr[k.g, k.z, k.y, k.x, rows].astype(F32)
    for i in range(3):
        v = v + k.rz[i, rows].astype(F32)
    return v


def square(k, v):
    k.sq = k.sq + jnp.sum(jnp.sum(v * v, axis=1, keepdims=True), axis=0, keepdims=True)


def flush(k, name, layer=None):
    src, dst = getattr(k, "s_" + name), getattr(k, "g_" + name)
    if layer is not None:
        src, dst = src.at[layer], dst.at[layer]
    copy = pltpu.make_async_copy(src, dst, sem(k))
    copy.start()
    k.flushed.append(copy)


def store_qkv(k, layer):
    v = own_sum(k, LAYER0 + layer * LAYER_ROWS + QKV, 48)
    square(k, v)
    k.s_qkv[layer, :, 0:512] = v[0:16]
    for pair in range(4):
        row, col = 16 + 16 * (pair // 2), 256 * (pair % 2)
        even = v[row : row + 16, col : col + 128]
        odd = v[row : row + 16, col + 128 : col + 256]
        left = lanes(even.shape) < 64
        k.s_qkv[layer, :, 512 + 128 * pair : 640 + 128 * pair] = jnp.where(left, even, roll64(odd))
        k.s_qkv[layer, :, 1024 + 128 * pair : 1152 + 128 * pair] = jnp.where(left, roll64(even), odd)
    flush(k, "qkv", layer)


def store_out(k, layer):
    v = own_sum(k, LAYER0 + layer * LAYER_ROWS + OUT, 16)
    square(k, v)
    k.s_out[layer] = v
    flush(k, "out", layer)


def store_up(k, layer):
    v = own_sum(k, LAYER0 + layer * LAYER_ROWS + UP, 64)
    square(k, v)
    for j in range(4):
        k.s_up[layer, :, 512 * j : 512 * j + 512] = v[16 * j : 16 * j + 16]
    flush(k, "up", layer)


def store_down(k, layer):
    v = own_sum(k, LAYER0 + layer * LAYER_ROWS + DOWN, 64)
    square(k, v)
    k.s_down[layer] = v
    flush(k, "down", layer)


def store_head(k):
    v = own_sum(k, HEAD, 16)[:, 0:256]
    square(k, v)
    k.s_head[...] = v
    flush(k, "head")


def store_rest(k):
    v = own_sum(k, EG, 16)
    square(k, v[:, 0:256])
    k.s_embed[:, 0:256] = v[0:8, 0:256]
    k.s_embed[:, 256:512] = v[8:16, 0:256]
    gains = jnp.where(k.g == 0, v[0:8, 256:512], v[8:16, 256:512])
    row, column = lax.broadcasted_iota(jnp.int32, (256, 16), 0), lax.broadcasted_iota(jnp.int32, (256, 16), 1)
    gains = exact(gains, jnp.where(row - 16 * k.s == column, 1.0, 0.0))[0:5]
    square(k, gains)
    k.s_gains[...] = gains
    flush(k, "embed")
    flush(k, "gains")


def store_ready(k):
    stores = [(range(EG, EG + 16), store_rest, ()), (range(HEAD, HEAD + 16), store_head, ())]
    for layer in range(2):
        base = LAYER0 + layer * LAYER_ROWS
        stores.append((range(base + QKV, base + QKV + 48), store_qkv, (layer,)))
        stores.append((range(base + OUT, base + OUT + 16), store_out, (layer,)))
        stores.append((range(base + UP, base + UP + 64), store_up, (layer,)))
        stores.append((range(base + DOWN, base + DOWN + 64), store_down, (layer,)))
    for rows, store, args in stores:
        if rows.start not in k.stored and k.summed.issuperset(range(rows.start, rows.stop, 16)):
            k.stored.add(rows.start)
            store(k, *args)


def finish_grads(k):
    g = k.g
    point(k, "tail")
    for name in PIECES:
        for _ in k.reduces[name]:
            store_ready(k)
    store_ready(k)
    lane = lanes((8, 128))
    k.stat[0] = jnp.where(lane == 0, k.sq, jnp.where(lane == 1, k.loss, 0.0))
    me = g * 16 + k.s
    sent, got = sem(k), sem(k)

    @pl.loop(1, 32)
    def _(i):
        t = lax.rem(me + i, 32)
        remote(k.stat.at[0], k.stat.at[i], sent, got, (t // 16, lax.rem(t, 16))).start()

    with scope("stats"):
        drain(got, k.stat.at[pl.ds(1, 31)])
        drain(sent, k.stat.at[pl.ds(1, 31)])
    k.stats[...] = jnp.sum(k.stat[...], axis=0)
    wait_all(k.flushed)


IN_NAMES = (
    "ids", "targets", "lengths", "w_qkv", "w_out", "w_up", "w_down", "embed", "head", "gains",
)
OUT_NAMES = ("g_qkv", "g_out", "g_up", "g_down", "g_embed", "g_head", "g_gains", "stats")
SEMS = 168


def scratch_shapes():
    shapes = {
        "pk": ((2, 4, 2, 2, ROWS, D), LOW),
        "gr": ((2, 4, 2, 2, ROWS, D), LOW),
        "rc": ((4, 2, 2, ROWS, D), LOW),
        "r2": ((4, 2, ROWS, D), LOW),
        "r1": ((4, ROWS, D), LOW),
        "rz": ((3, ROWS, D), LOW),
        "gain": ((8, D), F32),
        "shift": ((152, D), F32),
        "pool": ((56, D), F32),
        "up": ((144, D), F32),
        "stat": ((32, 8, 128), F32),
        "columns": ((128, 256), F32),
        "s_qkv": ((2, 16, 3 * D), F32),
        "s_out": ((2, 16, D), F32),
        "s_up": ((2, 16, 4 * D), F32),
        "s_down": ((2, 64, D), F32),
        "s_embed": ((8, D), F32),
        "s_head": ((16, 256), F32),
        "s_gains": ((5, 16), F32),
    }
    for layer in range(2):
        rows, pad = layer_sizes(layer)
        for name, shape, kind in (
            ("cos", (rows, 128), F32),
            ("sin", (rows, 128), F32),
            ("sendbox", (8, pad + rows, 128), LOW),
            ("inbox", (16, pad + rows, 128), LOW),
            ("abox", (8, pad, 128), LOW),
            ("home", (8, pad, 128), LOW),
            ("gsend", (8, pad, 128), LOW),
            ("gbox", (16, pad, 128), LOW),
            ("dbox", (8, pad, 128), LOW),
            ("kvbox", (8, rows, 128), LOW),
            ("back", (8, pad, 128), LOW),
            ("kvback", (8, rows, 128), LOW),
            ("lse", (8, rows, 128), F32),
            ("att", (8, rows, 128), F32),
            ("dkvt", (128, 16 * rows), F32),
            ("dkv", (16, rows, 128), F32),
            ("dkv_out", (8, rows, 128), F32),
            ("dkv_in", (8, rows, 128), F32),
            ("h_hidden", (rows, D), F32),
            ("h_normed", (rows, D), LOW),
            ("h_flat", (rows, D), LOW),
            ("h_middle", (rows, D), F32),
            ("h_second", (rows, D), LOW),
            ("h_pre", (rows, 4 * D), F32),
            ("h_act", (rows, 4 * D), LOW),
            ("h_gj", (rows, D), LOW),
        ):
            shapes[name + str(layer)] = (shape, kind)
    return shapes


SCRATCH = scratch_shapes()
PER_LAYER = (
    "cos", "sin", "sendbox", "inbox", "abox", "home", "gsend", "gbox", "dbox", "back", "lse", "att", "dkvt", "dkv",
    "dkv_out", "dkv_in", "kvbox", "kvback",
)
HELD = ("hidden", "normed", "flat", "middle", "second", "pre", "act", "gj")


def update_kernel(*refs):
    stats, sources, outs, loss_ref, norm_ref = refs[0], refs[1:29], refs[29:50], refs[50], refs[51]
    held, made, sems, out_sems = refs[52:59], refs[59:66], refs[66], refs[67]
    order = (4, 5, 6, 1, 0, 2, 3)
    for i in order:
        start_all([pltpu.make_async_copy(sources[7 * j + i], held[i].at[j], sems.at[i]) for j in range(4)])
    norm = jnp.sqrt(stats[0:1, 0:1])
    loss_ref[...] = stats[0:1, 1:2]
    norm_ref[...] = norm
    clip = jnp.minimum(1.0, CLIP_NORM / norm)
    for i in order:
        drain(sems.at[i], held[i])
        gradient, master, first, second = (held[i][j] for j in range(4))
        results = adam_update(master, gradient * clip, first, second, STEP_RATES[i], WEIGHT_DECAYS[i])
        for j in range(3):
            made[i][j] = results[j]
        start_all([pltpu.make_async_copy(made[i].at[j], outs[7 * j + i], out_sems.at[i]) for j in range(3)])
    for i in order:
        drain(out_sems.at[i], made[i])


def on_device_fast(byte_ids, targets, item_lengths, *arrays):
    masters, firsts, seconds = arrays[0:7], arrays[7:14], arrays[14:21]
    vmem, anywhere = pl.BlockSpec(memory_space=pltpu.VMEM), pl.BlockSpec(memory_space=pl.ANY)
    shard_shapes = [jax.ShapeDtypeStruct(master.shape, F32) for master in masters]
    outs = pl.pallas_call(
        kernel,
        name="step",
        out_shape=shard_shapes + [jax.ShapeDtypeStruct((8, 128), F32)],
        in_specs=[vmem, vmem, pl.BlockSpec(memory_space=pltpu.SMEM)] + [vmem] * 7,
        out_specs=[anywhere] * 7 + [vmem],
        scratch_shapes=[pltpu.VMEM(shape, kind) for shape, kind in SCRATCH.values()]
        + [pltpu.SemaphoreType.DMA((SEMS,))],
        compiler_params=pltpu.CompilerParams(collective_id=0, has_side_effects=True, vmem_limit_bytes=63 << 20),
    )(byte_ids, targets, item_lengths, *masters)
    grads, stats = outs[:7], outs[7]
    results = pl.pallas_call(
        update_kernel,
        name="update",
        out_shape=shard_shapes * 3 + [jax.ShapeDtypeStruct((1, 1), F32)] * 2,
        in_specs=[vmem] + [anywhere] * 28,
        out_specs=[anywhere] * 21 + [vmem] * 2,
        scratch_shapes=[pltpu.VMEM((count, *shard.shape), F32) for count in (4, 3) for shard in shard_shapes]
        + [pltpu.SemaphoreType.DMA((7,)), pltpu.SemaphoreType.DMA((7,))],
        compiler_params=pltpu.CompilerParams(vmem_limit_bytes=63 << 20),
    )(stats, *grads, *masters, *firsts, *seconds)
    return (results[21].reshape(()), results[22].reshape(()), *results[:21])


def solution(mesh):
    tuned = mesh.shape["dp"] == 2 and mesh.shape["seq"] == 16
    row = P(None, ("dp", "seq"), None)
    flat = P(("dp", "seq"), None)
    shards = (row, row, row, row, flat, flat, P(None, ("dp", "seq")))
    return jax.shard_map(
        on_device_fast if tuned else on_device_general,
        mesh=mesh,
        in_specs=(P("dp", "seq"), P("dp", "seq"), P("dp", None)) + shards * 3,
        out_specs=(P(), P()) + shards * 3,
        check_vma=False,
    )
```

```python
import contextlib
import functools

import jax
import jax.numpy as jnp
from jax import lax
from jax.experimental import pallas as pl
from jax.experimental.pallas import tpu as pltpu
from jax.sharding import PartitionSpec as P

HEADS = 8
VOCAB = 256
RATE = 3
STEP = 10

CLIP_NORM = 0.02
BETA_ONE = 0.9
BETA_TWO = 0.95
STEP_RATES = (0.03, 0.2, 0.03, 0.03, 0.6, 0.03, 0.2)
WEIGHT_DECAYS = (0.1, 0.1, 0.1, 0.1, 0.1, 0.1, 0.0)
EPSILON = 1e-08
NORM_EPS = 1e-05
MASK_FILL = -1e30


def shifted_2(value, axis, steps):
    count = lax.axis_size(axis)
    leading, last = (max(0, -steps), min(count, count - steps))
    return lax.ppermute(value, axis, [(source, source + steps) for source in range(leading, last)])


def to_low(values):
    return values.astype(jnp.bfloat16)


def layer_norm(values, gain):
    center = values - jnp.mean(values, axis=-1, keepdims=True)
    spread = jnp.mean(center * center, axis=-1, keepdims=True)
    return center * lax.rsqrt(spread + NORM_EPS) * gain


def rotate(joined, positions, num_heads):
    parts = joined.reshape(joined.shape[0], 3, num_heads, -1)
    half_size = parts.shape[-1] // 2
    freqs = 10000.0 ** (-jnp.arange(half_size, dtype=jnp.float32) / half_size)
    angles = positions.astype(jnp.float32)[:, None] * freqs[None, :]
    cosine = jnp.cos(angles)[:, None, :]
    sine = jnp.sin(angles)[:, None, :]

    def rotate_half(values):
        first_half = values[..., :half_size]
        second_half = values[..., half_size:]
        return jnp.concatenate(
            [first_half * cosine - second_half * sine, first_half * sine + second_half * cosine],
            axis=-1,
        )

    return (rotate_half(parts[:, 0]), rotate_half(parts[:, 1]), parts[:, 2])


def scores_for(q_low, k_low, query_pos, key_pos):
    scores = jnp.einsum(
        "rhe,phe->hrp", q_low, k_low, preferred_element_type=jnp.float32
    ) * q_low.shape[-1] ** (-0.5)
    causal = query_pos[:, None] >= key_pos[None, :]
    return (scores, causal)


def attend(q_low, k_low, v_low, query_pos):
    num_rows, num_heads, head_size = q_low.shape
    key_piece = (
        lax.all_gather(k_low, "seq", axis=0, tiled=True),
        lax.all_gather(v_low, "seq", axis=0, tiled=True),
    )
    running_max = jnp.full((num_heads, num_rows), MASK_FILL, jnp.float32)
    accum = jnp.zeros((num_rows, num_heads, head_size), jnp.float32)
    key_pos = jnp.arange(key_piece[0].shape[0], dtype=jnp.int32)
    scores, causal = scores_for(q_low, key_piece[0], query_pos, key_pos)
    scores = jnp.where(causal[None], scores, MASK_FILL)
    new_max = jnp.maximum(running_max, jnp.max(scores, axis=-1))
    factor = jnp.exp(running_max - new_max)
    attn_prob = jnp.where(causal[None], jnp.exp(scores - new_max[..., None]), 0.0)
    denom = jnp.sum(attn_prob, axis=-1)
    accum = accum * factor.T[:, :, None] + jnp.einsum(
        "hrp,phe->rhe", to_low(attn_prob), key_piece[1], preferred_element_type=jnp.float32
    )
    running_max, denom, accum = (new_max, denom, accum)
    return (accum / denom.T[:, :, None], (running_max + jnp.log(denom)).T)


def block_grads(q_low, grad_low, log_total, row_delta, query_pos, k_low, v_low, key_pos):
    scores, causal = scores_for(q_low, k_low, query_pos, key_pos)
    attn_prob = jnp.where(causal[None], jnp.exp(scores - log_total.T[:, :, None]), 0.0)
    grad_prob = jnp.einsum("rhe,phe->hrp", grad_low, v_low, preferred_element_type=jnp.float32)
    grad_score = to_low(attn_prob * (grad_prob - row_delta.T[:, :, None]))
    score_scale = q_low.shape[-1] ** (-0.5)
    grad_q = (
        jnp.einsum("hrp,phe->rhe", grad_score, k_low, preferred_element_type=jnp.float32)
        * score_scale
    )
    grad_k = (
        jnp.einsum("hrp,rhe->phe", grad_score, q_low, preferred_element_type=jnp.float32)
        * score_scale
    )
    grad_v = jnp.einsum(
        "hrp,rhe->phe", to_low(attn_prob), grad_low, preferred_element_type=jnp.float32
    )
    return (grad_q, grad_k, grad_v)


def attend_back(q_low, k_low, v_low, grad_low, log_total, row_delta, query_pos):
    key_piece = (
        lax.all_gather(k_low, "seq", axis=0, tiled=True),
        lax.all_gather(v_low, "seq", axis=0, tiled=True),
    )
    key_pos = jnp.arange(key_piece[0].shape[0], dtype=jnp.int32)
    grad_q = block_grads(
        q_low, grad_low, log_total, row_delta, query_pos, key_piece[0], key_piece[1], key_pos
    )[0]
    all_totals, all_deltas = (
        lax.all_gather(log_total, "seq", axis=0, tiled=True),
        lax.all_gather(row_delta, "seq", axis=0, tiled=True),
    )
    query_piece = (
        lax.all_gather(q_low, "seq", axis=0, tiled=True),
        lax.all_gather(grad_low, "seq", axis=0, tiled=True),
    )
    piece_rows = query_piece[0].shape[0]
    piece_pos = jnp.arange(piece_rows, dtype=jnp.int32)
    unused_q, grad_k_blk, grad_v_blk = block_grads(
        query_piece[0], query_piece[1], all_totals, all_deltas, piece_pos, k_low, v_low, query_pos
    )
    return (grad_q, grad_k_blk, grad_v_blk)


def layer_forward(hidden, weights, gain_pair, positions):
    w_joined, w_proj, w_rise, w_fall = weights
    num_rows = hidden.shape[0]
    normed = to_low(layer_norm(hidden, gain_pair[0]))
    joined = jnp.dot(normed, w_joined, preferred_element_type=jnp.float32)
    queries, keys, values = rotate(joined, positions, HEADS)
    q_low, k_low, v_low = (to_low(queries), to_low(keys), to_low(values))
    attended, log_total = attend(q_low, k_low, v_low, positions)
    flat_low = to_low(attended.reshape(num_rows, -1))
    middle = hidden + jnp.dot(flat_low, w_proj, preferred_element_type=jnp.float32)
    second = to_low(layer_norm(middle, gain_pair[1]))
    pre_act = jnp.dot(second, w_rise, preferred_element_type=jnp.float32)
    activated = to_low(jax.nn.gelu(pre_act))
    output = middle + jnp.dot(activated, w_fall, preferred_element_type=jnp.float32)
    saved = (
        normed,
        joined,
        q_low,
        k_low,
        v_low,
        attended,
        log_total,
        flat_low,
        middle,
        second,
        pre_act,
        activated,
    )
    return (output, saved)


def layer_backward(hidden, weights, gain_pair, positions, grad_out):
    w_joined, w_proj, w_rise, w_fall = weights
    unused_out, saved = layer_forward(hidden, weights, gain_pair, positions)
    (
        normed,
        joined,
        q_low,
        k_low,
        v_low,
        attended,
        log_total,
        flat_low,
        middle,
        second,
        pre_act,
        activated,
    ) = saved
    fall_low = to_low(grad_out)
    grad_fall = jnp.dot(activated.T, fall_low, preferred_element_type=jnp.float32)
    grad_act = jnp.dot(fall_low, w_fall.T, preferred_element_type=jnp.float32)
    grad_pre = to_low(jax.vjp(jax.nn.gelu, pre_act)[1](grad_act)[0])
    grad_rise = jnp.dot(second.T, grad_pre, preferred_element_type=jnp.float32)
    grad_second = jnp.dot(grad_pre, w_rise.T, preferred_element_type=jnp.float32)
    grad_middle_n, grad_gain_ffn = jax.vjp(layer_norm, middle, gain_pair[1])[1](grad_second)
    grad_middle = grad_out + grad_middle_n
    proj_low = to_low(grad_middle)
    grad_proj = jnp.dot(flat_low.T, proj_low, preferred_element_type=jnp.float32)
    grad_att = to_low(
        jnp.dot(proj_low, w_proj.T, preferred_element_type=jnp.float32).reshape(attended.shape)
    )
    row_delta = jnp.sum(grad_att.astype(jnp.float32) * attended, axis=-1)
    grad_q, grad_k, grad_v = attend_back(
        q_low, k_low, v_low, grad_att, log_total, row_delta, positions
    )

    def rotate_joined(joined_in):
        return rotate(joined_in, positions, HEADS)

    grad_joined = to_low(jax.vjp(rotate_joined, joined)[1]((grad_q, grad_k, grad_v))[0])
    grad_w_joined = jnp.dot(normed.T, grad_joined, preferred_element_type=jnp.float32)
    grad_normed = jnp.dot(grad_joined, w_joined.T, preferred_element_type=jnp.float32)
    grad_in_n, grad_gain_attn = jax.vjp(layer_norm, hidden, gain_pair[0])[1](grad_normed)
    return (
        grad_middle + grad_in_n,
        (grad_w_joined, grad_proj, grad_rise, grad_fall),
        jnp.stack([grad_gain_attn, grad_gain_ffn]),
    )


def adam_update(weight, gradient, moment_one, moment_two, step_rate, decay_rate):
    moment_one = BETA_ONE * moment_one + (1.0 - BETA_ONE) * gradient
    moment_two = BETA_TWO * moment_two + (1.0 - BETA_TWO) * gradient * gradient
    first_hat = moment_one / (1.0 - BETA_ONE**STEP)
    second_hat = moment_two / (1.0 - BETA_TWO**STEP)
    weight = weight - step_rate * (
        first_hat / (jnp.sqrt(second_hat) + EPSILON) + decay_rate * weight
    )
    return (weight, moment_one, moment_two)


def on_device_general(
    byte_ids,
    targets,
    item_lengths,
    w_qkv,
    w_out,
    w_up,
    w_down,
    embed,
    head,
    gains,
    mom_qkv,
    mom_out,
    mom_up,
    mom_down,
    mom_embed,
    mom_head,
    mom_gains,
    sec_qkv,
    sec_out,
    sec_up,
    sec_down,
    sec_embed,
    sec_head,
    sec_gains,
):
    low_qkv, low_out, low_up, low_down, low_embed, low_head, low_gains = (
        lax.all_gather(to_low(w_qkv), ("dp", "seq"), axis=1, tiled=True),
        lax.all_gather(to_low(w_out), ("dp", "seq"), axis=1, tiled=True),
        lax.all_gather(to_low(w_up), ("dp", "seq"), axis=1, tiled=True),
        lax.all_gather(to_low(w_down), ("dp", "seq"), axis=1, tiled=True),
        lax.all_gather(to_low(embed), ("dp", "seq"), axis=0, tiled=True),
        lax.all_gather(to_low(head), ("dp", "seq"), axis=0, tiled=True),
        lax.all_gather(to_low(gains), ("dp", "seq"), axis=1, tiled=True),
    )
    gain_rows = low_gains.astype(jnp.float32)
    byte_row = byte_ids[0]
    num_rows = byte_row.shape[0]
    short_rows = num_rows // RATE
    seq_place = lax.axis_index("seq")
    positions = seq_place * num_rows + jnp.arange(num_rows, dtype=jnp.int32)
    short_pos = seq_place * short_rows + jnp.arange(short_rows, dtype=jnp.int32)
    vocab_ids = jnp.arange(VOCAB, dtype=jnp.int32)
    one_hot_in = (byte_row[:, None] == vocab_ids[None, :]).astype(jnp.float32)
    embedded = jnp.dot(
        one_hot_in.astype(jnp.bfloat16), low_embed, preferred_element_type=jnp.float32
    )
    lower_weights = (low_qkv[0], low_out[0], low_up[0], low_down[0])
    upper_weights = (low_qkv[1], low_out[1], low_up[1], low_down[1])
    first_out, unused_first = layer_forward(embedded, lower_weights, gain_rows[0:2], positions)
    left_rim = shifted_2(first_out[num_rows - RATE + 1 :], "seq", 1)
    shifted = jnp.concatenate([left_rim, first_out[: num_rows - RATE + 1]], axis=0)
    pooled = jnp.mean(shifted.reshape(short_rows, RATE, -1), axis=1)
    short_out, unused_short = layer_forward(pooled, upper_weights, gain_rows[2:4], short_pos)
    upsampled = first_out + jnp.repeat(short_out, RATE, axis=0)
    top_gain = gain_rows[gain_rows.shape[0] - 1]
    final_low = to_low(layer_norm(upsampled, top_gain))
    logits = jnp.dot(final_low, low_head, preferred_element_type=jnp.float32)
    row_max = jnp.max(logits, axis=-1, keepdims=True)
    log_total = row_max[:, 0] + jnp.log(jnp.sum(jnp.exp(logits - row_max), axis=-1))
    one_hot_out = (targets[0][:, None] == vocab_ids[None, :]).astype(jnp.float32)
    picked = jnp.sum(one_hot_out * logits, axis=-1)
    lengths = item_lengths[0]
    ends = jnp.cumsum(lengths)
    doc_index = jnp.sum((positions[:, None] >= ends[None, :]).astype(jnp.int32), axis=1)
    item_ids = jnp.arange(lengths.shape[0], dtype=jnp.int32)
    doc_length = jnp.sum(
        jnp.where(item_ids[None, :] == doc_index[:, None], lengths[None, :], 0), axis=1
    ).astype(jnp.float32)
    loss_local = jnp.sum((log_total - picked) / doc_length)
    loss_sum = lax.psum(loss_local, ("dp", "seq"))
    grad_logits = to_low((jnp.exp(logits - log_total[:, None]) - one_hot_out) / doc_length[:, None])
    grad_head = jnp.dot(final_low.T, grad_logits, preferred_element_type=jnp.float32)
    grad_final = jnp.dot(grad_logits, low_head.T, preferred_element_type=jnp.float32)
    grad_upsampled, grad_gain_top = jax.vjp(layer_norm, upsampled, top_gain)[1](grad_final)
    grad_short = jnp.sum(grad_upsampled.reshape(short_rows, RATE, -1), axis=1)
    grad_pooled, upper_grads, upper_gain_grads = layer_backward(
        pooled, upper_weights, gain_rows[2:4], short_pos, grad_short
    )
    grad_shifted = jnp.repeat(grad_pooled / RATE, RATE, axis=0)
    rim_grad = shifted_2(grad_shifted[: RATE - 1], "seq", -1)
    grad_first = grad_upsampled + jnp.concatenate([grad_shifted[RATE - 1 :], rim_grad], axis=0)
    grad_embedded, lower_grads, lower_gain_grads = layer_backward(
        embedded, lower_weights, gain_rows[0:2], positions, grad_first
    )
    grad_embed = jnp.dot(one_hot_in.T, grad_embedded, precision=lax.Precision.HIGHEST)
    grad_gains = jnp.concatenate(
        [lower_gain_grads, upper_gain_grads, grad_gain_top[None, :]], axis=0
    )
    shard_grads = (
        lax.psum_scatter(
            jnp.stack([lower_grads[0], upper_grads[0]]),
            ("dp", "seq"),
            scatter_dimension=1,
            tiled=True,
        ),
        lax.psum_scatter(
            jnp.stack([lower_grads[1], upper_grads[1]]),
            ("dp", "seq"),
            scatter_dimension=1,
            tiled=True,
        ),
        lax.psum_scatter(
            jnp.stack([lower_grads[2], upper_grads[2]]),
            ("dp", "seq"),
            scatter_dimension=1,
            tiled=True,
        ),
        lax.psum_scatter(
            jnp.stack([lower_grads[3], upper_grads[3]]),
            ("dp", "seq"),
            scatter_dimension=1,
            tiled=True,
        ),
        lax.psum_scatter(grad_embed, ("dp", "seq"), scatter_dimension=0, tiled=True),
        lax.psum_scatter(grad_head, ("dp", "seq"), scatter_dimension=0, tiled=True),
        lax.psum_scatter(grad_gains, ("dp", "seq"), scatter_dimension=1, tiled=True),
    )
    squares = sum((jnp.sum(piece_grad * piece_grad) for piece_grad in shard_grads))
    total_squares = lax.psum(squares, ("dp", "seq"))
    grad_norm = jnp.sqrt(total_squares)
    clip_factor = jnp.minimum(1.0, CLIP_NORM / grad_norm)
    masters = (w_qkv, w_out, w_up, w_down, embed, head, gains)
    firsts = (mom_qkv, mom_out, mom_up, mom_down, mom_embed, mom_head, mom_gains)
    seconds = (sec_qkv, sec_out, sec_up, sec_down, sec_embed, sec_head, sec_gains)
    results = []
    for slot_index in range(7):
        results.append(
            adam_update(
                masters[slot_index],
                shard_grads[slot_index] * clip_factor,
                firsts[slot_index],
                seconds[slot_index],
                STEP_RATES[slot_index],
                WEIGHT_DECAYS[slot_index],
            )
        )
    return (
        loss_sum,
        grad_norm,
        results[0][0],
        results[1][0],
        results[2][0],
        results[3][0],
        results[4][0],
        results[5][0],
        results[6][0],
        results[0][1],
        results[1][1],
        results[2][1],
        results[3][1],
        results[4][1],
        results[5][1],
        results[6][1],
        results[0][2],
        results[1][2],
        results[2][2],
        results[3][2],
        results[4][2],
        results[5][2],
        results[6][2],
    )


LOW = jnp.bfloat16
F32 = jnp.float32
MESH = pl.DeviceIdType.MESH
D = 512

EG, LAYER0, LAYER_ROWS = 0, -32, 192
QKV, OUT, UP, DOWN = 0, 48, 64, 128
HEAD = LAYER0 + 2 * LAYER_ROWS
ROWS = HEAD + 16
PIECES = {
    "A": (0, 16, 16),
    "B": (16, 32, 64),
    "E": (64, 80, 96),
    "b": (96, 128, 160),
    "C": (160, 192, 224),
    "D": (224, 256, 288),
    "d": (288, 320, 336),
    "h": (336, 352, 368),
}
Z_LAST, Z_FIRST = "h", "h"
SCHEDULE = {
    "start": "BAbhBEAh",
    "heads": "dBAEbBCE",
    "f0_heads": "DAb",
    "f0_mid0": "C",
    "f0_part0": "dE",
    "f0_part1": "Cbh",
    "f0_home": "D",
    "f0_rim": "dC",
    "f1_sent": "D",
    "f1_got": "dh",
    "f1_part0": "D",
    "b1_ff": "d",
    "b1_sent": "dD",
    "b1_sums": "hDhd",
    "b1_rim": "CDC",
    "b0_ff": "BDB",
    "b0_sent": "bCEd",
    "b0_mid1": "E",
    "b0_part1": "B",
    "b0_keys1": "b",
    "b0_mid0": "C",
    "b0_part0": "h",
    "b0_keys0": "B",
    "b0_end": "E",
    "tail": "AbAEbh",
}


def dot(a, b):
    return jnp.dot(a, b, preferred_element_type=F32)


def dot_nt(a, b):
    return lax.dot_general(a, b, (((1,), (1,)), ((), ())), preferred_element_type=F32)


def dot_tn(a, b):
    return lax.dot_general(a, b, (((0,), (0,)), ((), ())), preferred_element_type=F32)


def low(v):
    return v.astype(LOW)


exact = functools.partial(jnp.dot, preferred_element_type=F32, precision=lax.Precision.HIGHEST)


def lanes(shape):
    return lax.broadcasted_iota(jnp.int32, shape, len(shape) - 1)


def roll64(v):
    return pltpu.roll(v, 64, 1)


def swap32(v):
    return jnp.where(lanes(v.shape) % 64 < 32, pltpu.roll(v, 96, 1), pltpu.roll(v, 32, 1))


def norm_parts(v):
    center = v - jnp.mean(v, axis=-1, keepdims=True)
    scale = lax.rsqrt(jnp.mean(center * center, axis=-1, keepdims=True) + NORM_EPS)
    return center * scale, scale


def norm_back(v, gain, grad):
    unit, scale = norm_parts(v)
    g = grad * gain
    out = scale * (g - jnp.mean(g, axis=-1, keepdims=True) - unit * jnp.mean(g * unit, axis=-1, keepdims=True))
    return out, jnp.sum(grad * unit, axis=0, keepdims=True)


GELU_A, GELU_B = 0.7978845608028654, 0.044715


def gelu(v):
    return 0.5 * v * (1.0 + jnp.tanh(GELU_A * (v + GELU_B * v * v * v)))


def gelu_grad(v):
    t = jnp.tanh(GELU_A * (v + GELU_B * v * v * v))
    return 0.5 * (1.0 + t) + 0.5 * v * (1.0 - t * t) * (GELU_A * (1.0 + 3.0 * GELU_B * v * v))


class Bag:
    pass


def scope(name):
    return contextlib.nullcontext()


def remote(src, dst, send, recv, device):
    return pltpu.make_async_remote_copy(
        src_ref=src, dst_ref=dst, send_sem=send, recv_sem=recv, device_id=device, device_id_type=MESH
    )


def pack_pair(block, odd):
    half = block.shape[0] // 2
    top, bottom = block[:half], block[half:]
    if odd:
        top = roll64(top)
    else:
        bottom = roll64(bottom)
    return jnp.where(lanes(top.shape) < 64, top, bottom)


def unpack_pair(even, odd):
    left = lanes(even.shape) < 64
    top = jnp.where(left, even, roll64(odd))
    bottom = jnp.where(left, roll64(even), odd)
    return jnp.concatenate([top, bottom], axis=0)


def unpack_left(x):
    left = lanes(x.shape) < 64
    return jnp.concatenate([jnp.where(left, x, 0.0), jnp.where(left, roll64(x), 0.0)], axis=0)


def unpack_right(x):
    left = lanes(x.shape) < 64
    return jnp.concatenate([jnp.where(left, 0.0, roll64(x)), jnp.where(left, 0.0, x)], axis=0)


def pack_left(x):
    half = x.shape[0] // 2
    return jnp.where(lanes((half, 128)) < 64, x[:half], roll64(x[half:]))


def pack_right(x):
    half = x.shape[0] // 2
    return jnp.where(lanes((half, 128)) < 64, roll64(x[:half]), x[half:])


def kernel(*refs):
    k = Bag()
    names = IN_NAMES + OUT_NAMES + tuple(SCRATCH)
    for name, ref in zip(names, refs[:-1]):
        setattr(k, name, ref)
    k.sems = refs[-1]
    for name in PER_LAYER:
        setattr(k, name, [getattr(k, name + "0", None), getattr(k, name + "1")])
    k.hold = []
    for layer in range(2):
        hold = Bag()
        for name in HELD:
            setattr(hold, name, getattr(k, "h_" + name + str(layer), None))
        k.hold.append(hold)
    g = lax.axis_index("dp")
    s = lax.axis_index("seq")
    z, y, x = s // 4, lax.rem(s // 2, 2), lax.rem(s, 2)
    k.g, k.s, k.z, k.y, k.x = g, s, z, y, x
    k.side = lax.rem(x + y, 2)
    k.cursor = 0

    def dev(g, z, y, x):
        return (g, z * 4 + y * 2 + x)

    k.dev = dev

    barrier = pltpu.get_barrier_semaphore()
    me = g * 16 + s

    @pl.loop(1, 32)
    def _(i):
        t = lax.rem(me + i, 32)
        pl.semaphore_signal(barrier, inc=1, device_id=(t // 16, lax.rem(t, 16)), device_id_type=MESH)

    own = k.pk.at[g, z, y, x]
    own[EG : EG + 16, 0:256] = low(jnp.concatenate([k.embed[:, 0:256], k.embed[:, 256:512]], axis=0))
    place = lanes((16, 256)) - 16 * s == lax.broadcasted_iota(jnp.int32, (16, 256), 0)
    gains = exact(k.gains[...], jnp.where(place, 1.0, 0.0))
    gains = jnp.concatenate([gains, jnp.zeros((3, 256), F32)], axis=0)
    gains = jnp.concatenate([jnp.where(g == 0, gains, 0.0), jnp.where(g == 1, gains, 0.0)], axis=0)
    own[EG : EG + 16, 256:512] = low(gains)
    k.columns[0:1, 0:144] = k.ids[...].astype(F32)
    k.columns[1:2, 0:144] = k.targets[...].astype(F32)
    pack_heads(k)
    pack_layer(k, own, 0)
    pack_layer(k, own, 1)
    own[HEAD : HEAD + 16, 0:256] = low(k.head[...])
    own[HEAD : HEAD + 16, 256:512] = jnp.zeros((16, 256), LOW)
    with scope("barrier"):
        pl.semaphore_wait(barrier, 31)
    k.gathers = {name: gather_piece(k, name, *rows) for name, rows in PIECES.items()}
    k.reduces = {name: reduce_piece(k, name, *rows) for name, rows in PIECES.items()}
    k.made, k.summed, k.stored = set(), set(), set()
    k.flushed, k.sq = [], jnp.zeros((1, 1), F32)
    point(k, "start")
    spread_heads(k)
    point(k, "heads")
    forward_backward(k)
    finish_grads(k)


def point(k, name):
    coming = name[0] in "sphf"
    for piece in SCHEDULE.get(name, ""):
        next((k.gathers if coming else k.reduces)[piece], None)
        if not coming:
            store_ready(k)


def touching(rows):
    return [name for name, (r0, _, r1) in PIECES.items() if r0 < rows.stop and r1 > rows.start]


def pair_kv(keys, vals):
    left = lanes(keys.shape) < 64
    return jnp.where(left, keys, roll64(vals)), jnp.where(left, roll64(keys), vals)


def pack_heads(k):
    row, lane = lax.broadcasted_iota(jnp.int32, (16, 128), 0), lanes((16, 128))
    ids = jnp.zeros((16, 128), F32)
    for j in range(3):
        part = pltpu.roll(k.columns[0:8, :], (64 - 48 * j) % 256, 1)[0:1, 0:128]
        ids = jnp.where((row == j) & (lane >= 64) & (lane < 112), part, ids)
    for pair in range(4):
        query = k.w_qkv[0, :, 128 * pair : 128 * pair + 128]
        keys = k.w_qkv[0, :, 512 + 128 * pair : 640 + 128 * pair]
        vals = k.w_qkv[0, :, 1024 + 128 * pair : 1152 + 128 * pair]
        for odd, kv in enumerate(pair_kv(keys, vals)):
            k.headout[2 * pair + odd, :, 0:128] = low(jnp.where(lane < 64, roll64(query) if odd else query, ids))
            k.headout[2 * pair + odd, :, 128:256] = low(kv)


def around(k, source, target, sent, got):
    for n in range(1, 16):
        c = lax.rem(k.s + n, 16)
        remote(source(c), target(k.s), sent, got, (k.g, c)).start()


def spread_heads(k):
    mine = k.g * 16 + k.s
    k.wbox[mine] = k.headout[lax.rem(k.s, 8)]
    k.head_sems = [sem(k), sem(k)]
    around(k, lambda c: k.headout.at[lax.rem(c, 8)], lambda c: k.wbox.at[k.g * 16 + c], *k.head_sems)


def take_heads(k):
    with scope("heads"):
        for semaphore in k.head_sems:
            drain(semaphore, k.wbox.at[pl.ds(0, 15)])
    share = k.wbox.at[pl.ds(16 * k.g, 16)]
    return Stage(k, share, [(share, share, k.dev(1 - k.g, k.z, k.y, k.x))])


def block_tables(k, b):
    cos_b, sin_b = k.cosb[pl.ds(b, 1), :], k.sinb[pl.ds(b, 1), :]
    cos_r, sin_r = k.cos[0][...], k.sin[0][...]
    return cos_b * cos_r - sin_b * sin_r, sin_b * cos_r + cos_b * sin_r


def kv_tables(cosine, sine):
    left = lanes(cosine.shape) < 64
    return jnp.where(left, cosine, 1.0), jnp.where(left, sine, 0.0)


def byte_rows(k):
    need(k, EG)
    packed = k.pk[:, :, :, :, EG : EG + 16, :].astype(F32).reshape(32, 16, 512)
    gains = jnp.sum(packed[:, :, 256:512], axis=0)
    k.gain[:, 0:256] = gains[0:8]
    k.gain[:, 256:512] = gains[8:16]
    table = jnp.concatenate(
        [packed[:, 0:8, 0:256].reshape(256, 256), packed[:, 8:16, 0:256].reshape(256, 256)], axis=1
    )
    k.table[...] = table
    unit, _ = norm_parts(table)
    k.normed[...] = low(unit * k.gain[0:1, :])


def head_rows(k):
    group = k.s // 8
    for b in range(16):
        k.columns[16 + 4 * b : 20 + 4 * b, 0:128] = k.wbox[group * 16 + b].astype(F32)[0:4, 0:128]
    columns = k.columns[...].T
    weights = k.wbox[...].astype(F32).reshape(512, 256)
    lane = lanes(weights.shape)
    k.wh[...] = low(jnp.where((lane >= 64) & (lane < 128), 0.0, weights))
    joined = dot(k.normed[...], k.wh[...])
    high = low(joined)
    rest = low(joined - high.astype(F32))
    for b in range(16):
        ids = [columns[64:112, 16 + 4 * b + j : 17 + 4 * b + j] for j in range(3)]
        hot = byte_matrix(jnp.concatenate(ids, axis=0).astype(jnp.int32))
        k.hot[b] = hot
        rows = dot(hot, high) + dot(hot, rest)
        cosine, sine = block_tables(k, b)
        k.q0[b] = low(rotate_block(rows[:, 0:128], cosine, sine) * 0.125)
        k.kv0[b] = low(rotate_block(rows[:, 128:256], *kv_tables(cosine, sine)))


def pack_layer(k, own, layer):
    base = LAYER0 + layer * LAYER_ROWS
    if layer == 1:
        own[base + QKV : base + QKV + 16, :] = low(k.w_qkv[layer, :, 0:512])
        for pair in range(4):
            keys = k.w_qkv[layer, :, 512 + 128 * pair : 640 + 128 * pair]
            vals = k.w_qkv[layer, :, 1024 + 128 * pair : 1152 + 128 * pair]
            row = base + QKV + 16 + 16 * (pair // 2)
            for odd, kv in enumerate(pair_kv(keys, vals)):
                col = 256 * (pair % 2) + 128 * odd
                own[row : row + 16, col : col + 128] = low(kv)
    own[base + OUT : base + OUT + 16, :] = low(k.w_out[layer])
    for j in range(4):
        own[base + UP + 16 * j : base + UP + 16 * j + 16, :] = low(k.w_up[layer, :, 512 * j : 512 * j + 512])
    own[base + DOWN : base + DOWN + 64, :] = low(k.w_down[layer])


def sem(k):
    k.cursor += 1
    assert k.cursor <= SEMS
    return k.sems.at[k.cursor - 1]


def start_all(copies):
    for copy in copies:
        copy.start()


def wait_all(copies):
    for copy in copies:
        copy.wait()


def drain(semaphore, ref):
    pltpu.make_async_copy(ref, ref, semaphore).wait()


class Stage:
    def __init__(self, k, total, moves, sent=None):
        self.total, self.sent, self.got = total, sem(k) if sent is None else sent, sem(k)
        start_all([remote(src, dst, self.sent, self.got, device) for src, dst, device in moves if src.shape[-2]])

    def wait(self):
        drain(self.got, self.total)
        drain(self.sent, self.total)


def gather_piece(k, name, r0, rm, r1):
    g, z, y, x, dev, pk = k.g, k.z, k.y, k.x, k.dev, k.pk
    a, b, every = pl.ds(r0, rm - r0), pl.ds(rm, r1 - rm), pl.ds(r0, r1 - r0)

    sent = sem(k)

    def stage(total, *moves):
        return Stage(k, total, [(ref, ref, device) for ref, device in moves], sent)

    def wait(waiting):
        with scope(f"gw_{name}"):
            waiting.wait()

    planes = pl.ds(z, 1) if name in Z_LAST else pl.ds(0, 4)

    def across():
        waiting = stage(
            pk.at[g, planes, y, x, every],
            (pk.at[g, planes, y, x, a], dev(g, z, 1 - y, x)),
            (pk.at[g, planes, y, x, b], dev(g, z, y, 1 - x)),
        )
        yield
        wait(waiting)
        waiting = stage(
            pk.at[g, planes, :, x, every],
            (pk.at[g, planes, :, x, a], dev(g, z, y, 1 - x)),
            (pk.at[g, planes, y, :, b], dev(g, z, 1 - y, x)),
        )
        yield
        wait(waiting)

    def along():
        def part(n):
            return pk.at[g, n, :, :, every] if name in Z_LAST else pk.at[g, n, y, x, every]

        waiting = stage(part(pl.ds(0, 3)), *[(part(z), dev(g, lax.rem(z + n, 4), y, x)) for n in (2, 1, 3)])
        yield
        wait(waiting)

    for way in (across, along) if name in Z_LAST else (along, across):
        yield from way()
    waiting = stage(pk.at[1 - g, :, :, :, every], (pk.at[g, :, :, :, every], dev(1 - g, z, y, x)))
    yield
    wait(waiting)
    yield


def need(k, row, count=16):
    for name in touching(range(row, row + count)):
        for _ in k.gathers[name]:
            pass


def block(k, row):
    need(k, row)
    return k.pk[:, :, :, :, row : row + 16, :].reshape(512, 512)


def put_block(k, row, value):
    k.made.add(row)
    k.gr[:, :, :, :, row : row + 16, :] = low(value).reshape(2, 4, 2, 2, 16, 512)


def down_block(k, row, c):
    need(k, row, 64)
    return k.pk[c // 2, (c % 2) * 2 : (c % 2) * 2 + 2, :, :, row : row + 64, :].reshape(512, 512)


def put_down(k, row, c, value):
    if c == 3:
        k.made.update(range(row, row + 64, 16))
    k.gr[c // 2, (c % 2) * 2 : (c % 2) * 2 + 2, :, :, row : row + 64, :] = low(value).reshape(2, 2, 2, 64, 512)


def my_blocks(k):
    return [4 * j + (k.g if half == 0 else 3 - k.g) for j in range(4) for half in range(2)]


def other_blocks(k):
    return [4 * j + (1 - k.g if half == 0 else 2 + k.g) for j in range(4) for half in range(2)]


def my_block(k, i):
    return 4 * (i // 2) + jnp.where(lax.rem(i, 2) == 0, k.g, 3 - k.g)


class Post:
    def __init__(self, k, source, groups):
        self.k, self.source = k, source
        self.sent, self.got = sem(k), [sem(k) for _ in range(groups)]

    def start(self, src, dst, got, device):
        k = self.k
        is_self = jnp.logical_and(device[0] == k.g, device[1] == k.s)

        @pl.when(is_self)
        def _():
            pltpu.make_async_copy(src, dst, got).start()

        @pl.when(jnp.logical_not(is_self))
        def _():
            remote(src, dst, self.sent, got, device).start()

    def finish(self, one_is_self):
        @pl.when(one_is_self)
        def _():
            drain(self.sent, self.source.at[pl.ds(0, 7)])

        @pl.when(jnp.logical_not(one_is_self))
        def _():
            drain(self.sent, self.source)


class ToHeads(Post):
    def __init__(self, k, source, target):
        super().__init__(k, source, 2)
        self.target = target

    def send(self):
        k = self.k
        for part in range(2):

            @pl.when(k.s // 8 == part)
            def _():
                for i in range(8):
                    h = lax.rem(k.s + i, 8)
                    self.start(self.source.at[h], self.target.at[k.s], self.got[part], (k.side, k.g * 8 + h))

    def take(self, part):
        drain(self.got[part], self.target.at[pl.ds(0, 4)])

    def done(self):
        k = self.k
        self.finish(jnp.logical_and(k.s // 8 == k.g, k.side == k.g))


class FromHeads(Post):
    def __init__(self, k, source, target):
        super().__init__(k, source, 1)
        self.target = target

    def send(self, i, b):
        k = self.k
        head = lax.rem(k.s, 8)
        self.start(self.source.at[i], self.target.at[head], self.got[0], (k.s // 8, b))

    def take(self):
        drain(self.got[0], self.target)

    def done(self):
        k = self.k
        self.finish(jnp.logical_and(k.s // 8 == k.g, k.side == k.g))


def rotate_block(v, cosine, sine):
    return v * cosine + swap32(v) * sine


def rotary_tables(k):
    lane = lanes((1, 128))
    freqs = jnp.zeros((1, 128), F32)
    for i in range(32):
        freqs = jnp.where(lane % 32 == i, 10000.0 ** (-i / 32), freqs)
    sign = jnp.where(lane % 64 < 32, -1.0, 1.0)
    rows, short = layer_sizes(0)[0], layer_sizes(1)[0]
    for cos, sin, count, first, step in (
        (k.cos[0], k.sin[0], rows, 0, 1),
        (k.cosb, k.sinb, 16, 0, rows),
        (k.cos[1], k.sin[1], short, k.s * short, 1),
    ):
        angles = (first + step * lax.broadcasted_iota(jnp.int32, (count, 1), 0)).astype(F32) * freqs
        cos[...] = jnp.cos(angles)
        sin[...] = jnp.sin(angles) * sign


def layer_sizes(layer):
    rows = 144 if layer == 0 else 48
    return rows, (rows // 2 + 15) // 16 * 16


def attend_loop(layer, part, body, between=None):
    if layer == 1:
        body(list(range(8)), 16)
        return
    for first in (0, 2):
        @pl.loop(first, first + 2)
        def _(n):
            body([part * 4 + n], 8 * part + 4 + 2 * first)

        if between is not None and first == 0:
            between()


def stack(pieces):
    return pieces[0] if len(pieces) == 1 else jnp.concatenate(pieces, axis=0)


def masked_scores(q, kv, places, plain):
    scores = dot_nt(q, kv)
    plain = plain // 128 * 128
    rest = scores[:, plain:]
    rest = jnp.where(lanes(rest.shape) + plain <= places, rest, MASK_FILL)
    return jnp.concatenate([scores[:, :plain], rest], axis=1) if plain else rest


def stacked_queries(k, layer, items):
    rows, pad = layer_sizes(layer)
    blocks = [my_block(k, i) for i in items]
    places = stack([b * rows + lax.broadcasted_iota(jnp.int32, (rows, 1), 0) for b in blocks])
    if layer == 0:
        return stack([k.q0[b] for b in blocks]), blocks, places
    q = stack([unpack_left(k.inbox[layer][b, 0:pad, :].astype(F32)[: rows // 2]) for b in blocks])
    return low(q * 0.125), blocks, places


def stacked_keys(k, layer, count):
    rows, pad = layer_sizes(layer)
    if layer == 0:
        return k.kv0[0:count].reshape(count * rows, 128)
    return k.inbox[layer][0:count, pad : pad + rows, :].reshape(count * rows, 128)


def attention_forward(k, layer, part, post, between):
    rows, pad = layer_sizes(layer)
    outbox, lse, keep = k.abox[layer], k.lse[layer], k.att[layer]

    def body(items, count):
        q, blocks, places = stacked_queries(k, layer, items)
        kv = stacked_keys(k, layer, count)
        scores = masked_scores(q, kv, places, 0 if layer == 1 else (count - 4) * rows)
        top = jnp.max(scores, axis=-1, keepdims=True)
        prob = jnp.exp(scores - top)
        total = jnp.sum(prob, axis=-1, keepdims=True)
        out = dot(low(prob), kv) / total
        stat = jnp.broadcast_to(top + jnp.log(total), out.shape)
        for n, (i, b) in enumerate(zip(items, blocks)):
            span = slice(n * rows, (n + 1) * rows)
            lse[i] = stat[span]
            keep[i] = out[span]
            outbox[i, 0 : rows // 2, :] = low(pack_right(out[span]))
            post.send(i, b)

    attend_loop(layer, part, body, between)


def attention_backward(k, layer, part, post, between=None):
    rows, pad = layer_sizes(layer)
    gradbox, lse, keep = k.gbox[layer], k.lse[layer], k.att[layer]
    dkvt, outbox = k.dkvt[layer], k.dbox[layer]

    def body(items, count):
        q, blocks, places = stacked_queries(k, layer, items)
        kv = stacked_keys(k, layer, count)
        grad = stack([unpack_right(gradbox[b].astype(F32)[: rows // 2]) for b in blocks])
        delta = jnp.sum(grad * stack([keep[i] for i in items]), axis=-1, keepdims=True)
        grad = low(grad)
        prob = jnp.exp(masked_scores(q, kv, places, 0 if layer == 1 else (count - 4) * rows) - stack([lse[i] for i in items])[:, 0:1])
        grad_prob = dot_nt(grad, kv)
        ds = low(prob * (grad_prob - delta))
        dq = dot(ds, kv) * 0.125
        if layer == 0:
            cosine, sine = block_tables(k, blocks[0])
            dq = rotate_block(jnp.where(lanes(dq.shape) < 64, dq, 0.0), cosine, -sine)
            k.gbytes[:, 0:128] += dot_tn(k.hot[blocks[0]], low(dq))
        for n, (i, b) in enumerate(zip(items, blocks) if layer == 1 else ()):
            outbox[i, 0 : rows // 2, :] = low(pack_left(dq[n * rows : (n + 1) * rows]))
            post.send(i, b)
        dkvt[:, 0 : count * rows] += dot_tn(q, ds) + dot_tn(grad, low(prob))

    attend_loop(layer, part, body, between)


class KeySums:
    def __init__(self, k, layer, part, post):
        rows, _ = layer_sizes(layer)
        self.k, self.layer, self.post = k, layer, post
        self.items = range(8) if layer == 1 else range(4 * part, 4 * part + 4)
        first, count = (0, 16) if layer == 1 else (8 * part, 8)
        k.dkv[layer][first : first + count] = (
            k.dkvt[layer][:, first * rows : (first + count) * rows].T.reshape(count, rows, 128)
        )
        others = other_blocks(k)
        for i in self.items:
            k.dkv_out[layer][i] = k.dkv[layer][others[i]]
        span = pl.ds(self.items[0], len(self.items))
        self.copy = Stage(
            k,
            k.dkv_in[layer].at[span],
            [(k.dkv_out[layer].at[span], k.dkv_in[layer].at[span], k.dev(1 - k.g, k.z, k.y, k.x))],
        )

    def send(self):
        k, layer = self.k, self.layer
        self.copy.wait()
        mine = my_blocks(k)
        for i in self.items:
            k.kvbox[layer][i] = low(k.dkv[layer][mine[i]] + k.dkv_in[layer][i])
            self.post.send(i, mine[i])


def send_rows(k, hidden):
    layer = 1
    rows, pad = layer_sizes(layer)
    base = LAYER0 + layer * LAYER_ROWS
    unit, _ = norm_parts(hidden)
    normed = low(unit * k.gain[2 * layer : 2 * layer + 1, :])
    k.hold[layer].normed[...] = normed
    cosine, sine = k.cos[layer][...], k.sin[layer][...]
    cos_kv, sin_kv = kv_tables(cosine, sine)
    sendbox = k.sendbox[layer]
    for part in range(3):
        joined = dot(normed, block(k, base + QKV + 16 * part))
        for n in range(4):
            piece = joined[:, 128 * n : 128 * n + 128]
            if part == 0:
                piece = rotate_block(piece, cosine, sine)
                sendbox[2 * n, 0 : rows // 2, :] = low(pack_pair(piece, 0))
                sendbox[2 * n + 1, 0 : rows // 2, :] = low(pack_pair(piece, 1))
            else:
                sendbox[4 * part - 4 + n, pad : pad + rows, :] = low(rotate_block(piece, cos_kv, sin_kv))
    inbox = k.inbox[layer]
    out = ToHeads(k, sendbox, inbox)
    out.send()
    point(k, "f1_sent")
    sent, shared = sem(k), [sem(k), sem(k)]
    mine = my_blocks(k)
    for part in range(2):
        if part == 1:
            point(k, "f1_take")
        with scope("take"):
            out.take(part)
        for b in mine[4 * part : 4 * part + 4]:
            ref = inbox.at[b, pl.ds(pad, rows)]
            remote(ref, ref, sent, shared[part], k.dev(1 - k.g, k.z, k.y, k.x)).start()
    point(k, "f1_got")
    k.pending += [out.done, lambda: drain(sent, inbox.at[pl.ds(0, 8), pl.ds(pad, rows)])]
    return shared


def layer_ahead(k, layer, hidden):
    rows, pad = layer_sizes(layer)
    base = LAYER0 + layer * LAYER_ROWS
    hold = k.hold[layer]
    home = k.home[layer]
    if layer == 0:
        point(k, "f0_got")
        shared = []
    else:
        hold.hidden[...] = hidden
        shared = send_rows(k, hidden)
    back = FromHeads(k, k.abox[layer], home)
    for part in range(2 - layer):
        for semaphore in shared:
            with scope("share"):
                drain(semaphore, k.inbox[layer].at[pl.ds(0, 4), pl.ds(pad, rows)])
        with scope("attend"):
            attention_forward(k, layer, part, back, lambda: point(k, f"f0_mid{part}"))
        point(k, f"f{layer}_part{part}")
    with scope("home"):
        back.take()
    point(k, f"f{layer}_home")
    if layer == 1:
        point(k, "f1_out")
    for n in range(4):
        pair = unpack_pair(
            home[2 * n].astype(F32)[: rows // 2], home[2 * n + 1].astype(F32)[: rows // 2]
        )
        hold.flat[:, 128 * n : 128 * n + 128] = low(pair)
    middle = hidden + dot(hold.flat[...], block(k, base + OUT))
    hold.middle[...] = middle
    unit, _ = norm_parts(middle)
    second = low(unit * k.gain[2 * layer + 1 : 2 * layer + 2, :])
    hold.second[...] = second
    for j in range(4):
        pre = dot(second, block(k, base + UP + 16 * j))
        hold.pre[:, 512 * j : 512 * j + 512] = pre
        hold.act[:, 512 * j : 512 * j + 512] = low(gelu(pre))
    point(k, f"f{layer}_up")
    need(k, base + DOWN, 64)
    falls = k.pk[:, :, :, :, base + DOWN : base + DOWN + 64, :].reshape(2048, 512)
    output = hold.middle[...] + dot(hold.act[...], falls)
    back.done()
    for done in k.pending:
        done()
    k.pending = []
    return output


def layer_back(k, layer, grad_out):
    rows, pad = layer_sizes(layer)
    base = LAYER0 + layer * LAYER_ROWS
    hold = k.hold[layer]
    fall = low(grad_out)
    grad_second = jnp.zeros((rows, D), F32)
    second = hold.second[...]
    for c in range(4):
        cols = slice(512 * c, 512 * c + 512)
        if layer == 1:
            put_down(k, base + DOWN, c, dot_tn(hold.act[:, cols], fall))
        grad_act = dot_nt(fall, down_block(k, base + DOWN, c))
        grad_pre = low(grad_act * gelu_grad(hold.pre[:, cols]))
        if layer == 1:
            put_block(k, base + UP + 16 * c, dot_tn(second, grad_pre))
        else:
            hold.gpre[:, cols] = grad_pre
        grad_second = grad_second + dot_nt(grad_pre, block(k, base + UP + 16 * c))
    if layer == 1:
        point(k, "b1_ff")
    gain = k.gain[2 * layer + 1 : 2 * layer + 2, :]
    grad_mid, k.gain_grads[2 * layer + 1] = norm_back(hold.middle[...], gain, grad_second)
    grad_middle = grad_out + grad_mid
    hold.middle[...] = grad_middle
    proj = low(grad_middle)
    if layer == 1:
        put_block(k, base + OUT, dot_tn(hold.flat[...], proj))
    grad_att = dot_nt(proj, block(k, base + OUT))
    gsend = k.gsend[layer]
    for n in range(4):
        piece = grad_att[:, 128 * n : 128 * n + 128]
        gsend[2 * n, 0 : rows // 2, :] = low(pack_pair(piece, 0))
        gsend[2 * n + 1, 0 : rows // 2, :] = low(pack_pair(piece, 1))
    out = ToHeads(k, gsend, k.gbox[layer])
    out.send()
    if layer == 0:
        put_block(k, base + OUT, dot_tn(hold.flat[...], proj))
        for c in range(4):
            cols = slice(512 * c, 512 * c + 512)
            put_down(k, base + DOWN, c, dot_tn(hold.act[:, cols], fall))
            put_block(k, base + UP + 16 * c, dot_tn(second, hold.gpre[:, cols]))
        point(k, "b0_ff")
    k.dkvt[layer][...] = jnp.zeros_like(k.dkvt[layer])
    point(k, f"b{layer}_sent")
    if layer == 0:
        return head_grads(k, out)
    back = k.back[layer]
    home_q = FromHeads(k, k.dbox[layer], back)
    home_kv = FromHeads(k, k.kvbox[layer], k.kvback[layer])
    with scope("take"):
        out.take(0)
        out.take(1)
    with scope("unattend"):
        attention_backward(k, layer, 0, home_q)
    sums = KeySums(k, layer, 0, home_kv)
    point(k, "b1_part0")
    with scope("sums"):
        sums.send()
    point(k, "b1_sums")
    with scope("home_q"):
        home_q.take()
    cosine, sine = k.cos[layer][...], k.sin[layer][...]
    cos_kv, sin_kv = kv_tables(cosine, sine)
    for part in range(3):
        if part == 1:
            with scope("home_kv"):
                home_kv.take()
            point(k, "b1_home")
        for n in range(4):
            if part == 0:
                piece = unpack_pair(
                    back[2 * n].astype(F32)[: rows // 2],
                    back[2 * n + 1].astype(F32)[: rows // 2],
                )
                piece = rotate_block(piece, cosine, -sine)
            else:
                piece = k.kvback[layer][4 * part - 4 + n].astype(F32)
                piece = rotate_block(piece, cos_kv, -sin_kv)
            hold.gj[:, 512 * part + 128 * n : 512 * part + 128 * n + 128] = low(piece)
    grad_normed = jnp.zeros((rows, D), F32)
    for part in range(3):
        gj = hold.gj[:, 512 * part : 512 * part + 512]
        grad_normed = grad_normed + dot_nt(gj, block(k, base + QKV + 16 * part))
    gain = k.gain[2 * layer : 2 * layer + 1, :]
    grad_in, k.gain_grads[2 * layer] = norm_back(hold.hidden[...], gain, grad_normed)
    return hold.middle[...] + grad_in, (out, home_q, home_kv)


def head_grads(k, out):
    own = dot_tn(byte_matrix(k.own_ids), low(k.hold[0].middle[...]))
    k.tgrad[...] = own
    k.gbytes[...] = jnp.zeros_like(k.gbytes)
    for part in (1, 0):
        with scope("take"):
            out.take(part)
        with scope("unattend"):
            attention_backward(k, 0, part, None, lambda: point(k, f"b0_mid{part}"))
        point(k, f"b0_part{part}")
        with scope("keysums"):
            sums = k.dkvt[0][:, 1152 * part : 1152 * part + 1152].T
            for i in range(8):
                cosine, sine = kv_tables(*block_tables(k, 8 * part + i))
                k.gkv[144 * i : 144 * i + 144, :] = low(rotate_block(sums[144 * i : 144 * i + 144], cosine, -sine))
            k.gbytes[:, 128:256] += dot_tn(k.hot[8 * part : 8 * part + 8].reshape(1152, 256), k.gkv[...])
        point(k, f"b0_keys{part}")
    gbytes = low(k.gbytes[...])
    k.headgrad[...] = low(dot_tn(k.normed[...], gbytes)).reshape(32, 16, 256)
    stage = Stage(
        k,
        k.headgot,
        [(k.headgrad.at[pl.ds(16 * (1 - k.g), 16)], k.headgot, k.dev(1 - k.g, k.z, k.y, k.x))],
    )
    grad, k.gain_grads[0] = norm_back(k.table[...], k.gain[0:1, :], dot_nt(gbytes, k.wh[...]))
    total = k.tgrad[...] + grad
    total = jnp.concatenate([total[:, 0:256].reshape(32, 8, 256), total[:, 256:512].reshape(32, 8, 256)], axis=1)
    k.gr[:, :, :, :, EG : EG + 16, 0:256] = low(total).reshape(2, 4, 2, 2, 16, 256)
    return stage, (out,)


def send_head_grads(k, stage):
    with scope("headcore"):
        stage.wait()
    total = k.headgrad[pl.ds(16 * k.g, 16)].astype(F32) + k.headgot[...].astype(F32)
    k.headsum[...] = low(total)
    k.headback[k.s] = k.headsum[k.s]
    k.head_sems = [sem(k), sem(k)]
    around(k, lambda c: k.headsum.at[c], lambda c: k.headback.at[c], *k.head_sems)


def store_heads(k):
    with scope("headback"):
        for semaphore in k.head_sems:
            drain(semaphore, k.headback.at[pl.ds(0, 15)])
    for pair in range(4):
        even, odd = (k.headback[h].astype(F32) + k.headback[8 + h].astype(F32) for h in (2 * pair, 2 * pair + 1))
        left = lanes((16, 128)) < 64
        query = jnp.where(left, even[:, 0:128], roll64(odd[:, 0:128]))
        keys, vals = pair_kv(even[:, 128:256], odd[:, 128:256])
        for at, value in ((0, query), (512, keys), (1024, vals)):
            square(k, value)
            k.s_qkv[0, :, at + 128 * pair : at + 128 * pair + 128] = value
    flush(k, "qkv", 0)


def finish_back(k, posts):
    for post in posts:
        post.done()


def byte_matrix(ids):
    return low(jnp.where(lanes((ids.shape[0], 256)) == ids, 1.0, 0.0))


def forward_backward(k):
    rows, short = 144, 48
    k.gain_grads, k.pending = [None] * 5, []
    rotary_tables(k)
    stage = take_heads(k)
    point(k, "f0_heads")
    byte_rows(k)
    with scope("headcore"):
        stage.wait()
    with scope("headrows"):
        head_rows(k)
    columns = k.columns[...].T
    k.own_ids, targets = columns[0:rows, 0:1].astype(jnp.int32), columns[0:rows, 1:2].astype(jnp.int32)
    first_in = dot(byte_matrix(k.own_ids), low(k.table[...]))
    first = layer_ahead(k, 0, first_in)
    k.shift[8 : 8 + rows, :] = first
    rim = remote(
        k.shift.at[pl.ds(rows, 8)], k.shift.at[pl.ds(0, 8)], sem(k), sem(k), (k.g, lax.rem(k.s + 1, 16))
    )

    @pl.when(k.s < 15)
    def _():
        rim.start()

    point(k, "f0_rim")

    @pl.when(k.s > 0)
    def _():
        rim.wait_recv()

    @pl.when(k.s == 0)
    def _():
        k.shift[0:8, :] = jnp.zeros((8, D), F32)

    @pl.when(k.s < 15)
    def _():
        rim.wait_send()

    def pool_matrix(shape, offset, axis):
        j = lax.broadcasted_iota(jnp.int32, shape, axis)
        t = lax.broadcasted_iota(jnp.int32, shape, 1 - axis) - offset
        return jnp.where((t >= 3 * j) & (t < 3 * j + 3), 1.0, 0.0)

    pooled = exact(pool_matrix((short, rows + 8), 6, 0), k.shift[...]) / 3.0
    point(k, "f0_end")
    short_out = layer_ahead(k, 1, pooled)
    upsampled = k.shift[8 : 8 + rows, :] + exact(pool_matrix((rows, short), 0, 1), short_out)
    gain = k.gain[4:5, :]
    unit, _ = norm_parts(upsampled)
    final = low(unit * gain)
    need(k, HEAD)
    head = k.pk[:, :, :, :, HEAD : HEAD + 16, 0:256].reshape(512, 256)
    logits = dot(final, head)
    top = jnp.max(logits, axis=-1, keepdims=True)
    log_total = top + jnp.log(jnp.sum(jnp.exp(logits - top), axis=-1, keepdims=True))
    hot = jnp.where(lanes((rows, 256)) == targets, 1.0, 0.0)
    picked = jnp.sum(hot * logits, axis=-1, keepdims=True)
    position = k.s * rows + lax.broadcasted_iota(jnp.int32, (rows, 1), 0)
    length = jnp.zeros((rows, 1), F32)
    begin = jnp.int32(0)
    for i in range(8):
        size = k.lengths[0, i]
        inside = (position >= begin) & (position < begin + size)
        length = jnp.where(inside, size.astype(F32), length)
        begin = begin + size
    k.loss = jnp.sum((log_total - picked) / length, axis=0, keepdims=True)
    grad_logits = low((jnp.exp(logits - log_total) - hot) / length)
    k.gr[:, :, :, :, HEAD : HEAD + 16, 0:256] = low(dot_tn(final, grad_logits)).reshape(2, 4, 2, 2, 16, 256)
    k.made.add(HEAD)
    k.gr[:, :, :, :, HEAD : HEAD + 16, 256:512] = jnp.zeros((2, 4, 2, 2, 16, 256), LOW)
    grad_final = dot_nt(grad_logits, head)
    grad_up, k.gain_grads[4] = norm_back(upsampled, gain, grad_final)
    k.up[...] = grad_up
    grad_short = exact(pool_matrix((short, rows), 0, 0), grad_up)
    grad_pooled, posts = layer_back(k, 1, grad_short)
    k.pool[0:short, :] = grad_pooled
    rim2 = remote(
        k.pool.at[pl.ds(0, 8)], k.pool.at[pl.ds(short, 8)], sem(k), sem(k), (k.g, lax.rem(k.s + 15, 16))
    )

    @pl.when(k.s > 0)
    def _():
        rim2.start()

    for part in range(3):
        gj = k.hold[1].gj[:, 512 * part : 512 * part + 512]
        put_block(k, LAYER0 + LAYER_ROWS + QKV + 16 * part, dot_tn(k.hold[1].normed[...], gj))
    finish_back(k, posts)
    point(k, "b1_rim")

    @pl.when(k.s < 15)
    def _():
        rim2.wait_recv()

    @pl.when(k.s == 15)
    def _():
        k.pool[short : short + 8, :] = jnp.zeros((8, D), F32)

    @pl.when(k.s > 0)
    def _():
        rim2.wait_send()

    t = lax.broadcasted_iota(jnp.int32, (rows, short + 8), 0)
    j = lax.broadcasted_iota(jnp.int32, (rows, short + 8), 1)
    spread = jnp.where((t + 2 >= 3 * j) & (t + 2 < 3 * j + 3), 1.0, 0.0)
    grad_first = k.up[...] + exact(spread, k.pool[...] / 3.0)
    stage, posts = layer_back(k, 0, grad_first)
    fill = [jnp.zeros((3, 256), F32)]
    gains = jnp.concatenate(
        [v[:, 0:256] for v in k.gain_grads] + fill + [v[:, 256:512] for v in k.gain_grads] + fill, axis=0
    )
    gains = jnp.broadcast_to(low(gains)[None], (32, 16, 256))
    k.gr[:, :, :, :, EG : EG + 16, 256:512] = gains.reshape(2, 4, 2, 2, 16, 256)
    k.made.add(EG)
    point(k, "b0_end")
    send_head_grads(k, stage)
    finish_back(k, posts)


def add_into(ref, other):
    ref[...] = low(ref[...].astype(F32) + other[...].astype(F32))


def reduce_piece(k, name, r0, rm, r1):
    g, z, y, x, dev, gr = k.g, k.z, k.y, k.x, k.dev, k.gr
    a, b, every = pl.ds(r0, rm - r0), pl.ds(rm, r1 - rm), pl.ds(r0, r1 - r0)
    assert k.made.issuperset(range(r0, r1, 16)), name
    sent = sem(k)
    waiting = Stage(
        k, k.rc.at[:, :, :, every], [(gr.at[1 - g, :, :, :, every], k.rc.at[:, :, :, every], dev(1 - g, z, y, x))], sent
    )
    yield
    with scope(f"rw_{name}"):
        waiting.wait()

    with scope("radd"):

        @pl.loop(0, 16)
        def _(n):
            place = (n // 4, lax.rem(n // 2, 2), lax.rem(n, 2), every)
            add_into(gr.at[(g,) + place], k.rc.at[place])

    def wait(waiting):
        with scope(f"rw_{name}"):
            waiting.wait()

    last = name in Z_FIRST
    planes, depth = (pl.ds(z, 1), 1) if last else (pl.ds(0, 4), 4)
    slots = pl.ds(0, depth)

    def plane(n):
        return z if last else n

    def across():
        waiting = Stage(
            k,
            k.r2.at[slots, :, every],
            [
                (gr.at[g, planes, :, 1 - x, a], k.r2.at[slots, :, a], dev(g, z, y, 1 - x)),
                (gr.at[g, planes, 1 - y, :, b], k.r2.at[slots, :, b], dev(g, z, 1 - y, x)),
            ],
            sent,
        )
        yield
        wait(waiting)

        @pl.loop(0, 2 * depth)
        def _(n):
            m, w = n // 2, lax.rem(n, 2)
            add_into(gr.at[g, plane(m), w, x, a], k.r2.at[m, w, a])
            if r1 > rm:
                add_into(gr.at[g, plane(m), y, w, b], k.r2.at[m, w, b])

        waiting = Stage(
            k,
            k.r1.at[slots, every],
            [
                (gr.at[g, planes, 1 - y, x, a], k.r1.at[slots, a], dev(g, z, 1 - y, x)),
                (gr.at[g, planes, y, 1 - x, b], k.r1.at[slots, b], dev(g, z, y, 1 - x)),
            ],
            sent,
        )
        yield
        wait(waiting)

        @pl.loop(0, depth)
        def _(n):
            add_into(gr.at[g, plane(n), y, x, every], k.r1.at[n, every])

    def along():
        moves = []
        for n in (2, 1, 3):
            to = lax.rem(z + n, 4)
            if last:
                moves.append((gr.at[g, to, :, :, every], k.rl.at[n - 1], dev(g, to, y, x)))
            else:
                moves.append((gr.at[g, to, y, x, every], k.rz.at[n - 1, every], dev(g, to, y, x)))
        waiting = Stage(k, k.rl if last else k.rz.at[:, every], moves, sent)
        yield
        wait(waiting)
        if last:
            for n in range(4):
                ref = gr.at[g, z, n // 2, n % 2, every]
                total = ref[...].astype(F32)
                for slot in range(3):
                    total = total + k.rl[slot, n // 2, n % 2].astype(F32)
                ref[...] = low(total)

    for way in (along, across) if last else (across, along):
        yield from way()
    if last:
        k.rz[:, every] = jnp.zeros((3, r1 - r0, D), LOW)
    k.summed.update(range(r0, r1, 16))
    yield


def own_sum(k, row, count):
    rows = pl.ds(row, count)
    v = k.gr[k.g, k.z, k.y, k.x, rows].astype(F32)
    for i in range(3):
        v = v + k.rz[i, rows].astype(F32)
    return v


def square(k, v):
    k.sq = k.sq + jnp.sum(jnp.sum(v * v, axis=1, keepdims=True), axis=0, keepdims=True)


def flush(k, name, layer=None):
    src, dst = getattr(k, "s_" + name), getattr(k, "g_" + name)
    if layer is not None:
        src, dst = src.at[layer], dst.at[layer]
    copy = pltpu.make_async_copy(src, dst, sem(k))
    copy.start()
    k.flushed.append(copy)


def store_qkv(k, layer):
    v = own_sum(k, LAYER0 + layer * LAYER_ROWS + QKV, 48)
    square(k, v)
    k.s_qkv[layer, :, 0:512] = v[0:16]
    for pair in range(4):
        row, col = 16 + 16 * (pair // 2), 256 * (pair % 2)
        even = v[row : row + 16, col : col + 128]
        odd = v[row : row + 16, col + 128 : col + 256]
        left = lanes(even.shape) < 64
        k.s_qkv[layer, :, 512 + 128 * pair : 640 + 128 * pair] = jnp.where(left, even, roll64(odd))
        k.s_qkv[layer, :, 1024 + 128 * pair : 1152 + 128 * pair] = jnp.where(left, roll64(even), odd)
    flush(k, "qkv", layer)


def store_out(k, layer):
    v = own_sum(k, LAYER0 + layer * LAYER_ROWS + OUT, 16)
    square(k, v)
    k.s_out[layer] = v
    flush(k, "out", layer)


def store_up(k, layer):
    v = own_sum(k, LAYER0 + layer * LAYER_ROWS + UP, 64)
    square(k, v)
    for j in range(4):
        k.s_up[layer, :, 512 * j : 512 * j + 512] = v[16 * j : 16 * j + 16]
    flush(k, "up", layer)


def store_down(k, layer):
    v = own_sum(k, LAYER0 + layer * LAYER_ROWS + DOWN, 64)
    square(k, v)
    k.s_down[layer] = v
    flush(k, "down", layer)


def store_head(k):
    v = own_sum(k, HEAD, 16)[:, 0:256]
    square(k, v)
    k.s_head[...] = v
    flush(k, "head")


def store_rest(k):
    v = own_sum(k, EG, 16)
    square(k, v[:, 0:256])
    k.s_embed[:, 0:256] = v[0:8, 0:256]
    k.s_embed[:, 256:512] = v[8:16, 0:256]
    gains = jnp.where(k.g == 0, v[0:8, 256:512], v[8:16, 256:512])
    row, column = lax.broadcasted_iota(jnp.int32, (256, 16), 0), lax.broadcasted_iota(jnp.int32, (256, 16), 1)
    gains = exact(gains, jnp.where(row - 16 * k.s == column, 1.0, 0.0))[0:5]
    square(k, gains)
    k.s_gains[...] = gains
    flush(k, "embed")
    flush(k, "gains")


def store_ready(k):
    stores = [(range(EG, EG + 16), store_rest, ()), (range(HEAD, HEAD + 16), store_head, ())]
    for layer in range(2):
        base = LAYER0 + layer * LAYER_ROWS
        if layer == 1:
            stores.append((range(base + QKV, base + QKV + 48), store_qkv, (layer,)))
        stores.append((range(base + OUT, base + OUT + 16), store_out, (layer,)))
        stores.append((range(base + UP, base + UP + 64), store_up, (layer,)))
        stores.append((range(base + DOWN, base + DOWN + 64), store_down, (layer,)))
    for rows, store, args in stores:
        if rows.start not in k.stored and k.summed.issuperset(range(rows.start, rows.stop, 16)):
            k.stored.add(rows.start)
            store(k, *args)


def finish_grads(k):
    g = k.g
    point(k, "tail")
    for name in PIECES:
        for _ in k.reduces[name]:
            store_ready(k)
    store_ready(k)
    store_heads(k)
    lane = lanes((8, 128))
    k.stat[0] = jnp.where(lane == 0, k.sq, jnp.where(lane == 1, k.loss, 0.0))
    me = g * 16 + k.s
    sent, got = sem(k), sem(k)

    @pl.loop(1, 32)
    def _(i):
        t = lax.rem(me + i, 32)
        remote(k.stat.at[0], k.stat.at[i], sent, got, (t // 16, lax.rem(t, 16))).start()

    with scope("stats"):
        drain(got, k.stat.at[pl.ds(1, 31)])
        drain(sent, k.stat.at[pl.ds(1, 31)])
    k.stats[...] = jnp.sum(k.stat[...], axis=0)
    wait_all(k.flushed)


IN_NAMES = (
    "ids", "targets", "lengths", "w_qkv", "w_out", "w_up", "w_down", "embed", "head", "gains",
)
OUT_NAMES = ("g_qkv", "g_out", "g_up", "g_down", "g_embed", "g_head", "g_gains", "stats")
SEMS = 128


LATER = (
    "sendbox", "inbox", "dbox", "kvbox", "back", "kvback", "dkv", "dkv_out", "dkv_in", "h_hidden", "h_normed", "h_gj"
)


def scratch_shapes():
    shapes = {
        "pk": ((2, 4, 2, 2, ROWS, D), LOW),
        "gr": ((2, 4, 2, 2, ROWS, D), LOW),
        "rc": ((4, 2, 2, ROWS, D), LOW),
        "r2": ((4, 2, ROWS, D), LOW),
        "r1": ((4, ROWS, D), LOW),
        "rz": ((3, ROWS, D), LOW),
        "rl": ((3, 2, 2, max([16] + [PIECES[n][2] - PIECES[n][0] for n in Z_FIRST]), D), LOW),
        "gain": ((8, D), F32),
        "shift": ((152, D), F32),
        "pool": ((56, D), F32),
        "up": ((144, D), F32),
        "stat": ((32, 8, 128), F32),
        "columns": ((128, 256), F32),
        "headout": ((8, 16, 256), LOW),
        "wbox": ((32, 16, 256), LOW),
        "wh": ((D, 256), LOW),
        "table": ((256, D), F32),
        "normed": ((256, D), LOW),
        "hot": ((16, 144, 256), LOW),
        "q0": ((16, 144, 128), LOW),
        "kv0": ((16, 144, 128), LOW),
        "cosb": ((16, 128), F32),
        "sinb": ((16, 128), F32),
        "tgrad": ((256, D), F32),
        "gbytes": ((256, 256), F32),
        "gkv": ((1152, 128), LOW),
        "headgrad": ((32, 16, 256), LOW),
        "headgot": ((16, 16, 256), LOW),
        "headsum": ((16, 16, 256), LOW),
        "headback": ((16, 16, 256), LOW),
        "s_qkv": ((2, 16, 3 * D), F32),
        "s_out": ((2, 16, D), F32),
        "s_up": ((2, 16, 4 * D), F32),
        "s_down": ((2, 64, D), F32),
        "s_embed": ((8, D), F32),
        "s_head": ((16, 256), F32),
        "s_gains": ((5, 16), F32),
    }
    for layer in range(2):
        rows, pad = layer_sizes(layer)
        for name, shape, kind in (
            ("cos", (rows, 128), F32),
            ("sin", (rows, 128), F32),
            ("sendbox", (8, pad + rows, 128), LOW),
            ("inbox", (16, pad + rows, 128), LOW),
            ("abox", (8, pad, 128), LOW),
            ("home", (8, pad, 128), LOW),
            ("gsend", (8, pad, 128), LOW),
            ("gbox", (16, pad, 128), LOW),
            ("dbox", (8, pad, 128), LOW),
            ("kvbox", (8, rows, 128), LOW),
            ("back", (8, pad, 128), LOW),
            ("kvback", (8, rows, 128), LOW),
            ("lse", (8, rows, 128), F32),
            ("att", (8, rows, 128), F32),
            ("dkvt", (128, 16 * rows), F32),
            ("dkv", (16, rows, 128), F32),
            ("dkv_out", (8, rows, 128), F32),
            ("dkv_in", (8, rows, 128), F32),
            ("h_hidden", (rows, D), F32),
            ("h_normed", (rows, D), LOW),
            ("h_flat", (rows, D), LOW),
            ("h_middle", (rows, D), F32),
            ("h_second", (rows, D), LOW),
            ("h_pre", (rows, 4 * D), F32),
            ("h_act", (rows, 4 * D), LOW),
            ("h_gj", (rows, 3 * D), LOW),
            ("h_gpre", (rows, 4 * D), LOW),
        ):
            if layer == 1 or name not in LATER:
                shapes[name + str(layer)] = (shape, kind)
    return shapes


SCRATCH = scratch_shapes()
PER_LAYER = (
    "cos", "sin", "sendbox", "inbox", "abox", "home", "gsend", "gbox", "dbox", "back", "lse", "att", "dkvt", "dkv",
    "dkv_out", "dkv_in", "kvbox", "kvback",
)
HELD = ("hidden", "normed", "flat", "middle", "second", "pre", "act", "gj", "gpre")


def update_kernel(*refs):
    stats, sources, outs, loss_ref, norm_ref = refs[0], refs[1:29], refs[29:50], refs[50], refs[51]
    held, made, sems, out_sems = refs[52:59], refs[59:66], refs[66], refs[67]
    order = (4, 5, 6, 1, 0, 2, 3)
    for i in order:
        start_all([pltpu.make_async_copy(sources[7 * j + i], held[i].at[j], sems.at[i]) for j in range(4)])
    norm = jnp.sqrt(stats[0:1, 0:1])
    loss_ref[...] = stats[0:1, 1:2]
    norm_ref[...] = norm
    clip = jnp.minimum(1.0, CLIP_NORM / norm)
    for i in order:
        drain(sems.at[i], held[i])
        gradient, master, first, second = (held[i][j] for j in range(4))
        results = adam_update(master, gradient * clip, first, second, STEP_RATES[i], WEIGHT_DECAYS[i])
        for j in range(3):
            made[i][j] = results[j]
        start_all([pltpu.make_async_copy(made[i].at[j], outs[7 * j + i], out_sems.at[i]) for j in range(3)])
    for i in order:
        drain(out_sems.at[i], made[i])


def on_device_fast(byte_ids, targets, item_lengths, *arrays):
    masters, firsts, seconds = arrays[0:7], arrays[7:14], arrays[14:21]
    vmem, anywhere = pl.BlockSpec(memory_space=pltpu.VMEM), pl.BlockSpec(memory_space=pl.ANY)
    shard_shapes = [jax.ShapeDtypeStruct(master.shape, F32) for master in masters]
    outs = pl.pallas_call(
        kernel,
        name="step",
        out_shape=shard_shapes + [jax.ShapeDtypeStruct((8, 128), F32)],
        in_specs=[vmem, vmem, pl.BlockSpec(memory_space=pltpu.SMEM)] + [vmem] * 7,
        out_specs=[anywhere] * 7 + [vmem],
        scratch_shapes=[pltpu.VMEM(shape, kind) for shape, kind in SCRATCH.values()]
        + [pltpu.SemaphoreType.DMA((SEMS,))],
        compiler_params=pltpu.CompilerParams(collective_id=0, has_side_effects=True, vmem_limit_bytes=63 << 20),
    )(byte_ids, targets, item_lengths, *masters)
    grads, stats = outs[:7], outs[7]
    results = pl.pallas_call(
        update_kernel,
        name="update",
        out_shape=shard_shapes * 3 + [jax.ShapeDtypeStruct((1, 1), F32)] * 2,
        in_specs=[vmem] + [anywhere] * 28,
        out_specs=[anywhere] * 21 + [vmem] * 2,
        scratch_shapes=[pltpu.VMEM((count, *shard.shape), F32) for count in (4, 3) for shard in shard_shapes]
        + [pltpu.SemaphoreType.DMA((7,)), pltpu.SemaphoreType.DMA((7,))],
        compiler_params=pltpu.CompilerParams(vmem_limit_bytes=63 << 20),
    )(stats, *grads, *masters, *firsts, *seconds)
    return (results[21].reshape(()), results[22].reshape(()), *results[:21])


def solution(mesh):
    tuned = mesh.shape["dp"] == 2 and mesh.shape["seq"] == 16
    row = P(None, ("dp", "seq"), None)
    flat = P(("dp", "seq"), None)
    shards = (row, row, row, row, flat, flat, P(None, ("dp", "seq")))
    return jax.shard_map(
        on_device_fast if tuned else on_device_general,
        mesh=mesh,
        in_specs=(P("dp", "seq"), P("dp", "seq"), P("dp", None)) + shards * 3,
        out_specs=(P(), P()) + shards * 3,
        check_vma=False,
    )
```

```python
import contextlib
import functools

import jax
import jax.numpy as jnp
from jax import lax
from jax.experimental import pallas as pl
from jax.experimental.pallas import tpu as pltpu
from jax.sharding import PartitionSpec as P

HEADS = 8
VOCAB = 256
RATE = 3
STEP = 10

CLIP_NORM = 0.02
BETA_ONE = 0.9
BETA_TWO = 0.95
STEP_RATES = (0.03, 0.2, 0.03, 0.03, 0.6, 0.03, 0.2)
WEIGHT_DECAYS = (0.1, 0.1, 0.1, 0.1, 0.1, 0.1, 0.0)
EPSILON = 1e-08
NORM_EPS = 1e-05
MASK_FILL = -1e30


def shifted_2(value, axis, steps):
    count = lax.axis_size(axis)
    leading, last = (max(0, -steps), min(count, count - steps))
    return lax.ppermute(value, axis, [(source, source + steps) for source in range(leading, last)])


def to_low(values):
    return values.astype(jnp.bfloat16)


def layer_norm(values, gain):
    center = values - jnp.mean(values, axis=-1, keepdims=True)
    spread = jnp.mean(center * center, axis=-1, keepdims=True)
    return center * lax.rsqrt(spread + NORM_EPS) * gain


def rotate(joined, positions, num_heads):
    parts = joined.reshape(joined.shape[0], 3, num_heads, -1)
    half_size = parts.shape[-1] // 2
    freqs = 10000.0 ** (-jnp.arange(half_size, dtype=jnp.float32) / half_size)
    angles = positions.astype(jnp.float32)[:, None] * freqs[None, :]
    cosine = jnp.cos(angles)[:, None, :]
    sine = jnp.sin(angles)[:, None, :]

    def rotate_half(values):
        first_half = values[..., :half_size]
        second_half = values[..., half_size:]
        return jnp.concatenate(
            [first_half * cosine - second_half * sine, first_half * sine + second_half * cosine],
            axis=-1,
        )

    return (rotate_half(parts[:, 0]), rotate_half(parts[:, 1]), parts[:, 2])


def scores_for(q_low, k_low, query_pos, key_pos):
    scores = jnp.einsum(
        "rhe,phe->hrp", q_low, k_low, preferred_element_type=jnp.float32
    ) * q_low.shape[-1] ** (-0.5)
    causal = query_pos[:, None] >= key_pos[None, :]
    return (scores, causal)


def attend(q_low, k_low, v_low, query_pos):
    num_rows, num_heads, head_size = q_low.shape
    key_piece = (
        lax.all_gather(k_low, "seq", axis=0, tiled=True),
        lax.all_gather(v_low, "seq", axis=0, tiled=True),
    )
    running_max = jnp.full((num_heads, num_rows), MASK_FILL, jnp.float32)
    accum = jnp.zeros((num_rows, num_heads, head_size), jnp.float32)
    key_pos = jnp.arange(key_piece[0].shape[0], dtype=jnp.int32)
    scores, causal = scores_for(q_low, key_piece[0], query_pos, key_pos)
    scores = jnp.where(causal[None], scores, MASK_FILL)
    new_max = jnp.maximum(running_max, jnp.max(scores, axis=-1))
    factor = jnp.exp(running_max - new_max)
    attn_prob = jnp.where(causal[None], jnp.exp(scores - new_max[..., None]), 0.0)
    denom = jnp.sum(attn_prob, axis=-1)
    accum = accum * factor.T[:, :, None] + jnp.einsum(
        "hrp,phe->rhe", to_low(attn_prob), key_piece[1], preferred_element_type=jnp.float32
    )
    running_max, denom, accum = (new_max, denom, accum)
    return (accum / denom.T[:, :, None], (running_max + jnp.log(denom)).T)


def block_grads(q_low, grad_low, log_total, row_delta, query_pos, k_low, v_low, key_pos):
    scores, causal = scores_for(q_low, k_low, query_pos, key_pos)
    attn_prob = jnp.where(causal[None], jnp.exp(scores - log_total.T[:, :, None]), 0.0)
    grad_prob = jnp.einsum("rhe,phe->hrp", grad_low, v_low, preferred_element_type=jnp.float32)
    grad_score = to_low(attn_prob * (grad_prob - row_delta.T[:, :, None]))
    score_scale = q_low.shape[-1] ** (-0.5)
    grad_q = (
        jnp.einsum("hrp,phe->rhe", grad_score, k_low, preferred_element_type=jnp.float32)
        * score_scale
    )
    grad_k = (
        jnp.einsum("hrp,rhe->phe", grad_score, q_low, preferred_element_type=jnp.float32)
        * score_scale
    )
    grad_v = jnp.einsum(
        "hrp,rhe->phe", to_low(attn_prob), grad_low, preferred_element_type=jnp.float32
    )
    return (grad_q, grad_k, grad_v)


def attend_back(q_low, k_low, v_low, grad_low, log_total, row_delta, query_pos):
    key_piece = (
        lax.all_gather(k_low, "seq", axis=0, tiled=True),
        lax.all_gather(v_low, "seq", axis=0, tiled=True),
    )
    key_pos = jnp.arange(key_piece[0].shape[0], dtype=jnp.int32)
    grad_q = block_grads(
        q_low, grad_low, log_total, row_delta, query_pos, key_piece[0], key_piece[1], key_pos
    )[0]
    all_totals, all_deltas = (
        lax.all_gather(log_total, "seq", axis=0, tiled=True),
        lax.all_gather(row_delta, "seq", axis=0, tiled=True),
    )
    query_piece = (
        lax.all_gather(q_low, "seq", axis=0, tiled=True),
        lax.all_gather(grad_low, "seq", axis=0, tiled=True),
    )
    piece_rows = query_piece[0].shape[0]
    piece_pos = jnp.arange(piece_rows, dtype=jnp.int32)
    unused_q, grad_k_blk, grad_v_blk = block_grads(
        query_piece[0], query_piece[1], all_totals, all_deltas, piece_pos, k_low, v_low, query_pos
    )
    return (grad_q, grad_k_blk, grad_v_blk)


def layer_forward(hidden, weights, gain_pair, positions):
    w_joined, w_proj, w_rise, w_fall = weights
    num_rows = hidden.shape[0]
    normed = to_low(layer_norm(hidden, gain_pair[0]))
    joined = jnp.dot(normed, w_joined, preferred_element_type=jnp.float32)
    queries, keys, values = rotate(joined, positions, HEADS)
    q_low, k_low, v_low = (to_low(queries), to_low(keys), to_low(values))
    attended, log_total = attend(q_low, k_low, v_low, positions)
    flat_low = to_low(attended.reshape(num_rows, -1))
    middle = hidden + jnp.dot(flat_low, w_proj, preferred_element_type=jnp.float32)
    second = to_low(layer_norm(middle, gain_pair[1]))
    pre_act = jnp.dot(second, w_rise, preferred_element_type=jnp.float32)
    activated = to_low(jax.nn.gelu(pre_act))
    output = middle + jnp.dot(activated, w_fall, preferred_element_type=jnp.float32)
    saved = (
        normed,
        joined,
        q_low,
        k_low,
        v_low,
        attended,
        log_total,
        flat_low,
        middle,
        second,
        pre_act,
        activated,
    )
    return (output, saved)


def layer_backward(hidden, weights, gain_pair, positions, grad_out):
    w_joined, w_proj, w_rise, w_fall = weights
    unused_out, saved = layer_forward(hidden, weights, gain_pair, positions)
    (
        normed,
        joined,
        q_low,
        k_low,
        v_low,
        attended,
        log_total,
        flat_low,
        middle,
        second,
        pre_act,
        activated,
    ) = saved
    fall_low = to_low(grad_out)
    grad_fall = jnp.dot(activated.T, fall_low, preferred_element_type=jnp.float32)
    grad_act = jnp.dot(fall_low, w_fall.T, preferred_element_type=jnp.float32)
    grad_pre = to_low(jax.vjp(jax.nn.gelu, pre_act)[1](grad_act)[0])
    grad_rise = jnp.dot(second.T, grad_pre, preferred_element_type=jnp.float32)
    grad_second = jnp.dot(grad_pre, w_rise.T, preferred_element_type=jnp.float32)
    grad_middle_n, grad_gain_ffn = jax.vjp(layer_norm, middle, gain_pair[1])[1](grad_second)
    grad_middle = grad_out + grad_middle_n
    proj_low = to_low(grad_middle)
    grad_proj = jnp.dot(flat_low.T, proj_low, preferred_element_type=jnp.float32)
    grad_att = to_low(
        jnp.dot(proj_low, w_proj.T, preferred_element_type=jnp.float32).reshape(attended.shape)
    )
    row_delta = jnp.sum(grad_att.astype(jnp.float32) * attended, axis=-1)
    grad_q, grad_k, grad_v = attend_back(
        q_low, k_low, v_low, grad_att, log_total, row_delta, positions
    )

    def rotate_joined(joined_in):
        return rotate(joined_in, positions, HEADS)

    grad_joined = to_low(jax.vjp(rotate_joined, joined)[1]((grad_q, grad_k, grad_v))[0])
    grad_w_joined = jnp.dot(normed.T, grad_joined, preferred_element_type=jnp.float32)
    grad_normed = jnp.dot(grad_joined, w_joined.T, preferred_element_type=jnp.float32)
    grad_in_n, grad_gain_attn = jax.vjp(layer_norm, hidden, gain_pair[0])[1](grad_normed)
    return (
        grad_middle + grad_in_n,
        (grad_w_joined, grad_proj, grad_rise, grad_fall),
        jnp.stack([grad_gain_attn, grad_gain_ffn]),
    )


def adam_update(weight, gradient, moment_one, moment_two, step_rate, decay_rate):
    moment_one = BETA_ONE * moment_one + (1.0 - BETA_ONE) * gradient
    moment_two = BETA_TWO * moment_two + (1.0 - BETA_TWO) * gradient * gradient
    first_hat = moment_one / (1.0 - BETA_ONE**STEP)
    second_hat = moment_two / (1.0 - BETA_TWO**STEP)
    weight = weight - step_rate * (
        first_hat / (jnp.sqrt(second_hat) + EPSILON) + decay_rate * weight
    )
    return (weight, moment_one, moment_two)


def on_device_general(
    byte_ids,
    targets,
    item_lengths,
    w_qkv,
    w_out,
    w_up,
    w_down,
    embed,
    head,
    gains,
    mom_qkv,
    mom_out,
    mom_up,
    mom_down,
    mom_embed,
    mom_head,
    mom_gains,
    sec_qkv,
    sec_out,
    sec_up,
    sec_down,
    sec_embed,
    sec_head,
    sec_gains,
):
    low_qkv, low_out, low_up, low_down, low_embed, low_head, low_gains = (
        lax.all_gather(to_low(w_qkv), ("dp", "seq"), axis=1, tiled=True),
        lax.all_gather(to_low(w_out), ("dp", "seq"), axis=1, tiled=True),
        lax.all_gather(to_low(w_up), ("dp", "seq"), axis=1, tiled=True),
        lax.all_gather(to_low(w_down), ("dp", "seq"), axis=1, tiled=True),
        lax.all_gather(to_low(embed), ("dp", "seq"), axis=0, tiled=True),
        lax.all_gather(to_low(head), ("dp", "seq"), axis=0, tiled=True),
        lax.all_gather(to_low(gains), ("dp", "seq"), axis=1, tiled=True),
    )
    gain_rows = low_gains.astype(jnp.float32)
    byte_row = byte_ids[0]
    num_rows = byte_row.shape[0]
    short_rows = num_rows // RATE
    seq_place = lax.axis_index("seq")
    positions = seq_place * num_rows + jnp.arange(num_rows, dtype=jnp.int32)
    short_pos = seq_place * short_rows + jnp.arange(short_rows, dtype=jnp.int32)
    vocab_ids = jnp.arange(VOCAB, dtype=jnp.int32)
    one_hot_in = (byte_row[:, None] == vocab_ids[None, :]).astype(jnp.float32)
    embedded = jnp.dot(
        one_hot_in.astype(jnp.bfloat16), low_embed, preferred_element_type=jnp.float32
    )
    lower_weights = (low_qkv[0], low_out[0], low_up[0], low_down[0])
    upper_weights = (low_qkv[1], low_out[1], low_up[1], low_down[1])
    first_out, unused_first = layer_forward(embedded, lower_weights, gain_rows[0:2], positions)
    left_rim = shifted_2(first_out[num_rows - RATE + 1 :], "seq", 1)
    shifted = jnp.concatenate([left_rim, first_out[: num_rows - RATE + 1]], axis=0)
    pooled = jnp.mean(shifted.reshape(short_rows, RATE, -1), axis=1)
    short_out, unused_short = layer_forward(pooled, upper_weights, gain_rows[2:4], short_pos)
    upsampled = first_out + jnp.repeat(short_out, RATE, axis=0)
    top_gain = gain_rows[gain_rows.shape[0] - 1]
    final_low = to_low(layer_norm(upsampled, top_gain))
    logits = jnp.dot(final_low, low_head, preferred_element_type=jnp.float32)
    row_max = jnp.max(logits, axis=-1, keepdims=True)
    log_total = row_max[:, 0] + jnp.log(jnp.sum(jnp.exp(logits - row_max), axis=-1))
    one_hot_out = (targets[0][:, None] == vocab_ids[None, :]).astype(jnp.float32)
    picked = jnp.sum(one_hot_out * logits, axis=-1)
    lengths = item_lengths[0]
    ends = jnp.cumsum(lengths)
    doc_index = jnp.sum((positions[:, None] >= ends[None, :]).astype(jnp.int32), axis=1)
    item_ids = jnp.arange(lengths.shape[0], dtype=jnp.int32)
    doc_length = jnp.sum(
        jnp.where(item_ids[None, :] == doc_index[:, None], lengths[None, :], 0), axis=1
    ).astype(jnp.float32)
    loss_local = jnp.sum((log_total - picked) / doc_length)
    loss_sum = lax.psum(loss_local, ("dp", "seq"))
    grad_logits = to_low((jnp.exp(logits - log_total[:, None]) - one_hot_out) / doc_length[:, None])
    grad_head = jnp.dot(final_low.T, grad_logits, preferred_element_type=jnp.float32)
    grad_final = jnp.dot(grad_logits, low_head.T, preferred_element_type=jnp.float32)
    grad_upsampled, grad_gain_top = jax.vjp(layer_norm, upsampled, top_gain)[1](grad_final)
    grad_short = jnp.sum(grad_upsampled.reshape(short_rows, RATE, -1), axis=1)
    grad_pooled, upper_grads, upper_gain_grads = layer_backward(
        pooled, upper_weights, gain_rows[2:4], short_pos, grad_short
    )
    grad_shifted = jnp.repeat(grad_pooled / RATE, RATE, axis=0)
    rim_grad = shifted_2(grad_shifted[: RATE - 1], "seq", -1)
    grad_first = grad_upsampled + jnp.concatenate([grad_shifted[RATE - 1 :], rim_grad], axis=0)
    grad_embedded, lower_grads, lower_gain_grads = layer_backward(
        embedded, lower_weights, gain_rows[0:2], positions, grad_first
    )
    grad_embed = jnp.dot(one_hot_in.T, grad_embedded, precision=lax.Precision.HIGHEST)
    grad_gains = jnp.concatenate(
        [lower_gain_grads, upper_gain_grads, grad_gain_top[None, :]], axis=0
    )
    shard_grads = (
        lax.psum_scatter(
            jnp.stack([lower_grads[0], upper_grads[0]]),
            ("dp", "seq"),
            scatter_dimension=1,
            tiled=True,
        ),
        lax.psum_scatter(
            jnp.stack([lower_grads[1], upper_grads[1]]),
            ("dp", "seq"),
            scatter_dimension=1,
            tiled=True,
        ),
        lax.psum_scatter(
            jnp.stack([lower_grads[2], upper_grads[2]]),
            ("dp", "seq"),
            scatter_dimension=1,
            tiled=True,
        ),
        lax.psum_scatter(
            jnp.stack([lower_grads[3], upper_grads[3]]),
            ("dp", "seq"),
            scatter_dimension=1,
            tiled=True,
        ),
        lax.psum_scatter(grad_embed, ("dp", "seq"), scatter_dimension=0, tiled=True),
        lax.psum_scatter(grad_head, ("dp", "seq"), scatter_dimension=0, tiled=True),
        lax.psum_scatter(grad_gains, ("dp", "seq"), scatter_dimension=1, tiled=True),
    )
    squares = sum((jnp.sum(piece_grad * piece_grad) for piece_grad in shard_grads))
    total_squares = lax.psum(squares, ("dp", "seq"))
    grad_norm = jnp.sqrt(total_squares)
    clip_factor = jnp.minimum(1.0, CLIP_NORM / grad_norm)
    masters = (w_qkv, w_out, w_up, w_down, embed, head, gains)
    firsts = (mom_qkv, mom_out, mom_up, mom_down, mom_embed, mom_head, mom_gains)
    seconds = (sec_qkv, sec_out, sec_up, sec_down, sec_embed, sec_head, sec_gains)
    results = []
    for slot_index in range(7):
        results.append(
            adam_update(
                masters[slot_index],
                shard_grads[slot_index] * clip_factor,
                firsts[slot_index],
                seconds[slot_index],
                STEP_RATES[slot_index],
                WEIGHT_DECAYS[slot_index],
            )
        )
    return (
        loss_sum,
        grad_norm,
        results[0][0],
        results[1][0],
        results[2][0],
        results[3][0],
        results[4][0],
        results[5][0],
        results[6][0],
        results[0][1],
        results[1][1],
        results[2][1],
        results[3][1],
        results[4][1],
        results[5][1],
        results[6][1],
        results[0][2],
        results[1][2],
        results[2][2],
        results[3][2],
        results[4][2],
        results[5][2],
        results[6][2],
    )


LOW = jnp.bfloat16
F32 = jnp.float32
MESH = pl.DeviceIdType.MESH
D = 512

EG, LAYER0, LAYER_ROWS = 0, -32, 192
QKV, OUT, UP, DOWN = 0, 48, 64, 128
ROWS = LAYER0 + 2 * LAYER_ROWS
PIECES = {
    "A": (0, 16, 16),
    "B": (16, 32, 64),
    "E": (64, 80, 96),
    "b": (96, 128, 160),
    "C": (160, 192, 224),
    "D": (224, 256, 288),
    "d": (288, 304, 320),
    "h": (320, 336, 352),
}
Z_LAST, Z_FIRST = "h", "h"
SCHEDULE = {
    "start": "AbhBh",
    "heads": "AbABCb",
    "f0_heads": "EDAB",
    "f0_got": "E",
    "f0_mid0": "C",
    "f0_part0": "d",
    "f0_mid1": "bE",
    "f0_part1": "hCBE",
    "f0_home": "d",
    "f0_rim": "DCd",
    "f1_sent": "Dh",
    "f1_take": "d",
    "f1_part0": "D",
    "b1_ff": "D",
    "b1_sent": "hD",
    "b1_part0": "d",
    "b1_sums": "dDh",
    "b1_rim": "CdC",
    "b0_ff": "bhBDb",
    "b0_sent": "EdC",
    "b0_part1": "E",
    "b0_keys1": "b",
    "b0_mid0": "C",
    "b0_part0": "B",
    "b0_end": "AEb",
    "tail": "ABEABh",
}


def dot(a, b):
    return jnp.dot(a, b, preferred_element_type=F32)


def dot_nt(a, b):
    return lax.dot_general(a, b, (((1,), (1,)), ((), ())), preferred_element_type=F32)


def dot_tn(a, b):
    return lax.dot_general(a, b, (((0,), (0,)), ((), ())), preferred_element_type=F32)


def low(v):
    return v.astype(LOW)


exact = functools.partial(jnp.dot, preferred_element_type=F32, precision=lax.Precision.HIGHEST)


def lanes(shape):
    return lax.broadcasted_iota(jnp.int32, shape, len(shape) - 1)


def roll64(v):
    return pltpu.roll(v, 64, 1)


def swap32(v):
    return jnp.where(lanes(v.shape) % 64 < 32, pltpu.roll(v, 96, 1), pltpu.roll(v, 32, 1))


def norm_parts(v):
    center = v - jnp.mean(v, axis=-1, keepdims=True)
    scale = lax.rsqrt(jnp.mean(center * center, axis=-1, keepdims=True) + NORM_EPS)
    return center * scale, scale


def norm_back(v, gain, grad):
    unit, scale = norm_parts(v)
    g = grad * gain
    out = scale * (g - jnp.mean(g, axis=-1, keepdims=True) - unit * jnp.mean(g * unit, axis=-1, keepdims=True))
    return out, jnp.sum(grad * unit, axis=0, keepdims=True)


GELU_A, GELU_B = 0.7978845608028654, 0.044715


def gelu(v):
    return 0.5 * v * (1.0 + jnp.tanh(GELU_A * (v + GELU_B * v * v * v)))


def gelu_grad(v):
    t = jnp.tanh(GELU_A * (v + GELU_B * v * v * v))
    return 0.5 * (1.0 + t) + 0.5 * v * (1.0 - t * t) * (GELU_A * (1.0 + 3.0 * GELU_B * v * v))


class Bag:
    pass


def scope(name):
    return contextlib.nullcontext()


def remote(src, dst, send, recv, device):
    return pltpu.make_async_remote_copy(
        src_ref=src, dst_ref=dst, send_sem=send, recv_sem=recv, device_id=device, device_id_type=MESH
    )


def pack_pair(block, odd):
    half = block.shape[0] // 2
    top, bottom = block[:half], block[half:]
    if odd:
        top = roll64(top)
    else:
        bottom = roll64(bottom)
    return jnp.where(lanes(top.shape) < 64, top, bottom)


def unpack_pair(even, odd):
    left = lanes(even.shape) < 64
    top = jnp.where(left, even, roll64(odd))
    bottom = jnp.where(left, roll64(even), odd)
    return jnp.concatenate([top, bottom], axis=0)


def unpack_left(x):
    left = lanes(x.shape) < 64
    return jnp.concatenate([jnp.where(left, x, 0.0), jnp.where(left, roll64(x), 0.0)], axis=0)


def unpack_right(x):
    left = lanes(x.shape) < 64
    return jnp.concatenate([jnp.where(left, 0.0, roll64(x)), jnp.where(left, 0.0, x)], axis=0)


def pack_left(x):
    half = x.shape[0] // 2
    return jnp.where(lanes((half, 128)) < 64, x[:half], roll64(x[half:]))


def pack_right(x):
    half = x.shape[0] // 2
    return jnp.where(lanes((half, 128)) < 64, roll64(x[:half]), x[half:])


def kernel(*refs):
    k = Bag()
    names = IN_NAMES + OUT_NAMES + tuple(SCRATCH)
    for name, ref in zip(names, refs[:-1]):
        setattr(k, name, ref)
    k.sems = refs[-1]
    for name in PER_LAYER:
        setattr(k, name, [getattr(k, name + "0", None), getattr(k, name + "1")])
    k.hold = []
    for layer in range(2):
        hold = Bag()
        for name in HELD:
            setattr(hold, name, getattr(k, "h_" + name + str(layer), None))
        k.hold.append(hold)
    g = lax.axis_index("dp")
    s = lax.axis_index("seq")
    z, y, x = s // 4, lax.rem(s // 2, 2), lax.rem(s, 2)
    k.g, k.s, k.z, k.y, k.x = g, s, z, y, x
    k.side = lax.rem(x + y, 2)
    k.cursor = 0

    def dev(g, z, y, x):
        return (g, z * 4 + y * 2 + x)

    k.dev = dev

    barrier = pltpu.get_barrier_semaphore()
    me = g * 16 + s

    @pl.loop(1, 32)
    def _(i):
        t = lax.rem(me + i, 32)
        pl.semaphore_signal(barrier, inc=1, device_id=(t // 16, lax.rem(t, 16)), device_id_type=MESH)

    own = k.pk.at[g, z, y, x]
    own[EG : EG + 16, 0:256] = low(jnp.concatenate([k.embed[:, 0:256], k.embed[:, 256:512]], axis=0))
    own[EG : EG + 16, 256:512] = low(k.head[...])
    k.columns[0:1, 0:144] = k.ids[...].astype(F32)
    k.columns[1:2, 0:144] = k.targets[...].astype(F32)
    pack_heads(k)
    pack_layer(k, own, 0)
    pack_layer(k, own, 1)
    with scope("barrier"):
        pl.semaphore_wait(barrier, 31)
    k.gathers = {name: gather_piece(k, name, *rows) for name, rows in PIECES.items()}
    k.reduces = {name: reduce_piece(k, name, *rows) for name, rows in PIECES.items()}
    k.made, k.summed, k.stored = set(), set(), set()
    k.flushed, k.sq = [], jnp.zeros((1, 1), F32)
    point(k, "start")
    spread_heads(k)
    point(k, "heads")
    forward_backward(k)
    finish_grads(k)


def point(k, name):
    coming = name[0] in "sphf"
    for piece in SCHEDULE.get(name, ""):
        next((k.gathers if coming else k.reduces)[piece], None)
        if not coming:
            store_ready(k)


def touching(rows):
    return [name for name, (r0, _, r1) in PIECES.items() if r0 < rows.stop and r1 > rows.start]


def pair_kv(keys, vals):
    left = lanes(keys.shape) < 64
    return jnp.where(left, keys, roll64(vals)), jnp.where(left, roll64(keys), vals)


def pack_heads(k):
    row, lane = lax.broadcasted_iota(jnp.int32, (16, 128), 0), lanes((16, 128))
    place = lanes((16, 128)) - 64 == lax.broadcasted_iota(jnp.int32, (16, 128), 0)
    gains = exact(k.gains[...], jnp.where(place, 1.0, 0.0))
    ids = jnp.concatenate([gains, jnp.zeros((3, 128), F32), jnp.zeros((8, 128), F32)], axis=0)
    for j in range(3):
        part = pltpu.roll(k.columns[0:8, :], (64 - 48 * j) % 256, 1)[0:1, 0:128]
        ids = jnp.where((row == 8 + j) & (lane >= 64) & (lane < 112), part, ids)
    for pair in range(4):
        query = k.w_qkv[0, :, 128 * pair : 128 * pair + 128]
        keys = k.w_qkv[0, :, 512 + 128 * pair : 640 + 128 * pair]
        vals = k.w_qkv[0, :, 1024 + 128 * pair : 1152 + 128 * pair]
        for odd, kv in enumerate(pair_kv(keys, vals)):
            k.headout[2 * pair + odd, :, 0:128] = low(jnp.where(lane < 64, roll64(query) if odd else query, ids))
            k.headout[2 * pair + odd, :, 128:256] = low(kv)


def around(k, source, target, sent, got):
    for n in range(1, 16):
        c = lax.rem(k.s + n, 16)
        remote(source(c), target(k.s), sent, got, (k.g, c)).start()


def spread_heads(k):
    mine = k.g * 16 + k.s
    k.wbox[mine] = k.headout[lax.rem(k.s, 8)]
    k.head_sems = [sem(k), sem(k)]
    around(k, lambda c: k.headout.at[lax.rem(c, 8)], lambda c: k.wbox.at[k.g * 16 + c], *k.head_sems)


def take_heads(k):
    with scope("heads"):
        for semaphore in k.head_sems:
            drain(semaphore, k.wbox.at[pl.ds(0, 15)])
    share = k.wbox.at[pl.ds(16 * k.g, 16)]
    return Stage(k, share, [(share, share, k.dev(1 - k.g, k.z, k.y, k.x))])


def block_tables(k, b):
    cos_b, sin_b = k.cosb[pl.ds(b, 1), :], k.sinb[pl.ds(b, 1), :]
    cos_r, sin_r = k.cos[0][...], k.sin[0][...]
    return cos_b * cos_r - sin_b * sin_r, sin_b * cos_r + cos_b * sin_r


def kv_tables(cosine, sine):
    left = lanes(cosine.shape) < 64
    return jnp.where(left, cosine, 1.0), jnp.where(left, sine, 0.0)


def lane_copies(shape, axis):
    narrow = lax.broadcasted_iota(jnp.int32, shape, axis)
    wide = lax.broadcasted_iota(jnp.int32, shape, 1 - axis)
    return jnp.where(narrow - 64 == wide % 16, 1.0, 0.0)


def device_lanes():
    shape = (32, 8, 512)
    return lanes(shape) // 16 == lax.broadcasted_iota(jnp.int32, shape, 0)


def byte_rows(k):
    need(k, EG)
    packed = k.pk[:, :, :, :, EG : EG + 16, 0:256].astype(F32).reshape(32, 16, 256)
    gains = low(k.wbox[...].astype(F32)[:, 0:8, 0:128].reshape(256, 128))
    gains = dot(gains, low(lane_copies((128, 512), 0))).reshape(32, 8, 512)
    k.gain[...] = jnp.sum(jnp.where(device_lanes(), gains, 0.0), axis=0)
    table = jnp.concatenate(
        [packed[:, 0:8].reshape(256, 256), packed[:, 8:16].reshape(256, 256)], axis=1
    )
    k.table[...] = table
    unit, _ = norm_parts(table)
    k.normed[...] = low(unit * k.gain[0:1, :])


def head_rows(k):
    group = k.s // 8
    for b in range(16):
        k.columns[16 + 4 * b : 20 + 4 * b, 0:128] = k.wbox[group * 16 + b].astype(F32)[8:12, 0:128]
    columns = k.columns[...].T
    weights = k.wbox[...].astype(F32).reshape(512, 256)
    lane = lanes(weights.shape)
    k.wh[...] = low(jnp.where((lane >= 64) & (lane < 128), 0.0, weights))
    joined = dot(k.normed[...], k.wh[...])
    high = low(joined)
    rest = low(joined - high.astype(F32))
    for b in range(16):
        ids = [columns[64:112, 16 + 4 * b + j : 17 + 4 * b + j] for j in range(3)]
        hot = byte_matrix(jnp.concatenate(ids, axis=0).astype(jnp.int32))
        k.hot[b] = hot
        rows = dot(hot, high) + dot(hot, rest)
        cosine, sine = block_tables(k, b)
        k.q0[b] = low(rotate_block(rows[:, 0:128], cosine, sine) * 0.125)
        k.kv0[b] = low(rotate_block(rows[:, 128:256], *kv_tables(cosine, sine)))


def pack_layer(k, own, layer):
    base = LAYER0 + layer * LAYER_ROWS
    if layer == 1:
        own[base + QKV : base + QKV + 16, :] = low(k.w_qkv[layer, :, 0:512])
        for pair in range(4):
            keys = k.w_qkv[layer, :, 512 + 128 * pair : 640 + 128 * pair]
            vals = k.w_qkv[layer, :, 1024 + 128 * pair : 1152 + 128 * pair]
            row = base + QKV + 16 + 16 * (pair // 2)
            for odd, kv in enumerate(pair_kv(keys, vals)):
                col = 256 * (pair % 2) + 128 * odd
                own[row : row + 16, col : col + 128] = low(kv)
    own[base + OUT : base + OUT + 16, :] = low(k.w_out[layer])
    for j in range(4):
        own[base + UP + 16 * j : base + UP + 16 * j + 16, :] = low(k.w_up[layer, :, 512 * j : 512 * j + 512])
    own[base + DOWN : base + DOWN + 64, :] = low(k.w_down[layer])


def sem(k):
    k.cursor += 1
    assert k.cursor <= SEMS
    return k.sems.at[k.cursor - 1]


def start_all(copies):
    for copy in copies:
        copy.start()


def wait_all(copies):
    for copy in copies:
        copy.wait()


def drain(semaphore, ref):
    pltpu.make_async_copy(ref, ref, semaphore).wait()


class Stage:
    def __init__(self, k, total, moves, sent=None):
        self.total, self.sent, self.got = total, sem(k) if sent is None else sent, sem(k)
        start_all([remote(src, dst, self.sent, self.got, device) for src, dst, device in moves if src.shape[-2]])

    def wait(self):
        drain(self.got, self.total)
        drain(self.sent, self.total)


def gather_piece(k, name, r0, rm, r1):
    g, z, y, x, dev, pk = k.g, k.z, k.y, k.x, k.dev, k.pk
    a, b, every = pl.ds(r0, rm - r0), pl.ds(rm, r1 - rm), pl.ds(r0, r1 - r0)

    sent = sem(k)

    def stage(total, *moves):
        return Stage(k, total, [(ref, ref, device) for ref, device in moves], sent)

    def wait(waiting):
        with scope(f"gw_{name}"):
            waiting.wait()

    planes = pl.ds(z, 1) if name in Z_LAST else pl.ds(0, 4)

    def across():
        waiting = stage(
            pk.at[g, planes, y, x, every],
            (pk.at[g, planes, y, x, a], dev(g, z, 1 - y, x)),
            (pk.at[g, planes, y, x, b], dev(g, z, y, 1 - x)),
        )
        yield
        wait(waiting)
        waiting = stage(
            pk.at[g, planes, :, x, every],
            (pk.at[g, planes, :, x, a], dev(g, z, y, 1 - x)),
            (pk.at[g, planes, y, :, b], dev(g, z, 1 - y, x)),
        )
        yield
        wait(waiting)

    def along():
        def part(n):
            return pk.at[g, n, :, :, every] if name in Z_LAST else pk.at[g, n, y, x, every]

        waiting = stage(part(pl.ds(0, 3)), *[(part(z), dev(g, lax.rem(z + n, 4), y, x)) for n in (2, 1, 3)])
        yield
        wait(waiting)

    for way in (across, along) if name in Z_LAST else (along, across):
        yield from way()
    waiting = stage(pk.at[1 - g, :, :, :, every], (pk.at[g, :, :, :, every], dev(1 - g, z, y, x)))
    yield
    wait(waiting)
    yield


def need(k, row, count=16):
    for name in touching(range(row, row + count)):
        for _ in k.gathers[name]:
            pass


def block(k, row):
    need(k, row)
    return k.pk[:, :, :, :, row : row + 16, :].reshape(512, 512)


def put_block(k, row, value):
    k.made.add(row)
    k.gr[:, :, :, :, row : row + 16, :] = low(value).reshape(2, 4, 2, 2, 16, 512)


def down_block(k, row, c):
    need(k, row, 64)
    return k.pk[c // 2, (c % 2) * 2 : (c % 2) * 2 + 2, :, :, row : row + 64, :].reshape(512, 512)


def put_down(k, row, c, value):
    if c == 3:
        k.made.update(range(row, row + 64, 16))
    k.gr[c // 2, (c % 2) * 2 : (c % 2) * 2 + 2, :, :, row : row + 64, :] = low(value).reshape(2, 2, 2, 64, 512)


def my_blocks(k):
    return [4 * j + (k.g if half == 0 else 3 - k.g) for j in range(4) for half in range(2)]


def other_blocks(k):
    return [4 * j + (1 - k.g if half == 0 else 2 + k.g) for j in range(4) for half in range(2)]


def my_block(k, i):
    return 4 * (i // 2) + jnp.where(lax.rem(i, 2) == 0, k.g, 3 - k.g)


class Post:
    def __init__(self, k, source, groups):
        self.k, self.source = k, source
        self.sent, self.got = sem(k), [sem(k) for _ in range(groups)]

    def start(self, src, dst, got, device):
        k = self.k
        is_self = jnp.logical_and(device[0] == k.g, device[1] == k.s)

        @pl.when(is_self)
        def _():
            pltpu.make_async_copy(src, dst, got).start()

        @pl.when(jnp.logical_not(is_self))
        def _():
            remote(src, dst, self.sent, got, device).start()

    def finish(self, one_is_self):
        @pl.when(one_is_self)
        def _():
            drain(self.sent, self.source.at[pl.ds(0, 7)])

        @pl.when(jnp.logical_not(one_is_self))
        def _():
            drain(self.sent, self.source)


class ToHeads(Post):
    def __init__(self, k, source, target):
        super().__init__(k, source, 2)
        self.target = target

    def send(self):
        k = self.k
        for part in range(2):

            @pl.when(k.s // 8 == part)
            def _():
                for i in range(8):
                    h = lax.rem(k.s + i, 8)
                    self.start(self.source.at[h], self.target.at[k.s], self.got[part], (k.side, k.g * 8 + h))

    def take(self, part):
        drain(self.got[part], self.target.at[pl.ds(0, 4)])

    def done(self):
        k = self.k
        self.finish(jnp.logical_and(k.s // 8 == k.g, k.side == k.g))


class FromHeads(Post):
    def __init__(self, k, source, target):
        super().__init__(k, source, 1)
        self.target = target

    def send(self, i, b):
        k = self.k
        head = lax.rem(k.s, 8)
        self.start(self.source.at[i], self.target.at[head], self.got[0], (k.s // 8, b))

    def take(self):
        drain(self.got[0], self.target)

    def done(self):
        k = self.k
        self.finish(jnp.logical_and(k.s // 8 == k.g, k.side == k.g))


def rotate_block(v, cosine, sine):
    return v * cosine + swap32(v) * sine


def rotary_tables(k):
    lane = lanes((1, 128))
    freqs = jnp.zeros((1, 128), F32)
    for i in range(32):
        freqs = jnp.where(lane % 32 == i, 10000.0 ** (-i / 32), freqs)
    sign = jnp.where(lane % 64 < 32, -1.0, 1.0)
    rows, short = layer_sizes(0)[0], layer_sizes(1)[0]
    for cos, sin, count, first, step in (
        (k.cos[0], k.sin[0], rows, 0, 1),
        (k.cosb, k.sinb, 16, 0, rows),
        (k.cos[1], k.sin[1], short, k.s * short, 1),
    ):
        angles = (first + step * lax.broadcasted_iota(jnp.int32, (count, 1), 0)).astype(F32) * freqs
        cos[...] = jnp.cos(angles)
        sin[...] = jnp.sin(angles) * sign


def layer_sizes(layer):
    rows = 144 if layer == 0 else 48
    return rows, (rows // 2 + 15) // 16 * 16


def attend_loop(layer, part, body, between=None):
    if layer == 1:
        body(list(range(8)), 16)
        return
    for first in (0, 2):
        @pl.loop(first, first + 2)
        def _(n):
            body([part * 4 + n], 8 * part + 4 + 2 * first)

        if between is not None and first == 0:
            between()


def stack(pieces):
    return pieces[0] if len(pieces) == 1 else jnp.concatenate(pieces, axis=0)


def masked_scores(q, kv, places, plain):
    scores = dot_nt(q, kv)
    plain = plain // 128 * 128
    rest = scores[:, plain:]
    rest = jnp.where(lanes(rest.shape) + plain <= places, rest, MASK_FILL)
    return jnp.concatenate([scores[:, :plain], rest], axis=1) if plain else rest


def stacked_queries(k, layer, items):
    rows, pad = layer_sizes(layer)
    blocks = [my_block(k, i) for i in items]
    places = stack([b * rows + lax.broadcasted_iota(jnp.int32, (rows, 1), 0) for b in blocks])
    if layer == 0:
        return stack([k.q0[b] for b in blocks]), blocks, places
    q = stack([unpack_left(k.inbox[layer][b, 0:pad, :].astype(F32)[: rows // 2]) for b in blocks])
    return low(q * 0.125), blocks, places


def stacked_keys(k, layer, count):
    rows, pad = layer_sizes(layer)
    if layer == 0:
        return k.kv0[0:count].reshape(count * rows, 128)
    return k.inbox[layer][0:count, pad : pad + rows, :].reshape(count * rows, 128)


def attention_forward(k, layer, part, post, between):
    rows, pad = layer_sizes(layer)
    outbox, lse, keep = k.abox[layer], k.lse[layer], k.att[layer]

    def body(items, count):
        q, blocks, places = stacked_queries(k, layer, items)
        kv = stacked_keys(k, layer, count)
        scores = masked_scores(q, kv, places, 0 if layer == 1 else (count - 4) * rows)
        top = jnp.max(scores, axis=-1, keepdims=True)
        prob = jnp.exp(scores - top)
        total = jnp.sum(prob, axis=-1, keepdims=True)
        out = dot(low(prob), kv) / total
        stat = jnp.broadcast_to(top + jnp.log(total), out.shape)
        for n, (i, b) in enumerate(zip(items, blocks)):
            span = slice(n * rows, (n + 1) * rows)
            lse[i] = stat[span]
            keep[i] = out[span]
            outbox[i, 0 : rows // 2, :] = low(pack_right(out[span]))
            post.send(i, b)

    attend_loop(layer, part, body, between)


def attention_backward(k, layer, part, post, between=None):
    rows, pad = layer_sizes(layer)
    gradbox, lse, keep = k.gbox[layer], k.lse[layer], k.att[layer]
    dkvt, outbox = k.dkvt[layer], k.dbox[layer]

    def body(items, count):
        q, blocks, places = stacked_queries(k, layer, items)
        kv = stacked_keys(k, layer, count)
        grad = stack([unpack_right(gradbox[b].astype(F32)[: rows // 2]) for b in blocks])
        delta = jnp.sum(grad * stack([keep[i] for i in items]), axis=-1, keepdims=True)
        grad = low(grad)
        prob = jnp.exp(masked_scores(q, kv, places, 0 if layer == 1 else (count - 4) * rows) - stack([lse[i] for i in items])[:, 0:1])
        grad_prob = dot_nt(grad, kv)
        ds = low(prob * (grad_prob - delta))
        dq = dot(ds, kv) * 0.125
        if layer == 0:
            cosine, sine = block_tables(k, blocks[0])
            dq = rotate_block(jnp.where(lanes(dq.shape) < 64, dq, 0.0), cosine, -sine)
            k.gbytes[:, 0:128] += dot_tn(k.hot[blocks[0]], low(dq))
        for n, (i, b) in enumerate(zip(items, blocks) if layer == 1 else ()):
            outbox[i, 0 : rows // 2, :] = low(pack_left(dq[n * rows : (n + 1) * rows]))
            post.send(i, b)
        dkvt[:, 0 : count * rows] += dot_tn(q, ds) + dot_tn(grad, low(prob))

    attend_loop(layer, part, body, between)


class KeySums:
    def __init__(self, k, layer, part, post):
        rows, _ = layer_sizes(layer)
        self.k, self.layer, self.post = k, layer, post
        self.items = range(8) if layer == 1 else range(4 * part, 4 * part + 4)
        first, count = (0, 16) if layer == 1 else (8 * part, 8)
        k.dkv[layer][first : first + count] = (
            k.dkvt[layer][:, first * rows : (first + count) * rows].T.reshape(count, rows, 128)
        )
        others = other_blocks(k)
        for i in self.items:
            k.dkv_out[layer][i] = k.dkv[layer][others[i]]
        span = pl.ds(self.items[0], len(self.items))
        self.copy = Stage(
            k,
            k.dkv_in[layer].at[span],
            [(k.dkv_out[layer].at[span], k.dkv_in[layer].at[span], k.dev(1 - k.g, k.z, k.y, k.x))],
        )

    def send(self):
        k, layer = self.k, self.layer
        self.copy.wait()
        mine = my_blocks(k)
        for i in self.items:
            k.kvbox[layer][i] = low(k.dkv[layer][mine[i]] + k.dkv_in[layer][i])
            self.post.send(i, mine[i])


def send_rows(k, hidden):
    layer = 1
    rows, pad = layer_sizes(layer)
    base = LAYER0 + layer * LAYER_ROWS
    unit, _ = norm_parts(hidden)
    normed = low(unit * k.gain[2 * layer : 2 * layer + 1, :])
    k.hold[layer].normed[...] = normed
    cosine, sine = k.cos[layer][...], k.sin[layer][...]
    cos_kv, sin_kv = kv_tables(cosine, sine)
    sendbox = k.sendbox[layer]
    for part in range(3):
        joined = dot(normed, block(k, base + QKV + 16 * part))
        for n in range(4):
            piece = joined[:, 128 * n : 128 * n + 128]
            if part == 0:
                piece = rotate_block(piece, cosine, sine)
                sendbox[2 * n, 0 : rows // 2, :] = low(pack_pair(piece, 0))
                sendbox[2 * n + 1, 0 : rows // 2, :] = low(pack_pair(piece, 1))
            else:
                sendbox[4 * part - 4 + n, pad : pad + rows, :] = low(rotate_block(piece, cos_kv, sin_kv))
    inbox = k.inbox[layer]
    out = ToHeads(k, sendbox, inbox)
    out.send()
    point(k, "f1_sent")
    sent, shared = sem(k), [sem(k), sem(k)]
    mine = my_blocks(k)
    for part in range(2):
        if part == 1:
            point(k, "f1_take")
        with scope("take"):
            out.take(part)
        for b in mine[4 * part : 4 * part + 4]:
            ref = inbox.at[b, pl.ds(pad, rows)]
            remote(ref, ref, sent, shared[part], k.dev(1 - k.g, k.z, k.y, k.x)).start()
    point(k, "f1_got")
    k.pending += [out.done, lambda: drain(sent, inbox.at[pl.ds(0, 8), pl.ds(pad, rows)])]
    return shared


def layer_ahead(k, layer, hidden):
    rows, pad = layer_sizes(layer)
    base = LAYER0 + layer * LAYER_ROWS
    hold = k.hold[layer]
    home = k.home[layer]
    if layer == 0:
        point(k, "f0_got")
        shared = []
    else:
        hold.hidden[...] = hidden
        shared = send_rows(k, hidden)
    back = FromHeads(k, k.abox[layer], home)
    for part in range(2 - layer):
        for semaphore in shared:
            with scope("share"):
                drain(semaphore, k.inbox[layer].at[pl.ds(0, 4), pl.ds(pad, rows)])
        with scope("attend"):
            attention_forward(k, layer, part, back, lambda: point(k, f"f0_mid{part}"))
        point(k, f"f{layer}_part{part}")
    with scope("home"):
        back.take()
    point(k, f"f{layer}_home")
    if layer == 1:
        point(k, "f1_out")
    for n in range(4):
        pair = unpack_pair(
            home[2 * n].astype(F32)[: rows // 2], home[2 * n + 1].astype(F32)[: rows // 2]
        )
        hold.flat[:, 128 * n : 128 * n + 128] = low(pair)
    middle = hidden + dot(hold.flat[...], block(k, base + OUT))
    hold.middle[...] = middle
    unit, _ = norm_parts(middle)
    second = low(unit * k.gain[2 * layer + 1 : 2 * layer + 2, :])
    hold.second[...] = second
    for j in range(4):
        pre = dot(second, block(k, base + UP + 16 * j))
        hold.pre[:, 512 * j : 512 * j + 512] = pre
        hold.act[:, 512 * j : 512 * j + 512] = low(gelu(pre))
    point(k, f"f{layer}_up")
    need(k, base + DOWN, 64)
    falls = k.pk[:, :, :, :, base + DOWN : base + DOWN + 64, :].reshape(2048, 512)
    output = hold.middle[...] + dot(hold.act[...], falls)
    back.done()
    for done in k.pending:
        done()
    k.pending = []
    return output


def layer_back(k, layer, grad_out):
    rows, pad = layer_sizes(layer)
    base = LAYER0 + layer * LAYER_ROWS
    hold = k.hold[layer]
    fall = low(grad_out)
    grad_second = jnp.zeros((rows, D), F32)
    second = hold.second[...]
    for c in range(4):
        cols = slice(512 * c, 512 * c + 512)
        if layer == 1:
            put_down(k, base + DOWN, c, dot_tn(hold.act[:, cols], fall))
        grad_act = dot_nt(fall, down_block(k, base + DOWN, c))
        grad_pre = low(grad_act * gelu_grad(hold.pre[:, cols]))
        if layer == 1:
            put_block(k, base + UP + 16 * c, dot_tn(second, grad_pre))
        else:
            hold.gpre[:, cols] = grad_pre
        grad_second = grad_second + dot_nt(grad_pre, block(k, base + UP + 16 * c))
    if layer == 1:
        point(k, "b1_ff")
    gain = k.gain[2 * layer + 1 : 2 * layer + 2, :]
    grad_mid, k.gain_grads[2 * layer + 1] = norm_back(hold.middle[...], gain, grad_second)
    grad_middle = grad_out + grad_mid
    hold.middle[...] = grad_middle
    proj = low(grad_middle)
    if layer == 1:
        put_block(k, base + OUT, dot_tn(hold.flat[...], proj))
    grad_att = dot_nt(proj, block(k, base + OUT))
    gsend = k.gsend[layer]
    for n in range(4):
        piece = grad_att[:, 128 * n : 128 * n + 128]
        gsend[2 * n, 0 : rows // 2, :] = low(pack_pair(piece, 0))
        gsend[2 * n + 1, 0 : rows // 2, :] = low(pack_pair(piece, 1))
    out = ToHeads(k, gsend, k.gbox[layer])
    out.send()
    if layer == 0:
        put_block(k, base + OUT, dot_tn(hold.flat[...], proj))
        for c in range(4):
            cols = slice(512 * c, 512 * c + 512)
            put_down(k, base + DOWN, c, dot_tn(hold.act[:, cols], fall))
            put_block(k, base + UP + 16 * c, dot_tn(second, hold.gpre[:, cols]))
        point(k, "b0_ff")
    k.dkvt[layer][...] = jnp.zeros_like(k.dkvt[layer])
    point(k, f"b{layer}_sent")
    if layer == 0:
        return head_grads(k, out)
    back = k.back[layer]
    home_q = FromHeads(k, k.dbox[layer], back)
    home_kv = FromHeads(k, k.kvbox[layer], k.kvback[layer])
    with scope("take"):
        out.take(0)
        out.take(1)
    with scope("unattend"):
        attention_backward(k, layer, 0, home_q)
    sums = KeySums(k, layer, 0, home_kv)
    point(k, "b1_part0")
    with scope("sums"):
        sums.send()
    point(k, "b1_sums")
    with scope("home_q"):
        home_q.take()
    cosine, sine = k.cos[layer][...], k.sin[layer][...]
    cos_kv, sin_kv = kv_tables(cosine, sine)
    for part in range(3):
        if part == 1:
            with scope("home_kv"):
                home_kv.take()
            point(k, "b1_home")
        for n in range(4):
            if part == 0:
                piece = unpack_pair(
                    back[2 * n].astype(F32)[: rows // 2],
                    back[2 * n + 1].astype(F32)[: rows // 2],
                )
                piece = rotate_block(piece, cosine, -sine)
            else:
                piece = k.kvback[layer][4 * part - 4 + n].astype(F32)
                piece = rotate_block(piece, cos_kv, -sin_kv)
            hold.gj[:, 512 * part + 128 * n : 512 * part + 128 * n + 128] = low(piece)
    grad_normed = jnp.zeros((rows, D), F32)
    for part in range(3):
        gj = hold.gj[:, 512 * part : 512 * part + 512]
        grad_normed = grad_normed + dot_nt(gj, block(k, base + QKV + 16 * part))
    gain = k.gain[2 * layer : 2 * layer + 1, :]
    grad_in, k.gain_grads[2 * layer] = norm_back(hold.hidden[...], gain, grad_normed)
    return hold.middle[...] + grad_in, (out, home_q, home_kv)


def head_grads(k, out):
    own = dot_tn(byte_matrix(k.own_ids), low(k.hold[0].middle[...]))
    k.tgrad[...] = own
    k.gbytes[...] = jnp.zeros_like(k.gbytes)
    for part in (1, 0):
        with scope("take"):
            out.take(part)
        with scope("unattend"):
            attention_backward(k, 0, part, None, lambda: point(k, f"b0_mid{part}"))
        point(k, f"b0_part{part}")
        with scope("keysums"):
            sums = k.dkvt[0][:, 1152 * part : 1152 * part + 1152].T
            for i in range(8):
                cosine, sine = kv_tables(*block_tables(k, 8 * part + i))
                k.gkv[144 * i : 144 * i + 144, :] = low(rotate_block(sums[144 * i : 144 * i + 144], cosine, -sine))
            k.gbytes[:, 128:256] += dot_tn(k.hot[8 * part : 8 * part + 8].reshape(1152, 256), k.gkv[...])
        point(k, f"b0_keys{part}")
    gbytes = low(k.gbytes[...])
    grad, k.gain_grads[0] = norm_back(k.table[...], k.gain[0:1, :], dot_nt(gbytes, k.wh[...]))
    gains = jnp.concatenate(k.gain_grads + [jnp.zeros((3, D), F32)], axis=0)
    gains = jnp.where(device_lanes(), jnp.broadcast_to(gains[None], (32, 8, 512)), 0.0).reshape(256, 512)
    gains = dot(low(gains), low(lane_copies((512, 128), 1))).reshape(32, 8, 128)
    gains = jnp.concatenate([gains, jnp.zeros((32, 8, 128), F32)], axis=1)
    heads = dot_tn(k.normed[...], gbytes).reshape(32, 16, 256)
    k.headgrad[:, :, 0:128] = low(heads[:, :, 0:128] + gains)
    k.headgrad[:, :, 128:256] = low(heads[:, :, 128:256])
    stage = Stage(
        k,
        k.headgot,
        [(k.headgrad.at[pl.ds(16 * (1 - k.g), 16)], k.headgot, k.dev(1 - k.g, k.z, k.y, k.x))],
    )
    total = k.tgrad[...] + grad
    total = jnp.concatenate([total[:, 0:256].reshape(32, 8, 256), total[:, 256:512].reshape(32, 8, 256)], axis=1)
    k.gr[:, :, :, :, EG : EG + 16, 0:256] = low(total).reshape(2, 4, 2, 2, 16, 256)
    return stage, (out,)


def send_head_grads(k, stage):
    with scope("headcore"):
        stage.wait()
    total = k.headgrad[pl.ds(16 * k.g, 16)].astype(F32) + k.headgot[...].astype(F32)
    k.headsum[...] = low(total)
    k.headback[k.s] = k.headsum[k.s]
    k.head_sems = [sem(k), sem(k)]
    around(k, lambda c: k.headsum.at[c], lambda c: k.headback.at[c], *k.head_sems)


def store_heads(k):
    with scope("headback"):
        for semaphore in k.head_sems:
            drain(semaphore, k.headback.at[pl.ds(0, 15)])
    for pair in range(4):
        even, odd = (k.headback[h].astype(F32) + k.headback[8 + h].astype(F32) for h in (2 * pair, 2 * pair + 1))
        left = lanes((16, 128)) < 64
        query = jnp.where(left, even[:, 0:128], roll64(odd[:, 0:128]))
        keys, vals = pair_kv(even[:, 128:256], odd[:, 128:256])
        for at, value in ((0, query), (512, keys), (1024, vals)):
            square(k, value)
            k.s_qkv[0, :, at + 128 * pair : at + 128 * pair + 128] = value
    flush(k, "qkv", 0)
    gains = sum(k.headback[c].astype(F32)[0:8, 0:128] for c in range(16))
    row, column = lax.broadcasted_iota(jnp.int32, (128, 16), 0), lax.broadcasted_iota(jnp.int32, (128, 16), 1)
    gains = exact(gains, jnp.where(row - 64 == column, 1.0, 0.0))[0:5]
    square(k, gains)
    k.s_gains[...] = gains
    flush(k, "gains")


def finish_back(k, posts):
    for post in posts:
        post.done()


def byte_matrix(ids):
    return low(jnp.where(lanes((ids.shape[0], 256)) == ids, 1.0, 0.0))


def forward_backward(k):
    rows, short = 144, 48
    k.gain_grads, k.pending = [None] * 5, []
    rotary_tables(k)
    stage = take_heads(k)
    point(k, "f0_heads")
    with scope("headcore"):
        stage.wait()
    byte_rows(k)
    with scope("headrows"):
        head_rows(k)
    columns = k.columns[...].T
    k.own_ids, targets = columns[0:rows, 0:1].astype(jnp.int32), columns[0:rows, 1:2].astype(jnp.int32)
    first_in = dot(byte_matrix(k.own_ids), low(k.table[...]))
    first = layer_ahead(k, 0, first_in)
    k.shift[8 : 8 + rows, :] = first
    rim = remote(
        k.shift.at[pl.ds(rows, 8)], k.shift.at[pl.ds(0, 8)], sem(k), sem(k), (k.g, lax.rem(k.s + 1, 16))
    )

    @pl.when(k.s < 15)
    def _():
        rim.start()

    point(k, "f0_rim")

    @pl.when(k.s > 0)
    def _():
        rim.wait_recv()

    @pl.when(k.s == 0)
    def _():
        k.shift[0:8, :] = jnp.zeros((8, D), F32)

    @pl.when(k.s < 15)
    def _():
        rim.wait_send()

    def pool_matrix(shape, offset, axis):
        j = lax.broadcasted_iota(jnp.int32, shape, axis)
        t = lax.broadcasted_iota(jnp.int32, shape, 1 - axis) - offset
        return jnp.where((t >= 3 * j) & (t < 3 * j + 3), 1.0, 0.0)

    pooled = exact(pool_matrix((short, rows + 8), 6, 0), k.shift[...]) / 3.0
    point(k, "f0_end")
    short_out = layer_ahead(k, 1, pooled)
    upsampled = k.shift[8 : 8 + rows, :] + exact(pool_matrix((rows, short), 0, 1), short_out)
    gain = k.gain[4:5, :]
    unit, _ = norm_parts(upsampled)
    final = low(unit * gain)
    head = k.pk[:, :, :, :, EG : EG + 16, 256:512].reshape(512, 256)
    logits = dot(final, head)
    top = jnp.max(logits, axis=-1, keepdims=True)
    log_total = top + jnp.log(jnp.sum(jnp.exp(logits - top), axis=-1, keepdims=True))
    hot = jnp.where(lanes((rows, 256)) == targets, 1.0, 0.0)
    picked = jnp.sum(hot * logits, axis=-1, keepdims=True)
    position = k.s * rows + lax.broadcasted_iota(jnp.int32, (rows, 1), 0)
    length = jnp.zeros((rows, 1), F32)
    begin = jnp.int32(0)
    for i in range(8):
        size = k.lengths[0, i]
        inside = (position >= begin) & (position < begin + size)
        length = jnp.where(inside, size.astype(F32), length)
        begin = begin + size
    k.loss = jnp.sum((log_total - picked) / length, axis=0, keepdims=True)
    grad_logits = low((jnp.exp(logits - log_total) - hot) / length)
    k.gr[:, :, :, :, EG : EG + 16, 256:512] = low(dot_tn(final, grad_logits)).reshape(2, 4, 2, 2, 16, 256)
    grad_final = dot_nt(grad_logits, head)
    grad_up, k.gain_grads[4] = norm_back(upsampled, gain, grad_final)
    k.up[...] = grad_up
    grad_short = exact(pool_matrix((short, rows), 0, 0), grad_up)
    grad_pooled, posts = layer_back(k, 1, grad_short)
    k.pool[0:short, :] = grad_pooled
    rim2 = remote(
        k.pool.at[pl.ds(0, 8)], k.pool.at[pl.ds(short, 8)], sem(k), sem(k), (k.g, lax.rem(k.s + 15, 16))
    )

    @pl.when(k.s > 0)
    def _():
        rim2.start()

    for part in range(3):
        gj = k.hold[1].gj[:, 512 * part : 512 * part + 512]
        put_block(k, LAYER0 + LAYER_ROWS + QKV + 16 * part, dot_tn(k.hold[1].normed[...], gj))
    finish_back(k, posts)
    point(k, "b1_rim")

    @pl.when(k.s < 15)
    def _():
        rim2.wait_recv()

    @pl.when(k.s == 15)
    def _():
        k.pool[short : short + 8, :] = jnp.zeros((8, D), F32)

    @pl.when(k.s > 0)
    def _():
        rim2.wait_send()

    t = lax.broadcasted_iota(jnp.int32, (rows, short + 8), 0)
    j = lax.broadcasted_iota(jnp.int32, (rows, short + 8), 1)
    spread = jnp.where((t + 2 >= 3 * j) & (t + 2 < 3 * j + 3), 1.0, 0.0)
    grad_first = k.up[...] + exact(spread, k.pool[...] / 3.0)
    stage, posts = layer_back(k, 0, grad_first)
    k.made.add(EG)
    point(k, "b0_end")
    send_head_grads(k, stage)
    finish_back(k, posts)


def add_into(ref, other):
    ref[...] = low(ref[...].astype(F32) + other[...].astype(F32))


def reduce_piece(k, name, r0, rm, r1):
    g, z, y, x, dev, gr = k.g, k.z, k.y, k.x, k.dev, k.gr
    a, b, every = pl.ds(r0, rm - r0), pl.ds(rm, r1 - rm), pl.ds(r0, r1 - r0)
    assert k.made.issuperset(range(r0, r1, 16)), name
    sent = sem(k)
    waiting = Stage(
        k, k.rc.at[:, :, :, every], [(gr.at[1 - g, :, :, :, every], k.rc.at[:, :, :, every], dev(1 - g, z, y, x))], sent
    )
    yield
    with scope(f"rw_{name}"):
        waiting.wait()

    with scope("radd"):

        @pl.loop(0, 16)
        def _(n):
            place = (n // 4, lax.rem(n // 2, 2), lax.rem(n, 2), every)
            add_into(gr.at[(g,) + place], k.rc.at[place])

    def wait(waiting):
        with scope(f"rw_{name}"):
            waiting.wait()

    last = name in Z_FIRST
    planes, depth = (pl.ds(z, 1), 1) if last else (pl.ds(0, 4), 4)
    slots = pl.ds(0, depth)

    def plane(n):
        return z if last else n

    def across():
        waiting = Stage(
            k,
            k.r2.at[slots, :, every],
            [
                (gr.at[g, planes, :, 1 - x, a], k.r2.at[slots, :, a], dev(g, z, y, 1 - x)),
                (gr.at[g, planes, 1 - y, :, b], k.r2.at[slots, :, b], dev(g, z, 1 - y, x)),
            ],
            sent,
        )
        yield
        wait(waiting)

        @pl.loop(0, 2 * depth)
        def _(n):
            m, w = n // 2, lax.rem(n, 2)
            add_into(gr.at[g, plane(m), w, x, a], k.r2.at[m, w, a])
            if r1 > rm:
                add_into(gr.at[g, plane(m), y, w, b], k.r2.at[m, w, b])

        waiting = Stage(
            k,
            k.r1.at[slots, every],
            [
                (gr.at[g, planes, 1 - y, x, a], k.r1.at[slots, a], dev(g, z, 1 - y, x)),
                (gr.at[g, planes, y, 1 - x, b], k.r1.at[slots, b], dev(g, z, y, 1 - x)),
            ],
            sent,
        )
        yield
        wait(waiting)

        @pl.loop(0, depth)
        def _(n):
            add_into(gr.at[g, plane(n), y, x, every], k.r1.at[n, every])

    def along():
        moves = []
        for n in (2, 1, 3):
            to = lax.rem(z + n, 4)
            if last:
                moves.append((gr.at[g, to, :, :, every], k.rl.at[n - 1], dev(g, to, y, x)))
            else:
                moves.append((gr.at[g, to, y, x, every], k.rz.at[n - 1, every], dev(g, to, y, x)))
        waiting = Stage(k, k.rl if last else k.rz.at[:, every], moves, sent)
        yield
        wait(waiting)
        if last:
            for n in range(4):
                ref = gr.at[g, z, n // 2, n % 2, every]
                total = ref[...].astype(F32)
                for slot in range(3):
                    total = total + k.rl[slot, n // 2, n % 2].astype(F32)
                ref[...] = low(total)

    for way in (along, across) if last else (across, along):
        yield from way()
    if last:
        k.rz[:, every] = jnp.zeros((3, r1 - r0, D), LOW)
    k.summed.update(range(r0, r1, 16))
    yield


def own_sum(k, row, count):
    rows = pl.ds(row, count)
    v = k.gr[k.g, k.z, k.y, k.x, rows].astype(F32)
    for i in range(3):
        v = v + k.rz[i, rows].astype(F32)
    return v


def square(k, v):
    k.sq = k.sq + jnp.sum(jnp.sum(v * v, axis=1, keepdims=True), axis=0, keepdims=True)


def flush(k, name, layer=None):
    src, dst = getattr(k, "s_" + name), getattr(k, "g_" + name)
    if layer is not None:
        src, dst = src.at[layer], dst.at[layer]
    copy = pltpu.make_async_copy(src, dst, sem(k))
    copy.start()
    k.flushed.append(copy)


def store_qkv(k, layer):
    v = own_sum(k, LAYER0 + layer * LAYER_ROWS + QKV, 48)
    square(k, v)
    k.s_qkv[layer, :, 0:512] = v[0:16]
    for pair in range(4):
        row, col = 16 + 16 * (pair // 2), 256 * (pair % 2)
        even = v[row : row + 16, col : col + 128]
        odd = v[row : row + 16, col + 128 : col + 256]
        left = lanes(even.shape) < 64
        k.s_qkv[layer, :, 512 + 128 * pair : 640 + 128 * pair] = jnp.where(left, even, roll64(odd))
        k.s_qkv[layer, :, 1024 + 128 * pair : 1152 + 128 * pair] = jnp.where(left, roll64(even), odd)
    flush(k, "qkv", layer)


def store_out(k, layer):
    v = own_sum(k, LAYER0 + layer * LAYER_ROWS + OUT, 16)
    square(k, v)
    k.s_out[layer] = v
    flush(k, "out", layer)


def store_up(k, layer):
    v = own_sum(k, LAYER0 + layer * LAYER_ROWS + UP, 64)
    square(k, v)
    for j in range(4):
        k.s_up[layer, :, 512 * j : 512 * j + 512] = v[16 * j : 16 * j + 16]
    flush(k, "up", layer)


def store_down(k, layer):
    v = own_sum(k, LAYER0 + layer * LAYER_ROWS + DOWN, 64)
    square(k, v)
    k.s_down[layer] = v
    flush(k, "down", layer)


def store_rest(k):
    v = own_sum(k, EG, 16)
    square(k, v)
    k.s_embed[:, 0:256] = v[0:8, 0:256]
    k.s_embed[:, 256:512] = v[8:16, 0:256]
    k.s_head[...] = v[:, 256:512]
    flush(k, "embed")
    flush(k, "head")


def store_ready(k):
    stores = [(range(EG, EG + 16), store_rest, ())]
    for layer in range(2):
        base = LAYER0 + layer * LAYER_ROWS
        if layer == 1:
            stores.append((range(base + QKV, base + QKV + 48), store_qkv, (layer,)))
        stores.append((range(base + OUT, base + OUT + 16), store_out, (layer,)))
        stores.append((range(base + UP, base + UP + 64), store_up, (layer,)))
        stores.append((range(base + DOWN, base + DOWN + 64), store_down, (layer,)))
    for rows, store, args in stores:
        if rows.start not in k.stored and k.summed.issuperset(range(rows.start, rows.stop, 16)):
            k.stored.add(rows.start)
            store(k, *args)


def finish_grads(k):
    g = k.g
    point(k, "tail")
    for name in PIECES:
        for _ in k.reduces[name]:
            store_ready(k)
    store_ready(k)
    store_heads(k)
    lane = lanes((8, 128))
    k.stat[0] = jnp.where(lane == 0, k.sq, jnp.where(lane == 1, k.loss, 0.0))
    me = g * 16 + k.s
    sent, got = sem(k), sem(k)

    @pl.loop(1, 32)
    def _(i):
        t = lax.rem(me + i, 32)
        remote(k.stat.at[0], k.stat.at[i], sent, got, (t // 16, lax.rem(t, 16))).start()

    with scope("stats"):
        drain(got, k.stat.at[pl.ds(1, 31)])
        drain(sent, k.stat.at[pl.ds(1, 31)])
    k.stats[...] = jnp.sum(k.stat[...], axis=0)
    wait_all(k.flushed)


IN_NAMES = (
    "ids", "targets", "lengths", "w_qkv", "w_out", "w_up", "w_down", "embed", "head", "gains",
)
OUT_NAMES = ("g_qkv", "g_out", "g_up", "g_down", "g_embed", "g_head", "g_gains", "stats")
SEMS = 128


LATER = (
    "sendbox", "inbox", "dbox", "kvbox", "back", "kvback", "dkv", "dkv_out", "dkv_in", "h_hidden", "h_normed", "h_gj"
)


def scratch_shapes():
    shapes = {
        "pk": ((2, 4, 2, 2, ROWS, D), LOW),
        "gr": ((2, 4, 2, 2, ROWS, D), LOW),
        "rc": ((4, 2, 2, ROWS, D), LOW),
        "r2": ((4, 2, ROWS, D), LOW),
        "r1": ((4, ROWS, D), LOW),
        "rz": ((3, ROWS, D), LOW),
        "rl": ((3, 2, 2, max([16] + [PIECES[n][2] - PIECES[n][0] for n in Z_FIRST]), D), LOW),
        "gain": ((8, D), F32),
        "shift": ((152, D), F32),
        "pool": ((56, D), F32),
        "up": ((144, D), F32),
        "stat": ((32, 8, 128), F32),
        "columns": ((128, 256), F32),
        "headout": ((8, 16, 256), LOW),
        "wbox": ((32, 16, 256), LOW),
        "wh": ((D, 256), LOW),
        "table": ((256, D), F32),
        "normed": ((256, D), LOW),
        "hot": ((16, 144, 256), LOW),
        "q0": ((16, 144, 128), LOW),
        "kv0": ((16, 144, 128), LOW),
        "cosb": ((16, 128), F32),
        "sinb": ((16, 128), F32),
        "tgrad": ((256, D), F32),
        "gbytes": ((256, 256), F32),
        "gkv": ((1152, 128), LOW),
        "headgrad": ((32, 16, 256), LOW),
        "headgot": ((16, 16, 256), LOW),
        "headsum": ((16, 16, 256), LOW),
        "headback": ((16, 16, 256), LOW),
        "s_qkv": ((2, 16, 3 * D), F32),
        "s_out": ((2, 16, D), F32),
        "s_up": ((2, 16, 4 * D), F32),
        "s_down": ((2, 64, D), F32),
        "s_embed": ((8, D), F32),
        "s_head": ((16, 256), F32),
        "s_gains": ((5, 16), F32),
    }
    for layer in range(2):
        rows, pad = layer_sizes(layer)
        for name, shape, kind in (
            ("cos", (rows, 128), F32),
            ("sin", (rows, 128), F32),
            ("sendbox", (8, pad + rows, 128), LOW),
            ("inbox", (16, pad + rows, 128), LOW),
            ("abox", (8, pad, 128), LOW),
            ("home", (8, pad, 128), LOW),
            ("gsend", (8, pad, 128), LOW),
            ("gbox", (16, pad, 128), LOW),
            ("dbox", (8, pad, 128), LOW),
            ("kvbox", (8, rows, 128), LOW),
            ("back", (8, pad, 128), LOW),
            ("kvback", (8, rows, 128), LOW),
            ("lse", (8, rows, 128), F32),
            ("att", (8, rows, 128), F32),
            ("dkvt", (128, 16 * rows), F32),
            ("dkv", (16, rows, 128), F32),
            ("dkv_out", (8, rows, 128), F32),
            ("dkv_in", (8, rows, 128), F32),
            ("h_hidden", (rows, D), F32),
            ("h_normed", (rows, D), LOW),
            ("h_flat", (rows, D), LOW),
            ("h_middle", (rows, D), F32),
            ("h_second", (rows, D), LOW),
            ("h_pre", (rows, 4 * D), F32),
            ("h_act", (rows, 4 * D), LOW),
            ("h_gj", (rows, 3 * D), LOW),
            ("h_gpre", (rows, 4 * D), LOW),
        ):
            if layer == 1 or name not in LATER:
                shapes[name + str(layer)] = (shape, kind)
    return shapes


SCRATCH = scratch_shapes()
PER_LAYER = (
    "cos", "sin", "sendbox", "inbox", "abox", "home", "gsend", "gbox", "dbox", "back", "lse", "att", "dkvt", "dkv",
    "dkv_out", "dkv_in", "kvbox", "kvback",
)
HELD = ("hidden", "normed", "flat", "middle", "second", "pre", "act", "gj", "gpre")


def update_kernel(*refs):
    stats, sources, outs, loss_ref, norm_ref = refs[0], refs[1:29], refs[29:50], refs[50], refs[51]
    held, made, sems, out_sems = refs[52:59], refs[59:66], refs[66], refs[67]
    order = (4, 5, 6, 1, 0, 2, 3)
    for i in order:
        start_all([pltpu.make_async_copy(sources[7 * j + i], held[i].at[j], sems.at[i]) for j in range(4)])
    norm = jnp.sqrt(stats[0:1, 0:1])
    loss_ref[...] = stats[0:1, 1:2]
    norm_ref[...] = norm
    clip = jnp.minimum(1.0, CLIP_NORM / norm)
    for i in order:
        drain(sems.at[i], held[i])
        gradient, master, first, second = (held[i][j] for j in range(4))
        gradient = gradient * clip
        first = BETA_ONE * first + (1.0 - BETA_ONE) * gradient
        second = BETA_TWO * second + (1.0 - BETA_TWO) * gradient * gradient
        step = first * (1.0 / (1.0 - BETA_ONE**STEP))
        spread = jnp.sqrt(second * (1.0 / (1.0 - BETA_TWO**STEP))) + EPSILON
        results = (master - STEP_RATES[i] * (step / spread + WEIGHT_DECAYS[i] * master), first, second)
        for j in range(3):
            made[i][j] = results[j]
        start_all([pltpu.make_async_copy(made[i].at[j], outs[7 * j + i], out_sems.at[i]) for j in range(3)])
    for i in order:
        drain(out_sems.at[i], made[i])


def on_device_fast(byte_ids, targets, item_lengths, *arrays):
    masters, firsts, seconds = arrays[0:7], arrays[7:14], arrays[14:21]
    vmem, anywhere = pl.BlockSpec(memory_space=pltpu.VMEM), pl.BlockSpec(memory_space=pl.ANY)
    shard_shapes = [jax.ShapeDtypeStruct(master.shape, F32) for master in masters]
    outs = pl.pallas_call(
        kernel,
        name="step",
        out_shape=shard_shapes + [jax.ShapeDtypeStruct((8, 128), F32)],
        in_specs=[vmem, vmem, pl.BlockSpec(memory_space=pltpu.SMEM)] + [vmem] * 7,
        out_specs=[anywhere] * 7 + [vmem],
        scratch_shapes=[pltpu.VMEM(shape, kind) for shape, kind in SCRATCH.values()]
        + [pltpu.SemaphoreType.DMA((SEMS,))],
        compiler_params=pltpu.CompilerParams(collective_id=0, has_side_effects=True, vmem_limit_bytes=63 << 20),
    )(byte_ids, targets, item_lengths, *masters)
    grads, stats = outs[:7], outs[7]
    results = pl.pallas_call(
        update_kernel,
        name="update",
        out_shape=shard_shapes * 3 + [jax.ShapeDtypeStruct((1, 1), F32)] * 2,
        in_specs=[vmem] + [anywhere] * 28,
        out_specs=[anywhere] * 21 + [vmem] * 2,
        scratch_shapes=[pltpu.VMEM((count, *shard.shape), F32) for count in (4, 3) for shard in shard_shapes]
        + [pltpu.SemaphoreType.DMA((7,)), pltpu.SemaphoreType.DMA((7,))],
        compiler_params=pltpu.CompilerParams(vmem_limit_bytes=63 << 20),
    )(stats, *grads, *masters, *firsts, *seconds)
    return (results[21].reshape(()), results[22].reshape(()), *results[:21])


def solution(mesh):
    tuned = mesh.shape["dp"] == 2 and mesh.shape["seq"] == 16
    row = P(None, ("dp", "seq"), None)
    flat = P(("dp", "seq"), None)
    shards = (row, row, row, row, flat, flat, P(None, ("dp", "seq")))
    return jax.shard_map(
        on_device_fast if tuned else on_device_general,
        mesh=mesh,
        in_specs=(P("dp", "seq"), P("dp", "seq"), P("dp", None)) + shards * 3,
        out_specs=(P(), P()) + shards * 3,
        check_vma=False,
    )
```

```python
import functools

import jax
import jax.numpy as jnp
from jax import lax
from jax.experimental import pallas as pl
from jax.experimental.pallas import tpu as pltpu
from jax.sharding import PartitionSpec as P

HEADS = 8
VOCAB = 256
RATE = 3
STEP = 10

CLIP_NORM = 0.02
BETA_ONE = 0.9
BETA_TWO = 0.95
STEP_RATES = (0.03, 0.2, 0.03, 0.03, 0.6, 0.03, 0.2)
WEIGHT_DECAYS = (0.1, 0.1, 0.1, 0.1, 0.1, 0.1, 0.0)
EPSILON = 1e-08
NORM_EPS = 1e-05
MASK_FILL = -1e30


def shifted_2(value, axis, steps):
    count = lax.axis_size(axis)
    leading, last = (max(0, -steps), min(count, count - steps))
    return lax.ppermute(value, axis, [(source, source + steps) for source in range(leading, last)])


def to_low(values):
    return values.astype(jnp.bfloat16)


def layer_norm(values, gain):
    center = values - jnp.mean(values, axis=-1, keepdims=True)
    spread = jnp.mean(center * center, axis=-1, keepdims=True)
    return center * lax.rsqrt(spread + NORM_EPS) * gain


def rotate(joined, positions, num_heads):
    parts = joined.reshape(joined.shape[0], 3, num_heads, -1)
    half_size = parts.shape[-1] // 2
    freqs = 10000.0 ** (-jnp.arange(half_size, dtype=jnp.float32) / half_size)
    angles = positions.astype(jnp.float32)[:, None] * freqs[None, :]
    cosine = jnp.cos(angles)[:, None, :]
    sine = jnp.sin(angles)[:, None, :]

    def rotate_half(values):
        first_half = values[..., :half_size]
        second_half = values[..., half_size:]
        return jnp.concatenate(
            [first_half * cosine - second_half * sine, first_half * sine + second_half * cosine],
            axis=-1,
        )

    return (rotate_half(parts[:, 0]), rotate_half(parts[:, 1]), parts[:, 2])


def scores_for(q_low, k_low, query_pos, key_pos):
    scores = jnp.einsum(
        "rhe,phe->hrp", q_low, k_low, preferred_element_type=jnp.float32
    ) * q_low.shape[-1] ** (-0.5)
    causal = query_pos[:, None] >= key_pos[None, :]
    return (scores, causal)


def attend(q_low, k_low, v_low, query_pos):
    num_rows, num_heads, head_size = q_low.shape
    key_piece = (
        lax.all_gather(k_low, "seq", axis=0, tiled=True),
        lax.all_gather(v_low, "seq", axis=0, tiled=True),
    )
    running_max = jnp.full((num_heads, num_rows), MASK_FILL, jnp.float32)
    accum = jnp.zeros((num_rows, num_heads, head_size), jnp.float32)
    key_pos = jnp.arange(key_piece[0].shape[0], dtype=jnp.int32)
    scores, causal = scores_for(q_low, key_piece[0], query_pos, key_pos)
    scores = jnp.where(causal[None], scores, MASK_FILL)
    new_max = jnp.maximum(running_max, jnp.max(scores, axis=-1))
    factor = jnp.exp(running_max - new_max)
    attn_prob = jnp.where(causal[None], jnp.exp(scores - new_max[..., None]), 0.0)
    denom = jnp.sum(attn_prob, axis=-1)
    accum = accum * factor.T[:, :, None] + jnp.einsum(
        "hrp,phe->rhe", to_low(attn_prob), key_piece[1], preferred_element_type=jnp.float32
    )
    running_max, denom, accum = (new_max, denom, accum)
    return (accum / denom.T[:, :, None], (running_max + jnp.log(denom)).T)


def block_grads(q_low, grad_low, log_total, row_delta, query_pos, k_low, v_low, key_pos):
    scores, causal = scores_for(q_low, k_low, query_pos, key_pos)
    attn_prob = jnp.where(causal[None], jnp.exp(scores - log_total.T[:, :, None]), 0.0)
    grad_prob = jnp.einsum("rhe,phe->hrp", grad_low, v_low, preferred_element_type=jnp.float32)
    grad_score = to_low(attn_prob * (grad_prob - row_delta.T[:, :, None]))
    score_scale = q_low.shape[-1] ** (-0.5)
    grad_q = (
        jnp.einsum("hrp,phe->rhe", grad_score, k_low, preferred_element_type=jnp.float32)
        * score_scale
    )
    grad_k = (
        jnp.einsum("hrp,rhe->phe", grad_score, q_low, preferred_element_type=jnp.float32)
        * score_scale
    )
    grad_v = jnp.einsum(
        "hrp,rhe->phe", to_low(attn_prob), grad_low, preferred_element_type=jnp.float32
    )
    return (grad_q, grad_k, grad_v)


def attend_back(q_low, k_low, v_low, grad_low, log_total, row_delta, query_pos):
    key_piece = (
        lax.all_gather(k_low, "seq", axis=0, tiled=True),
        lax.all_gather(v_low, "seq", axis=0, tiled=True),
    )
    key_pos = jnp.arange(key_piece[0].shape[0], dtype=jnp.int32)
    grad_q = block_grads(
        q_low, grad_low, log_total, row_delta, query_pos, key_piece[0], key_piece[1], key_pos
    )[0]
    all_totals, all_deltas = (
        lax.all_gather(log_total, "seq", axis=0, tiled=True),
        lax.all_gather(row_delta, "seq", axis=0, tiled=True),
    )
    query_piece = (
        lax.all_gather(q_low, "seq", axis=0, tiled=True),
        lax.all_gather(grad_low, "seq", axis=0, tiled=True),
    )
    piece_rows = query_piece[0].shape[0]
    piece_pos = jnp.arange(piece_rows, dtype=jnp.int32)
    unused_q, grad_k_blk, grad_v_blk = block_grads(
        query_piece[0], query_piece[1], all_totals, all_deltas, piece_pos, k_low, v_low, query_pos
    )
    return (grad_q, grad_k_blk, grad_v_blk)


def layer_forward(hidden, weights, gain_pair, positions):
    w_joined, w_proj, w_rise, w_fall = weights
    num_rows = hidden.shape[0]
    normed = to_low(layer_norm(hidden, gain_pair[0]))
    joined = jnp.dot(normed, w_joined, preferred_element_type=jnp.float32)
    queries, keys, values = rotate(joined, positions, HEADS)
    q_low, k_low, v_low = (to_low(queries), to_low(keys), to_low(values))
    attended, log_total = attend(q_low, k_low, v_low, positions)
    flat_low = to_low(attended.reshape(num_rows, -1))
    middle = hidden + jnp.dot(flat_low, w_proj, preferred_element_type=jnp.float32)
    second = to_low(layer_norm(middle, gain_pair[1]))
    pre_act = jnp.dot(second, w_rise, preferred_element_type=jnp.float32)
    activated = to_low(jax.nn.gelu(pre_act))
    output = middle + jnp.dot(activated, w_fall, preferred_element_type=jnp.float32)
    saved = (
        normed,
        joined,
        q_low,
        k_low,
        v_low,
        attended,
        log_total,
        flat_low,
        middle,
        second,
        pre_act,
        activated,
    )
    return (output, saved)


def layer_backward(hidden, weights, gain_pair, positions, grad_out):
    w_joined, w_proj, w_rise, w_fall = weights
    unused_out, saved = layer_forward(hidden, weights, gain_pair, positions)
    (
        normed,
        joined,
        q_low,
        k_low,
        v_low,
        attended,
        log_total,
        flat_low,
        middle,
        second,
        pre_act,
        activated,
    ) = saved
    fall_low = to_low(grad_out)
    grad_fall = jnp.dot(activated.T, fall_low, preferred_element_type=jnp.float32)
    grad_act = jnp.dot(fall_low, w_fall.T, preferred_element_type=jnp.float32)
    grad_pre = to_low(jax.vjp(jax.nn.gelu, pre_act)[1](grad_act)[0])
    grad_rise = jnp.dot(second.T, grad_pre, preferred_element_type=jnp.float32)
    grad_second = jnp.dot(grad_pre, w_rise.T, preferred_element_type=jnp.float32)
    grad_middle_n, grad_gain_ffn = jax.vjp(layer_norm, middle, gain_pair[1])[1](grad_second)
    grad_middle = grad_out + grad_middle_n
    proj_low = to_low(grad_middle)
    grad_proj = jnp.dot(flat_low.T, proj_low, preferred_element_type=jnp.float32)
    grad_att = to_low(
        jnp.dot(proj_low, w_proj.T, preferred_element_type=jnp.float32).reshape(attended.shape)
    )
    row_delta = jnp.sum(grad_att.astype(jnp.float32) * attended, axis=-1)
    grad_q, grad_k, grad_v = attend_back(
        q_low, k_low, v_low, grad_att, log_total, row_delta, positions
    )

    def rotate_joined(joined_in):
        return rotate(joined_in, positions, HEADS)

    grad_joined = to_low(jax.vjp(rotate_joined, joined)[1]((grad_q, grad_k, grad_v))[0])
    grad_w_joined = jnp.dot(normed.T, grad_joined, preferred_element_type=jnp.float32)
    grad_normed = jnp.dot(grad_joined, w_joined.T, preferred_element_type=jnp.float32)
    grad_in_n, grad_gain_attn = jax.vjp(layer_norm, hidden, gain_pair[0])[1](grad_normed)
    return (
        grad_middle + grad_in_n,
        (grad_w_joined, grad_proj, grad_rise, grad_fall),
        jnp.stack([grad_gain_attn, grad_gain_ffn]),
    )


def adam_update(weight, gradient, moment_one, moment_two, step_rate, decay_rate):
    moment_one = BETA_ONE * moment_one + (1.0 - BETA_ONE) * gradient
    moment_two = BETA_TWO * moment_two + (1.0 - BETA_TWO) * gradient * gradient
    first_hat = moment_one / (1.0 - BETA_ONE**STEP)
    second_hat = moment_two / (1.0 - BETA_TWO**STEP)
    weight = weight - step_rate * (
        first_hat / (jnp.sqrt(second_hat) + EPSILON) + decay_rate * weight
    )
    return (weight, moment_one, moment_two)


def on_device_general(
    byte_ids,
    targets,
    item_lengths,
    w_qkv,
    w_out,
    w_up,
    w_down,
    embed,
    head,
    gains,
    mom_qkv,
    mom_out,
    mom_up,
    mom_down,
    mom_embed,
    mom_head,
    mom_gains,
    sec_qkv,
    sec_out,
    sec_up,
    sec_down,
    sec_embed,
    sec_head,
    sec_gains,
):
    low_qkv, low_out, low_up, low_down, low_embed, low_head, low_gains = (
        lax.all_gather(to_low(w_qkv), ("dp", "seq"), axis=1, tiled=True),
        lax.all_gather(to_low(w_out), ("dp", "seq"), axis=1, tiled=True),
        lax.all_gather(to_low(w_up), ("dp", "seq"), axis=1, tiled=True),
        lax.all_gather(to_low(w_down), ("dp", "seq"), axis=1, tiled=True),
        lax.all_gather(to_low(embed), ("dp", "seq"), axis=0, tiled=True),
        lax.all_gather(to_low(head), ("dp", "seq"), axis=0, tiled=True),
        lax.all_gather(to_low(gains), ("dp", "seq"), axis=1, tiled=True),
    )
    gain_rows = low_gains.astype(jnp.float32)
    byte_row = byte_ids[0]
    num_rows = byte_row.shape[0]
    short_rows = num_rows // RATE
    seq_place = lax.axis_index("seq")
    positions = seq_place * num_rows + jnp.arange(num_rows, dtype=jnp.int32)
    short_pos = seq_place * short_rows + jnp.arange(short_rows, dtype=jnp.int32)
    vocab_ids = jnp.arange(VOCAB, dtype=jnp.int32)
    one_hot_in = (byte_row[:, None] == vocab_ids[None, :]).astype(jnp.float32)
    embedded = jnp.dot(
        one_hot_in.astype(jnp.bfloat16), low_embed, preferred_element_type=jnp.float32
    )
    lower_weights = (low_qkv[0], low_out[0], low_up[0], low_down[0])
    upper_weights = (low_qkv[1], low_out[1], low_up[1], low_down[1])
    first_out, unused_first = layer_forward(embedded, lower_weights, gain_rows[0:2], positions)
    left_rim = shifted_2(first_out[num_rows - RATE + 1 :], "seq", 1)
    shifted = jnp.concatenate([left_rim, first_out[: num_rows - RATE + 1]], axis=0)
    pooled = jnp.mean(shifted.reshape(short_rows, RATE, -1), axis=1)
    short_out, unused_short = layer_forward(pooled, upper_weights, gain_rows[2:4], short_pos)
    upsampled = first_out + jnp.repeat(short_out, RATE, axis=0)
    top_gain = gain_rows[gain_rows.shape[0] - 1]
    final_low = to_low(layer_norm(upsampled, top_gain))
    logits = jnp.dot(final_low, low_head, preferred_element_type=jnp.float32)
    row_max = jnp.max(logits, axis=-1, keepdims=True)
    log_total = row_max[:, 0] + jnp.log(jnp.sum(jnp.exp(logits - row_max), axis=-1))
    one_hot_out = (targets[0][:, None] == vocab_ids[None, :]).astype(jnp.float32)
    picked = jnp.sum(one_hot_out * logits, axis=-1)
    lengths = item_lengths[0]
    ends = jnp.cumsum(lengths)
    doc_index = jnp.sum((positions[:, None] >= ends[None, :]).astype(jnp.int32), axis=1)
    item_ids = jnp.arange(lengths.shape[0], dtype=jnp.int32)
    doc_length = jnp.sum(
        jnp.where(item_ids[None, :] == doc_index[:, None], lengths[None, :], 0), axis=1
    ).astype(jnp.float32)
    loss_local = jnp.sum((log_total - picked) / doc_length)
    loss_sum = lax.psum(loss_local, ("dp", "seq"))
    grad_logits = to_low((jnp.exp(logits - log_total[:, None]) - one_hot_out) / doc_length[:, None])
    grad_head = jnp.dot(final_low.T, grad_logits, preferred_element_type=jnp.float32)
    grad_final = jnp.dot(grad_logits, low_head.T, preferred_element_type=jnp.float32)
    grad_upsampled, grad_gain_top = jax.vjp(layer_norm, upsampled, top_gain)[1](grad_final)
    grad_short = jnp.sum(grad_upsampled.reshape(short_rows, RATE, -1), axis=1)
    grad_pooled, upper_grads, upper_gain_grads = layer_backward(
        pooled, upper_weights, gain_rows[2:4], short_pos, grad_short
    )
    grad_shifted = jnp.repeat(grad_pooled / RATE, RATE, axis=0)
    rim_grad = shifted_2(grad_shifted[: RATE - 1], "seq", -1)
    grad_first = grad_upsampled + jnp.concatenate([grad_shifted[RATE - 1 :], rim_grad], axis=0)
    grad_embedded, lower_grads, lower_gain_grads = layer_backward(
        embedded, lower_weights, gain_rows[0:2], positions, grad_first
    )
    grad_embed = jnp.dot(one_hot_in.T, grad_embedded, precision=lax.Precision.HIGHEST)
    grad_gains = jnp.concatenate(
        [lower_gain_grads, upper_gain_grads, grad_gain_top[None, :]], axis=0
    )
    shard_grads = (
        lax.psum_scatter(
            jnp.stack([lower_grads[0], upper_grads[0]]),
            ("dp", "seq"),
            scatter_dimension=1,
            tiled=True,
        ),
        lax.psum_scatter(
            jnp.stack([lower_grads[1], upper_grads[1]]),
            ("dp", "seq"),
            scatter_dimension=1,
            tiled=True,
        ),
        lax.psum_scatter(
            jnp.stack([lower_grads[2], upper_grads[2]]),
            ("dp", "seq"),
            scatter_dimension=1,
            tiled=True,
        ),
        lax.psum_scatter(
            jnp.stack([lower_grads[3], upper_grads[3]]),
            ("dp", "seq"),
            scatter_dimension=1,
            tiled=True,
        ),
        lax.psum_scatter(grad_embed, ("dp", "seq"), scatter_dimension=0, tiled=True),
        lax.psum_scatter(grad_head, ("dp", "seq"), scatter_dimension=0, tiled=True),
        lax.psum_scatter(grad_gains, ("dp", "seq"), scatter_dimension=1, tiled=True),
    )
    squares = sum((jnp.sum(piece_grad * piece_grad) for piece_grad in shard_grads))
    total_squares = lax.psum(squares, ("dp", "seq"))
    grad_norm = jnp.sqrt(total_squares)
    clip_factor = jnp.minimum(1.0, CLIP_NORM / grad_norm)
    masters = (w_qkv, w_out, w_up, w_down, embed, head, gains)
    firsts = (mom_qkv, mom_out, mom_up, mom_down, mom_embed, mom_head, mom_gains)
    seconds = (sec_qkv, sec_out, sec_up, sec_down, sec_embed, sec_head, sec_gains)
    results = []
    for slot_index in range(7):
        results.append(
            adam_update(
                masters[slot_index],
                shard_grads[slot_index] * clip_factor,
                firsts[slot_index],
                seconds[slot_index],
                STEP_RATES[slot_index],
                WEIGHT_DECAYS[slot_index],
            )
        )
    return (
        loss_sum,
        grad_norm,
        results[0][0],
        results[1][0],
        results[2][0],
        results[3][0],
        results[4][0],
        results[5][0],
        results[6][0],
        results[0][1],
        results[1][1],
        results[2][1],
        results[3][1],
        results[4][1],
        results[5][1],
        results[6][1],
        results[0][2],
        results[1][2],
        results[2][2],
        results[3][2],
        results[4][2],
        results[5][2],
        results[6][2],
    )


LOW = jnp.bfloat16
F32 = jnp.float32
MESH = pl.DeviceIdType.MESH
D = 512

EG, LAYER0, LAYER_ROWS = 0, -32, 192
QKV, OUT, UP, DOWN = 0, 48, 64, 128
ROWS = LAYER0 + 2 * LAYER_ROWS
PIECES = {
    "A": (0, 16, 16),
    "B": (16, 32, 64),
    "E": (64, 80, 96),
    "b": (96, 128, 160),
    "C": (160, 192, 224),
    "D": (224, 256, 288),
    "d": (288, 304, 320),
    "h": (320, 336, 352),
}
Z_LAST, Z_FIRST = "h", "h"
(
    START,
    HEADS,
    F0_HEADS,
    F0_GOT,
    F0_MID0,
    F0_MID1,
    F0_PART0,
    F0_PART1,
    F0_HOME,
    F0_UP,
    F0_RIM,
    F0_END,
    F1_SENT,
    F1_TAKE,
    F1_GOT,
    F1_PART0,
    F1_HOME,
    F1_OUT,
    F1_UP,
    B1_FF,
    B1_SENT,
    B1_PART0,
    B1_SUMS,
    B1_HOME,
    B1_RIM,
    B0_FF,
    B0_SENT,
    B0_MID0,
    B0_MID1,
    B0_PART0,
    B0_PART1,
    B0_KEYS0,
    B0_KEYS1,
    B0_END,
    TAIL,
) = range(35)
SCHEDULE = {
    START: "AbhBh",
    HEADS: "AbABCb",
    F0_HEADS: "EDAB",
    F0_GOT: "E",
    F0_MID0: "C",
    F0_PART0: "d",
    F0_MID1: "bE",
    F0_PART1: "hCBE",
    F0_HOME: "d",
    F0_RIM: "DCd",
    F1_SENT: "Dh",
    F1_TAKE: "d",
    F1_PART0: "D",
    B1_FF: "D",
    B1_SENT: "hD",
    B1_PART0: "d",
    B1_SUMS: "dDh",
    B1_RIM: "CdC",
    B0_FF: "bhBDb",
    B0_SENT: "EdC",
    B0_PART1: "E",
    B0_KEYS1: "b",
    B0_MID0: "C",
    B0_PART0: "B",
    B0_END: "AEb",
    TAIL: "ABEABh",
}


def dot(a, b):
    return jnp.dot(a, b, preferred_element_type=F32)


def dot_nt(a, b):
    return lax.dot_general(a, b, (((1,), (1,)), ((), ())), preferred_element_type=F32)


def dot_tn(a, b):
    return lax.dot_general(a, b, (((0,), (0,)), ((), ())), preferred_element_type=F32)


def low(v):
    return v.astype(LOW)


exact = functools.partial(jnp.dot, preferred_element_type=F32, precision=lax.Precision.HIGHEST)


def lanes(shape):
    return lax.broadcasted_iota(jnp.int32, shape, len(shape) - 1)


def roll64(v):
    return pltpu.roll(v, 64, 1)


def swap32(v):
    return jnp.where(lanes(v.shape) % 64 < 32, pltpu.roll(v, 96, 1), pltpu.roll(v, 32, 1))


def norm_parts(v):
    center = v - jnp.mean(v, axis=-1, keepdims=True)
    scale = lax.rsqrt(jnp.mean(center * center, axis=-1, keepdims=True) + NORM_EPS)
    return center * scale, scale


def norm_back(v, gain, grad):
    unit, scale = norm_parts(v)
    g = grad * gain
    out = scale * (g - jnp.mean(g, axis=-1, keepdims=True) - unit * jnp.mean(g * unit, axis=-1, keepdims=True))
    return out, jnp.sum(grad * unit, axis=0, keepdims=True)


GELU_A, GELU_B = 0.7978845608028654, 0.044715


def gelu(v):
    return 0.5 * v * (1.0 + jnp.tanh(GELU_A * (v + GELU_B * v * v * v)))


def gelu_grad(v):
    t = jnp.tanh(GELU_A * (v + GELU_B * v * v * v))
    return 0.5 * (1.0 + t) + 0.5 * v * (1.0 - t * t) * (GELU_A * (1.0 + 3.0 * GELU_B * v * v))


class Bag:
    pass


def remote(src, dst, send, recv, device):
    return pltpu.make_async_remote_copy(
        src_ref=src, dst_ref=dst, send_sem=send, recv_sem=recv, device_id=device, device_id_type=MESH
    )


def pack_pair(block, odd):
    half = block.shape[0] // 2
    top, bottom = block[:half], block[half:]
    if odd:
        top = roll64(top)
    else:
        bottom = roll64(bottom)
    return jnp.where(lanes(top.shape) < 64, top, bottom)


def unpack_pair(even, odd):
    left = lanes(even.shape) < 64
    top = jnp.where(left, even, roll64(odd))
    bottom = jnp.where(left, roll64(even), odd)
    return jnp.concatenate([top, bottom], axis=0)


def unpack_left(x):
    left = lanes(x.shape) < 64
    return jnp.concatenate([jnp.where(left, x, 0.0), jnp.where(left, roll64(x), 0.0)], axis=0)


def unpack_right(x):
    left = lanes(x.shape) < 64
    return jnp.concatenate([jnp.where(left, 0.0, roll64(x)), jnp.where(left, 0.0, x)], axis=0)


def pack_left(x):
    half = x.shape[0] // 2
    return jnp.where(lanes((half, 128)) < 64, x[:half], roll64(x[half:]))


def pack_right(x):
    half = x.shape[0] // 2
    return jnp.where(lanes((half, 128)) < 64, roll64(x[:half]), x[half:])


def kernel(*refs):
    k = Bag()
    names = IN_NAMES + OUT_NAMES + tuple(SCRATCH)
    for name, ref in zip(names, refs[:-1]):
        setattr(k, name, ref)
    k.sems = refs[-1]
    for name in PER_LAYER:
        setattr(k, name, [getattr(k, name + "0", None), getattr(k, name + "1")])
    k.hold = []
    for layer in range(2):
        hold = Bag()
        for name in HELD:
            setattr(hold, name, getattr(k, "h_" + name + str(layer), None))
        k.hold.append(hold)
    g = lax.axis_index("dp")
    s = lax.axis_index("seq")
    z, y, x = s // 4, lax.rem(s // 2, 2), lax.rem(s, 2)
    k.g, k.s, k.z, k.y, k.x = g, s, z, y, x
    k.side = lax.rem(x + y, 2)
    k.cursor = 0

    def dev(g, z, y, x):
        return (g, z * 4 + y * 2 + x)

    k.dev = dev

    barrier = pltpu.get_barrier_semaphore()
    me = g * 16 + s

    @pl.loop(1, 32)
    def _(i):
        t = lax.rem(me + i, 32)
        pl.semaphore_signal(barrier, inc=1, device_id=(t // 16, lax.rem(t, 16)), device_id_type=MESH)

    own = k.pk.at[g, z, y, x]
    own[EG : EG + 16, 0:256] = low(jnp.concatenate([k.embed[:, 0:256], k.embed[:, 256:512]], axis=0))
    own[EG : EG + 16, 256:512] = low(k.head[...])
    k.columns[0:1, 0:144] = k.ids[...].astype(F32)
    k.columns[1:2, 0:144] = k.targets[...].astype(F32)
    pack_heads(k)
    pack_layer(k, own, 0)
    pack_layer(k, own, 1)
    pl.semaphore_wait(barrier, 31)
    k.gathers = {name: gather_piece(k, name, *rows) for name, rows in PIECES.items()}
    k.reduces = {name: reduce_piece(k, name, *rows) for name, rows in PIECES.items()}
    k.made, k.summed, k.stored = set(), set(), set()
    k.flushed, k.sq = [], jnp.zeros((1, 1), F32)
    point(k, START)
    spread_heads(k)
    point(k, HEADS)
    forward_backward(k)
    finish_grads(k)


def point(k, name):
    coming = name < B1_FF
    for piece in SCHEDULE.get(name, ""):
        next((k.gathers if coming else k.reduces)[piece], None)
        if not coming:
            store_ready(k)


def touching(rows):
    return [name for name, (r0, _, r1) in PIECES.items() if r0 < rows.stop and r1 > rows.start]


def pair_kv(keys, vals):
    left = lanes(keys.shape) < 64
    return jnp.where(left, keys, roll64(vals)), jnp.where(left, roll64(keys), vals)


def pack_heads(k):
    row, lane = lax.broadcasted_iota(jnp.int32, (16, 128), 0), lanes((16, 128))
    place = lanes((16, 128)) - 64 == lax.broadcasted_iota(jnp.int32, (16, 128), 0)
    gains = exact(k.gains[...], jnp.where(place, 1.0, 0.0))
    ids = jnp.concatenate([gains, jnp.zeros((3, 128), F32), jnp.zeros((8, 128), F32)], axis=0)
    for j in range(3):
        part = pltpu.roll(k.columns[0:8, :], (64 - 48 * j) % 256, 1)[0:1, 0:128]
        ids = jnp.where((row == 8 + j) & (lane >= 64) & (lane < 112), part, ids)
    for pair in range(4):
        query = k.w_qkv[0, :, 128 * pair : 128 * pair + 128]
        keys = k.w_qkv[0, :, 512 + 128 * pair : 640 + 128 * pair]
        vals = k.w_qkv[0, :, 1024 + 128 * pair : 1152 + 128 * pair]
        for odd, kv in enumerate(pair_kv(keys, vals)):
            k.headout[2 * pair + odd, :, 0:128] = low(jnp.where(lane < 64, roll64(query) if odd else query, ids))
            k.headout[2 * pair + odd, :, 128:256] = low(kv)


def around(k, source, target, sent, got):
    for n in range(1, 16):
        c = lax.rem(k.s + n, 16)
        remote(source(c), target(k.s), sent, got, (k.g, c)).start()


def spread_heads(k):
    mine = k.g * 16 + k.s
    k.wbox[mine] = k.headout[lax.rem(k.s, 8)]
    k.head_sems = [sem(k), sem(k)]
    around(k, lambda c: k.headout.at[lax.rem(c, 8)], lambda c: k.wbox.at[k.g * 16 + c], *k.head_sems)


def take_heads(k):
    for semaphore in k.head_sems:
        drain(semaphore, k.wbox.at[pl.ds(0, 15)])
    share = k.wbox.at[pl.ds(16 * k.g, 16)]
    return Stage(k, share, [(share, share, k.dev(1 - k.g, k.z, k.y, k.x))])


def block_tables(k, b):
    cos_b, sin_b = k.cosb[pl.ds(b, 1), :], k.sinb[pl.ds(b, 1), :]
    cos_r, sin_r = k.cos[0][...], k.sin[0][...]
    return cos_b * cos_r - sin_b * sin_r, sin_b * cos_r + cos_b * sin_r


def kv_tables(cosine, sine):
    left = lanes(cosine.shape) < 64
    return jnp.where(left, cosine, 1.0), jnp.where(left, sine, 0.0)


def lane_copies(shape, axis):
    narrow = lax.broadcasted_iota(jnp.int32, shape, axis)
    wide = lax.broadcasted_iota(jnp.int32, shape, 1 - axis)
    return jnp.where(narrow - 64 == wide % 16, 1.0, 0.0)


def device_lanes():
    shape = (32, 8, 512)
    return lanes(shape) // 16 == lax.broadcasted_iota(jnp.int32, shape, 0)


def byte_rows(k):
    need(k, EG)
    packed = k.pk[:, :, :, :, EG : EG + 16, 0:256].astype(F32).reshape(32, 16, 256)
    gains = low(k.wbox[...].astype(F32)[:, 0:8, 0:128].reshape(256, 128))
    gains = dot(gains, low(lane_copies((128, 512), 0))).reshape(32, 8, 512)
    k.gain[...] = jnp.sum(jnp.where(device_lanes(), gains, 0.0), axis=0)
    table = jnp.concatenate(
        [packed[:, 0:8].reshape(256, 256), packed[:, 8:16].reshape(256, 256)], axis=1
    )
    k.table[...] = table
    unit, _ = norm_parts(table)
    k.normed[...] = low(unit * k.gain[0:1, :])


def head_rows(k):
    group = k.s // 8
    for b in range(16):
        k.columns[16 + 4 * b : 20 + 4 * b, 0:128] = k.wbox[group * 16 + b].astype(F32)[8:12, 0:128]
    columns = k.columns[...].T
    weights = k.wbox[...].astype(F32).reshape(512, 256)
    lane = lanes(weights.shape)
    k.wh[...] = low(jnp.where((lane >= 64) & (lane < 128), 0.0, weights))
    joined = dot(k.normed[...], k.wh[...])
    high = low(joined)
    rest = low(joined - high.astype(F32))
    for b in range(16):
        ids = [columns[64:112, 16 + 4 * b + j : 17 + 4 * b + j] for j in range(3)]
        hot = byte_matrix(jnp.concatenate(ids, axis=0).astype(jnp.int32))
        k.hot[b] = hot
        rows = dot(hot, high) + dot(hot, rest)
        cosine, sine = block_tables(k, b)
        k.q0[b] = low(rotate_block(rows[:, 0:128], cosine, sine) * 0.125)
        k.kv0[b] = low(rotate_block(rows[:, 128:256], *kv_tables(cosine, sine)))


def pack_layer(k, own, layer):
    base = LAYER0 + layer * LAYER_ROWS
    if layer == 1:
        own[base + QKV : base + QKV + 16, :] = low(k.w_qkv[layer, :, 0:512])
        for pair in range(4):
            keys = k.w_qkv[layer, :, 512 + 128 * pair : 640 + 128 * pair]
            vals = k.w_qkv[layer, :, 1024 + 128 * pair : 1152 + 128 * pair]
            row = base + QKV + 16 + 16 * (pair // 2)
            for odd, kv in enumerate(pair_kv(keys, vals)):
                col = 256 * (pair % 2) + 128 * odd
                own[row : row + 16, col : col + 128] = low(kv)
    own[base + OUT : base + OUT + 16, :] = low(k.w_out[layer])
    for j in range(4):
        own[base + UP + 16 * j : base + UP + 16 * j + 16, :] = low(k.w_up[layer, :, 512 * j : 512 * j + 512])
    own[base + DOWN : base + DOWN + 64, :] = low(k.w_down[layer])


def sem(k):
    k.cursor += 1
    assert k.cursor <= SEMS
    return k.sems.at[k.cursor - 1]


def start_all(copies):
    for copy in copies:
        copy.start()


def wait_all(copies):
    for copy in copies:
        copy.wait()


def drain(semaphore, ref):
    pltpu.make_async_copy(ref, ref, semaphore).wait()


class Stage:
    def __init__(self, k, total, moves, sent=None):
        self.total, self.sent, self.got = total, sem(k) if sent is None else sent, sem(k)
        start_all([remote(src, dst, self.sent, self.got, device) for src, dst, device in moves if src.shape[-2]])

    def wait(self):
        drain(self.got, self.total)
        drain(self.sent, self.total)


def gather_piece(k, name, r0, rm, r1):
    g, z, y, x, dev, pk = k.g, k.z, k.y, k.x, k.dev, k.pk
    a, b, every = pl.ds(r0, rm - r0), pl.ds(rm, r1 - rm), pl.ds(r0, r1 - r0)

    sent = sem(k)

    def stage(total, *moves):
        return Stage(k, total, [(ref, ref, device) for ref, device in moves], sent)

    def wait(waiting):
        waiting.wait()

    planes = pl.ds(z, 1) if name in Z_LAST else pl.ds(0, 4)

    def across():
        waiting = stage(
            pk.at[g, planes, y, x, every],
            (pk.at[g, planes, y, x, a], dev(g, z, 1 - y, x)),
            (pk.at[g, planes, y, x, b], dev(g, z, y, 1 - x)),
        )
        yield
        wait(waiting)
        waiting = stage(
            pk.at[g, planes, :, x, every],
            (pk.at[g, planes, :, x, a], dev(g, z, y, 1 - x)),
            (pk.at[g, planes, y, :, b], dev(g, z, 1 - y, x)),
        )
        yield
        wait(waiting)

    def along():
        def part(n):
            return pk.at[g, n, :, :, every] if name in Z_LAST else pk.at[g, n, y, x, every]

        waiting = stage(part(pl.ds(0, 3)), *[(part(z), dev(g, lax.rem(z + n, 4), y, x)) for n in (2, 1, 3)])
        yield
        wait(waiting)

    for way in (across, along) if name in Z_LAST else (along, across):
        yield from way()
    waiting = stage(pk.at[1 - g, :, :, :, every], (pk.at[g, :, :, :, every], dev(1 - g, z, y, x)))
    yield
    wait(waiting)
    yield


def need(k, row, count=16):
    for name in touching(range(row, row + count)):
        for _ in k.gathers[name]:
            pass


def block(k, row):
    need(k, row)
    return k.pk[:, :, :, :, row : row + 16, :].reshape(512, 512)


def put_block(k, row, value):
    k.made.add(row)
    k.gr[:, :, :, :, row : row + 16, :] = low(value).reshape(2, 4, 2, 2, 16, 512)


def down_block(k, row, c):
    need(k, row, 64)
    return k.pk[c // 2, (c % 2) * 2 : (c % 2) * 2 + 2, :, :, row : row + 64, :].reshape(512, 512)


def put_down(k, row, c, value):
    if c == 3:
        k.made.update(range(row, row + 64, 16))
    k.gr[c // 2, (c % 2) * 2 : (c % 2) * 2 + 2, :, :, row : row + 64, :] = low(value).reshape(2, 2, 2, 64, 512)


def my_blocks(k):
    return [4 * j + (k.g if half == 0 else 3 - k.g) for j in range(4) for half in range(2)]


def other_blocks(k):
    return [4 * j + (1 - k.g if half == 0 else 2 + k.g) for j in range(4) for half in range(2)]


def my_block(k, i):
    return 4 * (i // 2) + jnp.where(lax.rem(i, 2) == 0, k.g, 3 - k.g)


class Post:
    def __init__(self, k, source, groups):
        self.k, self.source = k, source
        self.sent, self.got = sem(k), [sem(k) for _ in range(groups)]

    def start(self, src, dst, got, device):
        k = self.k
        is_self = jnp.logical_and(device[0] == k.g, device[1] == k.s)

        @pl.when(is_self)
        def _():
            pltpu.make_async_copy(src, dst, got).start()

        @pl.when(jnp.logical_not(is_self))
        def _():
            remote(src, dst, self.sent, got, device).start()

    def finish(self, one_is_self):
        @pl.when(one_is_self)
        def _():
            drain(self.sent, self.source.at[pl.ds(0, 7)])

        @pl.when(jnp.logical_not(one_is_self))
        def _():
            drain(self.sent, self.source)


class ToHeads(Post):
    def __init__(self, k, source, target):
        super().__init__(k, source, 2)
        self.target = target

    def send(self):
        k = self.k
        for part in range(2):

            @pl.when(k.s // 8 == part)
            def _():
                for i in range(8):
                    h = lax.rem(k.s + i, 8)
                    self.start(self.source.at[h], self.target.at[k.s], self.got[part], (k.side, k.g * 8 + h))

    def take(self, part):
        drain(self.got[part], self.target.at[pl.ds(0, 4)])

    def done(self):
        k = self.k
        self.finish(jnp.logical_and(k.s // 8 == k.g, k.side == k.g))


class FromHeads(Post):
    def __init__(self, k, source, target):
        super().__init__(k, source, 1)
        self.target = target

    def send(self, i, b):
        k = self.k
        head = lax.rem(k.s, 8)
        self.start(self.source.at[i], self.target.at[head], self.got[0], (k.s // 8, b))

    def take(self):
        drain(self.got[0], self.target)

    def done(self):
        k = self.k
        self.finish(jnp.logical_and(k.s // 8 == k.g, k.side == k.g))


def rotate_block(v, cosine, sine):
    return v * cosine + swap32(v) * sine


def rotary_tables(k):
    lane = lanes((1, 128))
    freqs = jnp.zeros((1, 128), F32)
    for i in range(32):
        freqs = jnp.where(lane % 32 == i, 10000.0 ** (-i / 32), freqs)
    sign = jnp.where(lane % 64 < 32, -1.0, 1.0)
    rows, short = layer_sizes(0)[0], layer_sizes(1)[0]
    for cos, sin, count, first, step in (
        (k.cos[0], k.sin[0], rows, 0, 1),
        (k.cosb, k.sinb, 16, 0, rows),
        (k.cos[1], k.sin[1], short, k.s * short, 1),
    ):
        angles = (first + step * lax.broadcasted_iota(jnp.int32, (count, 1), 0)).astype(F32) * freqs
        cos[...] = jnp.cos(angles)
        sin[...] = jnp.sin(angles) * sign


def layer_sizes(layer):
    rows = 144 if layer == 0 else 48
    return rows, (rows // 2 + 15) // 16 * 16


def attend_loop(layer, part, body, between=None):
    if layer == 1:
        body(list(range(8)), 16)
        return
    for first in (0, 2):
        @pl.loop(first, first + 2)
        def _(n):
            body([part * 4 + n], 8 * part + 4 + 2 * first)

        if between is not None and first == 0:
            between()


def stack(pieces):
    return pieces[0] if len(pieces) == 1 else jnp.concatenate(pieces, axis=0)


def masked_scores(q, kv, places, plain):
    scores = dot_nt(q, kv)
    plain = plain // 128 * 128
    rest = scores[:, plain:]
    rest = jnp.where(lanes(rest.shape) + plain <= places, rest, MASK_FILL)
    return jnp.concatenate([scores[:, :plain], rest], axis=1) if plain else rest


def stacked_queries(k, layer, items):
    rows, pad = layer_sizes(layer)
    blocks = [my_block(k, i) for i in items]
    places = stack([b * rows + lax.broadcasted_iota(jnp.int32, (rows, 1), 0) for b in blocks])
    if layer == 0:
        return stack([k.q0[b] for b in blocks]), blocks, places
    q = stack([unpack_left(k.inbox[layer][b, 0:pad, :].astype(F32)[: rows // 2]) for b in blocks])
    return low(q * 0.125), blocks, places


def stacked_keys(k, layer, count):
    rows, pad = layer_sizes(layer)
    if layer == 0:
        return k.kv0[0:count].reshape(count * rows, 128)
    return k.inbox[layer][0:count, pad : pad + rows, :].reshape(count * rows, 128)


def attention_forward(k, layer, part, post, between):
    rows, pad = layer_sizes(layer)
    outbox, lse, keep = k.abox[layer], k.lse[layer], k.att[layer]

    def body(items, count):
        q, blocks, places = stacked_queries(k, layer, items)
        kv = stacked_keys(k, layer, count)
        scores = masked_scores(q, kv, places, 0 if layer == 1 else (count - 4) * rows)
        top = jnp.max(scores, axis=-1, keepdims=True)
        prob = jnp.exp(scores - top)
        total = jnp.sum(prob, axis=-1, keepdims=True)
        out = dot(low(prob), kv) / total
        stat = jnp.broadcast_to(top + jnp.log(total), out.shape)
        for n, (i, b) in enumerate(zip(items, blocks)):
            span = slice(n * rows, (n + 1) * rows)
            lse[i] = stat[span]
            keep[i] = out[span]
            outbox[i, 0 : rows // 2, :] = low(pack_right(out[span]))
            post.send(i, b)

    attend_loop(layer, part, body, between)


def attention_backward(k, layer, part, post, between=None):
    rows, pad = layer_sizes(layer)
    gradbox, lse, keep = k.gbox[layer], k.lse[layer], k.att[layer]
    dkvt, outbox = k.dkvt[layer], k.dbox[layer]

    def body(items, count):
        q, blocks, places = stacked_queries(k, layer, items)
        kv = stacked_keys(k, layer, count)
        grad = stack([unpack_right(gradbox[b].astype(F32)[: rows // 2]) for b in blocks])
        delta = jnp.sum(grad * stack([keep[i] for i in items]), axis=-1, keepdims=True)
        grad = low(grad)
        prob = jnp.exp(masked_scores(q, kv, places, 0 if layer == 1 else (count - 4) * rows) - stack([lse[i] for i in items])[:, 0:1])
        grad_prob = dot_nt(grad, kv)
        ds = low(prob * (grad_prob - delta))
        dq = dot(ds, kv) * 0.125
        if layer == 0:
            cosine, sine = block_tables(k, blocks[0])
            dq = rotate_block(jnp.where(lanes(dq.shape) < 64, dq, 0.0), cosine, -sine)
            k.gbytes[:, 0:128] += dot_tn(k.hot[blocks[0]], low(dq))
        for n, (i, b) in enumerate(zip(items, blocks) if layer == 1 else ()):
            outbox[i, 0 : rows // 2, :] = low(pack_left(dq[n * rows : (n + 1) * rows]))
            post.send(i, b)
        dkvt[:, 0 : count * rows] += dot_tn(q, ds) + dot_tn(grad, low(prob))

    attend_loop(layer, part, body, between)


class KeySums:
    def __init__(self, k, layer, part, post):
        rows, _ = layer_sizes(layer)
        self.k, self.layer, self.post = k, layer, post
        self.items = range(8) if layer == 1 else range(4 * part, 4 * part + 4)
        first, count = (0, 16) if layer == 1 else (8 * part, 8)
        k.dkv[layer][first : first + count] = (
            k.dkvt[layer][:, first * rows : (first + count) * rows].T.reshape(count, rows, 128)
        )
        others = other_blocks(k)
        for i in self.items:
            k.dkv_out[layer][i] = k.dkv[layer][others[i]]
        span = pl.ds(self.items[0], len(self.items))
        self.copy = Stage(
            k,
            k.dkv_in[layer].at[span],
            [(k.dkv_out[layer].at[span], k.dkv_in[layer].at[span], k.dev(1 - k.g, k.z, k.y, k.x))],
        )

    def send(self):
        k, layer = self.k, self.layer
        self.copy.wait()
        mine = my_blocks(k)
        for i in self.items:
            k.kvbox[layer][i] = low(k.dkv[layer][mine[i]] + k.dkv_in[layer][i])
            self.post.send(i, mine[i])


def send_rows(k, hidden):
    layer = 1
    rows, pad = layer_sizes(layer)
    base = LAYER0 + layer * LAYER_ROWS
    unit, _ = norm_parts(hidden)
    normed = low(unit * k.gain[2 * layer : 2 * layer + 1, :])
    k.hold[layer].normed[...] = normed
    cosine, sine = k.cos[layer][...], k.sin[layer][...]
    cos_kv, sin_kv = kv_tables(cosine, sine)
    sendbox = k.sendbox[layer]
    for part in range(3):
        joined = dot(normed, block(k, base + QKV + 16 * part))
        for n in range(4):
            piece = joined[:, 128 * n : 128 * n + 128]
            if part == 0:
                piece = rotate_block(piece, cosine, sine)
                sendbox[2 * n, 0 : rows // 2, :] = low(pack_pair(piece, 0))
                sendbox[2 * n + 1, 0 : rows // 2, :] = low(pack_pair(piece, 1))
            else:
                sendbox[4 * part - 4 + n, pad : pad + rows, :] = low(rotate_block(piece, cos_kv, sin_kv))
    inbox = k.inbox[layer]
    out = ToHeads(k, sendbox, inbox)
    out.send()
    point(k, F1_SENT)
    sent, shared = sem(k), [sem(k), sem(k)]
    mine = my_blocks(k)
    for part in range(2):
        if part == 1:
            point(k, F1_TAKE)
        out.take(part)
        for b in mine[4 * part : 4 * part + 4]:
            ref = inbox.at[b, pl.ds(pad, rows)]
            remote(ref, ref, sent, shared[part], k.dev(1 - k.g, k.z, k.y, k.x)).start()
    point(k, F1_GOT)
    k.pending += [out.done, lambda: drain(sent, inbox.at[pl.ds(0, 8), pl.ds(pad, rows)])]
    return shared


def layer_ahead(k, layer, hidden):
    rows, pad = layer_sizes(layer)
    base = LAYER0 + layer * LAYER_ROWS
    hold = k.hold[layer]
    home = k.home[layer]
    if layer == 0:
        point(k, F0_GOT)
        shared = []
    else:
        hold.hidden[...] = hidden
        shared = send_rows(k, hidden)
    back = FromHeads(k, k.abox[layer], home)
    for part in range(2 - layer):
        for semaphore in shared:
            drain(semaphore, k.inbox[layer].at[pl.ds(0, 4), pl.ds(pad, rows)])
        attention_forward(k, layer, part, back, lambda: point(k, (F0_MID0, F0_MID1)[part]))
        point(k, (F0_PART0, F0_PART1)[part] if layer == 0 else F1_PART0)
    back.take()
    point(k, (F0_HOME, F1_HOME)[layer])
    if layer == 1:
        point(k, F1_OUT)
    for n in range(4):
        pair = unpack_pair(
            home[2 * n].astype(F32)[: rows // 2], home[2 * n + 1].astype(F32)[: rows // 2]
        )
        hold.flat[:, 128 * n : 128 * n + 128] = low(pair)
    middle = hidden + dot(hold.flat[...], block(k, base + OUT))
    hold.middle[...] = middle
    unit, _ = norm_parts(middle)
    second = low(unit * k.gain[2 * layer + 1 : 2 * layer + 2, :])
    hold.second[...] = second
    for j in range(4):
        pre = dot(second, block(k, base + UP + 16 * j))
        hold.pre[:, 512 * j : 512 * j + 512] = pre
        hold.act[:, 512 * j : 512 * j + 512] = low(gelu(pre))
    point(k, (F0_UP, F1_UP)[layer])
    need(k, base + DOWN, 64)
    falls = k.pk[:, :, :, :, base + DOWN : base + DOWN + 64, :].reshape(2048, 512)
    output = hold.middle[...] + dot(hold.act[...], falls)
    back.done()
    for done in k.pending:
        done()
    k.pending = []
    return output


def layer_back(k, layer, grad_out):
    rows, pad = layer_sizes(layer)
    base = LAYER0 + layer * LAYER_ROWS
    hold = k.hold[layer]
    fall = low(grad_out)
    grad_second = jnp.zeros((rows, D), F32)
    second = hold.second[...]
    for c in range(4):
        cols = slice(512 * c, 512 * c + 512)
        if layer == 1:
            put_down(k, base + DOWN, c, dot_tn(hold.act[:, cols], fall))
        grad_act = dot_nt(fall, down_block(k, base + DOWN, c))
        grad_pre = low(grad_act * gelu_grad(hold.pre[:, cols]))
        if layer == 1:
            put_block(k, base + UP + 16 * c, dot_tn(second, grad_pre))
        else:
            hold.gpre[:, cols] = grad_pre
        grad_second = grad_second + dot_nt(grad_pre, block(k, base + UP + 16 * c))
    if layer == 1:
        point(k, B1_FF)
    gain = k.gain[2 * layer + 1 : 2 * layer + 2, :]
    grad_mid, k.gain_grads[2 * layer + 1] = norm_back(hold.middle[...], gain, grad_second)
    grad_middle = grad_out + grad_mid
    hold.middle[...] = grad_middle
    proj = low(grad_middle)
    if layer == 1:
        put_block(k, base + OUT, dot_tn(hold.flat[...], proj))
    grad_att = dot_nt(proj, block(k, base + OUT))
    gsend = k.gsend[layer]
    for n in range(4):
        piece = grad_att[:, 128 * n : 128 * n + 128]
        gsend[2 * n, 0 : rows // 2, :] = low(pack_pair(piece, 0))
        gsend[2 * n + 1, 0 : rows // 2, :] = low(pack_pair(piece, 1))
    out = ToHeads(k, gsend, k.gbox[layer])
    out.send()
    if layer == 0:
        put_block(k, base + OUT, dot_tn(hold.flat[...], proj))
        for c in range(4):
            cols = slice(512 * c, 512 * c + 512)
            put_down(k, base + DOWN, c, dot_tn(hold.act[:, cols], fall))
            put_block(k, base + UP + 16 * c, dot_tn(second, hold.gpre[:, cols]))
        point(k, B0_FF)
    k.dkvt[layer][...] = jnp.zeros_like(k.dkvt[layer])
    point(k, (B0_SENT, B1_SENT)[layer])
    if layer == 0:
        return head_grads(k, out)
    back = k.back[layer]
    home_q = FromHeads(k, k.dbox[layer], back)
    home_kv = FromHeads(k, k.kvbox[layer], k.kvback[layer])
    out.take(0)
    out.take(1)
    attention_backward(k, layer, 0, home_q)
    sums = KeySums(k, layer, 0, home_kv)
    point(k, B1_PART0)
    sums.send()
    point(k, B1_SUMS)
    home_q.take()
    cosine, sine = k.cos[layer][...], k.sin[layer][...]
    cos_kv, sin_kv = kv_tables(cosine, sine)
    for part in range(3):
        if part == 1:
            home_kv.take()
            point(k, B1_HOME)
        for n in range(4):
            if part == 0:
                piece = unpack_pair(
                    back[2 * n].astype(F32)[: rows // 2],
                    back[2 * n + 1].astype(F32)[: rows // 2],
                )
                piece = rotate_block(piece, cosine, -sine)
            else:
                piece = k.kvback[layer][4 * part - 4 + n].astype(F32)
                piece = rotate_block(piece, cos_kv, -sin_kv)
            hold.gj[:, 512 * part + 128 * n : 512 * part + 128 * n + 128] = low(piece)
    grad_normed = jnp.zeros((rows, D), F32)
    for part in range(3):
        gj = hold.gj[:, 512 * part : 512 * part + 512]
        grad_normed = grad_normed + dot_nt(gj, block(k, base + QKV + 16 * part))
    gain = k.gain[2 * layer : 2 * layer + 1, :]
    grad_in, k.gain_grads[2 * layer] = norm_back(hold.hidden[...], gain, grad_normed)
    return hold.middle[...] + grad_in, (out, home_q, home_kv)


def head_grads(k, out):
    own = dot_tn(byte_matrix(k.own_ids), low(k.hold[0].middle[...]))
    k.tgrad[...] = own
    k.gbytes[...] = jnp.zeros_like(k.gbytes)
    for part in (1, 0):
        out.take(part)
        attention_backward(k, 0, part, None, lambda: point(k, (B0_MID0, B0_MID1)[part]))
        point(k, (B0_PART0, B0_PART1)[part])
        sums = k.dkvt[0][:, 1152 * part : 1152 * part + 1152].T
        for i in range(8):
            cosine, sine = kv_tables(*block_tables(k, 8 * part + i))
            k.gkv[144 * i : 144 * i + 144, :] = low(rotate_block(sums[144 * i : 144 * i + 144], cosine, -sine))
        k.gbytes[:, 128:256] += dot_tn(k.hot[8 * part : 8 * part + 8].reshape(1152, 256), k.gkv[...])
        point(k, (B0_KEYS0, B0_KEYS1)[part])
    gbytes = low(k.gbytes[...])
    grad, k.gain_grads[0] = norm_back(k.table[...], k.gain[0:1, :], dot_nt(gbytes, k.wh[...]))
    gains = jnp.concatenate(k.gain_grads + [jnp.zeros((3, D), F32)], axis=0)
    gains = jnp.where(device_lanes(), jnp.broadcast_to(gains[None], (32, 8, 512)), 0.0).reshape(256, 512)
    gains = dot(low(gains), low(lane_copies((512, 128), 1))).reshape(32, 8, 128)
    gains = jnp.concatenate([gains, jnp.zeros((32, 8, 128), F32)], axis=1)
    heads = dot_tn(k.normed[...], gbytes).reshape(32, 16, 256)
    k.headgrad[:, :, 0:128] = low(heads[:, :, 0:128] + gains)
    k.headgrad[:, :, 128:256] = low(heads[:, :, 128:256])
    stage = Stage(
        k,
        k.headgot,
        [(k.headgrad.at[pl.ds(16 * (1 - k.g), 16)], k.headgot, k.dev(1 - k.g, k.z, k.y, k.x))],
    )
    total = k.tgrad[...] + grad
    total = jnp.concatenate([total[:, 0:256].reshape(32, 8, 256), total[:, 256:512].reshape(32, 8, 256)], axis=1)
    k.gr[:, :, :, :, EG : EG + 16, 0:256] = low(total).reshape(2, 4, 2, 2, 16, 256)
    return stage, (out,)


def send_head_grads(k, stage):
    stage.wait()
    total = k.headgrad[pl.ds(16 * k.g, 16)].astype(F32) + k.headgot[...].astype(F32)
    k.headsum[...] = low(total)
    k.headback[k.s] = k.headsum[k.s]
    k.head_sems = [sem(k), sem(k)]
    around(k, lambda c: k.headsum.at[c], lambda c: k.headback.at[c], *k.head_sems)


def store_heads(k):
    for semaphore in k.head_sems:
        drain(semaphore, k.headback.at[pl.ds(0, 15)])
    for pair in range(4):
        even, odd = (k.headback[h].astype(F32) + k.headback[8 + h].astype(F32) for h in (2 * pair, 2 * pair + 1))
        left = lanes((16, 128)) < 64
        query = jnp.where(left, even[:, 0:128], roll64(odd[:, 0:128]))
        keys, vals = pair_kv(even[:, 128:256], odd[:, 128:256])
        for at, value in ((0, query), (512, keys), (1024, vals)):
            square(k, value)
            k.s_qkv[0, :, at + 128 * pair : at + 128 * pair + 128] = value
    flush(k, "qkv", 0)
    gains = sum(k.headback[c].astype(F32)[0:8, 0:128] for c in range(16))
    row, column = lax.broadcasted_iota(jnp.int32, (128, 16), 0), lax.broadcasted_iota(jnp.int32, (128, 16), 1)
    gains = exact(gains, jnp.where(row - 64 == column, 1.0, 0.0))[0:5]
    square(k, gains)
    k.s_gains[...] = gains
    flush(k, "gains")


def finish_back(k, posts):
    for post in posts:
        post.done()


def byte_matrix(ids):
    return low(jnp.where(lanes((ids.shape[0], 256)) == ids, 1.0, 0.0))


def forward_backward(k):
    rows, short = 144, 48
    k.gain_grads, k.pending = [None] * 5, []
    rotary_tables(k)
    stage = take_heads(k)
    point(k, F0_HEADS)
    stage.wait()
    byte_rows(k)
    head_rows(k)
    columns = k.columns[...].T
    k.own_ids, targets = columns[0:rows, 0:1].astype(jnp.int32), columns[0:rows, 1:2].astype(jnp.int32)
    first_in = dot(byte_matrix(k.own_ids), low(k.table[...]))
    first = layer_ahead(k, 0, first_in)
    k.shift[8 : 8 + rows, :] = first
    rim = remote(
        k.shift.at[pl.ds(rows, 8)], k.shift.at[pl.ds(0, 8)], sem(k), sem(k), (k.g, lax.rem(k.s + 1, 16))
    )

    @pl.when(k.s < 15)
    def _():
        rim.start()

    point(k, F0_RIM)

    @pl.when(k.s > 0)
    def _():
        rim.wait_recv()

    @pl.when(k.s == 0)
    def _():
        k.shift[0:8, :] = jnp.zeros((8, D), F32)

    @pl.when(k.s < 15)
    def _():
        rim.wait_send()

    def pool_matrix(shape, offset, axis):
        j = lax.broadcasted_iota(jnp.int32, shape, axis)
        t = lax.broadcasted_iota(jnp.int32, shape, 1 - axis) - offset
        return jnp.where((t >= 3 * j) & (t < 3 * j + 3), 1.0, 0.0)

    pooled = exact(pool_matrix((short, rows + 8), 6, 0), k.shift[...]) / 3.0
    point(k, F0_END)
    short_out = layer_ahead(k, 1, pooled)
    upsampled = k.shift[8 : 8 + rows, :] + exact(pool_matrix((rows, short), 0, 1), short_out)
    gain = k.gain[4:5, :]
    unit, _ = norm_parts(upsampled)
    final = low(unit * gain)
    head = k.pk[:, :, :, :, EG : EG + 16, 256:512].reshape(512, 256)
    logits = dot(final, head)
    top = jnp.max(logits, axis=-1, keepdims=True)
    log_total = top + jnp.log(jnp.sum(jnp.exp(logits - top), axis=-1, keepdims=True))
    hot = jnp.where(lanes((rows, 256)) == targets, 1.0, 0.0)
    picked = jnp.sum(hot * logits, axis=-1, keepdims=True)
    position = k.s * rows + lax.broadcasted_iota(jnp.int32, (rows, 1), 0)
    length = jnp.zeros((rows, 1), F32)
    begin = jnp.int32(0)
    for i in range(8):
        size = k.lengths[0, i]
        inside = (position >= begin) & (position < begin + size)
        length = jnp.where(inside, size.astype(F32), length)
        begin = begin + size
    k.loss = jnp.sum((log_total - picked) / length, axis=0, keepdims=True)
    grad_logits = low((jnp.exp(logits - log_total) - hot) / length)
    k.gr[:, :, :, :, EG : EG + 16, 256:512] = low(dot_tn(final, grad_logits)).reshape(2, 4, 2, 2, 16, 256)
    grad_final = dot_nt(grad_logits, head)
    grad_up, k.gain_grads[4] = norm_back(upsampled, gain, grad_final)
    k.up[...] = grad_up
    grad_short = exact(pool_matrix((short, rows), 0, 0), grad_up)
    grad_pooled, posts = layer_back(k, 1, grad_short)
    k.pool[0:short, :] = grad_pooled
    rim2 = remote(
        k.pool.at[pl.ds(0, 8)], k.pool.at[pl.ds(short, 8)], sem(k), sem(k), (k.g, lax.rem(k.s + 15, 16))
    )

    @pl.when(k.s > 0)
    def _():
        rim2.start()

    for part in range(3):
        gj = k.hold[1].gj[:, 512 * part : 512 * part + 512]
        put_block(k, LAYER0 + LAYER_ROWS + QKV + 16 * part, dot_tn(k.hold[1].normed[...], gj))
    finish_back(k, posts)
    point(k, B1_RIM)

    @pl.when(k.s < 15)
    def _():
        rim2.wait_recv()

    @pl.when(k.s == 15)
    def _():
        k.pool[short : short + 8, :] = jnp.zeros((8, D), F32)

    @pl.when(k.s > 0)
    def _():
        rim2.wait_send()

    t = lax.broadcasted_iota(jnp.int32, (rows, short + 8), 0)
    j = lax.broadcasted_iota(jnp.int32, (rows, short + 8), 1)
    spread = jnp.where((t + 2 >= 3 * j) & (t + 2 < 3 * j + 3), 1.0, 0.0)
    grad_first = k.up[...] + exact(spread, k.pool[...] / 3.0)
    stage, posts = layer_back(k, 0, grad_first)
    k.made.add(EG)
    point(k, B0_END)
    send_head_grads(k, stage)
    finish_back(k, posts)


def add_into(ref, other):
    ref[...] = low(ref[...].astype(F32) + other[...].astype(F32))


def reduce_piece(k, name, r0, rm, r1):
    g, z, y, x, dev, gr = k.g, k.z, k.y, k.x, k.dev, k.gr
    a, b, every = pl.ds(r0, rm - r0), pl.ds(rm, r1 - rm), pl.ds(r0, r1 - r0)
    assert k.made.issuperset(range(r0, r1, 16)), name
    sent = sem(k)
    waiting = Stage(
        k, k.rc.at[:, :, :, every], [(gr.at[1 - g, :, :, :, every], k.rc.at[:, :, :, every], dev(1 - g, z, y, x))], sent
    )
    yield
    waiting.wait()


    @pl.loop(0, 16)
    def _(n):
        place = (n // 4, lax.rem(n // 2, 2), lax.rem(n, 2), every)
        add_into(gr.at[(g,) + place], k.rc.at[place])

    def wait(waiting):
        waiting.wait()

    last = name in Z_FIRST
    planes, depth = (pl.ds(z, 1), 1) if last else (pl.ds(0, 4), 4)
    slots = pl.ds(0, depth)

    def plane(n):
        return z if last else n

    def across():
        waiting = Stage(
            k,
            k.r2.at[slots, :, every],
            [
                (gr.at[g, planes, :, 1 - x, a], k.r2.at[slots, :, a], dev(g, z, y, 1 - x)),
                (gr.at[g, planes, 1 - y, :, b], k.r2.at[slots, :, b], dev(g, z, 1 - y, x)),
            ],
            sent,
        )
        yield
        wait(waiting)

        @pl.loop(0, 2 * depth)
        def _(n):
            m, w = n // 2, lax.rem(n, 2)
            add_into(gr.at[g, plane(m), w, x, a], k.r2.at[m, w, a])
            if r1 > rm:
                add_into(gr.at[g, plane(m), y, w, b], k.r2.at[m, w, b])

        waiting = Stage(
            k,
            k.r1.at[slots, every],
            [
                (gr.at[g, planes, 1 - y, x, a], k.r1.at[slots, a], dev(g, z, 1 - y, x)),
                (gr.at[g, planes, y, 1 - x, b], k.r1.at[slots, b], dev(g, z, y, 1 - x)),
            ],
            sent,
        )
        yield
        wait(waiting)

        @pl.loop(0, depth)
        def _(n):
            add_into(gr.at[g, plane(n), y, x, every], k.r1.at[n, every])

    def along():
        moves = []
        for n in (2, 1, 3):
            to = lax.rem(z + n, 4)
            if last:
                moves.append((gr.at[g, to, :, :, every], k.rl.at[n - 1], dev(g, to, y, x)))
            else:
                moves.append((gr.at[g, to, y, x, every], k.rz.at[n - 1, every], dev(g, to, y, x)))
        waiting = Stage(k, k.rl if last else k.rz.at[:, every], moves, sent)
        yield
        wait(waiting)
        if last:
            for n in range(4):
                ref = gr.at[g, z, n // 2, n % 2, every]
                total = ref[...].astype(F32)
                for slot in range(3):
                    total = total + k.rl[slot, n // 2, n % 2].astype(F32)
                ref[...] = low(total)

    for way in (along, across) if last else (across, along):
        yield from way()
    if last:
        k.rz[:, every] = jnp.zeros((3, r1 - r0, D), LOW)
    k.summed.update(range(r0, r1, 16))
    yield


def own_sum(k, row, count):
    rows = pl.ds(row, count)
    v = k.gr[k.g, k.z, k.y, k.x, rows].astype(F32)
    for i in range(3):
        v = v + k.rz[i, rows].astype(F32)
    return v


def square(k, v):
    k.sq = k.sq + jnp.sum(jnp.sum(v * v, axis=1, keepdims=True), axis=0, keepdims=True)


def flush(k, name, layer=None):
    src, dst = getattr(k, "s_" + name), getattr(k, "g_" + name)
    if layer is not None:
        src, dst = src.at[layer], dst.at[layer]
    copy = pltpu.make_async_copy(src, dst, sem(k))
    copy.start()
    k.flushed.append(copy)


def store_qkv(k, layer):
    v = own_sum(k, LAYER0 + layer * LAYER_ROWS + QKV, 48)
    square(k, v)
    k.s_qkv[layer, :, 0:512] = v[0:16]
    for pair in range(4):
        row, col = 16 + 16 * (pair // 2), 256 * (pair % 2)
        even = v[row : row + 16, col : col + 128]
        odd = v[row : row + 16, col + 128 : col + 256]
        left = lanes(even.shape) < 64
        k.s_qkv[layer, :, 512 + 128 * pair : 640 + 128 * pair] = jnp.where(left, even, roll64(odd))
        k.s_qkv[layer, :, 1024 + 128 * pair : 1152 + 128 * pair] = jnp.where(left, roll64(even), odd)
    flush(k, "qkv", layer)


def store_out(k, layer):
    v = own_sum(k, LAYER0 + layer * LAYER_ROWS + OUT, 16)
    square(k, v)
    k.s_out[layer] = v
    flush(k, "out", layer)


def store_up(k, layer):
    v = own_sum(k, LAYER0 + layer * LAYER_ROWS + UP, 64)
    square(k, v)
    for j in range(4):
        k.s_up[layer, :, 512 * j : 512 * j + 512] = v[16 * j : 16 * j + 16]
    flush(k, "up", layer)


def store_down(k, layer):
    v = own_sum(k, LAYER0 + layer * LAYER_ROWS + DOWN, 64)
    square(k, v)
    k.s_down[layer] = v
    flush(k, "down", layer)


def store_rest(k):
    v = own_sum(k, EG, 16)
    square(k, v)
    k.s_embed[:, 0:256] = v[0:8, 0:256]
    k.s_embed[:, 256:512] = v[8:16, 0:256]
    k.s_head[...] = v[:, 256:512]
    flush(k, "embed")
    flush(k, "head")


def store_ready(k):
    stores = [(range(EG, EG + 16), store_rest, ())]
    for layer in range(2):
        base = LAYER0 + layer * LAYER_ROWS
        if layer == 1:
            stores.append((range(base + QKV, base + QKV + 48), store_qkv, (layer,)))
        stores.append((range(base + OUT, base + OUT + 16), store_out, (layer,)))
        stores.append((range(base + UP, base + UP + 64), store_up, (layer,)))
        stores.append((range(base + DOWN, base + DOWN + 64), store_down, (layer,)))
    for rows, store, args in stores:
        if rows.start not in k.stored and k.summed.issuperset(range(rows.start, rows.stop, 16)):
            k.stored.add(rows.start)
            store(k, *args)


def finish_grads(k):
    g = k.g
    point(k, TAIL)
    for name in PIECES:
        for _ in k.reduces[name]:
            store_ready(k)
    store_ready(k)
    store_heads(k)
    lane = lanes((8, 128))
    k.stat[0] = jnp.where(lane == 0, k.sq, jnp.where(lane == 1, k.loss, 0.0))
    me = g * 16 + k.s
    sent, got = sem(k), sem(k)

    @pl.loop(1, 32)
    def _(i):
        t = lax.rem(me + i, 32)
        remote(k.stat.at[0], k.stat.at[i], sent, got, (t // 16, lax.rem(t, 16))).start()

    drain(got, k.stat.at[pl.ds(1, 31)])
    drain(sent, k.stat.at[pl.ds(1, 31)])
    k.stats[...] = jnp.sum(k.stat[...], axis=0)
    wait_all(k.flushed)


IN_NAMES = (
    "ids", "targets", "lengths", "w_qkv", "w_out", "w_up", "w_down", "embed", "head", "gains",
)
OUT_NAMES = ("g_qkv", "g_out", "g_up", "g_down", "g_embed", "g_head", "g_gains", "stats")
SEMS = 128


LATER = (
    "sendbox", "inbox", "dbox", "kvbox", "back", "kvback", "dkv", "dkv_out", "dkv_in", "h_hidden", "h_normed", "h_gj"
)


def scratch_shapes():
    shapes = {
        "pk": ((2, 4, 2, 2, ROWS, D), LOW),
        "gr": ((2, 4, 2, 2, ROWS, D), LOW),
        "rc": ((4, 2, 2, ROWS, D), LOW),
        "r2": ((4, 2, ROWS, D), LOW),
        "r1": ((4, ROWS, D), LOW),
        "rz": ((3, ROWS, D), LOW),
        "rl": ((3, 2, 2, max([16] + [PIECES[n][2] - PIECES[n][0] for n in Z_FIRST]), D), LOW),
        "gain": ((8, D), F32),
        "shift": ((152, D), F32),
        "pool": ((56, D), F32),
        "up": ((144, D), F32),
        "stat": ((32, 8, 128), F32),
        "columns": ((128, 256), F32),
        "headout": ((8, 16, 256), LOW),
        "wbox": ((32, 16, 256), LOW),
        "wh": ((D, 256), LOW),
        "table": ((256, D), F32),
        "normed": ((256, D), LOW),
        "hot": ((16, 144, 256), LOW),
        "q0": ((16, 144, 128), LOW),
        "kv0": ((16, 144, 128), LOW),
        "cosb": ((16, 128), F32),
        "sinb": ((16, 128), F32),
        "tgrad": ((256, D), F32),
        "gbytes": ((256, 256), F32),
        "gkv": ((1152, 128), LOW),
        "headgrad": ((32, 16, 256), LOW),
        "headgot": ((16, 16, 256), LOW),
        "headsum": ((16, 16, 256), LOW),
        "headback": ((16, 16, 256), LOW),
        "s_qkv": ((2, 16, 3 * D), F32),
        "s_out": ((2, 16, D), F32),
        "s_up": ((2, 16, 4 * D), F32),
        "s_down": ((2, 64, D), F32),
        "s_embed": ((8, D), F32),
        "s_head": ((16, 256), F32),
        "s_gains": ((5, 16), F32),
    }
    for layer in range(2):
        rows, pad = layer_sizes(layer)
        for name, shape, kind in (
            ("cos", (rows, 128), F32),
            ("sin", (rows, 128), F32),
            ("sendbox", (8, pad + rows, 128), LOW),
            ("inbox", (16, pad + rows, 128), LOW),
            ("abox", (8, pad, 128), LOW),
            ("home", (8, pad, 128), LOW),
            ("gsend", (8, pad, 128), LOW),
            ("gbox", (16, pad, 128), LOW),
            ("dbox", (8, pad, 128), LOW),
            ("kvbox", (8, rows, 128), LOW),
            ("back", (8, pad, 128), LOW),
            ("kvback", (8, rows, 128), LOW),
            ("lse", (8, rows, 128), F32),
            ("att", (8, rows, 128), F32),
            ("dkvt", (128, 16 * rows), F32),
            ("dkv", (16, rows, 128), F32),
            ("dkv_out", (8, rows, 128), F32),
            ("dkv_in", (8, rows, 128), F32),
            ("h_hidden", (rows, D), F32),
            ("h_normed", (rows, D), LOW),
            ("h_flat", (rows, D), LOW),
            ("h_middle", (rows, D), F32),
            ("h_second", (rows, D), LOW),
            ("h_pre", (rows, 4 * D), F32),
            ("h_act", (rows, 4 * D), LOW),
            ("h_gj", (rows, 3 * D), LOW),
            ("h_gpre", (rows, 4 * D), LOW),
        ):
            if layer == 1 or name not in LATER:
                shapes[name + str(layer)] = (shape, kind)
    return shapes


SCRATCH = scratch_shapes()
PER_LAYER = (
    "cos", "sin", "sendbox", "inbox", "abox", "home", "gsend", "gbox", "dbox", "back", "lse", "att", "dkvt", "dkv",
    "dkv_out", "dkv_in", "kvbox", "kvback",
)
HELD = ("hidden", "normed", "flat", "middle", "second", "pre", "act", "gj", "gpre")


def update_kernel(*refs):
    stats, sources, outs, loss_ref, norm_ref = refs[0], refs[1:29], refs[29:50], refs[50], refs[51]
    held, made, sems, out_sems = refs[52:59], refs[59:66], refs[66], refs[67]
    order = (4, 5, 6, 1, 0, 2, 3)
    for i in order:
        start_all([pltpu.make_async_copy(sources[7 * j + i], held[i].at[j], sems.at[i]) for j in range(4)])
    norm = jnp.sqrt(stats[0:1, 0:1])
    loss_ref[...] = stats[0:1, 1:2]
    norm_ref[...] = norm
    clip = jnp.minimum(1.0, CLIP_NORM / norm)
    for i in order:
        drain(sems.at[i], held[i])
        gradient, master, first, second = (held[i][j] for j in range(4))
        gradient = gradient * clip
        first = BETA_ONE * first + (1.0 - BETA_ONE) * gradient
        second = BETA_TWO * second + (1.0 - BETA_TWO) * gradient * gradient
        step = first * (1.0 / (1.0 - BETA_ONE**STEP))
        spread = jnp.sqrt(second * (1.0 / (1.0 - BETA_TWO**STEP))) + EPSILON
        results = (master - STEP_RATES[i] * (step / spread + WEIGHT_DECAYS[i] * master), first, second)
        for j in range(3):
            made[i][j] = results[j]
        start_all([pltpu.make_async_copy(made[i].at[j], outs[7 * j + i], out_sems.at[i]) for j in range(3)])
    for i in order:
        drain(out_sems.at[i], made[i])


def on_device_fast(byte_ids, targets, item_lengths, *arrays):
    masters, firsts, seconds = arrays[0:7], arrays[7:14], arrays[14:21]
    vmem, anywhere = pl.BlockSpec(memory_space=pltpu.VMEM), pl.BlockSpec(memory_space=pl.ANY)
    shard_shapes = [jax.ShapeDtypeStruct(master.shape, F32) for master in masters]
    outs = pl.pallas_call(
        kernel,
        name="step",
        out_shape=shard_shapes + [jax.ShapeDtypeStruct((8, 128), F32)],
        in_specs=[vmem, vmem, pl.BlockSpec(memory_space=pltpu.SMEM)] + [vmem] * 7,
        out_specs=[anywhere] * 7 + [vmem],
        scratch_shapes=[pltpu.VMEM(shape, kind) for shape, kind in SCRATCH.values()]
        + [pltpu.SemaphoreType.DMA((SEMS,))],
        compiler_params=pltpu.CompilerParams(collective_id=0, has_side_effects=True, vmem_limit_bytes=63 << 20),
    )(byte_ids, targets, item_lengths, *masters)
    grads, stats = outs[:7], outs[7]
    results = pl.pallas_call(
        update_kernel,
        name="update",
        out_shape=shard_shapes * 3 + [jax.ShapeDtypeStruct((1, 1), F32)] * 2,
        in_specs=[vmem] + [anywhere] * 28,
        out_specs=[anywhere] * 21 + [vmem] * 2,
        scratch_shapes=[pltpu.VMEM((count, *shard.shape), F32) for count in (4, 3) for shard in shard_shapes]
        + [pltpu.SemaphoreType.DMA((7,)), pltpu.SemaphoreType.DMA((7,))],
        compiler_params=pltpu.CompilerParams(vmem_limit_bytes=63 << 20),
    )(stats, *grads, *masters, *firsts, *seconds)
    return (results[21].reshape(()), results[22].reshape(()), *results[:21])


def solution(mesh):
    tuned = mesh.shape["dp"] == 2 and mesh.shape["seq"] == 16
    row = P(None, ("dp", "seq"), None)
    flat = P(("dp", "seq"), None)
    shards = (row, row, row, row, flat, flat, P(None, ("dp", "seq")))
    return jax.shard_map(
        on_device_fast if tuned else on_device_general,
        mesh=mesh,
        in_specs=(P("dp", "seq"), P("dp", "seq"), P("dp", None)) + shards * 3,
        out_specs=(P(), P()) + shards * 3,
        check_vma=False,
    )
```
